32 devices in a mesh: batch: 8 (over z, y), seq: 4 (over x, core).
Axes of the slice: x: 2, y: 2, z: 4, core: 2. Of those that a mesh axis runs over, the one named last changes fastest.
Arguments:
- layer_input: float32 [16, 512, 768], P('batch', 'seq'), may hold values from -6 to 6
- lengths: int32 [16], P('batch'), may hold values from 1 to 512, as said below
- attn_weight: float32 [4, 768, 768], P(None, 'batch')
- up_weight: float32 [768, 3072], P('batch'), may hold values from -0.21875 to 0.21875
- down_weight: float32 [3072, 768], P('batch'), may hold values from -0.109375 to 0.109375
- vectors: float32 [12, 768], P(None, 'batch')
- attn_moment: float32 [4, 768, 768], P(None, 'batch'), may hold values from -96 to 96
- up_moment: float32 [768, 3072], P('batch'), may hold values from -96 to 96
- down_moment: float32 [3072, 768], P('batch'), may hold values from -96 to 96
- vector_moment: float32 [12, 768], P(None, 'batch'), may hold values from -192 to 192
- out_grad: float32 [16, 512, 768], P('batch', 'seq'), may hold values from -6 to 6
- pool_grad: float32 [16, 768], P('batch', 'seq'), may hold values from -6 to 6
Outputs:
- layer_output: float32 [16, 512, 768], P('batch', 'seq')
- pooled: float32 [16, 768], P('batch', 'seq')
- input_grad: float32 [16, 512, 768], P('batch', 'seq')
- attn_grad: float32 [4, 768, 768], P(None, 'batch')
- up_grad: float32 [768, 3072], P('batch')
- down_grad: float32 [3072, 768], P('batch')
- vector_grad: float32 [12, 768], P(None, 'batch')
- attn_moment_new: float32 [4, 768, 768], P(None, 'batch')
- up_moment_new: float32 [768, 3072], P('batch')
- down_moment_new: float32 [3072, 768], P('batch')
- vector_moment_new: float32 [12, 768], P(None, 'batch')
- attn_new: float32 [4, 768, 768], P(None, 'batch')
- up_new: float32 [768, 3072], P('batch')
- down_new: float32 [3072, 768], P('batch')
- vectors_new: float32 [12, 768], P(None, 'batch')
The draws below stay inside these ranges and needn't reach their ends.
Inputs may be any that keep to these rules, and one draw needn't show every extreme that they name: `lengths`: among the 2 aligned rows of each batch index one row has length 512.
All inputs are finite; a program needn't handle non-finite values.
Results may differ from the reference program's by a relative error of at most 0.015.
The reference program's roundings to bfloat16 on the way count: a program that leaves them out, or rounds other values in their place, can miss the bound.
Values may be sent and summed in bfloat16 or wider, within the bound.
A program may use at most 320 MiB of HBM per device.

```python
import math
import jax
import jax.numpy as jnp
from jax import lax

D = 768
H = 12
HD = 64
FF = 3072
S = 512
B_DEV = 2
NS = 5
ROWS = 16
NVEC = 12


def draw_lengths(key, part):
    key = jax.random.fold_in(key, 11)
    draw_one, draw_two, draw_three = jax.random.split(key, 3)
    exponent = jax.random.randint(draw_one, (ROWS,), 0, 6)
    ceiling = jnp.minimum(jnp.left_shift(jnp.int32(16), exponent), S)
    raw_bits = jax.random.randint(draw_two, (ROWS,), 0, 1 << 30)
    short_len = raw_bits % ceiling + 1
    chosen = jax.random.randint(draw_three, (ROWS // B_DEV,), 0, B_DEV)
    position = jnp.arange(ROWS) % B_DEV
    longest = position == jnp.repeat(chosen, B_DEV)
    return jnp.where(longest, S, short_len).astype(jnp.int32)


def draw_attn_weight(key, part):
    key = jax.random.fold_in(key, 12)
    base_draw = jnp.clip(jax.random.normal(key, (4, D, D), jnp.float32), -3.0, 3.0)
    lift_scale = jnp.where(jnp.arange(4)[:, None, None] == 3, 4.0, 1.0)
    return (base_draw * lift_scale * D ** (-0.5)).astype(jnp.float32)


def draw_vectors(key, part):
    key = jax.random.fold_in(key, 13)
    base_draw = jnp.clip(0.35 * jax.random.normal(key, (NVEC, D), jnp.float32), -1.4, 1.4)
    row_number = jnp.arange(NVEC)[:, None]
    gain_rows = (row_number == 3) | (row_number == 5)
    return jnp.where(gain_rows, 1.0 + 0.5 * base_draw, base_draw).astype(jnp.float32)


def block_scale(stream_key, extent, shards, least, largest):
    gain, own = 1.0, jax.random.fold_in(stream_key, 6)
    for dim, blocks in shards:
        steps = jnp.exp(jax.random.uniform(jax.random.fold_in(own, dim), (blocks,), jnp.float32, least / len(shards), largest / len(shards)))
        gain = gain * jnp.repeat(steps, extent[dim] // blocks).reshape([-1 if axis == dim else 1 for axis in range(len(extent))])
    return gain


def noise(stream_key, dims, scale, limit, pieces=(), kind=jnp.bfloat16):
    factor_of = block_scale(stream_key, dims, pieces, -0.22, 0.18) if pieces else 1.0
    array = jax.random.normal(stream_key, dims, jnp.float32) * scale * factor_of
    return jnp.minimum(jnp.maximum(array, -limit), limit).astype(kind)


def setup_inputs(seed: int = 0) -> dict:
    key_of = jax.random.split(jax.random.key(seed), 13)
    layer_input = noise(key_of[0], (ROWS, S, D), 1.0, 6.0, ((0, 8), (1, 4)), jnp.float32)
    lengths = draw_lengths(jax.random.fold_in(key_of[12], 71), 0)
    attn_weight = draw_attn_weight(jax.random.fold_in(key_of[12], 71), 0)
    up_weight = noise(key_of[3], (D, FF), D ** -0.5, 0.21875, ((0, 8),), jnp.float32)
    down_weight = noise(key_of[4], (FF, D), FF ** -0.5, 0.109375, ((0, 8),), jnp.float32)
    vectors = draw_vectors(jax.random.fold_in(key_of[12], 71), 0)
    attn_moment = noise(key_of[6], (4, D, D), (4 * ROWS ** 0.5), 96.0, ((1, 8),), jnp.float32)
    up_moment = noise(key_of[7], (D, FF), (4 * ROWS ** 0.5), 96.0, ((0, 8),), jnp.float32)
    down_moment = noise(key_of[8], (FF, D), (4 * ROWS ** 0.5), 96.0, ((0, 8),), jnp.float32)
    vector_moment = noise(key_of[9], (NVEC, D), (8 * ROWS ** 0.5), 192.0, ((1, 8),), jnp.float32)
    out_grad = noise(key_of[10], (ROWS, S, D), 1.0, 6.0, ((0, 8), (1, 4)), jnp.float32)
    pool_grad = noise(key_of[11], (ROWS, D), 1.0, 6.0, ((0, 8), (1, 4)), jnp.float32)
    return {"layer_input": layer_input, "lengths": lengths, "attn_weight": attn_weight, "up_weight": up_weight, "down_weight": down_weight, "vectors": vectors, "attn_moment": attn_moment, "up_moment": up_moment, "down_moment": down_moment, "vector_moment": vector_moment, "out_grad": out_grad, "pool_grad": pool_grad}


@jax.custom_vjp
def low(v):
    return lax.optimization_barrier(v.astype(jnp.bfloat16)).astype(jnp.float32)

@jax.custom_vjp
def low_back(v):
    return v

def low_keep(v):
    return (low(v), None)

def low_pass(kept, grad):
    return (grad,)

def back_keep(v):
    return (v, None)

def back_low(kept, grad):
    return (low(grad),)
low.defvjp(low_keep, low_pass)
low_back.defvjp(back_keep, back_low)

def product(left, right):
    return jnp.dot(left, right, precision=lax.Precision.HIGHEST, preferred_element_type=jnp.float32)

def layer_norm(hidden, gain_row, shift_row):
    row_mean = lax.optimization_barrier(jnp.mean(hidden, axis=-1, keepdims=True))
    centred = hidden - row_mean
    spread = lax.rsqrt(lax.optimization_barrier(jnp.mean(centred * centred, axis=-1, keepdims=True)) + 1e-12)
    return centred * spread * gain_row + shift_row

def forward(attn_low, up_low, down_low, vector_low, group_input, group_lengths):
    attn_low = low(attn_low)
    up_low = low(up_low)
    down_low = low(down_low)
    vector_low = low(vector_low)
    row_count, row_span, model_width = group_input.shape
    tokens = group_input.reshape(row_count * row_span, model_width)
    token_low = low(tokens)
    query_block = low(low_back(product(token_low, attn_low[0]) + vector_low[0]))
    key_block = low(low_back(product(token_low, attn_low[1])))
    value_block = low(low_back(product(token_low, attn_low[2]) + vector_low[1]))
    query_heads = query_block.reshape(row_count, row_span, H, HD)
    key_heads = key_block.reshape(row_count, row_span, H, HD)
    value_heads = value_block.reshape(row_count, row_span, H, HD)
    raw_scores = jnp.einsum('rqhd,rkhd->rhqk', query_heads, key_heads, precision=lax.Precision.HIGHEST) * HD ** (-0.5)
    key_valid = jnp.arange(row_span, dtype=jnp.int32)[None, :] < group_lengths[:, None]
    scores = jnp.where(key_valid[:, None, None, :], low_back(raw_scores), -1e+30)
    softmax_prob = low(jax.nn.softmax(scores, axis=-1))
    mixed_out = jnp.einsum('rhqk,rkhd->rqhd', softmax_prob, value_heads, precision=lax.Precision.HIGHEST)
    context = low(low_back(mixed_out.reshape(row_count * row_span, model_width)))
    branch = low_back(product(context, attn_low[3]) + vector_low[2])
    normed_one = layer_norm(tokens + branch, vector_low[3], vector_low[4])
    pre_act = low_back(product(low(normed_one), up_low) + vector_low[8:].reshape(-1))
    act_low = low(jax.nn.gelu(pre_act, approximate=False))
    down_branch = low_back(product(act_low, down_low) + vector_low[7])
    output = layer_norm(normed_one + down_branch, vector_low[5], vector_low[6])
    out_rows = output.reshape(row_count, row_span, model_width)
    live_mask = key_valid.astype(out_rows.dtype)
    pooled = lax.optimization_barrier(jnp.sum(out_rows * live_mask[..., None], axis=1)) / group_lengths[:, None].astype(out_rows.dtype)
    return (out_rows, pooled)

def orthogonal(matrix):
    is_tall = matrix.shape[0] > matrix.shape[1]
    current = matrix.T if is_tall else matrix
    current = current / (jnp.sqrt(jnp.sum(current * current)) + 1e-07)
    for ns_turn in range(NS):
        gram_matrix = product(current, current.T)
        poly_part = -4.775 * gram_matrix + 2.0315 * product(gram_matrix, gram_matrix)
        current = 3.4445 * current + product(poly_part, current)
    return current.T if is_tall else current

def step_size(matrix):
    return 0.5 * math.sqrt(max(1.0, matrix.shape[0] / matrix.shape[1]))

def reference(layer_input, lengths, attn_weight, up_weight, down_weight, vectors, attn_moment, up_moment, down_moment, vector_moment, out_grad, pool_grad):

    def group_step(summed, group_index):
        row_start = group_index * B_DEV
        group_input = lax.dynamic_slice_in_dim(layer_input, row_start, B_DEV, 0)
        group_lengths = lax.dynamic_slice_in_dim(lengths, row_start, B_DEV, 0)
        group_out_grad = lax.dynamic_slice_in_dim(out_grad, row_start, B_DEV, 0)
        group_pool_grad = lax.dynamic_slice_in_dim(pool_grad, row_start, B_DEV, 0)
        live_mask = (jnp.arange(S, dtype=jnp.int32)[None, :] < group_lengths[:, None]).astype(layer_input.dtype)

        def group_forward(attn_low, up_low, down_low, vector_low, block_input):
            return forward(attn_low, up_low, down_low, vector_low, block_input, group_lengths)
        (out_rows, pooled), pull_back = jax.vjp(group_forward, attn_weight, up_weight, down_weight, vectors, group_input)
        grads = pull_back((group_out_grad * live_mask[..., None], group_pool_grad))
        summed = tuple((old + new for old, new in zip(summed, grads[:4])))
        return (summed, (out_rows, pooled, grads[4]))
    start_sums = (jnp.zeros_like(attn_weight), jnp.zeros_like(up_weight), jnp.zeros_like(down_weight), jnp.zeros_like(vectors))
    summed, stacked = lax.scan(group_step, start_sums, jnp.arange(ROWS // B_DEV, dtype=jnp.int32))
    attn_grad, up_grad, down_grad, vector_grad = summed
    layer_output = stacked[0].reshape(ROWS, S, D)
    pooled = stacked[1].reshape(ROWS, D)
    input_grad = stacked[2].reshape(ROWS, S, D)
    attn_next = 0.95 * attn_moment + attn_grad
    up_next = 0.95 * up_moment + up_grad
    down_next = 0.95 * down_moment + down_grad
    attn_new = jnp.stack([attn_weight[number] - step_size(attn_next[number]) * orthogonal(attn_next[number]) for number in range(4)])
    up_new = up_weight - step_size(up_next) * orthogonal(up_next)
    down_new = down_weight - step_size(down_next) * orthogonal(down_next)
    vector_next = 0.5 * vector_moment + vector_grad
    vectors_new = vectors - 0.03 / math.sqrt(ROWS) * vector_next
    return (layer_output, pooled, input_grad, attn_grad, up_grad, down_grad, vector_grad, attn_next, up_next, down_next, vector_next, attn_new, up_new, down_new, vectors_new)
```

```python
import math

import jax
import jax.numpy as jnp
from jax import lax
from jax.experimental import pallas as pl
from jax.experimental.pallas import tpu as pltpu
from jax.sharding import PartitionSpec as P

H = 12
HD = 64
NS = 5
SEQ = 4
HEADS = H // SEQ

norm_eps = 1e-12
tiny_norm = 1e-07
matrix_decay = 0.95
vector_decay = 0.5
matrix_rate = 0.5
vector_rate = 0.03

MESH = pl.DeviceIdType.MESH
F32 = jnp.float32
BF16 = jnp.bfloat16


def coords(n):
    b = lax.axis_index("batch")
    s = lax.axis_index("seq")
    return b, s, b // 2, b % 2, n // 2


def remote(src, dst, send, recv, device):
    return pltpu.make_async_remote_copy(
        src_ref=src, dst_ref=dst, send_sem=send, recv_sem=recv, device_id=device, device_id_type=MESH
    )


class GatherBatch:
    peers = ("batch",)

    def __init__(self, n, src):
        self.n = n
        self.ins = [src]
        self.outs = [jax.ShapeDtypeStruct((n,) + src.shape, src.dtype)]
        m = n // 2
        self.scratch = [pltpu.SemaphoreType.DMA((m,))] * 4 + [pltpu.SemaphoreType.DMA]

    def run(self, src, dst, zs, zr, ys, yr, own):
        b, s, hi, lo, m = coords(self.n)
        local = pltpu.make_async_copy(src, dst.at[b], own)
        local.start()
        pair = (hi * 2 + 1 - lo, s)
        out = []
        for d in range(1, m):
            c = remote(src, dst.at[b], zs.at[d], zr.at[d], (((hi + d) % m) * 2 + lo, s))
            c.start()
            out.append(c)
        first = remote(src, dst.at[b], ys.at[0], yr.at[0], pair)
        first.start()
        yield
        passed = [first]
        for d in range(1, m):
            out[d - 1].wait_recv()
            block = ((hi + m - d) % m) * 2 + lo
            c = remote(dst.at[block], dst.at[block], ys.at[d], yr.at[d], pair)
            c.start()
            passed.append(c)
            yield
        local.wait()
        for c in passed:
            c.wait()
        for c in out:
            c.wait_send()


class ScatterBatch:
    peers = ("batch",)

    def __init__(self, n, src, wire=BF16):
        self.n = n
        self.wire = wire
        self.ins = [src]
        shape = src.shape[1:]
        self.outs = [jax.ShapeDtypeStruct(shape, F32)]
        m = n // 2
        self.scratch = [pltpu.VMEM((m,) + shape, wire)] * 4 + [pltpu.SemaphoreType.DMA((m,))] * 4

    def run(self, src, dst, ysend, yrecv, zsend, zrecv, ys, yr, zs, zr):
        b, s, hi, lo, m = coords(self.n)
        pair = (hi * 2 + 1 - lo, s)
        first = {}
        order = list(range(1, m)) + [0]
        for d in order:
            h = (hi + d) % m
            ysend[d] = src[h * 2 + 1 - lo].astype(self.wire)
            first[d] = remote(ysend.at[d], yrecv.at[d], ys.at[d], yr.at[d], pair)
            first[d].start()
        yield
        second = []
        for d in range(1, m):
            h = (hi + d) % m
            first[d].wait_recv()
            zsend[d] = (src[h * 2 + lo] + yrecv[d].astype(F32)).astype(self.wire)
            c = remote(zsend.at[d], zrecv.at[d], zs.at[d], zr.at[d], (h * 2 + lo, s))
            c.start()
            second.append(c)
            yield
        first[0].wait_recv()
        total = src[b] + yrecv[0].astype(F32)
        for d in range(1, m):
            second[d - 1].wait_recv()
            total = total + zrecv[d].astype(F32)
        dst[...] = total
        for c in list(first.values()) + second:
            c.wait_send()


class GatherSeq:
    peers = ("seq",)

    def __init__(self, n, src):
        self.ins = [src]
        self.outs = [jax.ShapeDtypeStruct((SEQ,) + src.shape, src.dtype)]
        self.scratch = [pltpu.SemaphoreType.DMA((3,))] * 2 + [pltpu.SemaphoreType.DMA]

    def run(self, src, dst, ss, rs, own):
        b, s = lax.axis_index("batch"), lax.axis_index("seq")
        far, near = (s + 2) % 4, s + 1 - 2 * (s % 2)
        across = remote(src, dst.at[s], ss.at[0], rs.at[0], (b, far))
        across.start()
        local = pltpu.make_async_copy(src, dst.at[s], own)
        local.start()
        beside = remote(src, dst.at[s], ss.at[1], rs.at[1], (b, near))
        beside.start()
        yield
        across.wait_recv()
        passed = remote(dst.at[far], dst.at[far], ss.at[2], rs.at[2], (b, near))
        passed.start()
        yield
        local.wait()
        beside.wait()
        passed.wait()
        across.wait_send()


class ScatterSeq:
    peers = ("seq",)

    def __init__(self, n, src):
        self.ins = [src]
        shape = src.shape[1:]
        self.outs = [jax.ShapeDtypeStruct(shape, F32)]
        self.scratch = [
            pltpu.VMEM((2,) + shape, BF16),
            pltpu.VMEM((2,) + shape, BF16),
            pltpu.VMEM(shape, BF16),
            pltpu.VMEM(shape, BF16),
            pltpu.SemaphoreType.DMA((3,)),
            pltpu.SemaphoreType.DMA((3,)),
        ]

    def run(self, src, dst, near_out, near_in, far_out, far_in, ss, rs):
        b, s = lax.axis_index("batch"), lax.axis_index("seq")
        far, near = (s + 2) % 4, s + 1 - 2 * (s % 2)
        near_far = (near + 2) % 4
        near_out[1] = src[near_far].astype(BF16)
        one = remote(near_out.at[1], near_in.at[1], ss.at[1], rs.at[1], (b, near))
        one.start()
        near_out[0] = src[near].astype(BF16)
        two = remote(near_out.at[0], near_in.at[0], ss.at[0], rs.at[0], (b, near))
        two.start()
        yield
        one.wait_recv()
        far_out[...] = (src[far] + near_in[1].astype(F32)).astype(BF16)
        three = remote(far_out, far_in, ss.at[2], rs.at[2], (b, far))
        three.start()
        yield
        two.wait_recv()
        dst[...] = src[s] + near_in[0].astype(F32)
        yield
        three.wait_recv()
        dst[...] = dst[...] + far_in[...].astype(F32)
        one.wait_send()
        two.wait_send()
        three.wait_send()


class SwapSeq:
    peers = ("seq",)

    def __init__(self, n, src):
        self.ins = [src]
        self.outs = [jax.ShapeDtypeStruct(src.shape, src.dtype)]
        self.scratch = [pltpu.SemaphoreType.DMA((4,))] * 2 + [pltpu.SemaphoreType.DMA]

    def run(self, src, dst, ss, rs, own):
        b, s = lax.axis_index("batch"), lax.axis_index("seq")
        copies = []
        for k in (2, 3, 1):
            other = (s + k) % 4
            c = remote(src.at[other], dst.at[s], ss.at[k], rs.at[k], (b, other))
            c.start()
            copies.append(c)
        local = pltpu.make_async_copy(src.at[s], dst.at[s], own)
        local.start()
        yield
        local.wait()
        for c in copies:
            c.wait()


def owner_list(n):
    return [(0, 2), (1, 0), (n - 2, 2), (n - 1, 0), (n // 4, 0), (n // 2 + 1, 2)]


class ToOwners:
    peers = ("all",)

    def __init__(self, n, attn_piece, up_piece, down_piece):
        self.n = n
        self.ins = [attn_piece, up_piece, down_piece]
        self.outs = [
            jax.ShapeDtypeStruct((SEQ, n) + attn_piece.shape[1:], BF16),
            jax.ShapeDtypeStruct((SEQ, n) + up_piece.shape, BF16),
        ]
        self.scratch = [
            pltpu.SemaphoreType.DMA((6,)),
            pltpu.SemaphoreType.DMA((SEQ * n,)),
            pltpu.SemaphoreType.DMA,
        ]

    def run(self, attn, up, down, attn_in, wide_in, ss, rs, own):
        n = self.n
        b, s = lax.axis_index("batch"), lax.axis_index("seq")
        me = s * n + b
        for number in (5, 4, 0, 1, 2, 3):
            ob, os = owner_list(n)[number]
            mine = (b == ob) & (s == os)
            src = attn.at[number] if number < 4 else (up, down)[number - 4]
            dst = (attn_in if number < 4 else wide_in).at[s, b]

            @pl.when(jnp.logical_not(mine))
            def _(src=src, dst=dst, number=number, ob=ob, os=os):
                remote(src, dst, ss.at[number], rs.at[me], (ob, os)).start()

            @pl.when(mine)
            def _(src=src, dst=dst):
                pltpu.make_async_copy(src, dst, own).start()

        yield
        for number in (5, 4, 0, 1, 2, 3):
            ob, os = owner_list(n)[number]
            mine = (b == ob) & (s == os)
            src = attn.at[number] if number < 4 else (up, down)[number - 4]
            buf = attn_in if number < 4 else wide_in

            @pl.when(jnp.logical_not(mine))
            def _(src=src, buf=buf, number=number, ob=ob, os=os):
                remote(src, buf.at[s, b], ss.at[number], rs.at[me], (ob, os)).wait_send()

            @pl.when(mine)
            def _(src=src, buf=buf, number=number):
                pltpu.make_async_copy(src, buf.at[s, b], own).wait()

                @pl.loop(1, SEQ * n)
                def _(k):
                    other = (me + k) % (SEQ * n)
                    remote(
                        src, buf.at[other // n, other % n], ss.at[number], rs.at[other], (0, 0)
                    ).wait_recv()


class FromOwners:
    peers = ("all",)

    def __init__(self, n, attn_out, wide_out):
        self.n = n
        self.ins = [attn_out, wide_out]
        self.outs = [
            jax.ShapeDtypeStruct((4,) + attn_out.shape[2:], BF16),
            jax.ShapeDtypeStruct((2,) + wide_out.shape[2:], BF16),
        ]
        self.scratch = [
            pltpu.SemaphoreType.DMA((SEQ * n,)),
            pltpu.SemaphoreType.DMA((6,)),
            pltpu.SemaphoreType.DMA,
        ]

    def run(self, attn_out, wide_out, attn_in, wide_in, ss, rs, own):
        n = self.n
        b, s = lax.axis_index("batch"), lax.axis_index("seq")
        me = s * n + b
        for number in range(6):
            ob, os = owner_list(n)[number]
            mine = (b == ob) & (s == os)
            buf = attn_out if number < 4 else wide_out
            dst = attn_in.at[number] if number < 4 else wide_in.at[number - 4]

            @pl.when(mine)
            def _(buf=buf, dst=dst, number=number):
                pltpu.make_async_copy(buf.at[s, b], dst, own).start()

                @pl.loop(1, SEQ * n)
                def _(k):
                    other = (me + k) % (SEQ * n)
                    os, ob = other // n, other % n
                    remote(buf.at[os, ob], dst, ss.at[other], rs.at[number], (ob, os)).start()

        yield
        for number in range(6):
            ob, os = owner_list(n)[number]
            mine = (b == ob) & (s == os)
            buf = attn_out if number < 4 else wide_out
            dst = attn_in.at[number] if number < 4 else wide_in.at[number - 4]

            @pl.when(jnp.logical_not(mine))
            def _(buf=buf, dst=dst, number=number):
                remote(buf.at[s, b], dst, ss.at[me], rs.at[number], (0, 0)).wait_recv()

            @pl.when(mine)
            def _(buf=buf, dst=dst, number=number):
                pltpu.make_async_copy(buf.at[s, b], dst, own).wait()

                @pl.loop(1, SEQ * n)
                def _(k):
                    other = (me + k) % (SEQ * n)
                    os, ob = other // n, other % n
                    remote(buf.at[os, ob], dst, ss.at[other], rs.at[number], (0, 0)).wait_send()


def greet(n, kinds):
    b, s, hi, lo, m = coords(n)
    barrier = pltpu.get_barrier_semaphore()
    if "all" in kinds:
        me = s * n + b

        @pl.loop(1, SEQ * n)
        def _(k):
            other = (me + k) % (SEQ * n)
            pl.semaphore_signal(
                barrier, inc=1, device_id=(other % n, other // n), device_id_type=MESH
            )

        pl.semaphore_wait(barrier, SEQ * n - 1)
        return
    peers = []
    if "seq" in kinds:
        peers += [(b, (s + k) % 4) for k in (1, 2, 3)]
    if "batch" in kinds:
        peers += [(((hi + d) % m) * 2 + lo, s) for d in range(1, m)]
        peers += [(hi * 2 + 1 - lo, s)]
    for peer in peers:
        pl.semaphore_signal(barrier, inc=1, device_id=peer, device_id_type=MESH)
    pl.semaphore_wait(barrier, len(peers))


def exchange(n, collective_id, name, *ops):
    ins = [a for op in ops for a in op.ins]
    outs = [o for op in ops for o in op.outs]
    scratch = [c for op in ops for c in op.scratch]
    kinds = {k for op in ops for k in op.peers}

    def kernel(*refs):
        in_refs, out_refs = refs[: len(ins)], refs[len(ins) : len(ins) + len(outs)]
        scratch_refs = refs[len(ins) + len(outs) :]
        greet(n, kinds)
        live = []
        i = o = c = 0
        for op in ops:
            ni, no, nc = len(op.ins), len(op.outs), len(op.scratch)
            live.append(
                op.run(*in_refs[i : i + ni], *out_refs[o : o + no], *scratch_refs[c : c + nc])
            )
            i, o, c = i + ni, o + no, c + nc
        while live:
            still = []
            for step in live:
                try:
                    next(step)
                    still.append(step)
                except StopIteration:
                    pass
            live = still

    vmem = pl.BlockSpec(memory_space=pltpu.VMEM)
    return pl.pallas_call(
        kernel,
        out_shape=outs,
        in_specs=[vmem] * len(ins),
        out_specs=[vmem] * len(outs),
        scratch_shapes=scratch,
        compiler_params=pltpu.CompilerParams(
            collective_id=collective_id, has_side_effects=True, vmem_limit_bytes=60 * 2**20
        ),
        name=name,
    )(*ins)


def contract_last(left, right):
    return lax.dot_general(left, right, (((1,), (1,)), ((), ())), preferred_element_type=F32)


def contract_first(left, right):
    return lax.dot_general(left, right, (((0,), (0,)), ((), ())), preferred_element_type=F32)


def matmul(left, right):
    return jnp.dot(left, right, preferred_element_type=F32)


def exact_gelu(value_in):
    return jax.nn.gelu(value_in, approximate=False)


def normalize(hidden, gain_row):
    row_mean = jnp.mean(hidden, axis=-1, keepdims=True)
    centred = hidden - row_mean
    spread = lax.rsqrt(jnp.mean(centred * centred, axis=-1, keepdims=True) + norm_eps)
    scaled = centred * spread
    return (scaled * gain_row, scaled, spread)


def normalize_back(grad_in, scaled, spread, gain_row):
    weighted = grad_in * gain_row
    mean_first = jnp.mean(weighted, axis=-1, keepdims=True)
    second = jnp.mean(weighted * scaled, axis=-1, keepdims=True)
    return (
        spread * (weighted - mean_first - scaled * second),
        jnp.sum(grad_in * scaled, axis=0),
        jnp.sum(grad_in, axis=0),
    )


def poly_of(gram):
    eye = jnp.eye(gram.shape[0], dtype=bool)
    diag = jnp.sum(jnp.where(eye, gram, 0.0), axis=1)
    rest = jnp.where(eye, 0.0, gram)
    low = rest.astype(BF16)
    square = matmul(low, low) + (diag[:, None] + diag[None, :]) * rest
    square = square + jnp.where(eye, (diag * diag)[:, None], 0.0)
    poly = -4.775 * gram + 2.0315 * square
    poly_diag = jnp.sum(jnp.where(eye, poly, 0.0), axis=1)
    return poly_diag, jnp.where(eye, 0.0, poly).astype(BF16)


def orthogonal_rows(matrix):
    current = matrix.astype(F32)
    current = current / (jnp.sqrt(jnp.sum(current * current)) + tiny_norm)
    for _ in range(NS):
        low = current.astype(BF16)
        gram = sum(contract_last(low[k], low[k]) for k in range(low.shape[0]))
        diag, rest = poly_of(gram)
        moved = jnp.stack([matmul(rest, low[k]) for k in range(low.shape[0])])
        current = (3.4445 + diag)[None, :, None] * current + moved
    return current.astype(BF16)


def orthogonal_columns(matrix):
    current = matrix.astype(F32)
    current = current / (jnp.sqrt(jnp.sum(current * current)) + tiny_norm)
    for _ in range(NS):
        low = current.astype(BF16)
        diag, rest = poly_of(contract_first(low, low))
        current = (3.4445 + diag)[None, :] * current + matmul(low, rest)
    return current.astype(BF16)


def step_factor(rows_all, cols_all):
    return matrix_rate * math.sqrt(max(1.0, rows_all / cols_all))


def make_body(n):
    def body(
        layer_input,
        lengths,
        attn_weight,
        up_weight,
        down_weight,
        vectors,
        attn_moment,
        up_moment,
        down_moment,
        vector_moment,
        out_grad,
        pool_grad,
    ):
        rows, span, width = layer_input.shape
        local = rows * span
        span_all = span * SEQ
        own_rows = width // n
        quarter = width // SEQ
        hidden = up_weight.shape[1]
        hid_q = hidden // SEQ
        hid_own = hidden // n // SEQ
        seq_index = lax.axis_index("seq")

        def attn_quarter(stacked):
            part = lax.dynamic_index_in_dim(
                stacked.reshape(4, own_rows, SEQ, quarter), seq_index, 2, False
            )
            return part

        def up_quarter(matrix):
            return lax.dynamic_index_in_dim(
                matrix.reshape(own_rows, n, SEQ, hid_own), seq_index, 2, False
            ).reshape(own_rows, hid_q)

        def down_quarter(matrix):
            return lax.dynamic_index_in_dim(
                matrix.reshape(SEQ, hid_own, width), seq_index, 0, False
            )

        attn_low = attn_quarter(attn_weight).astype(BF16).transpose(1, 0, 2).reshape(own_rows, width)
        up_low = up_quarter(up_weight).astype(BF16)
        down_low = down_quarter(down_weight).astype(BF16)
        vec_low = vectors.astype(BF16).astype(F32)

        tokens = layer_input.reshape(local, width)
        token_own = tokens.astype(BF16)
        w_attn, vec_all, x_all, pool_all = exchange(
            n,
            0,
            "gather_attn",
            GatherBatch(n, attn_low),
            GatherBatch(n, vec_low),
            GatherSeq(n, token_own),
            GatherSeq(n, pool_grad),
        )
        w_attn = w_attn.reshape(width, width)
        w_qkv, w_out_part = w_attn[:, : 3 * quarter], w_attn[:, 3 * quarter :]
        vec_full = vec_all.transpose(1, 0, 2).reshape(-1, width)
        bias_out, gain_one, shift_one, gain_two, shift_two, bias_down = [
            vec_full[k] for k in range(2, 8)
        ]
        bias_qv = lax.dynamic_index_in_dim(
            vec_full[:2].reshape(2, SEQ, quarter), seq_index, 1, False
        )
        bias_qkv = jnp.concatenate([bias_qv[0], jnp.zeros_like(bias_qv[0]), bias_qv[1]])
        bias_up = lax.dynamic_index_in_dim(
            vec_full[8:].reshape(n, SEQ, hid_own), seq_index, 1, False
        ).reshape(hid_q)
        x_all = x_all.reshape(SEQ * local, width)
        pool_whole = pool_all.transpose(1, 0, 2).reshape(rows, width)

        qkv = (matmul(x_all, w_qkv) + bias_qkv).astype(BF16)
        qkv = qkv.reshape(SEQ, rows, span, 3, HEADS, HD).transpose(3, 1, 4, 0, 2, 5)
        query, key, value = qkv.reshape(3, rows, HEADS, span_all, HD)
        scale = HD ** (-0.5)
        scores = (
            jnp.einsum("rhqd,rhkd->rhqk", query, key, preferred_element_type=F32) * scale
        )
        key_valid = jnp.arange(span_all)[None, :] < lengths[:, None]
        scores = jnp.where(key_valid[:, None, None, :], scores, -1e30)
        exponent = jnp.exp(scores - jnp.max(scores, axis=-1, keepdims=True))
        prob = exponent / jnp.sum(exponent, axis=-1, keepdims=True)
        prob_low = prob.astype(BF16)
        mixed = jnp.einsum("rhqk,rhkd->rhqd", prob_low, value, preferred_element_type=F32)
        context_out = (
            mixed.astype(BF16)
            .reshape(rows, HEADS, SEQ, span, HD)
            .transpose(2, 0, 3, 1, 4)
            .reshape(SEQ, local, quarter)
        )
        context_in, w_out, w_up = exchange(
            n,
            1,
            "swap_context",
            SwapSeq(n, context_out),
            GatherSeq(n, w_out_part),
            GatherBatch(n, up_low),
        )
        context = context_in.transpose(1, 0, 2).reshape(local, width)
        w_out = w_out.transpose(1, 0, 2).reshape(width, width)
        w_up = w_up.reshape(width, hid_q)

        branch = matmul(context, w_out) + bias_out
        normed_part, scaled_one, spread_one = normalize(tokens + branch, gain_one)
        normed_one = normed_part + shift_one
        y_all, w_down = exchange(
            n,
            2,
            "gather_hidden",
            GatherSeq(n, normed_one.astype(BF16)),
            GatherBatch(n, down_low),
        )
        y_all = y_all.reshape(SEQ * local, width)
        w_down = w_down.reshape(hid_q, width)
        pre_act = matmul(y_all, w_up) + bias_up
        activated, gelu_pull = jax.vjp(exact_gelu, pre_act)
        act_low = activated.astype(BF16)
        down_part = matmul(act_low, w_down).reshape(SEQ, local, width)
        (down_sum,) = exchange(n, 3, "sum_down", ScatterSeq(n, down_part))
        output_part, scaled_two, spread_two = normalize(
            normed_one + down_sum + bias_down, gain_two
        )
        output = output_part + shift_two
        position = seq_index * span + jnp.arange(span)
        live_mask = (position[None, :] < lengths[:, None]).astype(F32)
        row_length = lengths.astype(F32)[:, None]
        out_rows = output.reshape(rows, span, width)
        partial_pool = jnp.sum(out_rows * live_mask[..., None], axis=1) / row_length
        upstream = (
            live_mask[..., None] * (out_grad + (pool_whole / row_length)[:, None, :])
        ).reshape(local, width)
        second_grad, grad_gain_two, grad_shift_two = normalize_back(
            upstream, scaled_two, spread_two, gain_two
        )
        z_low = second_grad.astype(BF16)
        grad_bias_down = jnp.sum(z_low.astype(F32), axis=0)
        z_all, pool_parts = exchange(
            n, 4, "gather_dz", GatherSeq(n, z_low), GatherSeq(n, partial_pool)
        )
        pooled = lax.dynamic_slice_in_dim(
            (pool_parts[0] + pool_parts[1]) + (pool_parts[2] + pool_parts[3]),
            seq_index * quarter,
            quarter,
            1,
        )
        z_all = z_all.reshape(SEQ * local, width)
        (pre_grad,) = gelu_pull(contract_last(z_all, w_down))
        pre_low = pre_grad.astype(BF16)
        grad_bias_up = jnp.sum(pre_low.astype(F32), axis=0)
        grad_down = contract_first(act_low, z_all)
        hidden_part = contract_last(pre_low, w_up).reshape(SEQ, local, width)
        hidden_sum, down_piece = exchange(
            n,
            5,
            "sum_hidden",
            ScatterSeq(n, hidden_part),
            ScatterBatch(n, grad_down.reshape(n, hid_own, width)),
        )
        grad_up = contract_first(y_all, pre_low)
        first_grad, grad_gain_one, grad_shift_one = normalize_back(
            hidden_sum + second_grad, scaled_one, spread_one, gain_one
        )
        a_low = first_grad.astype(BF16)
        grad_bias_out = jnp.sum(a_low.astype(F32), axis=0)
        context_grad = contract_last(a_low, w_out).astype(BF16)
        grad_out = contract_first(context, a_low)
        up_piece, context_back, out_part = exchange(
            n,
            6,
            "swap_dcontext",
            ScatterBatch(n, grad_up.reshape(n, own_rows, hid_q)),
            SwapSeq(n, context_grad.reshape(local, SEQ, quarter).transpose(1, 0, 2)),
            ScatterSeq(n, grad_out.reshape(width, SEQ, quarter).transpose(1, 0, 2)),
        )
        arriving = (
            context_back.reshape(SEQ, rows, span, HEADS, HD)
            .transpose(1, 3, 0, 2, 4)
            .reshape(rows, HEADS, span_all, HD)
        )
        prob_grad = jnp.einsum("rhqd,rhkd->rhqk", arriving, value, preferred_element_type=F32)
        row_delta = jnp.sum(prob * prob_grad, axis=-1, keepdims=True)
        score_grad = (prob * (prob_grad - row_delta)).astype(BF16)
        query_grad = (
            jnp.einsum("rhqk,rhkd->rhqd", score_grad, key, preferred_element_type=F32) * scale
        )
        key_grad = (
            jnp.einsum("rhqk,rhqd->rhkd", score_grad, query, preferred_element_type=F32) * scale
        )
        value_grad = jnp.einsum(
            "rhqk,rhqd->rhkd", prob_low, arriving, preferred_element_type=F32
        )
        qkv_grad = (
            jnp.stack([query_grad, key_grad, value_grad])
            .astype(BF16)
            .reshape(3, rows, HEADS, SEQ, span, HD)
            .transpose(3, 1, 4, 0, 2, 5)
            .reshape(SEQ * local, 3 * quarter)
        )
        input_part = contract_last(qkv_grad, w_qkv).reshape(SEQ, local, width)
        attn_local = jnp.concatenate([contract_first(x_all, qkv_grad), out_part], axis=1)
        bias_sums = jnp.sum(qkv_grad.astype(F32), axis=0).reshape(3, quarter)

        vec_head = jnp.zeros((2, SEQ, quarter), F32)
        vec_head = lax.dynamic_update_slice(
            vec_head, bias_sums[jnp.array([0, 2])][:, None], (0, seq_index, 0)
        ).reshape(2, width)
        vec_mid = jnp.stack(
            [
                grad_bias_out,
                grad_gain_one,
                grad_shift_one,
                grad_gain_two,
                grad_shift_two,
                grad_bias_down,
            ]
        )
        vec_tail = lax.dynamic_update_slice(
            jnp.zeros((n, SEQ, hid_own), F32),
            grad_bias_up.reshape(n, 1, hid_own),
            (0, seq_index, 0),
        ).reshape(-1, width)
        vec_local = jnp.concatenate([vec_head, vec_mid, vec_tail])
        vec_local = vec_local.reshape(-1, n, own_rows).transpose(1, 0, 2)
        input_sum, attn_piece, vec_piece = exchange(
            n,
            7,
            "sum_input",
            ScatterSeq(n, input_part),
            ScatterBatch(n, attn_local.reshape(n, own_rows, width)),
            ScatterBatch(n, vec_local, F32),
        )
        input_grad = input_sum + first_grad

        pieces = jnp.stack([attn_piece, up_piece]).astype(BF16)
        down_bf = down_piece.astype(BF16)
        attn_bf = pieces[0].reshape(own_rows, 4, quarter).transpose(1, 0, 2)
        up_bf = pieces[1]
        attn_send = (matrix_decay * attn_quarter(attn_moment) + attn_bf.astype(F32)).astype(BF16)
        up_send = (matrix_decay * up_quarter(up_moment) + up_bf.astype(F32)).astype(BF16)
        down_send = (matrix_decay * down_quarter(down_moment) + down_bf.astype(F32)).astype(BF16)
        attn_owned, wide_owned, attn_all, up_all, down_all, vec_parts = exchange(
            n,
            8,
            "to_owners",
            ToOwners(n, attn_send, up_send, down_send),
            GatherSeq(n, attn_bf),
            GatherSeq(n, up_bf),
            GatherSeq(n, down_bf),
            GatherSeq(n, vec_piece),
        )

        def join_attn(parts):
            return parts.astype(F32).transpose(1, 2, 0, 3).reshape(4, own_rows, width)

        def join_up(parts):
            return (
                parts.astype(F32)
                .reshape(SEQ, own_rows, n, hid_own)
                .transpose(1, 2, 0, 3)
                .reshape(own_rows, hidden)
            )

        def join_down(parts):
            return parts.astype(F32).reshape(SEQ * hid_own, width)

        attn_grad, up_grad, down_grad = join_attn(attn_all), join_up(up_all), join_down(down_all)
        vector_grad = (vec_parts[0] + vec_parts[1]) + (vec_parts[2] + vec_parts[3])
        attn_next = matrix_decay * attn_moment + attn_grad
        up_next = matrix_decay * up_moment + up_grad
        down_next = matrix_decay * down_moment + down_grad

        batch_index = lax.axis_index("batch")
        kind = jnp.int32(0)
        for number, (ob, os) in enumerate(owner_list(n)):
            here = (batch_index == ob) & (seq_index == os)
            kind = jnp.where(here, jnp.int32(max(1, number - 2)), kind)

        def idle(attn_in, wide_in):
            return attn_in, wide_in

        def square(attn_in, wide_in):
            whole = attn_in.reshape(SEQ, width, quarter).transpose(1, 0, 2).reshape(1, width, width)
            done = orthogonal_rows(whole)[0].reshape(width, SEQ, quarter).transpose(1, 0, 2)
            return done.reshape(attn_in.shape), wide_in

        def wide(attn_in, wide_in):
            done = orthogonal_rows(wide_in.reshape(SEQ, width, hid_q))
            return attn_in, done.reshape(wide_in.shape)

        def tall(attn_in, wide_in):
            done = orthogonal_columns(wide_in.reshape(hidden, width))
            return attn_in, done.reshape(wide_in.shape)

        attn_done, wide_done = lax.switch(kind, [idle, square, wide, tall], attn_owned, wide_owned)
        attn_back, wide_back = exchange(
            n, 9, "from_owners", FromOwners(n, attn_done, wide_done)
        )
        attn_orth, wide_orth = exchange(
            n, 10, "gather_orth", GatherSeq(n, attn_back), GatherSeq(n, wide_back)
        )
        factors = [
            step_factor(width, width),
            step_factor(width, hidden),
            step_factor(hidden, width),
        ]
        attn_new = attn_weight - factors[0] * join_attn(attn_orth)
        up_new = up_weight - factors[1] * join_up(wide_orth[:, 0])
        down_new = down_weight - factors[2] * join_down(wide_orth[:, 1])
        vector_next = vector_decay * vector_moment + vector_grad
        vectors_new = vectors - vector_rate / math.sqrt(rows * n) * vector_next
        return (
            out_rows,
            pooled,
            input_grad.reshape(rows, span, width),
            attn_grad,
            up_grad,
            down_grad,
            vector_grad,
            attn_next,
            up_next,
            down_next,
            vector_next,
            attn_new,
            up_new,
            down_new,
            vectors_new,
        )

    return body


def solution(mesh):
    placed = (
        P("batch", "seq", None),
        P("batch"),
        P(None, "batch", None),
        P("batch", None),
        P("batch", None),
        P(None, "batch"),
        P(None, "batch", None),
        P("batch", None),
        P("batch", None),
        P(None, "batch"),
        P("batch", "seq", None),
        P("batch", "seq"),
    )
    return jax.shard_map(
        make_body(mesh.shape["batch"]),
        mesh=mesh,
        in_specs=placed,
        out_specs=(
            P("batch", "seq", None),
            P("batch", "seq"),
            P("batch", "seq", None),
            P(None, "batch", None),
            P("batch", None),
            P("batch", None),
            P(None, "batch"),
            P(None, "batch", None),
            P("batch", None),
            P("batch", None),
            P(None, "batch"),
            P(None, "batch", None),
            P("batch", None),
            P("batch", None),
            P(None, "batch"),
        ),
        check_vma=False,
    )
```

```python
import math

import jax
import jax.numpy as jnp
from jax import lax
from jax.experimental import pallas as pl
from jax.experimental.pallas import tpu as pltpu
from jax.sharding import PartitionSpec as P

H = 12
HD = 64
NS = 5
SEQ = 4
HEADS = H // SEQ

norm_eps = 1e-12
tiny_norm = 1e-07
matrix_decay = 0.95
vector_decay = 0.5
matrix_rate = 0.5
vector_rate = 0.03

MESH = pl.DeviceIdType.MESH
F32 = jnp.float32
BF16 = jnp.bfloat16


def coords(n):
    b = lax.axis_index("batch")
    s = lax.axis_index("seq")
    return b, s, b // 2, b % 2, n // 2


def remote(src, dst, send, recv, device):
    return pltpu.make_async_remote_copy(
        src_ref=src, dst_ref=dst, send_sem=send, recv_sem=recv, device_id=device, device_id_type=MESH
    )


class GatherBatch:
    peers = ("batch",)

    def __init__(self, n, src):
        self.n = n
        self.ins = [src]
        self.outs = [jax.ShapeDtypeStruct((n,) + src.shape, src.dtype)]
        m = n // 2
        self.scratch = [pltpu.SemaphoreType.DMA((m,))] * 4 + [pltpu.SemaphoreType.DMA]

    def run(self, src, dst, zs, zr, ys, yr, own):
        b, s, hi, lo, m = coords(self.n)
        local = pltpu.make_async_copy(src, dst.at[b], own)
        local.start()
        pair = (hi * 2 + 1 - lo, s)
        out = []
        for d in range(1, m):
            c = remote(src, dst.at[b], zs.at[d], zr.at[d], (((hi + d) % m) * 2 + lo, s))
            c.start()
            out.append(c)
        first = remote(src, dst.at[b], ys.at[0], yr.at[0], pair)
        first.start()
        yield
        passed = [first]
        for d in range(1, m):
            out[d - 1].wait_recv()
            block = ((hi + m - d) % m) * 2 + lo
            c = remote(dst.at[block], dst.at[block], ys.at[d], yr.at[d], pair)
            c.start()
            passed.append(c)
            yield
        local.wait()
        for c in passed:
            c.wait()
        for c in out:
            c.wait_send()


class ScatterBatch:
    peers = ("batch",)

    def __init__(self, n, src, wire=BF16):
        self.n = n
        self.wire = wire
        self.ins = [src]
        shape = src.shape[1:]
        self.outs = [jax.ShapeDtypeStruct(shape, F32)]
        m = n // 2
        self.scratch = [pltpu.VMEM((m,) + shape, wire)] * 4 + [pltpu.SemaphoreType.DMA((m,))] * 4

    def run(self, src, dst, ysend, yrecv, zsend, zrecv, ys, yr, zs, zr):
        b, s, hi, lo, m = coords(self.n)
        pair = (hi * 2 + 1 - lo, s)
        first = {}
        order = list(range(1, m)) + [0]
        for d in order:
            h = (hi + d) % m
            ysend[d] = src[h * 2 + 1 - lo].astype(self.wire)
            first[d] = remote(ysend.at[d], yrecv.at[d], ys.at[d], yr.at[d], pair)
            first[d].start()
        yield
        second = []
        for d in range(1, m):
            h = (hi + d) % m
            first[d].wait_recv()
            zsend[d] = (src[h * 2 + lo] + yrecv[d].astype(F32)).astype(self.wire)
            c = remote(zsend.at[d], zrecv.at[d], zs.at[d], zr.at[d], (h * 2 + lo, s))
            c.start()
            second.append(c)
            yield
        first[0].wait_recv()
        total = src[b] + yrecv[0].astype(F32)
        for d in range(1, m):
            second[d - 1].wait_recv()
            total = total + zrecv[d].astype(F32)
        dst[...] = total
        for c in list(first.values()) + second:
            c.wait_send()


class GatherSeq:
    peers = ("seq",)

    def __init__(self, n, src):
        self.ins = [src]
        self.outs = [jax.ShapeDtypeStruct((SEQ,) + src.shape, src.dtype)]
        self.scratch = [pltpu.SemaphoreType.DMA((3,))] * 2 + [pltpu.SemaphoreType.DMA]

    def run(self, src, dst, ss, rs, own):
        b, s = lax.axis_index("batch"), lax.axis_index("seq")
        far, near = (s + 2) % 4, s + 1 - 2 * (s % 2)
        across = remote(src, dst.at[s], ss.at[0], rs.at[0], (b, far))
        across.start()
        local = pltpu.make_async_copy(src, dst.at[s], own)
        local.start()
        beside = remote(src, dst.at[s], ss.at[1], rs.at[1], (b, near))
        beside.start()
        yield
        across.wait_recv()
        passed = remote(dst.at[far], dst.at[far], ss.at[2], rs.at[2], (b, near))
        passed.start()
        yield
        local.wait()
        beside.wait()
        passed.wait()
        across.wait_send()


class ScatterSeq:
    peers = ("seq",)

    def __init__(self, n, src):
        self.ins = [src]
        shape = src.shape[1:]
        self.outs = [jax.ShapeDtypeStruct(shape, F32)]
        self.scratch = [
            pltpu.VMEM((2,) + shape, BF16),
            pltpu.VMEM((2,) + shape, BF16),
            pltpu.VMEM(shape, BF16),
            pltpu.VMEM(shape, BF16),
            pltpu.SemaphoreType.DMA((3,)),
            pltpu.SemaphoreType.DMA((3,)),
        ]

    def run(self, src, dst, near_out, near_in, far_out, far_in, ss, rs):
        b, s = lax.axis_index("batch"), lax.axis_index("seq")
        far, near = (s + 2) % 4, s + 1 - 2 * (s % 2)
        near_far = (near + 2) % 4
        near_out[1] = src[near_far].astype(BF16)
        one = remote(near_out.at[1], near_in.at[1], ss.at[1], rs.at[1], (b, near))
        one.start()
        near_out[0] = src[near].astype(BF16)
        two = remote(near_out.at[0], near_in.at[0], ss.at[0], rs.at[0], (b, near))
        two.start()
        yield
        one.wait_recv()
        far_out[...] = (src[far] + near_in[1].astype(F32)).astype(BF16)
        three = remote(far_out, far_in, ss.at[2], rs.at[2], (b, far))
        three.start()
        yield
        two.wait_recv()
        dst[...] = src[s] + near_in[0].astype(F32)
        yield
        three.wait_recv()
        dst[...] = dst[...] + far_in[...].astype(F32)
        one.wait_send()
        two.wait_send()
        three.wait_send()


class SwapSeq:
    peers = ("seq",)

    def __init__(self, n, src):
        self.ins = [src]
        self.outs = [jax.ShapeDtypeStruct(src.shape, src.dtype)]
        self.scratch = [pltpu.SemaphoreType.DMA((4,))] * 2 + [pltpu.SemaphoreType.DMA]

    def run(self, src, dst, ss, rs, own):
        b, s = lax.axis_index("batch"), lax.axis_index("seq")
        copies = []
        for k in (2, 3, 1):
            other = (s + k) % 4
            c = remote(src.at[other], dst.at[s], ss.at[k], rs.at[k], (b, other))
            c.start()
            copies.append(c)
        local = pltpu.make_async_copy(src.at[s], dst.at[s], own)
        local.start()
        yield
        local.wait()
        for c in copies:
            c.wait()


def owner_list(n):
    return [(0, 2), (1, 0), (n - 2, 2), (n - 1, 0), (n // 4, 0), (n // 2 + 1, 2)]


class Muon:
    peers = ("all",)

    def __init__(self, n, attn_piece, wide_piece):
        self.n = n
        self.ins = [attn_piece, wide_piece]
        rows, quarter = attn_piece.shape[1:]
        width = wide_piece.shape[2]
        self.outs = [
            jax.ShapeDtypeStruct((SEQ, 4, rows, quarter), BF16),
            jax.ShapeDtypeStruct((SEQ, 2, rows, width), BF16),
        ]
        size = n * rows
        dma = pltpu.SemaphoreType.DMA
        self.scratch = [
            pltpu.VMEM((SEQ, n, rows, quarter), BF16),
            pltpu.VMEM((SEQ, n, rows, width), BF16),
            pltpu.VMEM((size, SEQ * size), F32),
            pltpu.VMEM((size, SEQ * size), BF16),
            pltpu.VMEM((size, size), F32),
            pltpu.VMEM((size, size), BF16),
            pltpu.VMEM((size, size), BF16),
            pltpu.VMEM((size, 1), F32),
            dma((6,)),
            dma((SEQ * n,)),
            dma((SEQ * n,)),
            dma((6,)),
            dma((6, 3)),
            dma((6, 3)),
            dma((2,)),
        ]

    def run(
        self, attn, wide, attn_orth, wide_orth, attn_in, wide_in, x32, xlow, gram, gram_low, poly, diag,
        ss, rs, back_s, back_r, seq_s, seq_r, own,
    ):
        n = self.n
        b, s = lax.axis_index("batch"), lax.axis_index("seq")
        me = s * n + b
        far, near = (s + 2) % 4, s + 1 - 2 * (s % 2)
        size = x32.shape[0]
        width = wide.shape[2]
        quarter = attn.shape[2]
        places = owner_list(n)
        mine = [(b == ob) & (s == os) for ob, os in places]
        number = jnp.int32(0)
        for k in range(6):
            number = jnp.where(mine[k], jnp.int32(k), number)
        is_attn = mine[0] | mine[1] | mine[2] | mine[3]
        is_wide = mine[4] | mine[5]
        order = (5, 4, 0, 1, 2, 3)

        def piece(k):
            return attn.at[k] if k < 4 else wide.at[k - 4]

        def inbox(k):
            return attn_in if k < 4 else wide_in

        def result(k):
            return attn_orth.at[s, k] if k < 4 else wide_orth.at[s, k - 4]

        for k in order:
            ob, os = places[k]

            @pl.when(jnp.logical_not(mine[k]))
            def _(k=k, ob=ob, os=os):
                remote(piece(k), inbox(k).at[s, b], ss.at[k], rs.at[me], (ob, os)).start()

            @pl.when(mine[k])
            def _(k=k):
                pltpu.make_async_copy(piece(k), inbox(k).at[s, b], own.at[0]).start()

        yield
        yield
        yield
        yield

        def collect(buf):
            pltpu.make_async_copy(buf.at[s, b], buf.at[s, b], own.at[0]).wait()

            @pl.loop(1, SEQ * n)
            def _(k):
                other = (me + k) % (SEQ * n)
                place = buf.at[other // n, other % n]
                remote(place, place, ss.at[0], rs.at[other], (0, 0)).wait_recv()

        def give(buf, out, index):
            pltpu.make_async_copy(buf.at[s, b], out.at[s, index], own.at[1]).start()

            @pl.loop(1, SEQ * n)
            def _(k):
                other = (me + k) % (SEQ * n)
                os, ob = other // n, other % n
                remote(
                    buf.at[os, ob], out.at[os, index], back_s.at[other], back_r.at[number], (ob, os)
                ).start()

        def squares(buf):
            total = jnp.zeros((1, 1), F32)
            for k in range(SEQ):
                block = buf[k].astype(F32).reshape(size, buf.shape[3])
                total = total + jnp.sum(block * block, keepdims=True)
            return 1.0 / (jnp.sqrt(total) + tiny_norm)

        @pl.when(is_attn)
        def _():
            collect(attn_in)
            inverse = squares(attn_in)
            step = -(-quarter // 128) * 128
            span = SEQ * step
            x32[:, :span] = jnp.zeros((size, span), F32)
            for k in range(SEQ):
                block = attn_in[k].astype(F32).reshape(size, quarter)
                x32[:, k * step : k * step + quarter] = block * inverse
            xlow[:, :span] = x32[:, :span].astype(BF16)
            newton_schulz(
                x32.at[:, pl.ds(0, span)], xlow.at[:, pl.ds(0, span)], gram, gram_low, poly, diag
            )
            for k in range(SEQ):
                block = xlow[:, k * step : k * step + quarter]
                attn_in[k] = block.reshape(attn_in.shape[1:])
            give(attn_in, attn_orth, number)

        @pl.when(is_wide)
        def _():
            collect(wide_in)
            inverse = squares(wide_in)
            if width != size:
                x32[...] = jnp.zeros(x32.shape, F32)

            @pl.when(mine[4])
            def _():
                for k in range(SEQ):
                    block = wide_in[k].astype(F32).reshape(size, width)
                    x32[:, k * size : k * size + width] = block * inverse

            @pl.when(mine[5])
            def _():
                for k in range(SEQ):
                    block = wide_in[k].astype(F32).reshape(size, width)
                    x32[:width, k * size : (k + 1) * size] = block.T * inverse

            for k in range(SEQ):
                xlow[:, k * size : (k + 1) * size] = x32[:, k * size : (k + 1) * size].astype(BF16)
            newton_schulz(x32, xlow, gram, gram_low, poly, diag)

            @pl.when(mine[4])
            def _():
                for k in range(SEQ):
                    block = xlow[:, k * size : k * size + width]
                    wide_in[k] = block.reshape(wide_in.shape[1:])

            @pl.when(mine[5])
            def _():
                for k in range(SEQ):
                    block = x32[:width, k * size : (k + 1) * size].T.astype(BF16)
                    wide_in[k] = block.reshape(wide_in.shape[1:])

            give(wide_in, wide_orth, number - 4)

        def onward(k, step, source, target):
            out = attn_orth.at[source, k] if k < 4 else wide_orth.at[source, k - 4]
            return remote(out, out, seq_s.at[k, step], seq_r.at[k, step], (b, target))

        done = (0, 1, 2, 3, 4, 5)
        for k in done:

            @pl.when(jnp.logical_not(mine[k]))
            def _(k=k):
                remote(piece(k), result(k), ss.at[k], back_r.at[k], (0, 0)).wait_recv()

            @pl.when(mine[k])
            def _(k=k):
                pltpu.make_async_copy(piece(k), result(k), own.at[1]).wait()

            onward(k, 0, s, far).start()
            onward(k, 1, s, near).start()
        for k in done:
            onward(k, 0, far, far).wait_recv()
            onward(k, 2, far, near).start()
        for k in done:
            onward(k, 1, near, near).wait_recv()
            onward(k, 2, (near + 2) % 4, near).wait_recv()
            onward(k, 0, s, far).wait_send()
            onward(k, 1, s, near).wait_send()
            onward(k, 2, far, near).wait_send()

            @pl.when(jnp.logical_not(mine[k]))
            def _(k=k):
                remote(piece(k), inbox(k).at[s, b], ss.at[k], rs.at[me], (0, 0)).wait_send()

        def given(buf):
            @pl.loop(1, SEQ * n)
            def _(k):
                other = (me + k) % (SEQ * n)
                place = buf.at[other // n, other % n]
                remote(place, place, back_s.at[other], back_r.at[0], (0, 0)).wait_send()

        @pl.when(is_attn)
        def _():
            given(attn_in)

        @pl.when(is_wide)
        def _():
            given(wide_in)


def newton_schulz(x32, xlow, gram, gram_low, poly, diag):
    size, wide = x32.shape
    eye = lax.broadcasted_iota(jnp.int32, (size, size), 0) == lax.broadcasted_iota(
        jnp.int32, (size, size), 1
    )
    chunk = 768 if wide % 768 == 0 else 512

    @pl.loop(0, NS)
    def _(turn):
        whole = contract_last(xlow[...], xlow[...])
        gram[...] = whole
        gram_low[...] = jnp.where(eye, 0.0, whole).astype(BF16)
        whole = gram[...]
        on_diag = jnp.where(eye, whole, 0.0)
        down = jnp.sum(on_diag, axis=1, keepdims=True)
        along = jnp.sum(on_diag, axis=0, keepdims=True)
        square = (
            matmul(gram_low[...], gram_low[...])
            + (down + along) * jnp.where(eye, 0.0, whole)
            + jnp.where(eye, down * down, 0.0)
        )
        mixed = -4.775 * whole + 2.0315 * square
        diag[...] = jnp.sum(jnp.where(eye, mixed, 0.0), axis=1, keepdims=True) + 3.4445
        poly[...] = jnp.where(eye, 0.0, mixed).astype(BF16)
        for c in range(0, wide, chunk):
            moved = diag[...] * x32[:, c : c + chunk] + matmul(poly[...], xlow[:, c : c + chunk])
            x32[:, c : c + chunk] = moved
            xlow[:, c : c + chunk] = moved.astype(BF16)


def greet(n, kinds):
    b, s, hi, lo, m = coords(n)
    barrier = pltpu.get_barrier_semaphore()
    if "all" in kinds:
        me = s * n + b

        @pl.loop(1, SEQ * n)
        def _(k):
            other = (me + k) % (SEQ * n)
            pl.semaphore_signal(
                barrier, inc=1, device_id=(other % n, other // n), device_id_type=MESH
            )

        pl.semaphore_wait(barrier, SEQ * n - 1)
        return
    peers = []
    if "seq" in kinds:
        peers += [(b, (s + k) % 4) for k in (1, 2, 3)]
    if "batch" in kinds:
        peers += [(((hi + d) % m) * 2 + lo, s) for d in range(1, m)]
        peers += [(hi * 2 + 1 - lo, s)]
    for peer in peers:
        pl.semaphore_signal(barrier, inc=1, device_id=peer, device_id_type=MESH)
    pl.semaphore_wait(barrier, len(peers))


def exchange(n, collective_id, name, *ops):
    ins = [a for op in ops for a in op.ins]
    outs = [o for op in ops for o in op.outs]
    scratch = [c for op in ops for c in op.scratch]
    kinds = {k for op in ops for k in op.peers}

    def kernel(*refs):
        in_refs, out_refs = refs[: len(ins)], refs[len(ins) : len(ins) + len(outs)]
        scratch_refs = refs[len(ins) + len(outs) :]
        greet(n, kinds)
        live = []
        i = o = c = 0
        for op in ops:
            ni, no, nc = len(op.ins), len(op.outs), len(op.scratch)
            live.append(
                op.run(*in_refs[i : i + ni], *out_refs[o : o + no], *scratch_refs[c : c + nc])
            )
            i, o, c = i + ni, o + no, c + nc
        while live:
            still = []
            for step in live:
                try:
                    next(step)
                    still.append(step)
                except StopIteration:
                    pass
            live = still

    vmem = pl.BlockSpec(memory_space=pltpu.VMEM)
    return pl.pallas_call(
        kernel,
        out_shape=outs,
        in_specs=[vmem] * len(ins),
        out_specs=[vmem] * len(outs),
        scratch_shapes=scratch,
        compiler_params=pltpu.CompilerParams(
            collective_id=collective_id, has_side_effects=True, vmem_limit_bytes=60 * 2**20
        ),
        name=name,
    )(*ins)


def contract_last(left, right):
    return lax.dot_general(left, right, (((1,), (1,)), ((), ())), preferred_element_type=F32)


def contract_first(left, right):
    return lax.dot_general(left, right, (((0,), (0,)), ((), ())), preferred_element_type=F32)


def matmul(left, right):
    return jnp.dot(left, right, preferred_element_type=F32)


def exact_gelu(value_in):
    return jax.nn.gelu(value_in, approximate=False)


def normalize(hidden, gain_row):
    row_mean = jnp.mean(hidden, axis=-1, keepdims=True)
    centred = hidden - row_mean
    spread = lax.rsqrt(jnp.mean(centred * centred, axis=-1, keepdims=True) + norm_eps)
    scaled = centred * spread
    return (scaled * gain_row, scaled, spread)


def normalize_back(grad_in, scaled, spread, gain_row):
    weighted = grad_in * gain_row
    mean_first = jnp.mean(weighted, axis=-1, keepdims=True)
    second = jnp.mean(weighted * scaled, axis=-1, keepdims=True)
    return (
        spread * (weighted - mean_first - scaled * second),
        jnp.sum(grad_in * scaled, axis=0),
        jnp.sum(grad_in, axis=0),
    )


def step_factor(rows_all, cols_all):
    return matrix_rate * math.sqrt(max(1.0, rows_all / cols_all))


def make_body(n):
    def body(
        layer_input,
        lengths,
        attn_weight,
        up_weight,
        down_weight,
        vectors,
        attn_moment,
        up_moment,
        down_moment,
        vector_moment,
        out_grad,
        pool_grad,
    ):
        rows, span, width = layer_input.shape
        local = rows * span
        span_all = span * SEQ
        own_rows = width // n
        quarter = width // SEQ
        hidden = up_weight.shape[1]
        hid_q = hidden // SEQ
        hid_own = hidden // n // SEQ
        seq_index = lax.axis_index("seq")

        def attn_quarter(stacked):
            part = lax.dynamic_index_in_dim(
                stacked.reshape(4, own_rows, SEQ, quarter), seq_index, 2, False
            )
            return part

        def up_quarter(matrix):
            return lax.dynamic_index_in_dim(
                matrix.reshape(own_rows, n, SEQ, hid_own), seq_index, 2, False
            ).reshape(own_rows, hid_q)

        def down_quarter(matrix):
            return lax.dynamic_index_in_dim(
                matrix.reshape(SEQ, hid_own, width), seq_index, 0, False
            )

        attn_low = attn_quarter(attn_weight).astype(BF16).transpose(1, 0, 2).reshape(own_rows, width)
        up_low = up_quarter(up_weight).astype(BF16)
        down_low = down_quarter(down_weight).astype(BF16)
        vec_low = vectors.astype(BF16).astype(F32)

        tokens = layer_input.reshape(local, width)
        token_own = tokens.astype(BF16)
        w_attn, vec_all, x_all, pool_all = exchange(
            n,
            0,
            "gather_attn",
            GatherBatch(n, attn_low),
            GatherBatch(n, vec_low),
            GatherSeq(n, token_own),
            GatherSeq(n, pool_grad),
        )
        w_attn = w_attn.reshape(width, width)
        w_qkv, w_out_part = w_attn[:, : 3 * quarter], w_attn[:, 3 * quarter :]
        vec_full = vec_all.transpose(1, 0, 2).reshape(-1, width)
        bias_out, gain_one, shift_one, gain_two, shift_two, bias_down = [
            vec_full[k] for k in range(2, 8)
        ]
        bias_qv = lax.dynamic_index_in_dim(
            vec_full[:2].reshape(2, SEQ, quarter), seq_index, 1, False
        )
        bias_qkv = jnp.concatenate([bias_qv[0], jnp.zeros_like(bias_qv[0]), bias_qv[1]])
        bias_up = lax.dynamic_index_in_dim(
            vec_full[8:].reshape(n, SEQ, hid_own), seq_index, 1, False
        ).reshape(hid_q)
        x_all = x_all.reshape(SEQ * local, width)
        pool_whole = pool_all.transpose(1, 0, 2).reshape(rows, width)

        qkv = (matmul(x_all, w_qkv) + bias_qkv).astype(BF16)
        qkv = qkv.reshape(SEQ, rows, span, 3, HEADS, HD).transpose(3, 1, 4, 0, 2, 5)
        query, key, value = qkv.reshape(3, rows, HEADS, span_all, HD)
        scale = HD ** (-0.5)
        scores = (
            jnp.einsum("rhqd,rhkd->rhqk", query, key, preferred_element_type=F32) * scale
        )
        key_valid = jnp.arange(span_all)[None, :] < lengths[:, None]
        scores = jnp.where(key_valid[:, None, None, :], scores, -1e30)
        exponent = jnp.exp(scores - jnp.max(scores, axis=-1, keepdims=True))
        prob = exponent / jnp.sum(exponent, axis=-1, keepdims=True)
        prob_low = prob.astype(BF16)
        mixed = jnp.einsum("rhqk,rhkd->rhqd", prob_low, value, preferred_element_type=F32)
        context_out = (
            mixed.astype(BF16)
            .reshape(rows, HEADS, SEQ, span, HD)
            .transpose(2, 0, 3, 1, 4)
            .reshape(SEQ, local, quarter)
        )
        context_in, w_out, w_up = exchange(
            n,
            1,
            "swap_context",
            SwapSeq(n, context_out),
            GatherSeq(n, w_out_part),
            GatherBatch(n, up_low),
        )
        context = context_in.transpose(1, 0, 2).reshape(local, width)
        w_out = w_out.transpose(1, 0, 2).reshape(width, width)
        w_up = w_up.reshape(width, hid_q)

        branch = matmul(context, w_out) + bias_out
        normed_part, scaled_one, spread_one = normalize(tokens + branch, gain_one)
        normed_one = normed_part + shift_one
        y_all, w_down = exchange(
            n,
            2,
            "gather_hidden",
            GatherSeq(n, normed_one.astype(BF16)),
            GatherBatch(n, down_low),
        )
        y_all = y_all.reshape(SEQ * local, width)
        w_down = w_down.reshape(hid_q, width)
        pre_act = matmul(y_all, w_up) + bias_up
        activated, gelu_pull = jax.vjp(exact_gelu, pre_act)
        act_low = activated.astype(BF16)
        down_part = matmul(act_low, w_down).reshape(SEQ, local, width)
        (down_sum,) = exchange(n, 3, "sum_down", ScatterSeq(n, down_part))
        output_part, scaled_two, spread_two = normalize(
            normed_one + down_sum + bias_down, gain_two
        )
        output = output_part + shift_two
        position = seq_index * span + jnp.arange(span)
        live_mask = (position[None, :] < lengths[:, None]).astype(F32)
        row_length = lengths.astype(F32)[:, None]
        out_rows = output.reshape(rows, span, width)
        partial_pool = jnp.sum(out_rows * live_mask[..., None], axis=1) / row_length
        upstream = (
            live_mask[..., None] * (out_grad + (pool_whole / row_length)[:, None, :])
        ).reshape(local, width)
        second_grad, grad_gain_two, grad_shift_two = normalize_back(
            upstream, scaled_two, spread_two, gain_two
        )
        z_low = second_grad.astype(BF16)
        grad_bias_down = jnp.sum(z_low.astype(F32), axis=0)
        z_all, pool_parts = exchange(
            n, 4, "gather_dz", GatherSeq(n, z_low), GatherSeq(n, partial_pool)
        )
        pooled = lax.dynamic_slice_in_dim(
            (pool_parts[0] + pool_parts[1]) + (pool_parts[2] + pool_parts[3]),
            seq_index * quarter,
            quarter,
            1,
        )
        z_all = z_all.reshape(SEQ * local, width)
        (pre_grad,) = gelu_pull(contract_last(z_all, w_down))
        pre_low = pre_grad.astype(BF16)
        grad_bias_up = jnp.sum(pre_low.astype(F32), axis=0)
        grad_down = contract_first(act_low, z_all)
        hidden_part = contract_last(pre_low, w_up).reshape(SEQ, local, width)
        hidden_sum, down_piece = exchange(
            n,
            5,
            "sum_hidden",
            ScatterSeq(n, hidden_part),
            ScatterBatch(n, grad_down.reshape(n, hid_own, width)),
        )
        grad_up = contract_first(y_all, pre_low)
        first_grad, grad_gain_one, grad_shift_one = normalize_back(
            hidden_sum + second_grad, scaled_one, spread_one, gain_one
        )
        a_low = first_grad.astype(BF16)
        grad_bias_out = jnp.sum(a_low.astype(F32), axis=0)
        context_grad = contract_last(a_low, w_out).astype(BF16)
        grad_out = contract_first(context, a_low)
        up_piece, context_back, out_part = exchange(
            n,
            6,
            "swap_dcontext",
            ScatterBatch(n, grad_up.reshape(n, own_rows, hid_q)),
            SwapSeq(n, context_grad.reshape(local, SEQ, quarter).transpose(1, 0, 2)),
            ScatterSeq(n, grad_out.reshape(width, SEQ, quarter).transpose(1, 0, 2)),
        )
        arriving = (
            context_back.reshape(SEQ, rows, span, HEADS, HD)
            .transpose(1, 3, 0, 2, 4)
            .reshape(rows, HEADS, span_all, HD)
        )
        prob_grad = jnp.einsum("rhqd,rhkd->rhqk", arriving, value, preferred_element_type=F32)
        row_delta = jnp.sum(prob * prob_grad, axis=-1, keepdims=True)
        score_grad = (prob * (prob_grad - row_delta)).astype(BF16)
        query_grad = (
            jnp.einsum("rhqk,rhkd->rhqd", score_grad, key, preferred_element_type=F32) * scale
        )
        key_grad = (
            jnp.einsum("rhqk,rhqd->rhkd", score_grad, query, preferred_element_type=F32) * scale
        )
        value_grad = jnp.einsum(
            "rhqk,rhqd->rhkd", prob_low, arriving, preferred_element_type=F32
        )
        qkv_grad = (
            jnp.stack([query_grad, key_grad, value_grad])
            .astype(BF16)
            .reshape(3, rows, HEADS, SEQ, span, HD)
            .transpose(3, 1, 4, 0, 2, 5)
            .reshape(SEQ * local, 3 * quarter)
        )
        input_part = contract_last(qkv_grad, w_qkv).reshape(SEQ, local, width)
        attn_local = jnp.concatenate([contract_first(x_all, qkv_grad), out_part], axis=1)
        bias_sums = jnp.sum(qkv_grad.astype(F32), axis=0).reshape(3, quarter)

        vec_head = jnp.zeros((2, SEQ, quarter), F32)
        vec_head = lax.dynamic_update_slice(
            vec_head, bias_sums[jnp.array([0, 2])][:, None], (0, seq_index, 0)
        ).reshape(2, width)
        vec_mid = jnp.stack(
            [
                grad_bias_out,
                grad_gain_one,
                grad_shift_one,
                grad_gain_two,
                grad_shift_two,
                grad_bias_down,
            ]
        )
        vec_tail = lax.dynamic_update_slice(
            jnp.zeros((n, SEQ, hid_own), F32),
            grad_bias_up.reshape(n, 1, hid_own),
            (0, seq_index, 0),
        ).reshape(-1, width)
        vec_local = jnp.concatenate([vec_head, vec_mid, vec_tail])
        vec_local = vec_local.reshape(-1, n, own_rows).transpose(1, 0, 2)
        input_sum, attn_piece, vec_piece = exchange(
            n,
            7,
            "sum_input",
            ScatterSeq(n, input_part),
            ScatterBatch(n, attn_local.reshape(n, own_rows, width)),
            ScatterBatch(n, vec_local, F32),
        )
        input_grad = input_sum + first_grad

        attn_bf = attn_piece.astype(BF16).reshape(own_rows, 4, quarter).transpose(1, 0, 2)
        wide_bf = jnp.stack([up_piece, down_piece]).astype(BF16)
        attn_send = (matrix_decay * attn_quarter(attn_moment) + attn_bf.astype(F32)).astype(BF16)
        wide_moment = jnp.stack([up_quarter(up_moment), down_quarter(down_moment)])
        wide_send = (matrix_decay * wide_moment + wide_bf.astype(F32)).astype(BF16)
        short = -own_rows % 16
        attn_send = jnp.pad(attn_send, ((0, 0), (0, short), (0, 0)))
        wide_send = jnp.pad(wide_send, ((0, 0), (0, short), (0, 0)))
        attn_all, wide_all, vec_parts, attn_orth, wide_orth = exchange(
            n,
            8,
            "muon",
            GatherSeq(n, attn_bf),
            GatherSeq(n, wide_bf),
            GatherSeq(n, vec_piece),
            Muon(n, attn_send, wide_send),
        )
        attn_orth = attn_orth[:, :, :own_rows]
        wide_orth = wide_orth[:, :, :own_rows]

        def join_attn(parts):
            return parts.astype(F32).transpose(1, 2, 0, 3).reshape(4, own_rows, width)

        def join_up(parts):
            return (
                parts.astype(F32)
                .reshape(SEQ, own_rows, n, hid_own)
                .transpose(1, 2, 0, 3)
                .reshape(own_rows, hidden)
            )

        def join_down(parts):
            return parts.astype(F32).reshape(SEQ * hid_own, width)

        attn_grad = join_attn(attn_all)
        up_grad, down_grad = join_up(wide_all[:, 0]), join_down(wide_all[:, 1])
        vector_grad = (vec_parts[0] + vec_parts[1]) + (vec_parts[2] + vec_parts[3])
        attn_next = matrix_decay * attn_moment + attn_grad
        up_next = matrix_decay * up_moment + up_grad
        down_next = matrix_decay * down_moment + down_grad

        factors = [
            step_factor(width, width),
            step_factor(width, hidden),
            step_factor(hidden, width),
        ]
        attn_new = attn_weight - factors[0] * join_attn(attn_orth)
        up_new = up_weight - factors[1] * join_up(wide_orth[:, 0])
        down_new = down_weight - factors[2] * join_down(wide_orth[:, 1])
        vector_next = vector_decay * vector_moment + vector_grad
        vectors_new = vectors - vector_rate / math.sqrt(rows * n) * vector_next
        return (
            out_rows,
            pooled,
            input_grad.reshape(rows, span, width),
            attn_grad,
            up_grad,
            down_grad,
            vector_grad,
            attn_next,
            up_next,
            down_next,
            vector_next,
            attn_new,
            up_new,
            down_new,
            vectors_new,
        )

    return body


def solution(mesh):
    placed = (
        P("batch", "seq", None),
        P("batch"),
        P(None, "batch", None),
        P("batch", None),
        P("batch", None),
        P(None, "batch"),
        P(None, "batch", None),
        P("batch", None),
        P("batch", None),
        P(None, "batch"),
        P("batch", "seq", None),
        P("batch", "seq"),
    )
    return jax.shard_map(
        make_body(mesh.shape["batch"]),
        mesh=mesh,
        in_specs=placed,
        out_specs=(
            P("batch", "seq", None),
            P("batch", "seq"),
            P("batch", "seq", None),
            P(None, "batch", None),
            P("batch", None),
            P("batch", None),
            P(None, "batch"),
            P(None, "batch", None),
            P("batch", None),
            P("batch", None),
            P(None, "batch"),
            P(None, "batch", None),
            P("batch", None),
            P("batch", None),
            P(None, "batch"),
        ),
        check_vma=False,
    )
```

```python
import math

import jax
import jax.numpy as jnp
from jax import lax
from jax.experimental import pallas as pl
from jax.experimental.pallas import tpu as pltpu
from jax.sharding import PartitionSpec as P

H = 12
HD = 64
NS = 5
SEQ = 4
HEADS = H // SEQ

norm_eps = 1e-12
tiny_norm = 1e-07
matrix_decay = 0.95
vector_decay = 0.5
matrix_rate = 0.5
vector_rate = 0.03

MESH = pl.DeviceIdType.MESH
F32 = jnp.float32
BF16 = jnp.bfloat16


def coords(n):
    b = lax.axis_index("batch")
    s = lax.axis_index("seq")
    return b, s, b // 2, b % 2, n // 2


def remote(src, dst, send, recv, device):
    return pltpu.make_async_remote_copy(
        src_ref=src, dst_ref=dst, send_sem=send, recv_sem=recv, device_id=device, device_id_type=MESH
    )


class GatherBatch:
    peers = ("batch",)

    def __init__(self, n, src):
        self.n = n
        self.ins = [src]
        self.outs = [jax.ShapeDtypeStruct((n,) + src.shape, src.dtype)]
        m = n // 2
        self.scratch = [pltpu.SemaphoreType.DMA((m,))] * 4 + [pltpu.SemaphoreType.DMA]

    def run(self, src, dst, zs, zr, ys, yr, own):
        b, s, hi, lo, m = coords(self.n)
        local = pltpu.make_async_copy(src, dst.at[b], own)
        local.start()
        pair = (hi * 2 + 1 - lo, s)
        out = []
        for d in range(1, m):
            c = remote(src, dst.at[b], zs.at[d], zr.at[d], (((hi + d) % m) * 2 + lo, s))
            c.start()
            out.append(c)
        first = remote(src, dst.at[b], ys.at[0], yr.at[0], pair)
        first.start()
        yield
        passed = [first]
        for d in range(1, m):
            out[d - 1].wait_recv()
            block = ((hi + m - d) % m) * 2 + lo
            c = remote(dst.at[block], dst.at[block], ys.at[d], yr.at[d], pair)
            c.start()
            passed.append(c)
            yield
        local.wait()
        for c in passed:
            c.wait()
        for c in out:
            c.wait_send()


class ScatterBatch:
    peers = ("batch",)

    def __init__(self, n, src, wire=BF16):
        self.n = n
        self.wire = wire
        self.ins = [src]
        shape = src.shape[1:]
        self.outs = [jax.ShapeDtypeStruct(shape, F32)]
        m = n // 2
        self.scratch = [pltpu.VMEM((m,) + shape, wire)] * 4 + [pltpu.SemaphoreType.DMA((m,))] * 4

    def run(self, src, dst, ysend, yrecv, zsend, zrecv, ys, yr, zs, zr):
        b, s, hi, lo, m = coords(self.n)
        pair = (hi * 2 + 1 - lo, s)
        first = {}
        order = list(range(1, m)) + [0]
        for d in order:
            h = (hi + d) % m
            ysend[d] = src[h * 2 + 1 - lo].astype(self.wire)
            first[d] = remote(ysend.at[d], yrecv.at[d], ys.at[d], yr.at[d], pair)
            first[d].start()
        yield
        second = []
        for d in range(1, m):
            h = (hi + d) % m
            first[d].wait_recv()
            zsend[d] = (src[h * 2 + lo] + yrecv[d].astype(F32)).astype(self.wire)
            c = remote(zsend.at[d], zrecv.at[d], zs.at[d], zr.at[d], (h * 2 + lo, s))
            c.start()
            second.append(c)
            yield
        first[0].wait_recv()
        total = src[b] + yrecv[0].astype(F32)
        for d in range(1, m):
            second[d - 1].wait_recv()
            total = total + zrecv[d].astype(F32)
        dst[...] = total
        for c in list(first.values()) + second:
            c.wait_send()


class GatherSeq:
    peers = ("seq",)

    def __init__(self, n, src):
        self.ins = [src]
        self.outs = [jax.ShapeDtypeStruct((SEQ,) + src.shape, src.dtype)]
        self.scratch = [pltpu.SemaphoreType.DMA((3,))] * 2 + [pltpu.SemaphoreType.DMA]

    def run(self, src, dst, ss, rs, own):
        b, s = lax.axis_index("batch"), lax.axis_index("seq")
        far, near = (s + 2) % 4, s + 1 - 2 * (s % 2)
        across = remote(src, dst.at[s], ss.at[0], rs.at[0], (b, far))
        across.start()
        local = pltpu.make_async_copy(src, dst.at[s], own)
        local.start()
        beside = remote(src, dst.at[s], ss.at[1], rs.at[1], (b, near))
        beside.start()
        yield
        across.wait_recv()
        passed = remote(dst.at[far], dst.at[far], ss.at[2], rs.at[2], (b, near))
        passed.start()
        yield
        local.wait()
        beside.wait()
        passed.wait()
        across.wait_send()


class ScatterSeq:
    peers = ("seq",)

    def __init__(self, n, src):
        self.ins = [src]
        shape = src.shape[1:]
        self.outs = [jax.ShapeDtypeStruct(shape, F32)]
        self.scratch = [
            pltpu.VMEM((2,) + shape, BF16),
            pltpu.VMEM((2,) + shape, BF16),
            pltpu.VMEM(shape, BF16),
            pltpu.VMEM(shape, BF16),
            pltpu.SemaphoreType.DMA((3,)),
            pltpu.SemaphoreType.DMA((3,)),
        ]

    def run(self, src, dst, near_out, near_in, far_out, far_in, ss, rs):
        b, s = lax.axis_index("batch"), lax.axis_index("seq")
        far, near = (s + 2) % 4, s + 1 - 2 * (s % 2)
        near_far = (near + 2) % 4
        near_out[1] = src[near_far].astype(BF16)
        one = remote(near_out.at[1], near_in.at[1], ss.at[1], rs.at[1], (b, near))
        one.start()
        near_out[0] = src[near].astype(BF16)
        two = remote(near_out.at[0], near_in.at[0], ss.at[0], rs.at[0], (b, near))
        two.start()
        yield
        one.wait_recv()
        far_out[...] = (src[far] + near_in[1].astype(F32)).astype(BF16)
        three = remote(far_out, far_in, ss.at[2], rs.at[2], (b, far))
        three.start()
        yield
        two.wait_recv()
        dst[...] = src[s] + near_in[0].astype(F32)
        yield
        three.wait_recv()
        dst[...] = dst[...] + far_in[...].astype(F32)
        one.wait_send()
        two.wait_send()
        three.wait_send()


class SwapSeq:
    peers = ("seq",)

    def __init__(self, n, src):
        self.ins = [src]
        self.outs = [jax.ShapeDtypeStruct(src.shape, src.dtype)]
        self.scratch = [pltpu.SemaphoreType.DMA((4,))] * 2 + [pltpu.SemaphoreType.DMA]

    def run(self, src, dst, ss, rs, own):
        b, s = lax.axis_index("batch"), lax.axis_index("seq")
        copies = []
        for k in (2, 3, 1):
            other = (s + k) % 4
            c = remote(src.at[other], dst.at[s], ss.at[k], rs.at[k], (b, other))
            c.start()
            copies.append(c)
        local = pltpu.make_async_copy(src.at[s], dst.at[s], own)
        local.start()
        yield
        local.wait()
        for c in copies:
            c.wait()


def owner_list(n):
    return [(0, 2), (1, 0), (n - 2, 2), (n - 1, 0), (n // 4, 0), (n // 2 + 1, 2)]


class Muon:
    peers = ("all",)

    def __init__(self, n, attn_piece, wide_piece):
        self.n = n
        self.ins = [attn_piece, wide_piece]
        rows, quarter = attn_piece.shape[1:]
        width = wide_piece.shape[2]
        self.outs = [
            jax.ShapeDtypeStruct((SEQ, 4, rows, quarter), BF16),
            jax.ShapeDtypeStruct((SEQ, 2, rows, width), BF16),
        ]
        size = n * rows
        dma = pltpu.SemaphoreType.DMA
        self.scratch = [
            pltpu.VMEM((SEQ, n, rows, quarter), BF16),
            pltpu.VMEM((SEQ, n, rows, width), BF16),
            pltpu.VMEM((size, SEQ * size), F32),
            pltpu.VMEM((size, SEQ * size), BF16),
            pltpu.VMEM((size, size), F32),
            pltpu.VMEM((size, size), BF16),
            pltpu.VMEM((size, size), BF16),
            pltpu.VMEM((size, 1), F32),
            dma((6,)),
            dma((SEQ * n,)),
            dma((SEQ * n,)),
            dma((6,)),
            dma((6, 3)),
            dma((6, 3)),
            dma((2,)),
        ]

    def run(
        self, attn, wide, attn_orth, wide_orth, attn_in, wide_in, x32, xlow, gram, gram_low, poly, diag,
        ss, rs, back_s, back_r, seq_s, seq_r, own,
    ):
        n = self.n
        b, s = lax.axis_index("batch"), lax.axis_index("seq")
        me = s * n + b
        far, near = (s + 2) % 4, s + 1 - 2 * (s % 2)
        size = x32.shape[0]
        width = wide.shape[2]
        quarter = attn.shape[2]
        places = owner_list(n)
        mine = [(b == ob) & (s == os) for ob, os in places]
        number = jnp.int32(0)
        for k in range(6):
            number = jnp.where(mine[k], jnp.int32(k), number)
        is_attn = mine[0] | mine[1] | mine[2] | mine[3]
        is_wide = mine[4] | mine[5]
        order = (5, 4, 0, 1, 2, 3)

        def piece(k):
            return attn.at[k] if k < 4 else wide.at[k - 4]

        def inbox(k):
            return attn_in if k < 4 else wide_in

        def result(k):
            return attn_orth.at[s, k] if k < 4 else wide_orth.at[s, k - 4]

        for k in order:
            ob, os = places[k]

            @pl.when(jnp.logical_not(mine[k]))
            def _(k=k, ob=ob, os=os):
                remote(piece(k), inbox(k).at[s, b], ss.at[k], rs.at[me], (ob, os)).start()

            @pl.when(mine[k])
            def _(k=k):
                pltpu.make_async_copy(piece(k), inbox(k).at[s, b], own.at[0]).start()

        yield
        yield
        yield
        yield

        def collect(buf):
            pltpu.make_async_copy(buf.at[s, b], buf.at[s, b], own.at[0]).wait()

            @pl.loop(1, SEQ * n)
            def _(k):
                other = (me + k) % (SEQ * n)
                place = buf.at[other // n, other % n]
                remote(place, place, ss.at[0], rs.at[other], (0, 0)).wait_recv()

        def give(buf, out, index):
            pltpu.make_async_copy(buf.at[s, b], out.at[s, index], own.at[1]).start()

            @pl.loop(1, SEQ * n)
            def _(k):
                other = (me + k) % (SEQ * n)
                os, ob = other // n, other % n
                remote(
                    buf.at[os, ob], out.at[os, index], back_s.at[other], back_r.at[number], (ob, os)
                ).start()

        def squares(buf):
            total = jnp.zeros((1, 1), F32)
            for k in range(SEQ):
                block = buf[k].astype(F32).reshape(size, buf.shape[3])
                total = total + jnp.sum(block * block, keepdims=True)
            return 1.0 / (jnp.sqrt(total) + tiny_norm)

        @pl.when(is_attn)
        def _():
            collect(attn_in)
            inverse = squares(attn_in)
            step = -(-quarter // 128) * 128
            span = SEQ * step
            x32[:, :span] = jnp.zeros((size, span), F32)
            for k in range(SEQ):
                block = attn_in[k].astype(F32).reshape(size, quarter)
                x32[:, k * step : k * step + quarter] = block * inverse
            xlow[:, :span] = x32[:, :span].astype(BF16)
            newton_schulz(
                x32.at[:, pl.ds(0, span)], xlow.at[:, pl.ds(0, span)], gram, gram_low, poly, diag
            )
            for k in range(SEQ):
                block = xlow[:, k * step : k * step + quarter]
                attn_in[k] = block.reshape(attn_in.shape[1:])
            give(attn_in, attn_orth, number)

        @pl.when(is_wide)
        def _():
            collect(wide_in)
            inverse = squares(wide_in)
            if width != size:
                x32[...] = jnp.zeros(x32.shape, F32)

            @pl.when(mine[4])
            def _():
                for k in range(SEQ):
                    block = wide_in[k].astype(F32).reshape(size, width)
                    x32[:, k * size : k * size + width] = block * inverse

            @pl.when(mine[5])
            def _():
                for k in range(SEQ):
                    block = wide_in[k].astype(F32).reshape(size, width)
                    x32[:width, k * size : (k + 1) * size] = block.T * inverse

            for k in range(SEQ):
                xlow[:, k * size : (k + 1) * size] = x32[:, k * size : (k + 1) * size].astype(BF16)
            newton_schulz(x32, xlow, gram, gram_low, poly, diag)

            @pl.when(mine[4])
            def _():
                for k in range(SEQ):
                    block = xlow[:, k * size : k * size + width]
                    wide_in[k] = block.reshape(wide_in.shape[1:])

            @pl.when(mine[5])
            def _():
                for k in range(SEQ):
                    block = x32[:width, k * size : (k + 1) * size].T.astype(BF16)
                    wide_in[k] = block.reshape(wide_in.shape[1:])

            give(wide_in, wide_orth, number - 4)

        def onward(k, step, source, target):
            out = attn_orth.at[source, k] if k < 4 else wide_orth.at[source, k - 4]
            return remote(out, out, seq_s.at[k, step], seq_r.at[k, step], (b, target))

        done = (0, 1, 2, 3, 4, 5)
        for k in done:

            @pl.when(jnp.logical_not(mine[k]))
            def _(k=k):
                remote(piece(k), result(k), ss.at[k], back_r.at[k], (0, 0)).wait_recv()

            @pl.when(mine[k])
            def _(k=k):
                pltpu.make_async_copy(piece(k), result(k), own.at[1]).wait()

            onward(k, 0, s, far).start()
            onward(k, 1, s, near).start()
        for k in done:
            onward(k, 0, far, far).wait_recv()
            onward(k, 2, far, near).start()
        for k in done:
            onward(k, 1, near, near).wait_recv()
            onward(k, 2, (near + 2) % 4, near).wait_recv()
            onward(k, 0, s, far).wait_send()
            onward(k, 1, s, near).wait_send()
            onward(k, 2, far, near).wait_send()

            @pl.when(jnp.logical_not(mine[k]))
            def _(k=k):
                remote(piece(k), inbox(k).at[s, b], ss.at[k], rs.at[me], (0, 0)).wait_send()

        def given(buf):
            @pl.loop(1, SEQ * n)
            def _(k):
                other = (me + k) % (SEQ * n)
                place = buf.at[other // n, other % n]
                remote(place, place, back_s.at[other], back_r.at[0], (0, 0)).wait_send()

        @pl.when(is_attn)
        def _():
            given(attn_in)

        @pl.when(is_wide)
        def _():
            given(wide_in)


def newton_schulz(x32, xlow, gram, gram_low, poly, diag):
    size, wide = x32.shape
    eye = lax.broadcasted_iota(jnp.int32, (size, size), 0) == lax.broadcasted_iota(
        jnp.int32, (size, size), 1
    )
    chunk = 768 if wide % 768 == 0 else 512

    @pl.loop(0, NS)
    def _(turn):
        whole = contract_last(xlow[...], xlow[...])
        gram[...] = whole
        gram_low[...] = jnp.where(eye, 0.0, whole).astype(BF16)
        whole = gram[...]
        on_diag = jnp.where(eye, whole, 0.0)
        down = jnp.sum(on_diag, axis=1, keepdims=True)
        along = jnp.sum(on_diag, axis=0, keepdims=True)
        square = (
            matmul(gram_low[...], gram_low[...])
            + (down + along) * jnp.where(eye, 0.0, whole)
            + jnp.where(eye, down * down, 0.0)
        )
        mixed = -4.775 * whole + 2.0315 * square
        diag[...] = jnp.sum(jnp.where(eye, mixed, 0.0), axis=1, keepdims=True) + 3.4445
        poly[...] = jnp.where(eye, 0.0, mixed).astype(BF16)
        for c in range(0, wide, chunk):
            moved = diag[...] * x32[:, c : c + chunk] + matmul(poly[...], xlow[:, c : c + chunk])
            x32[:, c : c + chunk] = moved
            xlow[:, c : c + chunk] = moved.astype(BF16)


def greet(n, kinds):
    b, s, hi, lo, m = coords(n)
    barrier = pltpu.get_barrier_semaphore()
    if "all" in kinds:
        me = s * n + b

        @pl.loop(1, SEQ * n)
        def _(k):
            other = (me + k) % (SEQ * n)
            pl.semaphore_signal(
                barrier, inc=1, device_id=(other % n, other // n), device_id_type=MESH
            )

        pl.semaphore_wait(barrier, SEQ * n - 1)
        return
    peers = []
    if "seq" in kinds:
        peers += [(b, (s + k) % 4) for k in (1, 2, 3)]
    if "batch" in kinds:
        peers += [(((hi + d) % m) * 2 + lo, s) for d in range(1, m)]
        peers += [(hi * 2 + 1 - lo, s)]
    for peer in peers:
        pl.semaphore_signal(barrier, inc=1, device_id=peer, device_id_type=MESH)
    pl.semaphore_wait(barrier, len(peers))


def exchange(n, collective_id, name, *ops):
    ins = [a for op in ops for a in op.ins]
    outs = [o for op in ops for o in op.outs]
    scratch = [c for op in ops for c in op.scratch]
    kinds = {k for op in ops for k in op.peers}

    def kernel(*refs):
        in_refs, out_refs = refs[: len(ins)], refs[len(ins) : len(ins) + len(outs)]
        scratch_refs = refs[len(ins) + len(outs) :]
        greet(n, kinds)
        live = []
        i = o = c = 0
        for op in ops:
            ni, no, nc = len(op.ins), len(op.outs), len(op.scratch)
            live.append(
                op.run(*in_refs[i : i + ni], *out_refs[o : o + no], *scratch_refs[c : c + nc])
            )
            i, o, c = i + ni, o + no, c + nc
        while live:
            still = []
            for step in live:
                try:
                    next(step)
                    still.append(step)
                except StopIteration:
                    pass
            live = still

    vmem = pl.BlockSpec(memory_space=pltpu.VMEM)
    return pl.pallas_call(
        kernel,
        out_shape=outs,
        in_specs=[vmem] * len(ins),
        out_specs=[vmem] * len(outs),
        scratch_shapes=scratch,
        compiler_params=pltpu.CompilerParams(
            collective_id=collective_id, has_side_effects=True, vmem_limit_bytes=60 * 2**20
        ),
        name=name,
    )(*ins)


def contract_last(left, right):
    return lax.dot_general(left, right, (((1,), (1,)), ((), ())), preferred_element_type=F32)


def contract_first(left, right):
    return lax.dot_general(left, right, (((0,), (0,)), ((), ())), preferred_element_type=F32)


def matmul(left, right):
    return jnp.dot(left, right, preferred_element_type=F32)


def exact_gelu(value_in):
    return jax.nn.gelu(value_in, approximate=False)


def normalize(hidden, gain_row):
    row_mean = jnp.mean(hidden, axis=-1, keepdims=True)
    centred = hidden - row_mean
    spread = lax.rsqrt(jnp.mean(centred * centred, axis=-1, keepdims=True) + norm_eps)
    scaled = centred * spread
    return (scaled * gain_row, scaled, spread)


def normalize_back(grad_in, scaled, spread, gain_row):
    weighted = grad_in * gain_row
    mean_first = jnp.mean(weighted, axis=-1, keepdims=True)
    second = jnp.mean(weighted * scaled, axis=-1, keepdims=True)
    return (
        spread * (weighted - mean_first - scaled * second),
        jnp.sum(grad_in * scaled, axis=0),
        jnp.sum(grad_in, axis=0),
    )


class RowGather:
    @staticmethod
    def scratch():
        return [pltpu.SemaphoreType.DMA((2, 3)), pltpu.SemaphoreType.DMA((2, 3))]

    def __init__(self, buf, ss, rs):
        self.buf, self.ss, self.rs = buf, ss, rs
        self.b, self.s = lax.axis_index("batch"), lax.axis_index("seq")
        self.far, self.near = (self.s + 2) % 4, self.s + 1 - 2 * (self.s % 2)
        self.diag = (self.near + 2) % 4

    def copy(self, r, step, block, device):
        place = self.buf.at[r, block]
        return remote(place, place, self.ss.at[r, step], self.rs.at[r, step], (self.b, device))

    def start(self, r):
        self.copy(r, 0, self.s, self.far).start()
        self.copy(r, 1, self.s, self.near).start()

    def wait_near(self, r):
        self.copy(r, 1, self.near, self.near).wait_recv()

    def pass_far(self, r):
        self.copy(r, 0, self.far, self.far).wait_recv()
        self.copy(r, 2, self.far, self.near).start()

    def wait_diag(self, r):
        self.copy(r, 2, self.diag, self.near).wait_recv()

    def finish(self, r):
        self.copy(r, 0, self.s, self.far).wait_send()
        self.copy(r, 1, self.s, self.near).wait_send()
        self.copy(r, 2, self.far, self.near).wait_send()


class RowScatter:
    @staticmethod
    def scratch(rows, shape):
        return [
            pltpu.VMEM((rows, 2) + shape, BF16),
            pltpu.VMEM((rows, 2) + shape, BF16),
            pltpu.VMEM((rows,) + shape, BF16),
            pltpu.VMEM((rows,) + shape, BF16),
            pltpu.SemaphoreType.DMA((rows, 3)),
            pltpu.SemaphoreType.DMA((rows, 3)),
        ]

    def __init__(self, src, near_out, near_in, far_out, far_in, ss, rs):
        self.src = src
        self.near_out, self.near_in = near_out, near_in
        self.far_out, self.far_in = far_out, far_in
        self.ss, self.rs = ss, rs
        self.b, self.s = lax.axis_index("batch"), lax.axis_index("seq")
        self.far, self.near = (self.s + 2) % 4, self.s + 1 - 2 * (self.s % 2)
        self.diag = (self.near + 2) % 4

    def beside(self, r, k):
        return remote(
            self.near_out.at[r, k], self.near_in.at[r, k], self.ss.at[r, k], self.rs.at[r, k],
            (self.b, self.near),
        )

    def across(self, r):
        return remote(
            self.far_out.at[r], self.far_in.at[r], self.ss.at[r, 2], self.rs.at[r, 2],
            (self.b, self.far),
        )

    def send_near(self, r):
        self.near_out[r, 0] = self.src[r, self.near].astype(BF16)
        self.beside(r, 0).start()

    def send_diag(self, r):
        self.near_out[r, 1] = self.src[r, self.diag].astype(BF16)
        self.beside(r, 1).start()

    def cross(self, r):
        self.beside(r, 1).wait_recv()
        self.far_out[r] = (self.src[r, self.far] + self.near_in[r, 1].astype(F32)).astype(BF16)
        self.across(r).start()

    def total(self, r):
        self.beside(r, 0).wait_recv()
        part = self.src[r, self.s] + self.near_in[r, 0].astype(F32)
        self.across(r).wait_recv()
        return part + self.far_in[r].astype(F32)

    def finish(self, r):
        self.beside(r, 0).wait_send()
        self.beside(r, 1).wait_send()
        self.across(r).wait_send()


def gelu_parts(value):
    cdf = 0.5 * (1.0 + lax.erf(value * math.sqrt(0.5)))
    density = jnp.exp(-0.5 * value * value) * (1.0 / math.sqrt(2.0 * math.pi))
    return value * cdf, cdf + value * density


def row_sum(value):
    return jnp.sum(value, axis=0, keepdims=True)


def hidden_layer(n, normed, scaled_one, spread_one, w_up, w_down, vec, out_grad, pool_whole, lengths):
    rows, span, width = normed.shape
    hid_q = w_up.shape[1]
    aligned = (width // n) % 16 == 0
    block = (n, width // n)
    full = (rows, SEQ, span)
    outs = [
        jax.ShapeDtypeStruct((rows, span, width), F32),
        jax.ShapeDtypeStruct((rows, width), F32),
        jax.ShapeDtypeStruct((rows, span, width), F32),
        jax.ShapeDtypeStruct((8, width), F32),
        jax.ShapeDtypeStruct((width, hid_q), F32),
        jax.ShapeDtypeStruct((width // n, width) if aligned else (hid_q, width), F32),
    ]
    if aligned:
        batch_scratch = ScatterBatch(n, jax.ShapeDtypeStruct(block + (width,), F32)).scratch
        batch_scratch = batch_scratch + [pltpu.VMEM(block + (width,), F32)]
    else:
        batch_scratch = []
    scratch = (
        [
            pltpu.VMEM(full + (width,), BF16),
            pltpu.VMEM(full + (hid_q,), F32),
            pltpu.VMEM(full + (hid_q,), BF16),
            pltpu.VMEM(full + (width,), F32),
            pltpu.VMEM(full + (width,), BF16),
            pltpu.VMEM(full + (hid_q,), BF16),
            pltpu.VMEM(full + (width,), F32),
            pltpu.VMEM((rows, span, width), F32),
            pltpu.VMEM((SEQ, rows, width), F32),
            pltpu.SemaphoreType.DMA((3,)),
            pltpu.SemaphoreType.DMA((3,)),
        ]
        + RowGather.scratch() * 2
        + RowScatter.scratch(rows, (span, width)) * 2
    )

    def kernel(
        normed, scaled_one, spread_one, w_up, w_down, vec, out_grad, pool_whole, lengths,
        out_rows, pooled, first_grad, vec_grad, grad_up, grad_down,
        y_all, slope, act, z_part, dz_all, du_all, dy_part, second, pool_buf, pool_ss, pool_rs,
        *rest,
    ):
        greet(n, {"seq", "batch"} if aligned else {"seq"})
        b, s = lax.axis_index("batch"), lax.axis_index("seq")
        y_gather = RowGather(y_all, *rest[0:2])
        dz_gather = RowGather(dz_all, *rest[2:4])
        z_sum = RowScatter(z_part, *rest[4:10])
        dy_sum = RowScatter(dy_part, *rest[10:16])
        rest = rest[16:]
        far, near, diag = y_gather.far, y_gather.near, y_gather.diag
        gain_one, gain_two, shift_two = vec[1:2], vec[3:4], vec[4:5]
        bias_down, bias_up = vec[5:6], vec[6:7]

        for r in range(rows):
            y_all[r, s] = normed[r].astype(BF16)
            y_gather.start(r)

        def pair(ref, blocks):
            return jnp.concatenate([ref[i] for i in blocks], axis=0)

        def spread(ref, blocks, value):
            for k, i in enumerate(blocks):
                ref[i] = value[k * span : (k + 1) * span].astype(ref.dtype)

        def forward(blocks):
            pre = matmul(pair(y_all, blocks), w_up[...]) + bias_up
            value, rate = gelu_parts(pre)
            low = value.astype(BF16)
            spread(act, blocks, low)
            spread(slope, blocks, rate)
            spread(z_part, blocks, matmul(low, w_down[...]))

        forward([(r, s) for r in range(rows)])
        for r in range(rows):
            y_gather.wait_near(r)
        forward([(r, near) for r in range(rows)])
        for r in range(rows):
            z_sum.send_near(r)
        for r in range(rows):
            y_gather.pass_far(r)
            y_gather.wait_diag(r)
            forward([(r, diag), (r, far)])
            z_sum.send_diag(r)
            z_sum.cross(r)

        position = s * span + lax.broadcasted_iota(jnp.int32, (span, 1), 0)
        grad_gain_two = grad_shift_two = grad_bias_down = jnp.zeros((1, width), F32)
        for r in range(rows):
            hidden = normed[r] + (z_sum.total(r) + bias_down)
            centred = hidden - jnp.mean(hidden, axis=-1, keepdims=True)
            spread_two = lax.rsqrt(jnp.mean(centred * centred, axis=-1, keepdims=True) + norm_eps)
            scaled = centred * spread_two
            output = scaled * gain_two + shift_two
            out_rows[r] = output
            live = (position < lengths[r]).astype(F32)
            length = jnp.full((1, 1), lengths[r], jnp.int32).astype(F32)
            pool_buf[s, r : r + 1] = row_sum(output * live) / length
            upstream = live * (out_grad[r] + pool_whole[r : r + 1] / length)
            weighted = upstream * gain_two
            mean_first = jnp.mean(weighted, axis=-1, keepdims=True)
            mean_second = jnp.mean(weighted * scaled, axis=-1, keepdims=True)
            grad = spread_two * (weighted - mean_first - scaled * mean_second)
            second[r] = grad
            low = grad.astype(BF16)
            dz_all[r, s] = low
            dz_gather.start(r)
            grad_gain_two += row_sum(upstream * scaled)
            grad_shift_two += row_sum(upstream)
            grad_bias_down += row_sum(low.astype(F32))

        def pool_copy(k, block, device):
            place = pool_buf.at[block]
            return remote(place, place, pool_ss.at[k - 1], pool_rs.at[k - 1], (b, device))

        for k in (1, 2, 3):
            pool_copy(k, s, (s + k) % 4).start()

        def backward(blocks):
            rise = contract_last(pair(dz_all, blocks), w_down[...])
            low = (rise * pair(slope, blocks)).astype(BF16)
            spread(du_all, blocks, low)
            spread(dy_part, blocks, contract_last(low, w_up[...]))
            return row_sum(low.astype(F32))

        bias_grad = backward([(r, s) for r in range(rows)])
        for r in range(rows):
            dz_gather.wait_near(r)
        bias_grad += backward([(r, near) for r in range(rows)])
        for r in range(rows):
            dy_sum.send_near(r)
        for r in range(rows):
            dz_gather.pass_far(r)
            dz_gather.wait_diag(r)
            bias_grad += backward([(r, diag), (r, far)])
            dy_sum.send_diag(r)
            dy_sum.cross(r)

        tokens = rows * SEQ * span
        whole = contract_first(act[...].reshape(tokens, hid_q), dz_all[...].reshape(tokens, width))
        if aligned:
            scatter = ScatterBatch(n, jax.ShapeDtypeStruct(block + (width,), F32))
            local = rest[-1]
            local[...] = whole.reshape(block + (width,))
            moving = scatter.run(local, grad_down, *rest[:-1])
            next(moving)
        else:
            grad_down[...] = whole
        grad_up[...] = contract_first(
            y_all[...].reshape(tokens, width), du_all[...].reshape(tokens, hid_q)
        )

        grad_gain_one = grad_shift_one = grad_bias_out = jnp.zeros((1, width), F32)
        for r in range(rows):
            grad = dy_sum.total(r) + second[r]
            scaled = scaled_one[r]
            weighted = grad * gain_one
            mean_first = jnp.mean(weighted, axis=-1, keepdims=True)
            mean_second = jnp.mean(weighted * scaled, axis=-1, keepdims=True)
            first = spread_one[r] * (weighted - mean_first - scaled * mean_second)
            first_grad[r] = first
            grad_gain_one += row_sum(grad * scaled)
            grad_shift_one += row_sum(grad)
            grad_bias_out += row_sum(first.astype(BF16).astype(F32))
        for k, value in enumerate(
            (
                grad_bias_out, grad_gain_one, grad_shift_one, grad_gain_two, grad_shift_two,
                grad_bias_down, bias_grad, jnp.zeros((1, width), F32),
            )
        ):
            vec_grad[k : k + 1] = value

        for k in (1, 2, 3):
            pool_copy(k, (s + 4 - k) % 4, (s + k) % 4).wait_recv()
        pooled[...] = (pool_buf[0] + pool_buf[1]) + (pool_buf[2] + pool_buf[3])
        for k in (1, 2, 3):
            pool_copy(k, s, (s + k) % 4).wait_send()
        for r in range(rows):
            for op in (y_gather, z_sum, dz_gather, dy_sum):
                op.finish(r)
        if aligned:
            for _ in moving:
                pass

    vmem = pl.BlockSpec(memory_space=pltpu.VMEM)
    return pl.pallas_call(
        kernel,
        out_shape=outs,
        in_specs=[vmem] * 8 + [pl.BlockSpec(memory_space=pltpu.SMEM)],
        out_specs=[vmem] * len(outs),
        scratch_shapes=scratch + batch_scratch,
        compiler_params=pltpu.CompilerParams(
            collective_id=3, has_side_effects=True, vmem_limit_bytes=60 * 2**20
        ),
        name="hidden_layer",
    )(normed, scaled_one, spread_one, w_up, w_down, vec, out_grad, pool_whole, lengths)


def step_factor(rows_all, cols_all):
    return matrix_rate * math.sqrt(max(1.0, rows_all / cols_all))


def make_body(n):
    def body(
        layer_input,
        lengths,
        attn_weight,
        up_weight,
        down_weight,
        vectors,
        attn_moment,
        up_moment,
        down_moment,
        vector_moment,
        out_grad,
        pool_grad,
    ):
        rows, span, width = layer_input.shape
        local = rows * span
        span_all = span * SEQ
        own_rows = width // n
        quarter = width // SEQ
        hidden = up_weight.shape[1]
        hid_q = hidden // SEQ
        hid_own = hidden // n // SEQ
        seq_index = lax.axis_index("seq")

        def attn_quarter(stacked):
            part = lax.dynamic_index_in_dim(
                stacked.reshape(4, own_rows, SEQ, quarter), seq_index, 2, False
            )
            return part

        def up_quarter(matrix):
            return lax.dynamic_index_in_dim(
                matrix.reshape(own_rows, n, SEQ, hid_own), seq_index, 2, False
            ).reshape(own_rows, hid_q)

        def down_quarter(matrix):
            return lax.dynamic_index_in_dim(
                matrix.reshape(SEQ, hid_own, width), seq_index, 0, False
            )

        attn_low = attn_quarter(attn_weight).astype(BF16).transpose(1, 0, 2).reshape(own_rows, width)
        up_low = up_quarter(up_weight).astype(BF16)
        down_low = down_quarter(down_weight).astype(BF16)
        vec_low = vectors.astype(BF16).astype(F32)

        tokens = layer_input.reshape(local, width)
        token_own = tokens.astype(BF16)
        w_attn, vec_all, x_all, pool_all = exchange(
            n,
            0,
            "gather_attn",
            GatherBatch(n, attn_low),
            GatherBatch(n, vec_low),
            GatherSeq(n, token_own),
            GatherSeq(n, pool_grad),
        )
        w_attn = w_attn.reshape(width, width)
        w_qkv, w_out_part = w_attn[:, : 3 * quarter], w_attn[:, 3 * quarter :]
        vec_full = vec_all.transpose(1, 0, 2).reshape(-1, width)
        bias_out, gain_one, shift_one, gain_two, shift_two, bias_down = [
            vec_full[k] for k in range(2, 8)
        ]
        bias_qv = lax.dynamic_index_in_dim(
            vec_full[:2].reshape(2, SEQ, quarter), seq_index, 1, False
        )
        bias_qkv = jnp.concatenate([bias_qv[0], jnp.zeros_like(bias_qv[0]), bias_qv[1]])
        bias_up = lax.dynamic_index_in_dim(
            vec_full[8:].reshape(n, SEQ, hid_own), seq_index, 1, False
        ).reshape(hid_q)
        x_all = x_all.reshape(SEQ * local, width)
        pool_whole = pool_all.transpose(1, 0, 2).reshape(rows, width)

        qkv = (matmul(x_all, w_qkv) + bias_qkv).astype(BF16)
        qkv = qkv.reshape(SEQ, rows, span, 3, HEADS, HD).transpose(3, 1, 4, 0, 2, 5)
        query, key, value = qkv.reshape(3, rows, HEADS, span_all, HD)
        scale = HD ** (-0.5)
        scores = (
            jnp.einsum("rhqd,rhkd->rhqk", query, key, preferred_element_type=F32) * scale
        )
        key_valid = jnp.arange(span_all)[None, :] < lengths[:, None]
        scores = jnp.where(key_valid[:, None, None, :], scores, -1e30)
        exponent = jnp.exp(scores - jnp.max(scores, axis=-1, keepdims=True))
        prob = exponent / jnp.sum(exponent, axis=-1, keepdims=True)
        prob_low = prob.astype(BF16)
        mixed = jnp.einsum("rhqk,rhkd->rhqd", prob_low, value, preferred_element_type=F32)
        context_out = (
            mixed.astype(BF16)
            .reshape(rows, HEADS, SEQ, span, HD)
            .transpose(2, 0, 3, 1, 4)
            .reshape(SEQ, local, quarter)
        )
        context_in, w_out, w_up = exchange(
            n,
            1,
            "swap_context",
            SwapSeq(n, context_out),
            GatherSeq(n, w_out_part),
            GatherBatch(n, up_low),
        )
        context = context_in.transpose(1, 0, 2).reshape(local, width)
        w_out = w_out.transpose(1, 0, 2).reshape(width, width)
        w_up = w_up.reshape(width, hid_q)

        branch = matmul(context, w_out) + bias_out
        normed_part, scaled_one, spread_one = normalize(tokens + branch, gain_one)
        normed_one = normed_part + shift_one
        (w_down,) = exchange(n, 2, "gather_down", GatherBatch(n, down_low))
        w_down = w_down.reshape(hid_q, width)
        vec_rows = jnp.concatenate([vec_full[2:8], bias_up[None], jnp.zeros_like(bias_up[None])])
        shape = (rows, span, width)
        out_rows, pool_sum, first_grad, vec_grad, grad_up, down_piece = hidden_layer(
            n,
            normed_one.reshape(shape),
            scaled_one.reshape(shape),
            spread_one.reshape(rows, span, 1),
            w_up,
            w_down,
            vec_rows,
            out_grad,
            pool_whole,
            lengths,
        )
        if down_piece.shape[0] != own_rows:
            (down_piece,) = exchange(
                n, 4, "sum_grad_down", ScatterBatch(n, down_piece.reshape(n, hid_own, width))
            )
        pooled = lax.dynamic_slice_in_dim(pool_sum, seq_index * quarter, quarter, 1)
        first_grad = first_grad.reshape(local, width)
        a_low = first_grad.astype(BF16)
        context_grad = contract_last(a_low, w_out).astype(BF16)
        grad_out = contract_first(context, a_low)
        up_piece, context_back, out_part = exchange(
            n,
            6,
            "swap_dcontext",
            ScatterBatch(n, grad_up.reshape(n, own_rows, hid_q)),
            SwapSeq(n, context_grad.reshape(local, SEQ, quarter).transpose(1, 0, 2)),
            ScatterSeq(n, grad_out.reshape(width, SEQ, quarter).transpose(1, 0, 2)),
        )
        arriving = (
            context_back.reshape(SEQ, rows, span, HEADS, HD)
            .transpose(1, 3, 0, 2, 4)
            .reshape(rows, HEADS, span_all, HD)
        )
        prob_grad = jnp.einsum("rhqd,rhkd->rhqk", arriving, value, preferred_element_type=F32)
        row_delta = jnp.sum(prob * prob_grad, axis=-1, keepdims=True)
        score_grad = (prob * (prob_grad - row_delta)).astype(BF16)
        query_grad = (
            jnp.einsum("rhqk,rhkd->rhqd", score_grad, key, preferred_element_type=F32) * scale
        )
        key_grad = (
            jnp.einsum("rhqk,rhqd->rhkd", score_grad, query, preferred_element_type=F32) * scale
        )
        value_grad = jnp.einsum(
            "rhqk,rhqd->rhkd", prob_low, arriving, preferred_element_type=F32
        )
        qkv_grad = (
            jnp.stack([query_grad, key_grad, value_grad])
            .astype(BF16)
            .reshape(3, rows, HEADS, SEQ, span, HD)
            .transpose(3, 1, 4, 0, 2, 5)
            .reshape(SEQ * local, 3 * quarter)
        )
        input_part = contract_last(qkv_grad, w_qkv).reshape(SEQ, local, width)
        attn_local = jnp.concatenate([contract_first(x_all, qkv_grad), out_part], axis=1)
        bias_sums = jnp.sum(qkv_grad.astype(F32), axis=0).reshape(3, quarter)

        vec_head = jnp.zeros((2, SEQ, quarter), F32)
        vec_head = lax.dynamic_update_slice(
            vec_head, bias_sums[jnp.array([0, 2])][:, None], (0, seq_index, 0)
        ).reshape(2, width)
        vec_mid = vec_grad[:6]
        grad_bias_up = vec_grad[6]
        vec_tail = lax.dynamic_update_slice(
            jnp.zeros((n, SEQ, hid_own), F32),
            grad_bias_up.reshape(n, 1, hid_own),
            (0, seq_index, 0),
        ).reshape(-1, width)
        vec_local = jnp.concatenate([vec_head, vec_mid, vec_tail])
        vec_local = vec_local.reshape(-1, n, own_rows).transpose(1, 0, 2)
        input_sum, attn_piece, vec_piece = exchange(
            n,
            7,
            "sum_input",
            ScatterSeq(n, input_part),
            ScatterBatch(n, attn_local.reshape(n, own_rows, width)),
            ScatterBatch(n, vec_local, F32),
        )
        input_grad = input_sum + first_grad

        attn_bf = attn_piece.astype(BF16).reshape(own_rows, 4, quarter).transpose(1, 0, 2)
        wide_bf = jnp.stack([up_piece, down_piece]).astype(BF16)
        attn_send = (matrix_decay * attn_quarter(attn_moment) + attn_bf.astype(F32)).astype(BF16)
        wide_moment = jnp.stack([up_quarter(up_moment), down_quarter(down_moment)])
        wide_send = (matrix_decay * wide_moment + wide_bf.astype(F32)).astype(BF16)
        short = -own_rows % 16
        attn_send = jnp.pad(attn_send, ((0, 0), (0, short), (0, 0)))
        wide_send = jnp.pad(wide_send, ((0, 0), (0, short), (0, 0)))
        attn_all, wide_all, vec_parts, attn_orth, wide_orth = exchange(
            n,
            8,
            "muon",
            GatherSeq(n, attn_bf),
            GatherSeq(n, wide_bf),
            GatherSeq(n, vec_piece),
            Muon(n, attn_send, wide_send),
        )
        attn_orth = attn_orth[:, :, :own_rows]
        wide_orth = wide_orth[:, :, :own_rows]

        def join_attn(parts):
            return parts.astype(F32).transpose(1, 2, 0, 3).reshape(4, own_rows, width)

        def join_up(parts):
            return (
                parts.astype(F32)
                .reshape(SEQ, own_rows, n, hid_own)
                .transpose(1, 2, 0, 3)
                .reshape(own_rows, hidden)
            )

        def join_down(parts):
            return parts.astype(F32).reshape(SEQ * hid_own, width)

        attn_grad = join_attn(attn_all)
        up_grad, down_grad = join_up(wide_all[:, 0]), join_down(wide_all[:, 1])
        vector_grad = (vec_parts[0] + vec_parts[1]) + (vec_parts[2] + vec_parts[3])
        attn_next = matrix_decay * attn_moment + attn_grad
        up_next = matrix_decay * up_moment + up_grad
        down_next = matrix_decay * down_moment + down_grad

        factors = [
            step_factor(width, width),
            step_factor(width, hidden),
            step_factor(hidden, width),
        ]
        attn_new = attn_weight - factors[0] * join_attn(attn_orth)
        up_new = up_weight - factors[1] * join_up(wide_orth[:, 0])
        down_new = down_weight - factors[2] * join_down(wide_orth[:, 1])
        vector_next = vector_decay * vector_moment + vector_grad
        vectors_new = vectors - vector_rate / math.sqrt(rows * n) * vector_next
        return (
            out_rows,
            pooled,
            input_grad.reshape(rows, span, width),
            attn_grad,
            up_grad,
            down_grad,
            vector_grad,
            attn_next,
            up_next,
            down_next,
            vector_next,
            attn_new,
            up_new,
            down_new,
            vectors_new,
        )

    return body


def solution(mesh):
    placed = (
        P("batch", "seq", None),
        P("batch"),
        P(None, "batch", None),
        P("batch", None),
        P("batch", None),
        P(None, "batch"),
        P(None, "batch", None),
        P("batch", None),
        P("batch", None),
        P(None, "batch"),
        P("batch", "seq", None),
        P("batch", "seq"),
    )
    return jax.shard_map(
        make_body(mesh.shape["batch"]),
        mesh=mesh,
        in_specs=placed,
        out_specs=(
            P("batch", "seq", None),
            P("batch", "seq"),
            P("batch", "seq", None),
            P(None, "batch", None),
            P("batch", None),
            P("batch", None),
            P(None, "batch"),
            P(None, "batch", None),
            P("batch", None),
            P("batch", None),
            P(None, "batch"),
            P(None, "batch", None),
            P("batch", None),
            P("batch", None),
            P(None, "batch"),
        ),
        check_vma=False,
    )
```

```python
import math

import jax
import jax.numpy as jnp
from jax import lax
from jax.experimental import pallas as pl
from jax.experimental.pallas import tpu as pltpu
from jax.sharding import PartitionSpec as P

H = 12
HD = 64
NS = 5
SEQ = 4
HEADS = H // SEQ

norm_eps = 1e-12
tiny_norm = 1e-07
matrix_decay = 0.95
vector_decay = 0.5
matrix_rate = 0.5
vector_rate = 0.03

MESH = pl.DeviceIdType.MESH
F32 = jnp.float32
BF16 = jnp.bfloat16


def coords(n):
    b = lax.axis_index("batch")
    s = lax.axis_index("seq")
    return b, s, b // 2, b % 2, n // 2


def remote(src, dst, send, recv, device):
    return pltpu.make_async_remote_copy(
        src_ref=src, dst_ref=dst, send_sem=send, recv_sem=recv, device_id=device, device_id_type=MESH
    )


class GatherBatch:
    peers = ("batch",)

    def __init__(self, n, src):
        self.n = n
        self.ins = [src]
        self.outs = [jax.ShapeDtypeStruct((n,) + src.shape, src.dtype)]
        m = n // 2
        self.scratch = [pltpu.SemaphoreType.DMA((m,))] * 4 + [pltpu.SemaphoreType.DMA]

    def run(self, src, dst, zs, zr, ys, yr, own):
        b, s, hi, lo, m = coords(self.n)
        local = pltpu.make_async_copy(src, dst.at[b], own)
        local.start()
        pair = (hi * 2 + 1 - lo, s)
        out = []
        for d in range(1, m):
            c = remote(src, dst.at[b], zs.at[d], zr.at[d], (((hi + d) % m) * 2 + lo, s))
            c.start()
            out.append(c)
        first = remote(src, dst.at[b], ys.at[0], yr.at[0], pair)
        first.start()
        yield
        passed = [first]
        for d in range(1, m):
            out[d - 1].wait_recv()
            block = ((hi + m - d) % m) * 2 + lo
            c = remote(dst.at[block], dst.at[block], ys.at[d], yr.at[d], pair)
            c.start()
            passed.append(c)
            yield
        local.wait()
        for c in passed:
            c.wait()
        for c in out:
            c.wait_send()


class ScatterBatch:
    peers = ("batch",)

    def __init__(self, n, src, wire=BF16):
        self.n = n
        self.wire = wire
        self.ins = [src]
        shape = src.shape[1:]
        self.outs = [jax.ShapeDtypeStruct(shape, F32)]
        m = n // 2
        self.scratch = [pltpu.VMEM((m,) + shape, wire)] * 4 + [pltpu.SemaphoreType.DMA((m,))] * 4

    def run(self, src, dst, ysend, yrecv, zsend, zrecv, ys, yr, zs, zr):
        b, s, hi, lo, m = coords(self.n)
        pair = (hi * 2 + 1 - lo, s)
        first = {}
        order = list(range(1, m)) + [0]
        for d in order:
            h = (hi + d) % m
            ysend[d] = src[h * 2 + 1 - lo].astype(self.wire)
            first[d] = remote(ysend.at[d], yrecv.at[d], ys.at[d], yr.at[d], pair)
            first[d].start()
        yield
        second = []
        for d in range(1, m):
            h = (hi + d) % m
            first[d].wait_recv()
            zsend[d] = (src[h * 2 + lo] + yrecv[d].astype(F32)).astype(self.wire)
            c = remote(zsend.at[d], zrecv.at[d], zs.at[d], zr.at[d], (h * 2 + lo, s))
            c.start()
            second.append(c)
            yield
        first[0].wait_recv()
        total = src[b] + yrecv[0].astype(F32)
        for d in range(1, m):
            second[d - 1].wait_recv()
            total = total + zrecv[d].astype(F32)
        dst[...] = total
        for c in list(first.values()) + second:
            c.wait_send()


class GatherSeq:
    peers = ("seq",)

    def __init__(self, n, src):
        self.ins = [src]
        self.outs = [jax.ShapeDtypeStruct((SEQ,) + src.shape, src.dtype)]
        self.scratch = [pltpu.SemaphoreType.DMA((3,))] * 2 + [pltpu.SemaphoreType.DMA]

    def run(self, src, dst, ss, rs, own):
        b, s = lax.axis_index("batch"), lax.axis_index("seq")
        far, near = (s + 2) % 4, s + 1 - 2 * (s % 2)
        across = remote(src, dst.at[s], ss.at[0], rs.at[0], (b, far))
        across.start()
        local = pltpu.make_async_copy(src, dst.at[s], own)
        local.start()
        beside = remote(src, dst.at[s], ss.at[1], rs.at[1], (b, near))
        beside.start()
        yield
        across.wait_recv()
        passed = remote(dst.at[far], dst.at[far], ss.at[2], rs.at[2], (b, near))
        passed.start()
        yield
        local.wait()
        beside.wait()
        passed.wait()
        across.wait_send()


class ScatterSeq:
    peers = ("seq",)

    def __init__(self, n, src):
        self.ins = [src]
        shape = src.shape[1:]
        self.outs = [jax.ShapeDtypeStruct(shape, F32)]
        self.scratch = [
            pltpu.VMEM((2,) + shape, BF16),
            pltpu.VMEM((2,) + shape, BF16),
            pltpu.VMEM(shape, BF16),
            pltpu.VMEM(shape, BF16),
            pltpu.SemaphoreType.DMA((3,)),
            pltpu.SemaphoreType.DMA((3,)),
        ]

    def run(self, src, dst, near_out, near_in, far_out, far_in, ss, rs):
        b, s = lax.axis_index("batch"), lax.axis_index("seq")
        far, near = (s + 2) % 4, s + 1 - 2 * (s % 2)
        near_far = (near + 2) % 4
        near_out[1] = src[near_far].astype(BF16)
        one = remote(near_out.at[1], near_in.at[1], ss.at[1], rs.at[1], (b, near))
        one.start()
        near_out[0] = src[near].astype(BF16)
        two = remote(near_out.at[0], near_in.at[0], ss.at[0], rs.at[0], (b, near))
        two.start()
        yield
        one.wait_recv()
        far_out[...] = (src[far] + near_in[1].astype(F32)).astype(BF16)
        three = remote(far_out, far_in, ss.at[2], rs.at[2], (b, far))
        three.start()
        yield
        two.wait_recv()
        dst[...] = src[s] + near_in[0].astype(F32)
        yield
        three.wait_recv()
        dst[...] = dst[...] + far_in[...].astype(F32)
        one.wait_send()
        two.wait_send()
        three.wait_send()


class SwapSeq:
    peers = ("seq",)

    def __init__(self, n, src):
        self.ins = [src]
        self.outs = [jax.ShapeDtypeStruct(src.shape, src.dtype)]
        self.scratch = [pltpu.SemaphoreType.DMA((4,))] * 2 + [pltpu.SemaphoreType.DMA]

    def run(self, src, dst, ss, rs, own):
        b, s = lax.axis_index("batch"), lax.axis_index("seq")
        copies = []
        for k in (2, 3, 1):
            other = (s + k) % 4
            c = remote(src.at[other], dst.at[s], ss.at[k], rs.at[k], (b, other))
            c.start()
            copies.append(c)
        local = pltpu.make_async_copy(src.at[s], dst.at[s], own)
        local.start()
        yield
        local.wait()
        for c in copies:
            c.wait()


def owner_list(n):
    return [(0, 2), (1, 0), (n - 2, 2), (n - 1, 0), (n // 4, 0), (n // 2 + 1, 2)]


class Muon:
    peers = ("all",)

    def __init__(self, n, attn_piece, wide_piece):
        self.n = n
        self.ins = [attn_piece, wide_piece]
        rows, quarter = attn_piece.shape[1:]
        width = wide_piece.shape[2]
        self.outs = [
            jax.ShapeDtypeStruct((SEQ, 4, rows, quarter), BF16),
            jax.ShapeDtypeStruct((SEQ, 2, rows, width), BF16),
        ]
        size = n * rows
        dma = pltpu.SemaphoreType.DMA
        self.scratch = [
            pltpu.VMEM((SEQ, n, rows, quarter), BF16),
            pltpu.VMEM((SEQ, n, rows, width), BF16),
            pltpu.VMEM((size, SEQ * size), F32),
            pltpu.VMEM((size, SEQ * size), BF16),
            pltpu.VMEM((size, size), F32),
            pltpu.VMEM((size, size), BF16),
            pltpu.VMEM((size, size), BF16),
            pltpu.VMEM((size, 1), F32),
            dma((6,)),
            dma((SEQ * n,)),
            dma((SEQ * n,)),
            dma((6,)),
            dma((6, 3)),
            dma((6, 3)),
            dma((2,)),
        ]

    def run(
        self, attn, wide, attn_orth, wide_orth, attn_in, wide_in, x32, xlow, gram, gram_low, poly, diag,
        ss, rs, back_s, back_r, seq_s, seq_r, own,
    ):
        n = self.n
        b, s = lax.axis_index("batch"), lax.axis_index("seq")
        me = s * n + b
        far, near = (s + 2) % 4, s + 1 - 2 * (s % 2)
        size = x32.shape[0]
        width = wide.shape[2]
        quarter = attn.shape[2]
        places = owner_list(n)
        mine = [(b == ob) & (s == os) for ob, os in places]
        number = jnp.int32(0)
        for k in range(6):
            number = jnp.where(mine[k], jnp.int32(k), number)
        is_attn = mine[0] | mine[1] | mine[2] | mine[3]
        is_wide = mine[4] | mine[5]
        order = (5, 4, 0, 1, 2, 3)

        def piece(k):
            return attn.at[k] if k < 4 else wide.at[k - 4]

        def inbox(k):
            return attn_in if k < 4 else wide_in

        def result(k):
            return attn_orth.at[s, k] if k < 4 else wide_orth.at[s, k - 4]

        for k in order:
            ob, os = places[k]

            @pl.when(jnp.logical_not(mine[k]))
            def _(k=k, ob=ob, os=os):
                remote(piece(k), inbox(k).at[s, b], ss.at[k], rs.at[me], (ob, os)).start()

            @pl.when(mine[k])
            def _(k=k):
                pltpu.make_async_copy(piece(k), inbox(k).at[s, b], own.at[0]).start()

        yield
        yield
        yield
        yield

        def collect(buf):
            pltpu.make_async_copy(buf.at[s, b], buf.at[s, b], own.at[0]).wait()

            @pl.loop(1, SEQ * n)
            def _(k):
                other = (me + k) % (SEQ * n)
                place = buf.at[other // n, other % n]
                remote(place, place, ss.at[0], rs.at[other], (0, 0)).wait_recv()

        def give(buf, out, index):
            pltpu.make_async_copy(buf.at[s, b], out.at[s, index], own.at[1]).start()

            @pl.loop(1, SEQ * n)
            def _(k):
                other = (me + k) % (SEQ * n)
                os, ob = other // n, other % n
                remote(
                    buf.at[os, ob], out.at[os, index], back_s.at[other], back_r.at[number], (ob, os)
                ).start()

        def squares(buf):
            total = jnp.zeros((1, 1), F32)
            for k in range(SEQ):
                block = buf[k].astype(F32).reshape(size, buf.shape[3])
                total = total + jnp.sum(block * block, keepdims=True)
            return 1.0 / (jnp.sqrt(total) + tiny_norm)

        @pl.when(is_attn)
        def _():
            collect(attn_in)
            inverse = squares(attn_in)
            step = -(-quarter // 128) * 128
            span = SEQ * step
            x32[:, :span] = jnp.zeros((size, span), F32)
            for k in range(SEQ):
                block = attn_in[k].astype(F32).reshape(size, quarter)
                x32[:, k * step : k * step + quarter] = block * inverse
            xlow[:, :span] = x32[:, :span].astype(BF16)
            newton_schulz(
                x32.at[:, pl.ds(0, span)], xlow.at[:, pl.ds(0, span)], gram, gram_low, poly, diag
            )
            for k in range(SEQ):
                block = xlow[:, k * step : k * step + quarter]
                attn_in[k] = block.reshape(attn_in.shape[1:])
            give(attn_in, attn_orth, number)

        @pl.when(is_wide)
        def _():
            collect(wide_in)
            inverse = squares(wide_in)
            if width != size:
                x32[...] = jnp.zeros(x32.shape, F32)

            @pl.when(mine[4])
            def _():
                for k in range(SEQ):
                    block = wide_in[k].astype(F32).reshape(size, width)
                    x32[:, k * size : k * size + width] = block * inverse

            @pl.when(mine[5])
            def _():
                for k in range(SEQ):
                    block = wide_in[k].astype(F32).reshape(size, width)
                    x32[:width, k * size : (k + 1) * size] = block.T * inverse

            for k in range(SEQ):
                xlow[:, k * size : (k + 1) * size] = x32[:, k * size : (k + 1) * size].astype(BF16)
            newton_schulz(x32, xlow, gram, gram_low, poly, diag)

            @pl.when(mine[4])
            def _():
                for k in range(SEQ):
                    block = xlow[:, k * size : k * size + width]
                    wide_in[k] = block.reshape(wide_in.shape[1:])

            @pl.when(mine[5])
            def _():
                for k in range(SEQ):
                    block = x32[:width, k * size : (k + 1) * size].T.astype(BF16)
                    wide_in[k] = block.reshape(wide_in.shape[1:])

            give(wide_in, wide_orth, number - 4)

        def onward(k, step, source, target):
            out = attn_orth.at[source, k] if k < 4 else wide_orth.at[source, k - 4]
            return remote(out, out, seq_s.at[k, step], seq_r.at[k, step], (b, target))

        done = (0, 1, 2, 3, 4, 5)
        for k in done:

            @pl.when(jnp.logical_not(mine[k]))
            def _(k=k):
                remote(piece(k), result(k), ss.at[k], back_r.at[k], (0, 0)).wait_recv()

            @pl.when(mine[k])
            def _(k=k):
                pltpu.make_async_copy(piece(k), result(k), own.at[1]).wait()

            onward(k, 0, s, far).start()
            onward(k, 1, s, near).start()
        for k in done:
            onward(k, 0, far, far).wait_recv()
            onward(k, 2, far, near).start()
        for k in done:
            onward(k, 1, near, near).wait_recv()
            onward(k, 2, (near + 2) % 4, near).wait_recv()
            onward(k, 0, s, far).wait_send()
            onward(k, 1, s, near).wait_send()
            onward(k, 2, far, near).wait_send()

            @pl.when(jnp.logical_not(mine[k]))
            def _(k=k):
                remote(piece(k), inbox(k).at[s, b], ss.at[k], rs.at[me], (0, 0)).wait_send()

        def given(buf):
            @pl.loop(1, SEQ * n)
            def _(k):
                other = (me + k) % (SEQ * n)
                place = buf.at[other // n, other % n]
                remote(place, place, back_s.at[other], back_r.at[0], (0, 0)).wait_send()

        @pl.when(is_attn)
        def _():
            given(attn_in)

        @pl.when(is_wide)
        def _():
            given(wide_in)


def newton_schulz(x32, xlow, gram, gram_low, poly, diag):
    size, wide = x32.shape
    eye = lax.broadcasted_iota(jnp.int32, (size, size), 0) == lax.broadcasted_iota(
        jnp.int32, (size, size), 1
    )
    chunk = 768 if wide % 768 == 0 else 512

    @pl.loop(0, NS)
    def _(turn):
        whole = contract_last(xlow[...], xlow[...])
        gram[...] = whole
        gram_low[...] = jnp.where(eye, 0.0, whole).astype(BF16)
        whole = gram[...]
        on_diag = jnp.where(eye, whole, 0.0)
        down = jnp.sum(on_diag, axis=1, keepdims=True)
        along = jnp.sum(on_diag, axis=0, keepdims=True)
        square = (
            matmul(gram_low[...], gram_low[...])
            + (down + along) * jnp.where(eye, 0.0, whole)
            + jnp.where(eye, down * down, 0.0)
        )
        mixed = -4.775 * whole + 2.0315 * square
        diag[...] = jnp.sum(jnp.where(eye, mixed, 0.0), axis=1, keepdims=True) + 3.4445
        poly[...] = jnp.where(eye, 0.0, mixed).astype(BF16)
        for c in range(0, wide, chunk):
            moved = diag[...] * x32[:, c : c + chunk] + matmul(poly[...], xlow[:, c : c + chunk])
            x32[:, c : c + chunk] = moved
            xlow[:, c : c + chunk] = moved.astype(BF16)


def greet(n, kinds):
    b, s, hi, lo, m = coords(n)
    barrier = pltpu.get_barrier_semaphore()
    if "all" in kinds:
        me = s * n + b

        @pl.loop(1, SEQ * n)
        def _(k):
            other = (me + k) % (SEQ * n)
            pl.semaphore_signal(
                barrier, inc=1, device_id=(other % n, other // n), device_id_type=MESH
            )

        pl.semaphore_wait(barrier, SEQ * n - 1)
        return
    peers = []
    if "seq" in kinds:
        peers += [(b, (s + k) % 4) for k in (1, 2, 3)]
    if "batch" in kinds:
        peers += [(((hi + d) % m) * 2 + lo, s) for d in range(1, m)]
        peers += [(hi * 2 + 1 - lo, s)]
    for peer in peers:
        pl.semaphore_signal(barrier, inc=1, device_id=peer, device_id_type=MESH)
    pl.semaphore_wait(barrier, len(peers))


def exchange(n, collective_id, name, *ops):
    ins = [a for op in ops for a in op.ins]
    outs = [o for op in ops for o in op.outs]
    scratch = [c for op in ops for c in op.scratch]
    kinds = {k for op in ops for k in op.peers}

    def kernel(*refs):
        in_refs, out_refs = refs[: len(ins)], refs[len(ins) : len(ins) + len(outs)]
        scratch_refs = refs[len(ins) + len(outs) :]
        greet(n, kinds)
        live = []
        i = o = c = 0
        for op in ops:
            ni, no, nc = len(op.ins), len(op.outs), len(op.scratch)
            live.append(
                op.run(*in_refs[i : i + ni], *out_refs[o : o + no], *scratch_refs[c : c + nc])
            )
            i, o, c = i + ni, o + no, c + nc
        while live:
            still = []
            for step in live:
                try:
                    next(step)
                    still.append(step)
                except StopIteration:
                    pass
            live = still

    vmem = pl.BlockSpec(memory_space=pltpu.VMEM)
    return pl.pallas_call(
        kernel,
        out_shape=outs,
        in_specs=[vmem] * len(ins),
        out_specs=[vmem] * len(outs),
        scratch_shapes=scratch,
        compiler_params=pltpu.CompilerParams(
            collective_id=collective_id, has_side_effects=True, vmem_limit_bytes=60 * 2**20
        ),
        name=name,
    )(*ins)


def contract_last(left, right):
    return lax.dot_general(left, right, (((1,), (1,)), ((), ())), preferred_element_type=F32)


def contract_first(left, right):
    return lax.dot_general(left, right, (((0,), (0,)), ((), ())), preferred_element_type=F32)


def matmul(left, right):
    return jnp.dot(left, right, preferred_element_type=F32)


def exact_gelu(value_in):
    return jax.nn.gelu(value_in, approximate=False)


def normalize(hidden, gain_row):
    row_mean = jnp.mean(hidden, axis=-1, keepdims=True)
    centred = hidden - row_mean
    spread = lax.rsqrt(jnp.mean(centred * centred, axis=-1, keepdims=True) + norm_eps)
    scaled = centred * spread
    return (scaled * gain_row, scaled, spread)


def normalize_back(grad_in, scaled, spread, gain_row):
    weighted = grad_in * gain_row
    mean_first = jnp.mean(weighted, axis=-1, keepdims=True)
    second = jnp.mean(weighted * scaled, axis=-1, keepdims=True)
    return (
        spread * (weighted - mean_first - scaled * second),
        jnp.sum(grad_in * scaled, axis=0),
        jnp.sum(grad_in, axis=0),
    )


class RowGather:
    @staticmethod
    def scratch():
        return [pltpu.SemaphoreType.DMA((2, 3)), pltpu.SemaphoreType.DMA((2, 3))]

    def __init__(self, buf, ss, rs):
        self.buf, self.ss, self.rs = buf, ss, rs
        self.b, self.s = lax.axis_index("batch"), lax.axis_index("seq")
        self.far, self.near = (self.s + 2) % 4, self.s + 1 - 2 * (self.s % 2)
        self.diag = (self.near + 2) % 4

    def copy(self, r, step, block, device):
        place = self.buf.at[r, block]
        return remote(place, place, self.ss.at[r, step], self.rs.at[r, step], (self.b, device))

    def start(self, r):
        self.copy(r, 0, self.s, self.far).start()
        self.copy(r, 1, self.s, self.near).start()

    def wait_near(self, r):
        self.copy(r, 1, self.near, self.near).wait_recv()

    def pass_far(self, r):
        self.copy(r, 0, self.far, self.far).wait_recv()
        self.copy(r, 2, self.far, self.near).start()

    def wait_diag(self, r):
        self.copy(r, 2, self.diag, self.near).wait_recv()

    def finish(self, r):
        self.copy(r, 0, self.s, self.far).wait_send()
        self.copy(r, 1, self.s, self.near).wait_send()
        self.copy(r, 2, self.far, self.near).wait_send()


class RowScatter:
    @staticmethod
    def scratch(rows, shape):
        return [
            pltpu.VMEM((rows, 2) + shape, BF16),
            pltpu.VMEM((rows, 2) + shape, BF16),
            pltpu.VMEM((rows,) + shape, BF16),
            pltpu.VMEM((rows,) + shape, BF16),
            pltpu.SemaphoreType.DMA((rows, 3)),
            pltpu.SemaphoreType.DMA((rows, 3)),
        ]

    def __init__(self, src, near_out, near_in, far_out, far_in, ss, rs):
        self.src = src
        self.near_out, self.near_in = near_out, near_in
        self.far_out, self.far_in = far_out, far_in
        self.ss, self.rs = ss, rs
        self.b, self.s = lax.axis_index("batch"), lax.axis_index("seq")
        self.far, self.near = (self.s + 2) % 4, self.s + 1 - 2 * (self.s % 2)
        self.diag = (self.near + 2) % 4

    def beside(self, r, k):
        return remote(
            self.near_out.at[r, k], self.near_in.at[r, k], self.ss.at[r, k], self.rs.at[r, k],
            (self.b, self.near),
        )

    def across(self, r):
        return remote(
            self.far_out.at[r], self.far_in.at[r], self.ss.at[r, 2], self.rs.at[r, 2],
            (self.b, self.far),
        )

    def send_near(self, r):
        self.near_out[r, 0] = self.src[r, self.near].astype(BF16)
        self.beside(r, 0).start()

    def send_diag(self, r):
        self.near_out[r, 1] = self.src[r, self.diag].astype(BF16)
        self.beside(r, 1).start()

    def cross(self, r):
        self.beside(r, 1).wait_recv()
        self.far_out[r] = (self.src[r, self.far] + self.near_in[r, 1].astype(F32)).astype(BF16)
        self.across(r).start()

    def total(self, r):
        self.beside(r, 0).wait_recv()
        part = self.src[r, self.s] + self.near_in[r, 0].astype(F32)
        self.across(r).wait_recv()
        return part + self.far_in[r].astype(F32)

    def finish(self, r):
        self.beside(r, 0).wait_send()
        self.beside(r, 1).wait_send()
        self.across(r).wait_send()


def gelu_parts(value):
    cdf = 0.5 * (1.0 + lax.erf(value * math.sqrt(0.5)))
    density = jnp.exp(-0.5 * value * value) * (1.0 / math.sqrt(2.0 * math.pi))
    return value * cdf, cdf + value * density


def row_sum(value):
    return jnp.sum(value, axis=0, keepdims=True)


def hidden_layer(n, normed, scaled_one, spread_one, w_up, w_down, vec, out_grad, pool_whole, lengths):
    rows, span, width = normed.shape
    hid_q = w_up.shape[1]
    aligned = (width // n) % 16 == 0
    block = (n, width // n)
    full = (rows, SEQ, span)
    outs = [
        jax.ShapeDtypeStruct((rows, span, width), F32),
        jax.ShapeDtypeStruct((rows, width), F32),
        jax.ShapeDtypeStruct((rows, span, width), F32),
        jax.ShapeDtypeStruct((8, width), F32),
        jax.ShapeDtypeStruct((width, hid_q), F32),
        jax.ShapeDtypeStruct((width // n, width) if aligned else (hid_q, width), F32),
    ]
    if aligned:
        batch_scratch = ScatterBatch(n, jax.ShapeDtypeStruct(block + (width,), F32)).scratch
        batch_scratch = batch_scratch + [pltpu.VMEM(block + (width,), F32)]
    else:
        batch_scratch = []
    scratch = (
        [
            pltpu.VMEM(full + (width,), BF16),
            pltpu.VMEM(full + (hid_q,), F32),
            pltpu.VMEM(full + (hid_q,), BF16),
            pltpu.VMEM(full + (width,), F32),
            pltpu.VMEM(full + (width,), BF16),
            pltpu.VMEM(full + (hid_q,), BF16),
            pltpu.VMEM(full + (width,), F32),
            pltpu.VMEM((rows, span, width), F32),
            pltpu.VMEM((SEQ, rows, width), F32),
            pltpu.SemaphoreType.DMA((3,)),
            pltpu.SemaphoreType.DMA((3,)),
        ]
        + RowGather.scratch() * 2
        + RowScatter.scratch(rows, (span, width)) * 2
    )

    def kernel(
        normed, scaled_one, spread_one, w_up, w_down, vec, out_grad, pool_whole, lengths,
        out_rows, pooled, first_grad, vec_grad, grad_up, grad_down,
        y_all, slope, act, z_part, dz_all, du_all, dy_part, second, pool_buf, pool_ss, pool_rs,
        *rest,
    ):
        greet(n, {"seq", "batch"} if aligned else {"seq"})
        b, s = lax.axis_index("batch"), lax.axis_index("seq")
        y_gather = RowGather(y_all, *rest[0:2])
        dz_gather = RowGather(dz_all, *rest[2:4])
        z_sum = RowScatter(z_part, *rest[4:10])
        dy_sum = RowScatter(dy_part, *rest[10:16])
        rest = rest[16:]
        far, near, diag = y_gather.far, y_gather.near, y_gather.diag
        gain_one, gain_two, shift_two = vec[1:2], vec[3:4], vec[4:5]
        bias_down, bias_up = vec[5:6], vec[6:7]

        for r in range(rows):
            y_all[r, s] = normed[r].astype(BF16)
            y_gather.start(r)

        def pair(ref, blocks):
            return jnp.concatenate([ref[i] for i in blocks], axis=0)

        def spread(ref, blocks, value):
            for k, i in enumerate(blocks):
                ref[i] = value[k * span : (k + 1) * span].astype(ref.dtype)

        def forward(blocks):
            pre = matmul(pair(y_all, blocks), w_up[...]) + bias_up
            value, rate = gelu_parts(pre)
            low = value.astype(BF16)
            spread(act, blocks, low)
            spread(slope, blocks, rate)
            spread(z_part, blocks, matmul(low, w_down[...]))

        forward([(r, s) for r in range(rows)])
        for r in range(rows):
            y_gather.wait_near(r)
        forward([(r, near) for r in range(rows)])
        for r in range(rows):
            z_sum.send_near(r)
        for r in range(rows):
            y_gather.pass_far(r)
            y_gather.wait_diag(r)
            forward([(r, diag), (r, far)])
            z_sum.send_diag(r)
            z_sum.cross(r)

        position = s * span + lax.broadcasted_iota(jnp.int32, (span, 1), 0)
        grad_gain_two = grad_shift_two = grad_bias_down = jnp.zeros((1, width), F32)
        for r in range(rows):
            hidden = normed[r] + (z_sum.total(r) + bias_down)
            centred = hidden - jnp.mean(hidden, axis=-1, keepdims=True)
            spread_two = lax.rsqrt(jnp.mean(centred * centred, axis=-1, keepdims=True) + norm_eps)
            scaled = centred * spread_two
            output = scaled * gain_two + shift_two
            out_rows[r] = output
            live = (position < lengths[r]).astype(F32)
            length = jnp.full((1, 1), lengths[r], jnp.int32).astype(F32)
            pool_buf[s, r : r + 1] = row_sum(output * live) / length
            upstream = live * (out_grad[r] + pool_whole[r : r + 1] / length)
            weighted = upstream * gain_two
            mean_first = jnp.mean(weighted, axis=-1, keepdims=True)
            mean_second = jnp.mean(weighted * scaled, axis=-1, keepdims=True)
            grad = spread_two * (weighted - mean_first - scaled * mean_second)
            second[r] = grad
            low = grad.astype(BF16)
            dz_all[r, s] = low
            dz_gather.start(r)
            grad_gain_two += row_sum(upstream * scaled)
            grad_shift_two += row_sum(upstream)
            grad_bias_down += row_sum(low.astype(F32))

        def pool_copy(k, block, device):
            place = pool_buf.at[block]
            return remote(place, place, pool_ss.at[k - 1], pool_rs.at[k - 1], (b, device))

        for k in (1, 2, 3):
            pool_copy(k, s, (s + k) % 4).start()

        def backward(blocks):
            rise = contract_last(pair(dz_all, blocks), w_down[...])
            low = (rise * pair(slope, blocks)).astype(BF16)
            spread(du_all, blocks, low)
            spread(dy_part, blocks, contract_last(low, w_up[...]))
            return row_sum(low.astype(F32))

        bias_grad = backward([(r, s) for r in range(rows)])
        for r in range(rows):
            dz_gather.wait_near(r)
        bias_grad += backward([(r, near) for r in range(rows)])
        for r in range(rows):
            dy_sum.send_near(r)
        for r in range(rows):
            dz_gather.pass_far(r)
            dz_gather.wait_diag(r)
            bias_grad += backward([(r, diag), (r, far)])
            dy_sum.send_diag(r)
            dy_sum.cross(r)

        tokens = rows * SEQ * span
        whole = contract_first(act[...].reshape(tokens, hid_q), dz_all[...].reshape(tokens, width))
        if aligned:
            scatter = ScatterBatch(n, jax.ShapeDtypeStruct(block + (width,), F32))
            local = rest[-1]
            local[...] = whole.reshape(block + (width,))
            moving = scatter.run(local, grad_down, *rest[:-1])
            next(moving)
        else:
            grad_down[...] = whole
        grad_up[...] = contract_first(
            y_all[...].reshape(tokens, width), du_all[...].reshape(tokens, hid_q)
        )

        grad_gain_one = grad_shift_one = grad_bias_out = jnp.zeros((1, width), F32)
        for r in range(rows):
            grad = dy_sum.total(r) + second[r]
            scaled = scaled_one[r]
            weighted = grad * gain_one
            mean_first = jnp.mean(weighted, axis=-1, keepdims=True)
            mean_second = jnp.mean(weighted * scaled, axis=-1, keepdims=True)
            first = spread_one[r] * (weighted - mean_first - scaled * mean_second)
            first_grad[r] = first
            grad_gain_one += row_sum(grad * scaled)
            grad_shift_one += row_sum(grad)
            grad_bias_out += row_sum(first.astype(BF16).astype(F32))
        for k, value in enumerate(
            (
                grad_bias_out, grad_gain_one, grad_shift_one, grad_gain_two, grad_shift_two,
                grad_bias_down, bias_grad, jnp.zeros((1, width), F32),
            )
        ):
            vec_grad[k : k + 1] = value

        for k in (1, 2, 3):
            pool_copy(k, (s + 4 - k) % 4, (s + k) % 4).wait_recv()
        pooled[...] = (pool_buf[0] + pool_buf[1]) + (pool_buf[2] + pool_buf[3])
        for k in (1, 2, 3):
            pool_copy(k, s, (s + k) % 4).wait_send()
        for r in range(rows):
            for op in (y_gather, z_sum, dz_gather, dy_sum):
                op.finish(r)
        if aligned:
            for _ in moving:
                pass

    vmem = pl.BlockSpec(memory_space=pltpu.VMEM)
    return pl.pallas_call(
        kernel,
        out_shape=outs,
        in_specs=[vmem] * 8 + [pl.BlockSpec(memory_space=pltpu.SMEM)],
        out_specs=[vmem] * len(outs),
        scratch_shapes=scratch + batch_scratch,
        compiler_params=pltpu.CompilerParams(
            collective_id=3, has_side_effects=True, vmem_limit_bytes=60 * 2**20
        ),
        name="hidden_layer",
    )(normed, scaled_one, spread_one, w_up, w_down, vec, out_grad, pool_whole, lengths)


class RowSwap:
    @staticmethod
    def scratch(shape):
        return [
            pltpu.VMEM(shape, BF16),
            pltpu.VMEM(shape, BF16),
            pltpu.SemaphoreType.DMA((2, 4)),
            pltpu.SemaphoreType.DMA((2, 4)),
        ]

    def __init__(self, src, dst, ss, rs):
        self.src, self.dst, self.ss, self.rs = src, dst, ss, rs
        self.b, self.s = lax.axis_index("batch"), lax.axis_index("seq")

    def copy(self, r, k):
        other = (self.s + k) % 4
        return remote(
            self.src.at[other, r], self.dst.at[self.s, r], self.ss.at[r, k], self.rs.at[r, k],
            (self.b, other),
        )

    def start(self, r):
        for k in (2, 3, 1):
            self.copy(r, k).start()
        self.dst[self.s, r] = self.src[self.s, r]

    def wait(self, r):
        for k in (2, 3, 1):
            self.copy(r, k).wait_recv()

    def finish(self, r):
        for k in (2, 3, 1):
            self.copy(r, k).wait_send()


def step(op):
    try:
        next(op)
    except StopIteration:
        pass


def drain(op):
    for _ in op:
        pass


def attend(n, tokens, attn_own, up_own, down_own, vec_own, pool_own, lengths):
    rows, span, width = tokens.shape
    quarter = width // SEQ
    span_all = span * SEQ
    aligned = attn_own.shape[0] != width
    own_rows = width // n
    shape = jax.ShapeDtypeStruct
    outs = [
        shape((rows, span, width), F32),
        shape((rows, span, width), F32),
        shape((rows, span, 1), F32),
        shape((width, width), BF16),
        shape((8, width), F32),
        shape((rows, width), F32),
        shape((rows, SEQ, span, width), BF16),
        shape((rows, span_all, 3 * quarter), BF16),
        shape((rows, HEADS, span_all, span_all), F32),
        shape((rows, span, width), BF16),
    ]
    vec_op, pool_op = GatherBatch(n, vec_own), GatherSeq(n, pool_own)
    out_op = GatherSeq(n, shape((width, quarter), BF16))
    weight_ops = [GatherBatch(n, own) for own in (attn_own, up_own, down_own)] if aligned else []
    outs += [op.outs[0] for op in weight_ops]
    scratch = (
        [pltpu.VMEM(vec_op.outs[0].shape, F32)]
        + vec_op.scratch
        + [pltpu.VMEM(pool_op.outs[0].shape, F32)]
        + pool_op.scratch
        + [pltpu.VMEM((width, quarter), BF16), pltpu.VMEM((SEQ, width, quarter), BF16)]
        + out_op.scratch
        + RowGather.scratch()
        + RowSwap.scratch((SEQ, rows, span, quarter))
        + [c for op in weight_ops for c in op.scratch]
    )

    def kernel(tokens, attn_own, up_own, down_own, vec_own, pool_own, lengths, *rest):
        (
            normed, scaled_one, spread_one, w_out, vec, pool_whole, x_all, qkv, prob, context,
        ) = rest[:10]
        rest = rest[10:]
        if aligned:
            w_attn, w_up, w_down = rest[:3]
            rest = rest[3:]
        greet(n, {"seq", "batch"})
        s = lax.axis_index("seq")
        x_gather = RowGather(x_all, *rest[15:17])
        swap = RowSwap(*rest[17:21])
        context_out, context_in = rest[17:19]
        for r in range(rows):
            x_all[r, s] = tokens[r].astype(BF16)
            x_gather.start(r)
        vec_parts, pool_parts = rest[0], rest[6]
        out_own, out_parts = rest[10:12]
        if aligned:
            attn_move = weight_ops[0].run(attn_own, w_attn, *rest[21:26])
            up_move = weight_ops[1].run(up_own, w_up, *rest[26:31])
            down_move = weight_ops[2].run(down_own, w_down, *rest[31:36])
            step(attn_move)
        vec_move = vec_op.run(vec_own, vec_parts, *rest[1:6])
        pool_move = pool_op.run(pool_own, pool_parts, *rest[7:10])
        step(vec_move)
        step(pool_move)
        if aligned:
            step(attn_move)
        x_gather.pass_far(0)
        if aligned:
            step(attn_move)
        step(vec_move)
        x_gather.pass_far(1)
        step(pool_move)
        if aligned:
            drain(attn_move)
            step(up_move)
            weights = w_attn[...].reshape(width, width)
        else:
            weights = attn_own[...]
        drain(vec_move)
        drain(pool_move)
        total = vec_parts[0]
        for k in range(1, n):
            total = total + vec_parts[k]
        vec[...] = total
        pool_whole[...] = jnp.concatenate([pool_parts[k] for k in range(SEQ)], axis=1)
        out_own[...] = weights[:, 3 * quarter :]
        out_move = out_op.run(out_own, out_parts, *rest[12:15])
        step(out_move)
        w_qkv = weights[:, : 3 * quarter]
        bias = vec[7:8, : 3 * quarter]

        pending = [up_move, up_move, up_move, up_move, down_move, down_move, down_move] if aligned else []
        column = lax.broadcasted_iota(jnp.int32, (1, span_all), 1)
        for r in range(rows):
            x_gather.wait_near(r)
            x_gather.wait_diag(r)
            block = matmul(x_all[r].reshape(span_all, width), w_qkv) + bias
            qkv[r] = block.astype(BF16)
            valid = column < lengths[r]
            mixed = []
            for h in range(HEADS):
                query, key, value = [
                    qkv[r, :, k * quarter + h * HD : k * quarter + (h + 1) * HD] for k in range(3)
                ]
                scores = contract_last(query * jnp.bfloat16(HD**-0.5), key)
                scores = jnp.where(valid, scores, -1e30)
                exponent = jnp.exp(scores - jnp.max(scores, axis=-1, keepdims=True))
                weight = exponent * (1.0 / jnp.sum(exponent, axis=-1, keepdims=True))
                prob[r, h] = weight
                mixed.append(matmul(weight.astype(BF16), value))
                if pending:
                    step(pending.pop(0))
            if r == 0:
                step(out_move)
            mixed = jnp.concatenate(mixed, axis=1).astype(BF16)
            for k in range(SEQ):
                context_out[k, r] = mixed[k * span : (k + 1) * span]
            swap.start(r)
        drain(out_move)
        w_out[...] = jnp.concatenate([out_parts[k] for k in range(SEQ)], axis=1)
        while pending:
            step(pending.pop(0))
        for r in range(rows):
            swap.wait(r)
            context[r] = jnp.concatenate([context_in[k, r] for k in range(SEQ)], axis=1)
        branch = matmul(context[...].reshape(rows * span, width), w_out[...]) + vec[0:1]
        for r in range(rows):
            hidden = tokens[r] + branch[r * span : (r + 1) * span]
            centred = hidden - jnp.mean(hidden, axis=-1, keepdims=True)
            spread = lax.rsqrt(jnp.mean(centred * centred, axis=-1, keepdims=True) + norm_eps)
            scaled = centred * spread
            scaled_one[r] = scaled
            spread_one[r] = spread
            normed[r] = scaled * vec[1:2] + vec[2:3]
        for r in range(rows):
            x_gather.finish(r)
            swap.finish(r)
        if aligned:
            drain(up_move)
            drain(down_move)

    vmem = pl.BlockSpec(memory_space=pltpu.VMEM)
    return pl.pallas_call(
        kernel,
        out_shape=outs,
        in_specs=[vmem] * 6 + [pl.BlockSpec(memory_space=pltpu.SMEM)],
        out_specs=[vmem] * len(outs),
        scratch_shapes=scratch,
        compiler_params=pltpu.CompilerParams(
            collective_id=0, has_side_effects=True, vmem_limit_bytes=60 * 2**20
        ),
        name="attend",
    )(tokens, attn_own, up_own, down_own, vec_own, pool_own, lengths)


def attend_back(n, first_grad, w_out, context, qkv, prob, x_all, w_attn, grad_up):
    rows, span, width = first_grad.shape
    quarter = width // SEQ
    span_all = span * SEQ
    own_rows = width // n
    aligned = own_rows % 16 == 0
    scale = HD**-0.5
    shape = jax.ShapeDtypeStruct
    outs = [shape((rows, span, width), F32), shape((1, 3 * quarter), F32)]
    if aligned:
        locals_ = [shape((n, own_rows, c), F32) for c in (3 * quarter, quarter)]
        batch_ops = [ScatterBatch(n, a) for a in [grad_up] + locals_]
        outs += [op.outs[0] for op in batch_ops]
    else:
        locals_, batch_ops = [], []
        outs += [shape((width, 3 * quarter), F32), shape((width, quarter), F32)]
    scratch = (
        RowSwap.scratch((SEQ, rows, span, quarter))
        + [pltpu.VMEM((1, SEQ, width, quarter), F32)]
        + RowScatter.scratch(1, (width, quarter))
        + [pltpu.VMEM((rows, SEQ, span, width), F32)]
        + RowScatter.scratch(rows, (span, width))
        + [pltpu.VMEM((rows, span_all, 3 * quarter), BF16)]
        + [pltpu.VMEM(a.shape, F32) for a in locals_]
        + [c for op in batch_ops for c in op.scratch]
    )

    def kernel(first_grad, w_out, context, qkv, prob, x_all, w_attn, grad_up, *rest):
        input_grad, bias_sums = rest[:2]
        results = rest[2 : 5 if aligned else 4]
        rest = rest[5 if aligned else 4 :]
        greet(n, {"seq", "batch"} if aligned else {"seq"})
        swap = RowSwap(*rest[0:4])
        grad_context, arrived = rest[0:2]
        out_part = rest[4]
        out_sum = RowScatter(out_part, *rest[5:11])
        x_part = rest[11]
        x_sum = RowScatter(x_part, *rest[12:18])
        grad_qkv = rest[18]
        rest = rest[19:]
        if aligned:
            local_qkv, local_out = rest[:2]
            up_move = batch_ops[0].run(grad_up, results[0], *rest[2:10])
            qkv_move = batch_ops[1].run(local_qkv, results[1], *rest[10:18])
            out_move = batch_ops[2].run(local_out, results[2], *rest[18:26])
        low = first_grad[...].astype(BF16).reshape(rows * span, width)
        rise = contract_last(low, w_out[...]).astype(BF16)
        for r in range(rows):
            for k in range(SEQ):
                grad_context[k, r] = rise[
                    r * span : (r + 1) * span, k * quarter : (k + 1) * quarter
                ]
            swap.start(r)
        if aligned:
            step(up_move)
        whole = contract_first(context[...].reshape(rows * span, width), low)
        for k in range(SEQ):
            out_part[0, k] = whole[:, k * quarter : (k + 1) * quarter]
        out_sum.send_diag(0)
        out_sum.send_near(0)
        w_qkv = w_attn[:, : 3 * quarter]
        sums = jnp.zeros((1, 3 * quarter), F32)
        for r in range(rows):
            swap.wait(r)
            upstream = [arrived[k, r] for k in range(SEQ)]
            upstream = jnp.concatenate(upstream, axis=0)
            query_grads, key_grads, value_grads = [], [], []
            for h in range(HEADS):
                query, key, value = [
                    qkv[r, :, k * quarter + h * HD : k * quarter + (h + 1) * HD] for k in range(3)
                ]
                above = upstream[:, h * HD : (h + 1) * HD]
                weight = prob[r, h]
                prob_grad = contract_last(above, value)
                delta = jnp.sum(weight * prob_grad, axis=-1, keepdims=True)
                score_grad = (weight * (prob_grad - delta)).astype(BF16)
                query_grads.append(matmul(score_grad, key) * scale)
                key_grads.append(contract_first(query, score_grad) * scale)
                value_grads.append(contract_first(above, weight.astype(BF16)))
                if aligned:
                    step(up_move)
            across = jnp.concatenate(key_grads + value_grads, axis=0).T
            block = jnp.concatenate(query_grads + [across], axis=1).astype(BF16)
            grad_qkv[r] = block
            sums += row_sum(block.astype(F32))
            x_part[r] = contract_last(block, w_qkv).reshape(SEQ, span, width)
            x_sum.send_diag(r)
            x_sum.send_near(r)
            if r == 0:
                out_sum.cross(0)
            x_sum.cross(r)
        bias_sums[...] = sums
        whole = contract_first(
            x_all[...].reshape(rows * span_all, width),
            grad_qkv[...].reshape(rows * span_all, 3 * quarter),
        )
        if aligned:
            local_qkv[...] = whole.reshape(local_qkv.shape)
            step(qkv_move)
            local_out[...] = out_sum.total(0).reshape(local_out.shape)
            step(out_move)
            drain(up_move)
        else:
            results[0][...] = whole
            results[1][...] = out_sum.total(0)
        for r in range(rows):
            input_grad[r] = x_sum.total(r) + first_grad[r]
        out_sum.finish(0)
        for r in range(rows):
            swap.finish(r)
            x_sum.finish(r)
        if aligned:
            drain(qkv_move)
            drain(out_move)

    vmem = pl.BlockSpec(memory_space=pltpu.VMEM)
    return pl.pallas_call(
        kernel,
        out_shape=outs,
        in_specs=[vmem] * 8,
        out_specs=[vmem] * len(outs),
        scratch_shapes=scratch,
        compiler_params=pltpu.CompilerParams(
            collective_id=4, has_side_effects=True, vmem_limit_bytes=60 * 2**20
        ),
        name="attend_back",
    )(first_grad, w_out, context, qkv, prob, x_all, w_attn, grad_up)


def step_factor(rows_all, cols_all):
    return matrix_rate * math.sqrt(max(1.0, rows_all / cols_all))


def make_body(n):
    def body(
        layer_input,
        lengths,
        attn_weight,
        up_weight,
        down_weight,
        vectors,
        attn_moment,
        up_moment,
        down_moment,
        vector_moment,
        out_grad,
        pool_grad,
    ):
        rows, span, width = layer_input.shape
        own_rows = width // n
        quarter = width // SEQ
        hidden = up_weight.shape[1]
        hid_q = hidden // SEQ
        hid_own = hidden // n // SEQ
        seq_index = lax.axis_index("seq")

        def attn_quarter(stacked):
            part = lax.dynamic_index_in_dim(
                stacked.reshape(4, own_rows, SEQ, quarter), seq_index, 2, False
            )
            return part

        def up_quarter(matrix):
            return lax.dynamic_index_in_dim(
                matrix.reshape(own_rows, n, SEQ, hid_own), seq_index, 2, False
            ).reshape(own_rows, hid_q)

        def down_quarter(matrix):
            return lax.dynamic_index_in_dim(
                matrix.reshape(SEQ, hid_own, width), seq_index, 0, False
            )

        attn_low = attn_quarter(attn_weight).astype(BF16).transpose(1, 0, 2).reshape(own_rows, width)
        up_low = up_quarter(up_weight).astype(BF16)
        down_low = down_quarter(down_weight).astype(BF16)
        vec_low = vectors.astype(BF16).astype(F32)
        placed = lax.dynamic_update_slice(
            jnp.zeros((vectors.shape[0], n, own_rows), F32),
            vec_low[:, None],
            (0, lax.axis_index("batch"), 0),
        ).reshape(-1, width)
        bias_up = lax.dynamic_index_in_dim(
            placed[8:].reshape(n, SEQ, hid_own), seq_index, 1, False
        ).reshape(1, hid_q)
        bias_qv = lax.dynamic_index_in_dim(
            placed[:2].reshape(2, SEQ, quarter), seq_index, 1, False
        )
        blank = jnp.zeros((quarter,), F32)
        bias_qkv = jnp.concatenate([bias_qv[0], blank, bias_qv[1], blank])[None]
        vec_own = jnp.concatenate([placed[2:8], bias_up, bias_qkv])
        aligned = own_rows % 16 == 0
        own = [attn_low, up_low, down_low]
        if not aligned:
            own = exchange(n, 1, "gather_weights", *[GatherBatch(n, a) for a in own])
            own = [a.reshape(width, width) for a in own]
        (
            normed_one, scaled_one, spread_one, w_out, vec_rows, pool_whole, x_all, qkv, prob, context,
            *weights,
        ) = attend(n, layer_input, *own, vec_own, pool_grad, lengths)
        w_attn, w_up, w_down = [a.reshape(width, width) for a in (weights if aligned else own)]
        out_rows, pool_sum, first_grad, vec_grad, grad_up, down_piece = hidden_layer(
            n, normed_one, scaled_one, spread_one, w_up, w_down, vec_rows, out_grad, pool_whole, lengths
        )
        pooled = lax.dynamic_slice_in_dim(pool_sum, seq_index * quarter, quarter, 1)
        back = attend_back(
            n, first_grad, w_out, context, qkv, prob, x_all, w_attn,
            grad_up.reshape(n, own_rows, hid_q) if aligned else grad_up,
        )
        input_grad, bias_sums = back[:2]
        if aligned:
            up_piece, qkv_piece, out_piece = back[2:]
        else:
            down_piece, up_piece, qkv_piece, out_piece = exchange(
                n,
                2,
                "sum_grads",
                *[
                    ScatterBatch(n, a.reshape(n, own_rows, -1))
                    for a in (down_piece, grad_up, back[2], back[3])
                ],
            )
        attn_piece = jnp.concatenate([qkv_piece, out_piece], axis=1)
        bias_sums = bias_sums.reshape(3, quarter)

        vec_head = jnp.zeros((2, SEQ, quarter), F32)
        vec_head = lax.dynamic_update_slice(
            vec_head, bias_sums[jnp.array([0, 2])][:, None], (0, seq_index, 0)
        ).reshape(2, width)
        vec_mid = vec_grad[:6]
        grad_bias_up = vec_grad[6]
        vec_tail = lax.dynamic_update_slice(
            jnp.zeros((n, SEQ, hid_own), F32),
            grad_bias_up.reshape(n, 1, hid_own),
            (0, seq_index, 0),
        ).reshape(-1, width)
        vec_local = jnp.concatenate([vec_head, vec_mid, vec_tail])
        vec_local = vec_local.reshape(-1, n, own_rows).transpose(1, 0, 2)
        (vec_piece,) = exchange(n, 7, "sum_vectors", ScatterBatch(n, vec_local, F32))
        attn_bf = attn_piece.astype(BF16).reshape(own_rows, 4, quarter).transpose(1, 0, 2)
        wide_bf = jnp.stack([up_piece, down_piece]).astype(BF16)
        attn_send = (matrix_decay * attn_quarter(attn_moment) + attn_bf.astype(F32)).astype(BF16)
        wide_moment = jnp.stack([up_quarter(up_moment), down_quarter(down_moment)])
        wide_send = (matrix_decay * wide_moment + wide_bf.astype(F32)).astype(BF16)
        short = -own_rows % 16
        attn_send = jnp.pad(attn_send, ((0, 0), (0, short), (0, 0)))
        wide_send = jnp.pad(wide_send, ((0, 0), (0, short), (0, 0)))
        attn_all, wide_all, vec_parts, attn_orth, wide_orth = exchange(
            n,
            8,
            "muon",
            GatherSeq(n, attn_bf),
            GatherSeq(n, wide_bf),
            GatherSeq(n, vec_piece),
            Muon(n, attn_send, wide_send),
        )
        attn_orth = attn_orth[:, :, :own_rows]
        wide_orth = wide_orth[:, :, :own_rows]

        def join_attn(parts):
            return parts.astype(F32).transpose(1, 2, 0, 3).reshape(4, own_rows, width)

        def join_up(parts):
            return (
                parts.astype(F32)
                .reshape(SEQ, own_rows, n, hid_own)
                .transpose(1, 2, 0, 3)
                .reshape(own_rows, hidden)
            )

        def join_down(parts):
            return parts.astype(F32).reshape(SEQ * hid_own, width)

        attn_grad = join_attn(attn_all)
        up_grad, down_grad = join_up(wide_all[:, 0]), join_down(wide_all[:, 1])
        vector_grad = (vec_parts[0] + vec_parts[1]) + (vec_parts[2] + vec_parts[3])
        attn_next = matrix_decay * attn_moment + attn_grad
        up_next = matrix_decay * up_moment + up_grad
        down_next = matrix_decay * down_moment + down_grad

        factors = [
            step_factor(width, width),
            step_factor(width, hidden),
            step_factor(hidden, width),
        ]
        attn_new = attn_weight - factors[0] * join_attn(attn_orth)
        up_new = up_weight - factors[1] * join_up(wide_orth[:, 0])
        down_new = down_weight - factors[2] * join_down(wide_orth[:, 1])
        vector_next = vector_decay * vector_moment + vector_grad
        vectors_new = vectors - vector_rate / math.sqrt(rows * n) * vector_next
        return (
            out_rows,
            pooled,
            input_grad,
            attn_grad,
            up_grad,
            down_grad,
            vector_grad,
            attn_next,
            up_next,
            down_next,
            vector_next,
            attn_new,
            up_new,
            down_new,
            vectors_new,
        )

    return body


def solution(mesh):
    placed = (
        P("batch", "seq", None),
        P("batch"),
        P(None, "batch", None),
        P("batch", None),
        P("batch", None),
        P(None, "batch"),
        P(None, "batch", None),
        P("batch", None),
        P("batch", None),
        P(None, "batch"),
        P("batch", "seq", None),
        P("batch", "seq"),
    )
    return jax.shard_map(
        make_body(mesh.shape["batch"]),
        mesh=mesh,
        in_specs=placed,
        out_specs=(
            P("batch", "seq", None),
            P("batch", "seq"),
            P("batch", "seq", None),
            P(None, "batch", None),
            P("batch", None),
            P("batch", None),
            P(None, "batch"),
            P(None, "batch", None),
            P("batch", None),
            P("batch", None),
            P(None, "batch"),
            P(None, "batch", None),
            P("batch", None),
            P("batch", None),
            P(None, "batch"),
        ),
        check_vma=False,
    )
```

```python
import math

import jax
import jax.numpy as jnp
from jax import lax
from jax.experimental import pallas as pl
from jax.experimental.pallas import tpu as pltpu
from jax.sharding import PartitionSpec as P

H = 12
HD = 64
NS = 5
SEQ = 4
HEADS = H // SEQ

norm_eps = 1e-12
tiny_norm = 1e-07
matrix_decay = 0.95
vector_decay = 0.5
matrix_rate = 0.5
vector_rate = 0.03

MESH = pl.DeviceIdType.MESH
F32 = jnp.float32
BF16 = jnp.bfloat16


def coords(n):
    b = lax.axis_index("batch")
    s = lax.axis_index("seq")
    return b, s, b // 2, b % 2, n // 2


def remote(src, dst, send, recv, device):
    return pltpu.make_async_remote_copy(
        src_ref=src, dst_ref=dst, send_sem=send, recv_sem=recv, device_id=device, device_id_type=MESH
    )


class GatherBatch:
    peers = ("batch",)

    def __init__(self, n, src):
        self.n = n
        self.ins = [src]
        self.outs = [jax.ShapeDtypeStruct((n,) + src.shape, src.dtype)]
        m = n // 2
        self.scratch = [pltpu.SemaphoreType.DMA((m,))] * 4 + [pltpu.SemaphoreType.DMA]

    def run(self, src, dst, zs, zr, ys, yr, own):
        b, s, hi, lo, m = coords(self.n)
        local = pltpu.make_async_copy(src, dst.at[b], own)
        local.start()
        pair = (hi * 2 + 1 - lo, s)
        out = []
        for d in range(1, m):
            c = remote(src, dst.at[b], zs.at[d], zr.at[d], (((hi + d) % m) * 2 + lo, s))
            c.start()
            out.append(c)
        first = remote(src, dst.at[b], ys.at[0], yr.at[0], pair)
        first.start()
        yield
        passed = [first]
        for d in range(1, m):
            out[d - 1].wait_recv()
            block = ((hi + m - d) % m) * 2 + lo
            c = remote(dst.at[block], dst.at[block], ys.at[d], yr.at[d], pair)
            c.start()
            passed.append(c)
            yield
        local.wait()
        for c in passed:
            c.wait()
        for c in out:
            c.wait_send()


class ScatterBatch:
    peers = ("batch",)

    def __init__(self, n, src, wire=BF16):
        self.n = n
        self.wire = wire
        self.ins = [src]
        shape = src.shape[1:]
        self.outs = [jax.ShapeDtypeStruct(shape, F32)]
        m = n // 2
        self.scratch = [pltpu.VMEM((m,) + shape, wire)] * 4 + [pltpu.SemaphoreType.DMA((m,))] * 4

    def run(self, src, dst, ysend, yrecv, zsend, zrecv, ys, yr, zs, zr):
        b, s, hi, lo, m = coords(self.n)
        pair = (hi * 2 + 1 - lo, s)
        first = {}
        order = list(range(1, m)) + [0]
        for d in order:
            h = (hi + d) % m
            ysend[d] = src[h * 2 + 1 - lo].astype(self.wire)
            first[d] = remote(ysend.at[d], yrecv.at[d], ys.at[d], yr.at[d], pair)
            first[d].start()
        yield
        second = []
        for d in range(1, m):
            h = (hi + d) % m
            first[d].wait_recv()
            zsend[d] = (src[h * 2 + lo] + yrecv[d].astype(F32)).astype(self.wire)
            c = remote(zsend.at[d], zrecv.at[d], zs.at[d], zr.at[d], (h * 2 + lo, s))
            c.start()
            second.append(c)
            yield
        first[0].wait_recv()
        total = src[b] + yrecv[0].astype(F32)
        for d in range(1, m):
            second[d - 1].wait_recv()
            total = total + zrecv[d].astype(F32)
        dst[...] = total
        for c in list(first.values()) + second:
            c.wait_send()


class GatherSeq:
    peers = ("seq",)

    def __init__(self, n, src):
        self.ins = [src]
        self.outs = [jax.ShapeDtypeStruct((SEQ,) + src.shape, src.dtype)]
        self.scratch = [pltpu.SemaphoreType.DMA((3,))] * 2 + [pltpu.SemaphoreType.DMA]

    def run(self, src, dst, ss, rs, own):
        b, s = lax.axis_index("batch"), lax.axis_index("seq")
        far, near = (s + 2) % 4, s + 1 - 2 * (s % 2)
        across = remote(src, dst.at[s], ss.at[0], rs.at[0], (b, far))
        across.start()
        local = pltpu.make_async_copy(src, dst.at[s], own)
        local.start()
        beside = remote(src, dst.at[s], ss.at[1], rs.at[1], (b, near))
        beside.start()
        yield
        across.wait_recv()
        passed = remote(dst.at[far], dst.at[far], ss.at[2], rs.at[2], (b, near))
        passed.start()
        yield
        local.wait()
        beside.wait()
        passed.wait()
        across.wait_send()


class ScatterSeq:
    peers = ("seq",)

    def __init__(self, n, src):
        self.ins = [src]
        shape = src.shape[1:]
        self.outs = [jax.ShapeDtypeStruct(shape, F32)]
        self.scratch = [
            pltpu.VMEM((2,) + shape, BF16),
            pltpu.VMEM((2,) + shape, BF16),
            pltpu.VMEM(shape, BF16),
            pltpu.VMEM(shape, BF16),
            pltpu.SemaphoreType.DMA((3,)),
            pltpu.SemaphoreType.DMA((3,)),
        ]

    def run(self, src, dst, near_out, near_in, far_out, far_in, ss, rs):
        b, s = lax.axis_index("batch"), lax.axis_index("seq")
        far, near = (s + 2) % 4, s + 1 - 2 * (s % 2)
        near_far = (near + 2) % 4
        near_out[1] = src[near_far].astype(BF16)
        one = remote(near_out.at[1], near_in.at[1], ss.at[1], rs.at[1], (b, near))
        one.start()
        near_out[0] = src[near].astype(BF16)
        two = remote(near_out.at[0], near_in.at[0], ss.at[0], rs.at[0], (b, near))
        two.start()
        yield
        one.wait_recv()
        far_out[...] = (src[far] + near_in[1].astype(F32)).astype(BF16)
        three = remote(far_out, far_in, ss.at[2], rs.at[2], (b, far))
        three.start()
        yield
        two.wait_recv()
        dst[...] = src[s] + near_in[0].astype(F32)
        yield
        three.wait_recv()
        dst[...] = dst[...] + far_in[...].astype(F32)
        one.wait_send()
        two.wait_send()
        three.wait_send()


class SwapSeq:
    peers = ("seq",)

    def __init__(self, n, src):
        self.ins = [src]
        self.outs = [jax.ShapeDtypeStruct(src.shape, src.dtype)]
        self.scratch = [pltpu.SemaphoreType.DMA((4,))] * 2 + [pltpu.SemaphoreType.DMA]

    def run(self, src, dst, ss, rs, own):
        b, s = lax.axis_index("batch"), lax.axis_index("seq")
        copies = []
        for k in (2, 3, 1):
            other = (s + k) % 4
            c = remote(src.at[other], dst.at[s], ss.at[k], rs.at[k], (b, other))
            c.start()
            copies.append(c)
        local = pltpu.make_async_copy(src.at[s], dst.at[s], own)
        local.start()
        yield
        local.wait()
        for c in copies:
            c.wait()


def owner_list(n):
    return [(0, 2), (1, 0), (n - 2, 2), (n - 1, 0), (n // 4, 0), (n // 2 + 1, 2)]


class Muon:
    peers = ("all",)

    def __init__(self, n, attn_piece, wide_piece):
        self.n = n
        self.ins = [attn_piece, wide_piece]
        rows, quarter = attn_piece.shape[1:]
        width = wide_piece.shape[2]
        self.outs = [
            jax.ShapeDtypeStruct((SEQ, 4, rows, quarter), BF16),
            jax.ShapeDtypeStruct((SEQ, 2, rows, width), BF16),
        ]
        size = n * rows
        dma = pltpu.SemaphoreType.DMA
        self.scratch = [
            pltpu.VMEM((SEQ, n, rows, quarter), BF16),
            pltpu.VMEM((SEQ, n, rows, width), BF16),
            pltpu.VMEM((size, SEQ * size), F32),
            pltpu.VMEM((size, SEQ * size), BF16),
            pltpu.VMEM((size, size), F32),
            pltpu.VMEM((size, size), BF16),
            pltpu.VMEM((size, size), BF16),
            pltpu.VMEM((size, 1), F32),
            dma((6,)),
            dma((SEQ * n,)),
            dma((SEQ * n,)),
            dma((6,)),
            dma((6, 3)),
            dma((6, 3)),
            dma((2,)),
        ]

    def run(
        self, attn, wide, attn_orth, wide_orth, attn_in, wide_in, x32, xlow, gram, gram_low, poly, diag,
        ss, rs, back_s, back_r, seq_s, seq_r, own,
    ):
        n = self.n
        b, s = lax.axis_index("batch"), lax.axis_index("seq")
        me = s * n + b
        far, near = (s + 2) % 4, s + 1 - 2 * (s % 2)
        size = x32.shape[0]
        width = wide.shape[2]
        quarter = attn.shape[2]
        places = owner_list(n)
        mine = [(b == ob) & (s == os) for ob, os in places]
        number = jnp.int32(0)
        for k in range(6):
            number = jnp.where(mine[k], jnp.int32(k), number)
        is_attn = mine[0] | mine[1] | mine[2] | mine[3]
        is_wide = mine[4] | mine[5]
        order = (5, 4, 0, 1, 2, 3)

        def piece(k):
            return attn.at[k] if k < 4 else wide.at[k - 4]

        def inbox(k):
            return attn_in if k < 4 else wide_in

        def result(k):
            return attn_orth.at[s, k] if k < 4 else wide_orth.at[s, k - 4]

        for k in order:
            ob, os = places[k]

            @pl.when(jnp.logical_not(mine[k]))
            def _(k=k, ob=ob, os=os):
                remote(piece(k), inbox(k).at[s, b], ss.at[k], rs.at[me], (ob, os)).start()

            @pl.when(mine[k])
            def _(k=k):
                pltpu.make_async_copy(piece(k), inbox(k).at[s, b], own.at[0]).start()

        yield
        yield
        yield
        yield

        def collect(buf):
            pltpu.make_async_copy(buf.at[s, b], buf.at[s, b], own.at[0]).wait()

            @pl.loop(1, SEQ * n)
            def _(k):
                other = (me + k) % (SEQ * n)
                place = buf.at[other // n, other % n]
                remote(place, place, ss.at[0], rs.at[other], (0, 0)).wait_recv()

        def give(buf, out, index):
            pltpu.make_async_copy(buf.at[s, b], out.at[s, index], own.at[1]).start()

            @pl.loop(1, SEQ * n)
            def _(k):
                other = (me + k) % (SEQ * n)
                os, ob = other // n, other % n
                remote(
                    buf.at[os, ob], out.at[os, index], back_s.at[other], back_r.at[number], (ob, os)
                ).start()

        def squares(buf):
            total = jnp.zeros((1, 1), F32)
            for k in range(SEQ):
                block = buf[k].astype(F32).reshape(size, buf.shape[3])
                total = total + jnp.sum(block * block, keepdims=True)
            return 1.0 / (jnp.sqrt(total) + tiny_norm)

        @pl.when(is_attn)
        def _():
            collect(attn_in)
            inverse = squares(attn_in)
            step = -(-quarter // 128) * 128
            span = SEQ * step
            x32[:, :span] = jnp.zeros((size, span), F32)
            for k in range(SEQ):
                block = attn_in[k].astype(F32).reshape(size, quarter)
                x32[:, k * step : k * step + quarter] = block * inverse
            xlow[:, :span] = x32[:, :span].astype(BF16)
            newton_schulz(
                x32.at[:, pl.ds(0, span)], xlow.at[:, pl.ds(0, span)], gram, gram_low, poly, diag
            )
            for k in range(SEQ):
                block = xlow[:, k * step : k * step + quarter]
                attn_in[k] = block.reshape(attn_in.shape[1:])
            give(attn_in, attn_orth, number)

        @pl.when(is_wide)
        def _():
            collect(wide_in)
            inverse = squares(wide_in)
            if width != size:
                x32[...] = jnp.zeros(x32.shape, F32)

            @pl.when(mine[4])
            def _():
                for k in range(SEQ):
                    block = wide_in[k].astype(F32).reshape(size, width)
                    x32[:, k * size : k * size + width] = block * inverse

            @pl.when(mine[5])
            def _():
                for k in range(SEQ):
                    block = wide_in[k].astype(F32).reshape(size, width)
                    x32[:width, k * size : (k + 1) * size] = block.T * inverse

            for k in range(SEQ):
                xlow[:, k * size : (k + 1) * size] = x32[:, k * size : (k + 1) * size].astype(BF16)
            newton_schulz(x32, xlow, gram, gram_low, poly, diag)

            @pl.when(mine[4])
            def _():
                for k in range(SEQ):
                    block = xlow[:, k * size : k * size + width]
                    wide_in[k] = block.reshape(wide_in.shape[1:])

            @pl.when(mine[5])
            def _():
                for k in range(SEQ):
                    block = x32[:width, k * size : (k + 1) * size].T.astype(BF16)
                    wide_in[k] = block.reshape(wide_in.shape[1:])

            give(wide_in, wide_orth, number - 4)

        def onward(k, step, source, target):
            out = attn_orth.at[source, k] if k < 4 else wide_orth.at[source, k - 4]
            return remote(out, out, seq_s.at[k, step], seq_r.at[k, step], (b, target))

        done = (0, 1, 2, 3, 4, 5)
        for k in done:

            @pl.when(jnp.logical_not(mine[k]))
            def _(k=k):
                remote(piece(k), result(k), ss.at[k], back_r.at[k], (0, 0)).wait_recv()

            @pl.when(mine[k])
            def _(k=k):
                pltpu.make_async_copy(piece(k), result(k), own.at[1]).wait()

            onward(k, 0, s, far).start()
            onward(k, 1, s, near).start()
        for k in done:
            onward(k, 0, far, far).wait_recv()
            onward(k, 2, far, near).start()
        for k in done:
            onward(k, 1, near, near).wait_recv()
            onward(k, 2, (near + 2) % 4, near).wait_recv()
            onward(k, 0, s, far).wait_send()
            onward(k, 1, s, near).wait_send()
            onward(k, 2, far, near).wait_send()

            @pl.when(jnp.logical_not(mine[k]))
            def _(k=k):
                remote(piece(k), inbox(k).at[s, b], ss.at[k], rs.at[me], (0, 0)).wait_send()

        def given(buf):
            @pl.loop(1, SEQ * n)
            def _(k):
                other = (me + k) % (SEQ * n)
                place = buf.at[other // n, other % n]
                remote(place, place, back_s.at[other], back_r.at[0], (0, 0)).wait_send()

        @pl.when(is_attn)
        def _():
            given(attn_in)

        @pl.when(is_wide)
        def _():
            given(wide_in)


def newton_schulz(x32, xlow, gram, gram_low, poly, diag):
    size, wide = x32.shape
    eye = lax.broadcasted_iota(jnp.int32, (size, size), 0) == lax.broadcasted_iota(
        jnp.int32, (size, size), 1
    )
    chunk = 768 if wide % 768 == 0 else 512

    @pl.loop(0, NS)
    def _(turn):
        whole = contract_last(xlow[...], xlow[...])
        gram[...] = whole
        gram_low[...] = jnp.where(eye, 0.0, whole).astype(BF16)
        whole = gram[...]
        on_diag = jnp.where(eye, whole, 0.0)
        down = jnp.sum(on_diag, axis=1, keepdims=True)
        along = jnp.sum(on_diag, axis=0, keepdims=True)
        square = (
            matmul(gram_low[...], gram_low[...])
            + (down + along) * jnp.where(eye, 0.0, whole)
            + jnp.where(eye, down * down, 0.0)
        )
        mixed = -4.775 * whole + 2.0315 * square
        diag[...] = jnp.sum(jnp.where(eye, mixed, 0.0), axis=1, keepdims=True) + 3.4445
        poly[...] = jnp.where(eye, 0.0, mixed).astype(BF16)
        for c in range(0, wide, chunk):
            moved = diag[...] * x32[:, c : c + chunk] + matmul(poly[...], xlow[:, c : c + chunk])
            x32[:, c : c + chunk] = moved
            xlow[:, c : c + chunk] = moved.astype(BF16)


def greet_peers(n, kinds):
    b, s, hi, lo, m = coords(n)
    peers = []
    if "seq" in kinds:
        peers += [(b, (s + k) % 4) for k in (1, 2, 3)]
    if "batch" in kinds:
        peers += [(((hi + d) % m) * 2 + lo, s) for d in range(1, m)]
        peers += [(hi * 2 + 1 - lo, s)]
    return peers


def greet_signal(n, kinds):
    b, s = lax.axis_index("batch"), lax.axis_index("seq")
    barrier = pltpu.get_barrier_semaphore()
    if "all" in kinds:
        me = s * n + b

        @pl.loop(1, SEQ * n)
        def _(k):
            other = (me + k) % (SEQ * n)
            pl.semaphore_signal(
                barrier, inc=1, device_id=(other % n, other // n), device_id_type=MESH
            )

        return
    for peer in greet_peers(n, kinds):
        pl.semaphore_signal(barrier, inc=1, device_id=peer, device_id_type=MESH)


def greet_wait(n, kinds):
    count = SEQ * n - 1 if "all" in kinds else len(greet_peers(n, kinds))
    pl.semaphore_wait(pltpu.get_barrier_semaphore(), count)


def greet(n, kinds):
    greet_signal(n, kinds)
    greet_wait(n, kinds)


def run_together(*live):
    live = list(live)
    while live:
        still = []
        for op in live:
            try:
                next(op)
                still.append(op)
            except StopIteration:
                pass
        live = still


def exchange(n, collective_id, name, *ops):
    ins = [a for op in ops for a in op.ins]
    outs = [o for op in ops for o in op.outs]
    scratch = [c for op in ops for c in op.scratch]
    kinds = {k for op in ops for k in op.peers}

    def kernel(*refs):
        in_refs, out_refs = refs[: len(ins)], refs[len(ins) : len(ins) + len(outs)]
        scratch_refs = refs[len(ins) + len(outs) :]
        greet(n, kinds)
        live = []
        i = o = c = 0
        for op in ops:
            ni, no, nc = len(op.ins), len(op.outs), len(op.scratch)
            live.append(
                op.run(*in_refs[i : i + ni], *out_refs[o : o + no], *scratch_refs[c : c + nc])
            )
            i, o, c = i + ni, o + no, c + nc
        run_together(*live)

    vmem = pl.BlockSpec(memory_space=pltpu.VMEM)
    return pl.pallas_call(
        kernel,
        out_shape=outs,
        in_specs=[vmem] * len(ins),
        out_specs=[vmem] * len(outs),
        scratch_shapes=scratch,
        compiler_params=pltpu.CompilerParams(
            collective_id=collective_id, has_side_effects=True, vmem_limit_bytes=60 * 2**20
        ),
        name=name,
    )(*ins)


def contract_last(left, right):
    return lax.dot_general(left, right, (((1,), (1,)), ((), ())), preferred_element_type=F32)


def contract_first(left, right):
    return lax.dot_general(left, right, (((0,), (0,)), ((), ())), preferred_element_type=F32)


def matmul(left, right):
    return jnp.dot(left, right, preferred_element_type=F32)


def exact_gelu(value_in):
    return jax.nn.gelu(value_in, approximate=False)


def normalize(hidden, gain_row):
    row_mean = jnp.mean(hidden, axis=-1, keepdims=True)
    centred = hidden - row_mean
    spread = lax.rsqrt(jnp.mean(centred * centred, axis=-1, keepdims=True) + norm_eps)
    scaled = centred * spread
    return (scaled * gain_row, scaled, spread)


def normalize_back(grad_in, scaled, spread, gain_row):
    weighted = grad_in * gain_row
    mean_first = jnp.mean(weighted, axis=-1, keepdims=True)
    second = jnp.mean(weighted * scaled, axis=-1, keepdims=True)
    return (
        spread * (weighted - mean_first - scaled * second),
        jnp.sum(grad_in * scaled, axis=0),
        jnp.sum(grad_in, axis=0),
    )


class RowGather:
    @staticmethod
    def scratch():
        return [pltpu.SemaphoreType.DMA((2, 3)), pltpu.SemaphoreType.DMA((2, 3))]

    def __init__(self, buf, ss, rs):
        self.buf, self.ss, self.rs = buf, ss, rs
        self.b, self.s = lax.axis_index("batch"), lax.axis_index("seq")
        self.far, self.near = (self.s + 2) % 4, self.s + 1 - 2 * (self.s % 2)
        self.diag = (self.near + 2) % 4

    def copy(self, r, step, block, device):
        place = self.buf.at[r, block]
        return remote(place, place, self.ss.at[r, step], self.rs.at[r, step], (self.b, device))

    def start(self, r):
        self.copy(r, 0, self.s, self.far).start()
        self.copy(r, 1, self.s, self.near).start()

    def wait_near(self, r):
        self.copy(r, 1, self.near, self.near).wait_recv()

    def pass_far(self, r):
        self.copy(r, 0, self.far, self.far).wait_recv()
        self.copy(r, 2, self.far, self.near).start()

    def wait_diag(self, r):
        self.copy(r, 2, self.diag, self.near).wait_recv()

    def finish(self, r):
        self.copy(r, 0, self.s, self.far).wait_send()
        self.copy(r, 1, self.s, self.near).wait_send()
        self.copy(r, 2, self.far, self.near).wait_send()


class RowScatter:
    @staticmethod
    def scratch(rows, shape):
        return [
            pltpu.VMEM((rows, 2) + shape, BF16),
            pltpu.VMEM((rows, 2) + shape, BF16),
            pltpu.VMEM((rows,) + shape, BF16),
            pltpu.VMEM((rows,) + shape, BF16),
            pltpu.SemaphoreType.DMA((rows, 3)),
            pltpu.SemaphoreType.DMA((rows, 3)),
        ]

    def __init__(self, src, near_out, near_in, far_out, far_in, ss, rs):
        self.src = src
        self.near_out, self.near_in = near_out, near_in
        self.far_out, self.far_in = far_out, far_in
        self.ss, self.rs = ss, rs
        self.b, self.s = lax.axis_index("batch"), lax.axis_index("seq")
        self.far, self.near = (self.s + 2) % 4, self.s + 1 - 2 * (self.s % 2)
        self.diag = (self.near + 2) % 4

    def beside(self, r, k):
        return remote(
            self.near_out.at[r, k], self.near_in.at[r, k], self.ss.at[r, k], self.rs.at[r, k],
            (self.b, self.near),
        )

    def across(self, r):
        return remote(
            self.far_out.at[r], self.far_in.at[r], self.ss.at[r, 2], self.rs.at[r, 2],
            (self.b, self.far),
        )

    def send_near(self, r):
        self.near_out[r, 0] = self.src[r, self.near].astype(BF16)
        self.beside(r, 0).start()

    def send_diag(self, r):
        self.near_out[r, 1] = self.src[r, self.diag].astype(BF16)
        self.beside(r, 1).start()

    def cross(self, r):
        self.beside(r, 1).wait_recv()
        self.far_out[r] = (self.src[r, self.far] + self.near_in[r, 1].astype(F32)).astype(BF16)
        self.across(r).start()

    def total(self, r):
        self.beside(r, 0).wait_recv()
        part = self.src[r, self.s] + self.near_in[r, 0].astype(F32)
        self.across(r).wait_recv()
        return part + self.far_in[r].astype(F32)

    def finish(self, r):
        self.beside(r, 0).wait_send()
        self.beside(r, 1).wait_send()
        self.across(r).wait_send()


def gelu_parts(value):
    cdf = 0.5 * (1.0 + lax.erf(value * math.sqrt(0.5)))
    density = jnp.exp(-0.5 * value * value) * (1.0 / math.sqrt(2.0 * math.pi))
    return value * cdf, cdf + value * density


def row_sum(value):
    return jnp.sum(value, axis=0, keepdims=True)


def hidden_layer(n, normed, scaled_one, spread_one, w_up, w_down, vec, out_grad, pool_whole, lengths):
    rows, span, width = normed.shape
    hid_q = w_up.shape[1]
    aligned = (width // n) % 16 == 0
    block = (n, width // n)
    full = (rows, SEQ, span)
    outs = [
        jax.ShapeDtypeStruct((rows, span, width), F32),
        jax.ShapeDtypeStruct((rows, width), F32),
        jax.ShapeDtypeStruct((rows, span, width), F32),
        jax.ShapeDtypeStruct((8, width), F32),
        jax.ShapeDtypeStruct((width, hid_q), F32),
        jax.ShapeDtypeStruct((width // n, width) if aligned else (hid_q, width), F32),
    ]
    if aligned:
        batch_scratch = ScatterBatch(n, jax.ShapeDtypeStruct(block + (width,), F32)).scratch
        batch_scratch = batch_scratch + [pltpu.VMEM(block + (width,), F32)]
    else:
        batch_scratch = []
    scratch = (
        [
            pltpu.VMEM(full + (width,), BF16),
            pltpu.VMEM(full + (hid_q,), F32),
            pltpu.VMEM(full + (hid_q,), BF16),
            pltpu.VMEM(full + (width,), F32),
            pltpu.VMEM(full + (width,), BF16),
            pltpu.VMEM(full + (hid_q,), BF16),
            pltpu.VMEM(full + (width,), F32),
            pltpu.VMEM((rows, span, width), F32),
            pltpu.VMEM((SEQ, rows, width), F32),
            pltpu.SemaphoreType.DMA((3,)),
            pltpu.SemaphoreType.DMA((3,)),
        ]
        + RowGather.scratch() * 2
        + RowScatter.scratch(rows, (span, width)) * 2
    )

    def kernel(
        normed, scaled_one, spread_one, w_up, w_down, vec, out_grad, pool_whole, lengths,
        out_rows, pooled, first_grad, vec_grad, grad_up, grad_down,
        y_all, slope, act, z_part, dz_all, du_all, dy_part, second, pool_buf, pool_ss, pool_rs,
        *rest,
    ):
        greet(n, {"seq", "batch"} if aligned else {"seq"})
        b, s = lax.axis_index("batch"), lax.axis_index("seq")
        y_gather = RowGather(y_all, *rest[0:2])
        dz_gather = RowGather(dz_all, *rest[2:4])
        z_sum = RowScatter(z_part, *rest[4:10])
        dy_sum = RowScatter(dy_part, *rest[10:16])
        rest = rest[16:]
        far, near, diag = y_gather.far, y_gather.near, y_gather.diag
        gain_one, gain_two, shift_two = vec[1:2], vec[3:4], vec[4:5]
        bias_down, bias_up = vec[5:6], vec[6:7]

        for r in range(rows):
            y_all[r, s] = normed[r].astype(BF16)
            y_gather.start(r)

        def pair(ref, blocks):
            return jnp.concatenate([ref[i] for i in blocks], axis=0)

        def spread(ref, blocks, value):
            for k, i in enumerate(blocks):
                ref[i] = value[k * span : (k + 1) * span].astype(ref.dtype)

        def forward(blocks):
            pre = matmul(pair(y_all, blocks), w_up[...]) + bias_up
            value, rate = gelu_parts(pre)
            low = value.astype(BF16)
            spread(act, blocks, low)
            spread(slope, blocks, rate)
            spread(z_part, blocks, matmul(low, w_down[...]))

        forward([(r, s) for r in range(rows)])
        for r in range(rows):
            y_gather.wait_near(r)
        forward([(r, near) for r in range(rows)])
        for r in range(rows):
            z_sum.send_near(r)
        for r in range(rows):
            y_gather.pass_far(r)
            y_gather.wait_diag(r)
            forward([(r, diag), (r, far)])
            z_sum.send_diag(r)
            z_sum.cross(r)

        position = s * span + lax.broadcasted_iota(jnp.int32, (span, 1), 0)
        grad_gain_two = grad_shift_two = grad_bias_down = jnp.zeros((1, width), F32)
        for r in range(rows):
            hidden = normed[r] + (z_sum.total(r) + bias_down)
            centred = hidden - jnp.mean(hidden, axis=-1, keepdims=True)
            spread_two = lax.rsqrt(jnp.mean(centred * centred, axis=-1, keepdims=True) + norm_eps)
            scaled = centred * spread_two
            output = scaled * gain_two + shift_two
            out_rows[r] = output
            live = (position < lengths[r]).astype(F32)
            length = jnp.full((1, 1), lengths[r], jnp.int32).astype(F32)
            pool_buf[s, r : r + 1] = row_sum(output * live) / length
            upstream = live * (out_grad[r] + pool_whole[r : r + 1] / length)
            weighted = upstream * gain_two
            mean_first = jnp.mean(weighted, axis=-1, keepdims=True)
            mean_second = jnp.mean(weighted * scaled, axis=-1, keepdims=True)
            grad = spread_two * (weighted - mean_first - scaled * mean_second)
            second[r] = grad
            low = grad.astype(BF16)
            dz_all[r, s] = low
            dz_gather.start(r)
            grad_gain_two += row_sum(upstream * scaled)
            grad_shift_two += row_sum(upstream)
            grad_bias_down += row_sum(low.astype(F32))

        def pool_copy(k, block, device):
            place = pool_buf.at[block]
            return remote(place, place, pool_ss.at[k - 1], pool_rs.at[k - 1], (b, device))

        for k in (1, 2, 3):
            pool_copy(k, s, (s + k) % 4).start()

        def backward(blocks):
            rise = contract_last(pair(dz_all, blocks), w_down[...])
            low = (rise * pair(slope, blocks)).astype(BF16)
            spread(du_all, blocks, low)
            spread(dy_part, blocks, contract_last(low, w_up[...]))
            return row_sum(low.astype(F32))

        bias_grad = backward([(r, s) for r in range(rows)])
        for r in range(rows):
            dz_gather.wait_near(r)
        bias_grad += backward([(r, near) for r in range(rows)])
        for r in range(rows):
            dy_sum.send_near(r)
        for r in range(rows):
            dz_gather.pass_far(r)
            dz_gather.wait_diag(r)
            bias_grad += backward([(r, diag), (r, far)])
            dy_sum.send_diag(r)
            dy_sum.cross(r)

        tokens = rows * SEQ * span
        whole = contract_first(act[...].reshape(tokens, hid_q), dz_all[...].reshape(tokens, width))
        if aligned:
            scatter = ScatterBatch(n, jax.ShapeDtypeStruct(block + (width,), F32))
            local = rest[-1]
            local[...] = whole.reshape(block + (width,))
            moving = scatter.run(local, grad_down, *rest[:-1])
            next(moving)
        else:
            grad_down[...] = whole
        grad_up[...] = contract_first(
            y_all[...].reshape(tokens, width), du_all[...].reshape(tokens, hid_q)
        )

        grad_gain_one = grad_shift_one = grad_bias_out = jnp.zeros((1, width), F32)
        for r in range(rows):
            grad = dy_sum.total(r) + second[r]
            scaled = scaled_one[r]
            weighted = grad * gain_one
            mean_first = jnp.mean(weighted, axis=-1, keepdims=True)
            mean_second = jnp.mean(weighted * scaled, axis=-1, keepdims=True)
            first = spread_one[r] * (weighted - mean_first - scaled * mean_second)
            first_grad[r] = first
            grad_gain_one += row_sum(grad * scaled)
            grad_shift_one += row_sum(grad)
            grad_bias_out += row_sum(first.astype(BF16).astype(F32))
        for k, value in enumerate(
            (
                grad_bias_out, grad_gain_one, grad_shift_one, grad_gain_two, grad_shift_two,
                grad_bias_down, bias_grad, jnp.zeros((1, width), F32),
            )
        ):
            vec_grad[k : k + 1] = value

        for k in (1, 2, 3):
            pool_copy(k, (s + 4 - k) % 4, (s + k) % 4).wait_recv()
        pooled[...] = (pool_buf[0] + pool_buf[1]) + (pool_buf[2] + pool_buf[3])
        for k in (1, 2, 3):
            pool_copy(k, s, (s + k) % 4).wait_send()
        for r in range(rows):
            for op in (y_gather, z_sum, dz_gather, dy_sum):
                op.finish(r)
        if aligned:
            for _ in moving:
                pass

    vmem = pl.BlockSpec(memory_space=pltpu.VMEM)
    return pl.pallas_call(
        kernel,
        out_shape=outs,
        in_specs=[vmem] * 8 + [pl.BlockSpec(memory_space=pltpu.SMEM)],
        out_specs=[vmem] * len(outs),
        scratch_shapes=scratch + batch_scratch,
        compiler_params=pltpu.CompilerParams(
            collective_id=3, has_side_effects=True, vmem_limit_bytes=60 * 2**20
        ),
        name="hidden_layer",
    )(normed, scaled_one, spread_one, w_up, w_down, vec, out_grad, pool_whole, lengths)


class RowSwap:
    @staticmethod
    def scratch(shape):
        return [
            pltpu.VMEM(shape, BF16),
            pltpu.VMEM(shape, BF16),
            pltpu.SemaphoreType.DMA((2, 4)),
            pltpu.SemaphoreType.DMA((2, 4)),
        ]

    def __init__(self, src, dst, ss, rs):
        self.src, self.dst, self.ss, self.rs = src, dst, ss, rs
        self.b, self.s = lax.axis_index("batch"), lax.axis_index("seq")

    def copy(self, r, k):
        other = (self.s + k) % 4
        return remote(
            self.src.at[other, r], self.dst.at[self.s, r], self.ss.at[r, k], self.rs.at[r, k],
            (self.b, other),
        )

    def start(self, r):
        for k in (2, 3, 1):
            self.copy(r, k).start()
        self.dst[self.s, r] = self.src[self.s, r]

    def wait(self, r):
        for k in (2, 3, 1):
            self.copy(r, k).wait_recv()

    def finish(self, r):
        for k in (2, 3, 1):
            self.copy(r, k).wait_send()


def step(op):
    try:
        next(op)
    except StopIteration:
        pass


def drain(op):
    for _ in op:
        pass


def attend(n, tokens, attn_own, up_own, down_own, vec_own, pool_own, lengths):
    rows, span, width = tokens.shape
    quarter = width // SEQ
    span_all = span * SEQ
    aligned = attn_own.ndim == 3
    own_rows = width // n
    shape = jax.ShapeDtypeStruct
    low_shape = shape((own_rows, width), BF16)
    outs = [
        shape((rows, span, width), F32),
        shape((rows, span, width), F32),
        shape((rows, span, 1), F32),
        shape((width, width), BF16),
        shape((8, width), F32),
        shape((rows, width), F32),
        shape((rows, SEQ, span, width), BF16),
        shape((rows, span_all, 3 * quarter), BF16),
        shape((rows, HEADS, span_all, span_all), F32),
        shape((rows, span, width), BF16),
    ]
    vec_op, pool_op = GatherBatch(n, vec_own), GatherSeq(n, pool_own)
    out_op = GatherSeq(n, shape((width, quarter), BF16))
    weight_ops = [GatherBatch(n, low_shape)] * 3 if aligned else []
    outs += [op.outs[0] for op in weight_ops]
    scratch = (
        [pltpu.VMEM(vec_op.outs[0].shape, F32)]
        + vec_op.scratch
        + [pltpu.VMEM(pool_op.outs[0].shape, F32)]
        + pool_op.scratch
        + [pltpu.VMEM((width, quarter), BF16), pltpu.VMEM((SEQ, width, quarter), BF16)]
        + out_op.scratch
        + RowGather.scratch()
        + RowSwap.scratch((SEQ, rows, span, quarter))
        + [c for op in weight_ops for c in op.scratch]
        + [pltpu.VMEM(low_shape.shape, BF16)] * len(weight_ops)
    )

    def kernel(tokens, attn_own, up_own, down_own, vec_own, pool_own, lengths, *rest):
        (
            normed, scaled_one, spread_one, w_out, vec, pool_whole, x_all, qkv, prob, context,
        ) = rest[:10]
        rest = rest[10:]
        if aligned:
            w_attn, w_up, w_down = rest[:3]
            rest = rest[3:]
        greet_signal(n, {"seq", "batch"})
        s = lax.axis_index("seq")
        if aligned:
            attn_low, up_low, down_low = rest[36:39]
            for k in range(SEQ):

                @pl.when(s == k)
                def _(k=k):
                    part = [attn_own[j, :, k * quarter : (k + 1) * quarter] for j in range(4)]
                    attn_low[...] = jnp.concatenate(part, axis=1).astype(BF16)

        for r in range(rows):
            x_all[r, s] = tokens[r].astype(BF16)
        greet_wait(n, {"seq", "batch"})
        x_gather = RowGather(x_all, *rest[15:17])
        swap = RowSwap(*rest[17:21])
        context_out, context_in = rest[17:19]
        for r in range(rows):
            x_gather.start(r)
        vec_parts, pool_parts = rest[0], rest[6]
        out_own, out_parts = rest[10:12]
        if aligned:
            attn_move = weight_ops[0].run(attn_low, w_attn, *rest[21:26])
            up_move = weight_ops[1].run(up_low, w_up, *rest[26:31])
            down_move = weight_ops[2].run(down_low, w_down, *rest[31:36])
            step(attn_move)
        vec_move = vec_op.run(vec_own, vec_parts, *rest[1:6])
        pool_move = pool_op.run(pool_own, pool_parts, *rest[7:10])
        step(vec_move)
        step(pool_move)
        if aligned:
            for k in range(SEQ):

                @pl.when(s == k)
                def _(k=k):
                    up_low[...] = take_up(up_own[...].astype(BF16), n, k)
                    down_low[...] = down_own[k * own_rows : (k + 1) * own_rows].astype(BF16)

            step(attn_move)
        x_gather.pass_far(0)
        if aligned:
            step(attn_move)
        step(vec_move)
        x_gather.pass_far(1)
        step(pool_move)
        if aligned:
            drain(attn_move)
            step(up_move)
            weights = w_attn[...].reshape(width, width)
        else:
            weights = attn_own[...]
        drain(vec_move)
        drain(pool_move)
        if aligned:
            whole = jnp.concatenate([vec_parts[k] for k in range(n)], axis=1)

            def here(make):
                return sum(jnp.where(s == k, make(k), 0.0) for k in range(SEQ))

            vec[0:6] = whole[2:8]
            hid = width // n
            vec[6:7] = here(
                lambda k: jnp.concatenate(
                    [
                        whole[8 + f // width : 9 + f // width, f % width : f % width + hid]
                        for f in ((b * SEQ + k) * hid for b in range(n))
                    ],
                    axis=1,
                )
            )
            blank = jnp.zeros((1, quarter), F32)
            vec[7:8] = here(
                lambda k: jnp.concatenate(
                    [
                        whole[0:1, k * quarter : (k + 1) * quarter],
                        blank,
                        whole[1:2, k * quarter : (k + 1) * quarter],
                        blank,
                    ],
                    axis=1,
                )
            )
        else:
            total = vec_parts[0]
            for k in range(1, n):
                total = total + vec_parts[k]
            vec[...] = total
        pool_whole[...] = jnp.concatenate([pool_parts[k] for k in range(SEQ)], axis=1)
        out_own[...] = weights[:, 3 * quarter :]
        out_move = out_op.run(out_own, out_parts, *rest[12:15])
        step(out_move)
        w_qkv = weights[:, : 3 * quarter]
        bias = vec[7:8, : 3 * quarter]

        pending = [up_move, up_move, up_move, up_move, down_move, down_move, down_move] if aligned else []
        column = lax.broadcasted_iota(jnp.int32, (1, span_all), 1)
        for r in range(rows):
            x_gather.wait_near(r)
            x_gather.wait_diag(r)
            block = matmul(x_all[r].reshape(span_all, width), w_qkv) + bias
            qkv[r] = block.astype(BF16)
            valid = column < lengths[r]
            mixed = []
            for h in range(HEADS):
                query, key, value = [
                    qkv[r, :, k * quarter + h * HD : k * quarter + (h + 1) * HD] for k in range(3)
                ]
                scores = contract_last(query * jnp.bfloat16(HD**-0.5), key)
                scores = jnp.where(valid, scores, -1e30)
                exponent = jnp.exp(scores - jnp.max(scores, axis=-1, keepdims=True))
                weight = exponent * (1.0 / jnp.sum(exponent, axis=-1, keepdims=True))
                prob[r, h] = weight
                mixed.append(matmul(weight.astype(BF16), value))
                if pending:
                    step(pending.pop(0))
            if r == 0:
                step(out_move)
            mixed = jnp.concatenate(mixed, axis=1).astype(BF16)
            for k in range(SEQ):
                context_out[k, r] = mixed[k * span : (k + 1) * span]
            swap.start(r)
        drain(out_move)
        w_out[...] = jnp.concatenate([out_parts[k] for k in range(SEQ)], axis=1)
        while pending:
            step(pending.pop(0))
        for r in range(rows):
            swap.wait(r)
            context[r] = jnp.concatenate([context_in[k, r] for k in range(SEQ)], axis=1)
        branch = matmul(context[...].reshape(rows * span, width), w_out[...]) + vec[0:1]
        for r in range(rows):
            hidden = tokens[r] + branch[r * span : (r + 1) * span]
            centred = hidden - jnp.mean(hidden, axis=-1, keepdims=True)
            spread = lax.rsqrt(jnp.mean(centred * centred, axis=-1, keepdims=True) + norm_eps)
            scaled = centred * spread
            scaled_one[r] = scaled
            spread_one[r] = spread
            normed[r] = scaled * vec[1:2] + vec[2:3]
        for r in range(rows):
            x_gather.finish(r)
            swap.finish(r)
        if aligned:
            drain(up_move)
            drain(down_move)

    vmem = pl.BlockSpec(memory_space=pltpu.VMEM)
    return pl.pallas_call(
        kernel,
        out_shape=outs,
        in_specs=[vmem] * 6 + [pl.BlockSpec(memory_space=pltpu.SMEM)],
        out_specs=[vmem] * len(outs),
        scratch_shapes=scratch,
        compiler_params=pltpu.CompilerParams(
            collective_id=0, has_side_effects=True, vmem_limit_bytes=60 * 2**20
        ),
        name="attend",
    )(tokens, attn_own, up_own, down_own, vec_own, pool_own, lengths)


def attend_back(n, first_grad, w_out, context, qkv, prob, x_all, w_attn, grad_up):
    rows, span, width = first_grad.shape
    quarter = width // SEQ
    span_all = span * SEQ
    own_rows = width // n
    aligned = own_rows % 16 == 0
    scale = HD**-0.5
    shape = jax.ShapeDtypeStruct
    outs = [shape((rows, span, width), F32), shape((1, 3 * quarter), F32)]
    if aligned:
        locals_ = [shape((n, own_rows, c), F32) for c in (3 * quarter, quarter)]
        batch_ops = [ScatterBatch(n, a) for a in [grad_up] + locals_]
        outs += [op.outs[0] for op in batch_ops]
    else:
        locals_, batch_ops = [], []
        outs += [shape((width, 3 * quarter), F32), shape((width, quarter), F32)]
    scratch = (
        RowSwap.scratch((SEQ, rows, span, quarter))
        + [pltpu.VMEM((1, SEQ, width, quarter), F32)]
        + RowScatter.scratch(1, (width, quarter))
        + [pltpu.VMEM((rows, SEQ, span, width), F32)]
        + RowScatter.scratch(rows, (span, width))
        + [pltpu.VMEM((rows, span_all, 3 * quarter), BF16)]
        + [pltpu.VMEM(a.shape, F32) for a in locals_]
        + [c for op in batch_ops for c in op.scratch]
    )

    def kernel(first_grad, w_out, context, qkv, prob, x_all, w_attn, grad_up, *rest):
        input_grad, bias_sums = rest[:2]
        results = rest[2 : 5 if aligned else 4]
        rest = rest[5 if aligned else 4 :]
        greet(n, {"seq", "batch"} if aligned else {"seq"})
        swap = RowSwap(*rest[0:4])
        grad_context, arrived = rest[0:2]
        out_part = rest[4]
        out_sum = RowScatter(out_part, *rest[5:11])
        x_part = rest[11]
        x_sum = RowScatter(x_part, *rest[12:18])
        grad_qkv = rest[18]
        rest = rest[19:]
        if aligned:
            local_qkv, local_out = rest[:2]
            up_move = batch_ops[0].run(grad_up, results[0], *rest[2:10])
            qkv_move = batch_ops[1].run(local_qkv, results[1], *rest[10:18])
            out_move = batch_ops[2].run(local_out, results[2], *rest[18:26])
        low = first_grad[...].astype(BF16).reshape(rows * span, width)
        rise = contract_last(low, w_out[...]).astype(BF16)
        for r in range(rows):
            for k in range(SEQ):
                grad_context[k, r] = rise[
                    r * span : (r + 1) * span, k * quarter : (k + 1) * quarter
                ]
            swap.start(r)
        if aligned:
            step(up_move)
        whole = contract_first(context[...].reshape(rows * span, width), low)
        for k in range(SEQ):
            out_part[0, k] = whole[:, k * quarter : (k + 1) * quarter]
        out_sum.send_diag(0)
        out_sum.send_near(0)
        w_qkv = w_attn[:, : 3 * quarter]
        sums = jnp.zeros((1, 3 * quarter), F32)
        for r in range(rows):
            swap.wait(r)
            upstream = [arrived[k, r] for k in range(SEQ)]
            upstream = jnp.concatenate(upstream, axis=0)
            query_grads, key_grads, value_grads = [], [], []
            for h in range(HEADS):
                query, key, value = [
                    qkv[r, :, k * quarter + h * HD : k * quarter + (h + 1) * HD] for k in range(3)
                ]
                above = upstream[:, h * HD : (h + 1) * HD]
                weight = prob[r, h]
                prob_grad = contract_last(above, value)
                delta = jnp.sum(weight * prob_grad, axis=-1, keepdims=True)
                score_grad = (weight * (prob_grad - delta)).astype(BF16)
                query_grads.append(matmul(score_grad, key) * scale)
                key_grads.append(contract_first(query, score_grad) * scale)
                value_grads.append(contract_first(above, weight.astype(BF16)))
                if aligned:
                    step(up_move)
            across = jnp.concatenate(key_grads + value_grads, axis=0).T
            block = jnp.concatenate(query_grads + [across], axis=1).astype(BF16)
            grad_qkv[r] = block
            sums += row_sum(block.astype(F32))
            x_part[r] = contract_last(block, w_qkv).reshape(SEQ, span, width)
            x_sum.send_diag(r)
            x_sum.send_near(r)
            if r == 0:
                out_sum.cross(0)
            x_sum.cross(r)
        bias_sums[...] = sums
        whole = contract_first(
            x_all[...].reshape(rows * span_all, width),
            grad_qkv[...].reshape(rows * span_all, 3 * quarter),
        )
        if aligned:
            local_qkv[...] = whole.reshape(local_qkv.shape)
            step(qkv_move)
            local_out[...] = out_sum.total(0).reshape(local_out.shape)
            step(out_move)
            drain(up_move)
        else:
            results[0][...] = whole
            results[1][...] = out_sum.total(0)
        for r in range(rows):
            input_grad[r] = x_sum.total(r) + first_grad[r]
        out_sum.finish(0)
        for r in range(rows):
            swap.finish(r)
            x_sum.finish(r)
        if aligned:
            drain(qkv_move)
            drain(out_move)

    vmem = pl.BlockSpec(memory_space=pltpu.VMEM)
    return pl.pallas_call(
        kernel,
        out_shape=outs,
        in_specs=[vmem] * 8,
        out_specs=[vmem] * len(outs),
        scratch_shapes=scratch,
        compiler_params=pltpu.CompilerParams(
            collective_id=4, has_side_effects=True, vmem_limit_bytes=60 * 2**20
        ),
        name="attend_back",
    )(first_grad, w_out, context, qkv, prob, x_all, w_attn, grad_up)


def join_up_parts(parts, n):
    hid_own = parts[0].shape[1] // n
    return jnp.concatenate(
        [parts[k][:, b * hid_own : (b + 1) * hid_own] for b in range(n) for k in range(SEQ)], axis=1
    )


def take_up(matrix, n, k):
    hid_own = matrix.shape[1] // n // SEQ
    return jnp.concatenate(
        [
            matrix[:, (b * SEQ + k) * hid_own : (b * SEQ + k + 1) * hid_own]
            for b in range(n)
        ],
        axis=1,
    )


def muon(
    n, qkv_piece, out_piece, up_piece, down_piece, bias_sums, vec_grad, attn_moment, up_moment, down_moment
):
    rows, width = up_piece.shape
    quarter = width // SEQ
    hid_own = rows
    n_vec = 8 + SEQ
    shape = jax.ShapeDtypeStruct
    attn_op = GatherSeq(n, shape((4, rows, quarter), BF16))
    wide_op = GatherSeq(n, shape((2, rows, width), BF16))
    vec_sum = ScatterBatch(n, shape((n, n_vec, rows), F32), F32)
    vec_op = GatherSeq(n, shape((n_vec, rows), F32))
    main = Muon(n, shape((4, rows, quarter), BF16), shape((2, rows, width), BF16))
    outs = [attn_op.outs[0], wide_op.outs[0], shape((n_vec, rows), F32)] + main.outs
    groups = [
        [
            pltpu.VMEM((4, rows, quarter), BF16),
            pltpu.VMEM((2, rows, width), BF16),
            pltpu.VMEM((4, rows, quarter), BF16),
            pltpu.VMEM((2, rows, width), BF16),
            pltpu.VMEM((n, n_vec, rows), F32),
            pltpu.VMEM((n_vec, rows), F32),
            pltpu.VMEM((SEQ, n_vec, rows), F32),
        ]
    ] + [op.scratch for op in (attn_op, wide_op, vec_sum, vec_op, main)]

    def kernel(
        qkv_piece, out_piece, up_piece, down_piece, bias_sums, vec_grad,
        attn_moment, up_moment, down_moment,
        attn_all, wide_all, vec_total, attn_orth, wide_orth, *rest,
    ):
        greet_signal(n, {"all"})
        parts, i = [], 0
        for group in groups:
            parts.append(rest[i : i + len(group)])
            i += len(group)
        attn_bf, wide_bf, attn_send, wide_send, vec_local, vec_piece, vec_parts = parts[0]
        s = lax.axis_index("seq")
        for j in range(3):
            attn_bf[j] = qkv_piece[:, j * quarter : (j + 1) * quarter].astype(BF16)
        attn_bf[3] = out_piece[...].astype(BF16)
        wide_bf[0] = up_piece[...].astype(BF16)
        wide_bf[1] = down_piece[...].astype(BF16)
        for k in range(SEQ):

            @pl.when(s == k)
            def _(k=k):
                for j in range(4):
                    old = attn_moment[j, :, k * quarter : (k + 1) * quarter]
                    attn_send[j] = (matrix_decay * old + attn_bf[j].astype(F32)).astype(BF16)
                old = take_up(up_moment[...], n, k)
                wide_send[0] = (matrix_decay * old + wide_bf[0].astype(F32)).astype(BF16)
                old = down_moment[k * hid_own : (k + 1) * hid_own]
                wide_send[1] = (matrix_decay * old + wide_bf[1].astype(F32)).astype(BF16)

        greet_wait(n, {"all"})

        def vectors():
            def here(k, value):
                return jnp.where(s == k, value, 0.0)

            lines = [
                jnp.concatenate(
                    [here(k, bias_sums[:, j * quarter : (j + 1) * quarter]) for k in range(SEQ)], axis=1
                )
                for j in (0, 2)
            ]
            lines += [vec_grad[j : j + 1] for j in range(6)]
            hidden = vec_grad[6:7]
            pieces = [
                here(k, hidden[:, b * hid_own : (b + 1) * hid_own]) for b in range(n) for k in range(SEQ)
            ]
            each = n * SEQ // 4
            lines += [jnp.concatenate(pieces[j * each : (j + 1) * each], axis=1) for j in range(4)]
            whole = jnp.concatenate(lines, axis=0)
            for b in range(n):
                vec_local[b] = whole[:, b * rows : (b + 1) * rows]
            yield from vec_sum.run(vec_local, vec_piece, *parts[3])
            yield from vec_op.run(vec_piece, vec_parts, *parts[4])
            vec_total[...] = (vec_parts[0] + vec_parts[1]) + (vec_parts[2] + vec_parts[3])

        run_together(
            main.run(attn_send, wide_send, attn_orth, wide_orth, *parts[5]),
            attn_op.run(attn_bf, attn_all, *parts[1]),
            wide_op.run(wide_bf, wide_all, *parts[2]),
            vectors(),
        )

    vmem = pl.BlockSpec(memory_space=pltpu.VMEM)
    ins = (
        qkv_piece, out_piece, up_piece, down_piece, bias_sums, vec_grad, attn_moment, up_moment, down_moment
    )
    return pl.pallas_call(
        kernel,
        out_shape=outs,
        in_specs=[vmem] * len(ins),
        out_specs=[vmem] * len(outs),
        scratch_shapes=[c for group in groups for c in group],
        compiler_params=pltpu.CompilerParams(
            collective_id=8, has_side_effects=True, vmem_limit_bytes=62 * 2**20
        ),
        name="muon",
    )(*ins)


def finish(
    n, attn_all, wide_all, attn_orth, wide_orth, vec_total,
    attn_weight, up_weight, down_weight, vectors, attn_moment, up_moment, down_moment, vector_moment,
    factors, vector_step,
):
    rows = wide_all.shape[2]

    def kernel(
        attn_all, wide_all, attn_orth, wide_orth, vec_total,
        attn_weight, up_weight, down_weight, vectors, attn_moment, up_moment, down_moment, vector_moment,
        attn_grad, up_grad, down_grad, vec_grad, attn_next, up_next, down_next, vec_next,
        attn_new, up_new, down_new, vec_new,
    ):
        for j in range(4):
            grad = jnp.concatenate([attn_all[k, j] for k in range(SEQ)], axis=1).astype(F32)
            attn_grad[j] = grad
            attn_next[j] = matrix_decay * attn_moment[j] + grad
            orth = jnp.concatenate([attn_orth[k, j] for k in range(SEQ)], axis=1).astype(F32)
            attn_new[j] = attn_weight[j] - factors[0] * orth
        grad = join_up_parts([wide_all[k, 0] for k in range(SEQ)], n).astype(F32)
        up_grad[...] = grad
        up_next[...] = matrix_decay * up_moment[...] + grad
        orth = join_up_parts([wide_orth[k, 0] for k in range(SEQ)], n).astype(F32)
        up_new[...] = up_weight[...] - factors[1] * orth
        for k in range(SEQ):
            part = pl.ds(k * rows, rows)
            grad = wide_all[k, 1].astype(F32)
            down_grad[part] = grad
            down_next[part] = matrix_decay * down_moment[part] + grad
            down_new[part] = down_weight[part] - factors[2] * wide_orth[k, 1].astype(F32)
        vec_grad[...] = vec_total[...]
        moved = vector_decay * vector_moment[...] + vec_total[...]
        vec_next[...] = moved
        vec_new[...] = vectors[...] - vector_step * moved

    vmem = pl.BlockSpec(memory_space=pltpu.VMEM)
    ins = (
        attn_all, wide_all, attn_orth, wide_orth, vec_total,
        attn_weight, up_weight, down_weight, vectors, attn_moment, up_moment, down_moment, vector_moment,
    )
    outs = [jax.ShapeDtypeStruct(a.shape, F32) for a in (attn_weight, up_weight, down_weight, vectors)] * 3
    return pl.pallas_call(
        kernel,
        out_shape=outs,
        in_specs=[vmem] * len(ins),
        out_specs=[vmem] * len(outs),
        compiler_params=pltpu.CompilerParams(vmem_limit_bytes=60 * 2**20),
        name="finish",
    )(*ins)


def step_factor(rows_all, cols_all):
    return matrix_rate * math.sqrt(max(1.0, rows_all / cols_all))


def make_body(n):
    def body(
        layer_input,
        lengths,
        attn_weight,
        up_weight,
        down_weight,
        vectors,
        attn_moment,
        up_moment,
        down_moment,
        vector_moment,
        out_grad,
        pool_grad,
    ):
        rows, span, width = layer_input.shape
        own_rows = width // n
        quarter = width // SEQ
        hidden = up_weight.shape[1]
        hid_q = hidden // SEQ
        hid_own = hidden // n // SEQ
        seq_index = lax.axis_index("seq")

        def attn_quarter(stacked):
            part = lax.dynamic_index_in_dim(
                stacked.reshape(4, own_rows, SEQ, quarter), seq_index, 2, False
            )
            return part

        def up_quarter(matrix):
            return lax.dynamic_index_in_dim(
                matrix.reshape(own_rows, n, SEQ, hid_own), seq_index, 2, False
            ).reshape(own_rows, hid_q)

        def down_quarter(matrix):
            return lax.dynamic_index_in_dim(
                matrix.reshape(SEQ, hid_own, width), seq_index, 0, False
            )

        aligned = own_rows % 16 == 0
        if aligned:
            own = [attn_weight, up_weight, down_weight]
            vec_own = vectors.astype(BF16).astype(F32)
        else:
            attn_low = attn_quarter(attn_weight).astype(BF16).transpose(1, 0, 2).reshape(own_rows, width)
            up_low = up_quarter(up_weight).astype(BF16)
            down_low = down_quarter(down_weight).astype(BF16)
            vec_low = vectors.astype(BF16).astype(F32)
            placed = lax.dynamic_update_slice(
                jnp.zeros((vectors.shape[0], n, own_rows), F32),
                vec_low[:, None],
                (0, lax.axis_index("batch"), 0),
            ).reshape(-1, width)
            bias_up = lax.dynamic_index_in_dim(
                placed[8:].reshape(n, SEQ, hid_own), seq_index, 1, False
            ).reshape(1, hid_q)
            bias_qv = lax.dynamic_index_in_dim(
                placed[:2].reshape(2, SEQ, quarter), seq_index, 1, False
            )
            blank = jnp.zeros((quarter,), F32)
            bias_qkv = jnp.concatenate([bias_qv[0], blank, bias_qv[1], blank])[None]
            vec_own = jnp.concatenate([placed[2:8], bias_up, bias_qkv])
            own = exchange(
                n, 1, "gather_weights", *[GatherBatch(n, a) for a in (attn_low, up_low, down_low)]
            )
            own = [a.reshape(width, width) for a in own]
        (
            normed_one, scaled_one, spread_one, w_out, vec_rows, pool_whole, x_all, qkv, prob, context,
            *weights,
        ) = attend(n, layer_input, *own, vec_own, pool_grad, lengths)
        w_attn, w_up, w_down = [a.reshape(width, width) for a in (weights if aligned else own)]
        out_rows, pool_sum, first_grad, vec_grad, grad_up, down_piece = hidden_layer(
            n, normed_one, scaled_one, spread_one, w_up, w_down, vec_rows, out_grad, pool_whole, lengths
        )
        pooled = lax.dynamic_slice_in_dim(pool_sum, seq_index * quarter, quarter, 1)
        back = attend_back(
            n, first_grad, w_out, context, qkv, prob, x_all, w_attn,
            grad_up.reshape(n, own_rows, hid_q) if aligned else grad_up,
        )
        input_grad, bias_sums = back[:2]
        if aligned:
            up_piece, qkv_piece, out_piece = back[2:]
        else:
            down_piece, up_piece, qkv_piece, out_piece = exchange(
                n,
                2,
                "sum_grads",
                *[
                    ScatterBatch(n, a.reshape(n, own_rows, -1))
                    for a in (down_piece, grad_up, back[2], back[3])
                ],
            )
        factors = [
            step_factor(width, width),
            step_factor(width, hidden),
            step_factor(hidden, width),
        ]
        vector_step = vector_rate / math.sqrt(rows * n)
        if aligned:
            attn_all, wide_all, vec_total, attn_orth, wide_orth = muon(
                n, qkv_piece, out_piece, up_piece, down_piece, bias_sums, vec_grad,
                attn_moment, up_moment, down_moment,
            )
            return (out_rows, pooled, input_grad) + tuple(
                finish(
                    n, attn_all, wide_all, attn_orth, wide_orth, vec_total,
                    attn_weight, up_weight, down_weight, vectors,
                    attn_moment, up_moment, down_moment, vector_moment, factors, vector_step,
                )
            )
        attn_piece = jnp.concatenate([qkv_piece, out_piece], axis=1)
        bias_sums = bias_sums.reshape(3, quarter)

        vec_head = jnp.zeros((2, SEQ, quarter), F32)
        vec_head = lax.dynamic_update_slice(
            vec_head, bias_sums[jnp.array([0, 2])][:, None], (0, seq_index, 0)
        ).reshape(2, width)
        vec_mid = vec_grad[:6]
        grad_bias_up = vec_grad[6]
        vec_tail = lax.dynamic_update_slice(
            jnp.zeros((n, SEQ, hid_own), F32),
            grad_bias_up.reshape(n, 1, hid_own),
            (0, seq_index, 0),
        ).reshape(-1, width)
        vec_local = jnp.concatenate([vec_head, vec_mid, vec_tail])
        vec_local = vec_local.reshape(-1, n, own_rows).transpose(1, 0, 2)
        (vec_piece,) = exchange(n, 7, "sum_vectors", ScatterBatch(n, vec_local, F32))
        attn_bf = attn_piece.astype(BF16).reshape(own_rows, 4, quarter).transpose(1, 0, 2)
        wide_bf = jnp.stack([up_piece, down_piece]).astype(BF16)
        attn_send = (matrix_decay * attn_quarter(attn_moment) + attn_bf.astype(F32)).astype(BF16)
        wide_moment = jnp.stack([up_quarter(up_moment), down_quarter(down_moment)])
        wide_send = (matrix_decay * wide_moment + wide_bf.astype(F32)).astype(BF16)
        short = -own_rows % 16
        attn_send = jnp.pad(attn_send, ((0, 0), (0, short), (0, 0)))
        wide_send = jnp.pad(wide_send, ((0, 0), (0, short), (0, 0)))
        attn_all, wide_all, vec_parts, attn_orth, wide_orth = exchange(
            n,
            8,
            "muon",
            GatherSeq(n, attn_bf),
            GatherSeq(n, wide_bf),
            GatherSeq(n, vec_piece),
            Muon(n, attn_send, wide_send),
        )
        attn_orth = attn_orth[:, :, :own_rows]
        wide_orth = wide_orth[:, :, :own_rows]

        def join_attn(parts):
            return parts.astype(F32).transpose(1, 2, 0, 3).reshape(4, own_rows, width)

        def join_up(parts):
            return (
                parts.astype(F32)
                .reshape(SEQ, own_rows, n, hid_own)
                .transpose(1, 2, 0, 3)
                .reshape(own_rows, hidden)
            )

        def join_down(parts):
            return parts.astype(F32).reshape(SEQ * hid_own, width)

        attn_grad = join_attn(attn_all)
        up_grad, down_grad = join_up(wide_all[:, 0]), join_down(wide_all[:, 1])
        vector_grad = (vec_parts[0] + vec_parts[1]) + (vec_parts[2] + vec_parts[3])
        attn_next = matrix_decay * attn_moment + attn_grad
        up_next = matrix_decay * up_moment + up_grad
        down_next = matrix_decay * down_moment + down_grad

        attn_new = attn_weight - factors[0] * join_attn(attn_orth)
        up_new = up_weight - factors[1] * join_up(wide_orth[:, 0])
        down_new = down_weight - factors[2] * join_down(wide_orth[:, 1])
        vector_next = vector_decay * vector_moment + vector_grad
        vectors_new = vectors - vector_step * vector_next
        return (
            out_rows,
            pooled,
            input_grad,
            attn_grad,
            up_grad,
            down_grad,
            vector_grad,
            attn_next,
            up_next,
            down_next,
            vector_next,
            attn_new,
            up_new,
            down_new,
            vectors_new,
        )

    return body


def solution(mesh):
    placed = (
        P("batch", "seq", None),
        P("batch"),
        P(None, "batch", None),
        P("batch", None),
        P("batch", None),
        P(None, "batch"),
        P(None, "batch", None),
        P("batch", None),
        P("batch", None),
        P(None, "batch"),
        P("batch", "seq", None),
        P("batch", "seq"),
    )
    return jax.shard_map(
        make_body(mesh.shape["batch"]),
        mesh=mesh,
        in_specs=placed,
        out_specs=(
            P("batch", "seq", None),
            P("batch", "seq"),
            P("batch", "seq", None),
            P(None, "batch", None),
            P("batch", None),
            P("batch", None),
            P(None, "batch"),
            P(None, "batch", None),
            P("batch", None),
            P("batch", None),
            P(None, "batch"),
            P(None, "batch", None),
            P("batch", None),
            P("batch", None),
            P(None, "batch"),
        ),
        check_vma=False,
    )
```

```python
import math
import types

import jax
import jax.numpy as jnp
from jax import lax
from jax.experimental import pallas as pl
from jax.experimental.pallas import tpu as pltpu
from jax.sharding import PartitionSpec as P

H = 12
HD = 64
NS = 5
SEQ = 4
HEADS = H // SEQ

norm_eps = 1e-12
tiny_norm = 1e-07
matrix_decay = 0.95
vector_decay = 0.5
matrix_rate = 0.5
vector_rate = 0.03

MESH = pl.DeviceIdType.MESH
F32 = jnp.float32
BF16 = jnp.bfloat16


def coords(n):
    b = lax.axis_index("batch")
    s = lax.axis_index("seq")
    return b, s, b // 2, b % 2, n // 2


def remote(src, dst, send, recv, device):
    return pltpu.make_async_remote_copy(
        src_ref=src, dst_ref=dst, send_sem=send, recv_sem=recv, device_id=device, device_id_type=MESH
    )


class GatherBatch:
    peers = ("batch",)

    def __init__(self, n, src, eager=True):
        self.n = n
        self.eager = eager
        self.ins = [src]
        self.outs = [jax.ShapeDtypeStruct((n,) + src.shape, src.dtype)]
        m = n // 2
        self.scratch = [pltpu.SemaphoreType.DMA((m,))] * 4 + [pltpu.SemaphoreType.DMA]

    def run(self, src, dst, zs, zr, ys, yr, own):
        b, s, hi, lo, m = coords(self.n)
        local = pltpu.make_async_copy(src, dst.at[b], own)
        local.start()
        pair = (hi * 2 + 1 - lo, s)
        out = []
        for d in range(1, m):
            c = remote(src, dst.at[b], zs.at[d], zr.at[d], (((hi + d) % m) * 2 + lo, s))
            c.start()
            out.append(c)
        first = remote(src, dst.at[b], ys.at[0], yr.at[0], pair)
        if self.eager:
            first.start()
        yield
        passed = [first]
        for d in range(1, m):
            if d == 1 and not self.eager:
                first.start()
            out[d - 1].wait_recv()
            block = ((hi + m - d) % m) * 2 + lo
            c = remote(dst.at[block], dst.at[block], ys.at[d], yr.at[d], pair)
            c.start()
            passed.append(c)
            yield
        local.wait()
        for c in passed:
            c.wait()
        for c in out:
            c.wait_send()


class GatherDirect:
    peers = ("all",)

    def __init__(self, n, src):
        self.n = n
        self.ins = [src]
        self.outs = [jax.ShapeDtypeStruct((n,) + src.shape, src.dtype)]
        self.scratch = [pltpu.SemaphoreType.DMA((n,))] * 2 + [pltpu.SemaphoreType.DMA]

    def run(self, src, dst, ss, rs, own):
        n = self.n
        b, s = lax.axis_index("batch"), lax.axis_index("seq")
        local = pltpu.make_async_copy(src, dst.at[b], own)
        local.start()
        copies = [
            remote(src, dst.at[b], ss.at[k], rs.at[k], ((b + k) % n, s)) for k in range(1, n)
        ]
        for c in copies:
            c.start()
        yield
        local.wait()
        for c in copies:
            c.wait()


class ScatterBatch:
    peers = ("batch",)

    def __init__(self, n, src, wire=BF16):
        self.n = n
        self.wire = wire
        self.ins = [src]
        shape = src.shape[1:]
        self.outs = [jax.ShapeDtypeStruct(shape, F32)]
        m = n // 2
        self.scratch = [pltpu.VMEM((m,) + shape, wire)] * 4 + [pltpu.SemaphoreType.DMA((m,))] * 4

    def run(self, src, dst, ysend, yrecv, zsend, zrecv, ys, yr, zs, zr):
        b, s, hi, lo, m = coords(self.n)
        pair = (hi * 2 + 1 - lo, s)
        first = {}
        order = list(range(1, m)) + [0]
        for d in order:
            h = (hi + d) % m
            ysend[d] = src[h * 2 + 1 - lo].astype(self.wire)
            first[d] = remote(ysend.at[d], yrecv.at[d], ys.at[d], yr.at[d], pair)
            first[d].start()
        yield
        second = []
        for d in range(1, m):
            h = (hi + d) % m
            first[d].wait_recv()
            zsend[d] = (src[h * 2 + lo] + yrecv[d].astype(F32)).astype(self.wire)
            c = remote(zsend.at[d], zrecv.at[d], zs.at[d], zr.at[d], (h * 2 + lo, s))
            c.start()
            second.append(c)
            yield
        first[0].wait_recv()
        total = src[b] + yrecv[0].astype(F32)
        for d in range(1, m):
            second[d - 1].wait_recv()
            total = total + zrecv[d].astype(F32)
        dst[...] = total
        for c in list(first.values()) + second:
            c.wait_send()


class GatherSeq:
    peers = ("seq",)

    def __init__(self, n, src):
        self.ins = [src]
        self.outs = [jax.ShapeDtypeStruct((SEQ,) + src.shape, src.dtype)]
        self.scratch = [pltpu.SemaphoreType.DMA((3,))] * 2 + [pltpu.SemaphoreType.DMA]

    def run(self, src, dst, ss, rs, own):
        b, s = lax.axis_index("batch"), lax.axis_index("seq")
        far, near = (s + 2) % 4, s + 1 - 2 * (s % 2)
        across = remote(src, dst.at[s], ss.at[0], rs.at[0], (b, far))
        across.start()
        local = pltpu.make_async_copy(src, dst.at[s], own)
        local.start()
        beside = remote(src, dst.at[s], ss.at[1], rs.at[1], (b, near))
        beside.start()
        yield
        across.wait_recv()
        passed = remote(dst.at[far], dst.at[far], ss.at[2], rs.at[2], (b, near))
        passed.start()
        yield
        local.wait()
        beside.wait()
        passed.wait()
        across.wait_send()


def owner_list(n):
    return [(0, 2), (1, 0), (n - 2, 2), (n - 1, 0), (n // 4, 0), (n // 2 + 1, 2)]


class OwnerMail:
    @staticmethod
    def scratch(n, count, relayed=None):
        dma = pltpu.SemaphoreType.DMA
        base = [dma((count,)), dma((SEQ * n,)), dma]
        if relayed is not None:
            base += [pltpu.VMEM((count,) + relayed, BF16), dma((count,)), dma((count,))]
        return base

    def __init__(self, n, places, inbox, ss, rs, own, relayed=None, relay_s=None, relay_r=None):
        self.n, self.places, self.inbox, self.ss, self.rs, self.own = n, places, inbox, ss, rs, own
        self.relayed, self.relay_s, self.relay_r = relayed, relay_s, relay_r
        self.b, self.s = lax.axis_index("batch"), lax.axis_index("seq")
        self.me = self.s * n + self.b
        self.mine = [(self.b == ob) & (self.s == os) for ob, os in places]

    def indirect(self, k):
        ob, os = self.places[k]
        other_plane = self.b // 2 != ob // 2
        corner = (self.b % 2 != ob % 2) & (self.s // 2 != os // 2)
        column = (self.b % 2 == ob % 2) & (self.s // 2 == os // 2)
        return other_plane & corner, other_plane & column

    def copy(self, k, src):
        ob, os = self.places[k]
        place = self.inbox.at[self.s, self.b]
        return remote(src, place, self.ss.at[k], self.rs.at[self.me], (ob, os))

    def aside(self, k, src):
        across = self.b + 1 - 2 * (self.b % 2)
        return remote(
            src, self.relayed.at[k], self.ss.at[k], self.relay_r.at[k], (across, (self.s + 2) % 4)
        )

    def pass_copy(self, k):
        block, seq = self.b + 1 - 2 * (self.b % 2), (self.s + 2) % 4
        place = self.inbox.at[seq, block]
        return remote(
            self.relayed.at[k], place, self.relay_s.at[k], self.rs.at[seq * self.n + block], self.places[k]
        )

    def send(self, k, src):
        direct = jnp.logical_not(self.mine[k])
        if self.relayed is not None:
            by_relay, _ = self.indirect(k)
            direct = direct & jnp.logical_not(by_relay)

            @pl.when(by_relay)
            def _():
                self.aside(k, src).start()

        @pl.when(direct)
        def _():
            self.copy(k, src).start()

        @pl.when(self.mine[k])
        def _():
            pltpu.make_async_copy(src, self.inbox.at[self.s, self.b], self.own).start()

    def relay(self, k):
        @pl.when(self.indirect(k)[1])
        def _():
            place = self.relayed.at[k]
            remote(place, place, self.relay_s.at[k], self.relay_r.at[k], (0, 0)).wait_recv()
            self.pass_copy(k).start()

    def collect(self):
        place = self.inbox.at[self.s, self.b]
        pltpu.make_async_copy(place, place, self.own).wait()

        @pl.loop(1, SEQ * self.n)
        def _(k):
            other = (self.me + k) % (SEQ * self.n)
            place = self.inbox.at[other // self.n, other % self.n]
            remote(place, place, self.ss.at[0], self.rs.at[other], (0, 0)).wait_recv()

    def finish(self, k, src):
        @pl.when(jnp.logical_not(self.mine[k]))
        def _():
            self.copy(k, src).wait_send()

        if self.relayed is not None:

            @pl.when(self.indirect(k)[1])
            def _():
                self.pass_copy(k).wait_send()


class Muon:
    peers = ("all",)

    def __init__(self, n, attn_piece, wide_piece=None, wide_in=None):
        self.n = n
        self.ready = wide_in is not None
        self.ins = [attn_piece, wide_in if self.ready else wide_piece]
        rows, quarter = attn_piece.shape[1:]
        width = self.ins[1].shape[-1]
        self.outs = [
            jax.ShapeDtypeStruct((SEQ, 4, rows, quarter), BF16),
            jax.ShapeDtypeStruct((SEQ, 2, rows, width), BF16),
        ]
        size = n * rows
        dma = pltpu.SemaphoreType.DMA
        self.scratch = [
            pltpu.VMEM((SEQ, n, rows, quarter), BF16),
            pltpu.VMEM((SEQ, n, rows, width), BF16),
            pltpu.VMEM((2, n // 2, rows, width), BF16),
            pltpu.VMEM((size, SEQ * size), F32),
            pltpu.VMEM((size, SEQ * size), BF16),
            pltpu.VMEM((size, size), F32),
            pltpu.VMEM((size, size), BF16),
            pltpu.VMEM((size, size), BF16),
            pltpu.VMEM((size, 1), F32),
            dma((SEQ * n,)),
            dma((6,)),
            dma((2, n // 2)),
            dma((2, n // 2)),
            dma((6, 3)),
            dma((6, 3)),
            dma,
        ]
        self.scratch += OwnerMail.scratch(n, 4)
        if not self.ready:
            self.scratch += OwnerMail.scratch(n, 2) + [pltpu.VMEM((SEQ, n, rows, width), BF16)]

    def run(
        self, attn, wide, attn_orth, wide_orth, attn_in, wide_out, relayed, x32, xlow, gram, gram_low, poly, diag,
        back_s, back_r, relay_s, relay_r, seq_s, seq_r, own, *mails,
    ):
        n = self.n
        b, s, hi, lo, m = coords(n)
        far, near = (s + 2) % 4, s + 1 - 2 * (s % 2)
        me = s * n + b
        size = x32.shape[0]
        width = wide.shape[-1]
        quarter = attn.shape[2]
        places = owner_list(n)
        attn_mail = OwnerMail(n, places[:4], attn_in, *mails[:3])
        wide_in = wide
        if not self.ready:
            wide_in = mails[6]
            wide_mail = OwnerMail(n, places[4:], wide_in, *mails[3:6])
        mine = [(b == ob) & (s == os) for ob, os in places]
        number = jnp.int32(0)
        for k in range(6):
            number = jnp.where(mine[k], jnp.int32(k), number)
        is_attn = mine[0] | mine[1] | mine[2] | mine[3]
        is_wide = mine[4] | mine[5]

        if not self.ready:
            for k in range(2):
                wide_mail.send(k, wide.at[k])
        def send_attn():
            for k in range(4):
                attn_mail.send(k, attn.at[k])

        if self.ready:
            self.send_attn = send_attn
        else:
            send_attn()

        if not self.ready:
            for _ in range(4):
                yield

        load = pltpu.make_async_copy(wide_in, wide_out, own)

        def result(k):
            return attn_orth.at[s, k] if k < 4 else wide_orth.at[s, k - 4]

        def others(act):
            @pl.loop(1, SEQ * n)
            def _(k):
                other = (me + k) % (SEQ * n)
                act(other, other % n, other // n)

        def give_attn():
            pltpu.make_async_copy(attn_in.at[s, b], attn_orth.at[s, number], own).start()

            def act(other, ob, os):
                remote(
                    attn_in.at[os, ob], attn_orth.at[os, number], back_s.at[other], back_r.at[number], (ob, os)
                ).start()

            others(act)

        def give_wide():
            index = number - 4
            pltpu.make_async_copy(wide_out.at[s, b], wide_orth.at[s, index], own).start()

            def act(other, ob, os):
                oh, ol = ob // 2, ob % 2
                up = hi < m // 2
                away = jnp.where(up, oh - hi, hi - oh)
                relay = (away > 0) & (os // 2 != s // 2)
                stop = jnp.where(ol == lo, os, (os + 2) % 4)
                src = wide_out.at[os, ob]

                @pl.when(relay)
                def _():
                    slot = jnp.maximum(away - 1, 0)
                    remote(
                        src, relayed.at[index, slot], back_s.at[other], relay_r.at[index, slot],
                        (hi * 2 + ol, stop),
                    ).start()

                @pl.when(jnp.logical_not(relay))
                def _():
                    remote(
                        src, wide_orth.at[os, index], back_s.at[other], back_r.at[number], (ob, os)
                    ).start()

            others(act)

        def squares(buf):
            total = jnp.zeros((1, 1), F32)
            for k in range(SEQ):
                block = buf[k].astype(F32).reshape(size, buf.shape[3])
                total = total + jnp.sum(block * block, keepdims=True)
            return 1.0 / (jnp.sqrt(total) + tiny_norm)

        def prepare():
            @pl.when(is_wide)
            def _():
                if not self.ready:
                    wide_mail.collect()
                load.start()
                load.wait()
                inverse = squares(wide_out)
                if width != size:
                    x32[...] = jnp.zeros(x32.shape, F32)

                @pl.when(mine[4])
                def _():
                    for k in range(SEQ):
                        block = wide_out[k].astype(F32).reshape(size, width)
                        x32[:, k * size : k * size + width] = block * inverse

                @pl.when(mine[5])
                def _():
                    for k in range(SEQ):
                        block = wide_out[k].astype(F32).reshape(size, width)
                        x32[:width, k * size : (k + 1) * size] = block.T * inverse

                for k in range(SEQ):
                    xlow[:, k * size : (k + 1) * size] = x32[:, k * size : (k + 1) * size].astype(BF16)

        def attn_turn():
            @pl.when(is_attn)
            def _():
                attn_mail.collect()
                inverse = squares(attn_in)
                span = SEQ * quarter
                whole = jnp.concatenate(
                    [attn_in[k].reshape(size, quarter) for k in range(SEQ)], axis=1
                )
                x32[:, :span] = whole.astype(F32) * inverse
                xlow[:, :span] = x32[:, :span].astype(BF16)
                square_x, square_low = x32.at[:, pl.ds(0, span)], xlow.at[:, pl.ds(0, span)]

                @pl.loop(0, NS)
                def _(turn):
                    schulz_poly(square_low, gram, gram_low, poly, diag)
                    schulz_move(square_x, square_low, poly, diag)

                for k in range(SEQ):
                    block = xlow[:, k * quarter : (k + 1) * quarter]
                    attn_in[k] = block.reshape(attn_in.shape[1:])
                give_attn()

        if not self.ready:
            prepare()
        else:
            self.prepare, self.attn_turn = prepare, attn_turn
            yield

        for _ in range(NS):

            @pl.when(is_wide)
            def _():
                schulz_poly(xlow, gram, gram_low, poly, diag)

            yield

            @pl.when(is_wide)
            def _():
                schulz_move(x32, xlow, poly, diag)

            yield

        @pl.when(is_wide)
        def _():
            @pl.when(mine[4])
            def _():
                for k in range(SEQ):
                    block = xlow[:, k * size : k * size + width]
                    wide_out[k] = block.reshape(wide_out.shape[1:])

            @pl.when(mine[5])
            def _():
                for k in range(SEQ):
                    block = x32[:width, k * size : (k + 1) * size].T.astype(BF16)
                    wide_out[k] = block.reshape(wide_out.shape[1:])

            give_wide()

        def routes(k):
            ob, os = places[k]
            oh, ol = ob // 2, ob % 2
            same_x = s // 2 == os // 2
            here = (hi == oh) & (((lo == ol) & jnp.logical_not(same_x)) | ((lo != ol) & same_x))
            target = jnp.where(lo == ol, s, far)
            ahead = range(oh + 1, m) if oh < m // 2 else range(oh - 1, -1, -1)
            return here, target, list(enumerate(ahead))

        def relay_copy(k, slot, block, target):
            return remote(
                relayed.at[k - 4, slot], wide_orth.at[target, k - 4], relay_s.at[k - 4, slot], back_r.at[k],
                (block * 2 + lo, target),
            )

        def onward(k, step, source, target):
            out = attn_orth.at[source, k] if k < 4 else wide_orth.at[source, k - 4]
            return remote(out, out, seq_s.at[k, step], seq_r.at[k, step], (b, target))

        if not self.ready:
            attn_turn()
        done = (0, 1, 2, 3, 4, 5)

        def returned(k):
            @pl.when(jnp.logical_not(mine[k]))
            def _():
                remote(result(k), result(k), seq_s.at[k, 0], back_r.at[k], (0, 0)).wait_recv()

            @pl.when(mine[k])
            def _():
                pltpu.make_async_copy(result(k), result(k), own).wait()

            onward(k, 0, s, far).start()
            onward(k, 1, s, near).start()

        def passed(k):
            onward(k, 0, far, far).wait_recv()
            onward(k, 2, far, near).start()

        for k in (4, 5):
            here, target, ahead = routes(k)

            @pl.when(here)
            def _(k=k, target=target, ahead=ahead):
                for slot, block in ahead:
                    place = relayed.at[k - 4, slot]
                    remote(place, place, relay_s.at[0, 0], relay_r.at[k - 4, slot], (0, 0)).wait_recv()
                    relay_copy(k, slot, block, target).start()

        for k in done[:4]:
            returned(k)
        for k in done[:4]:
            passed(k)
        for k in done[4:]:
            returned(k)
        for k in done[4:]:
            passed(k)
        for k in done:
            onward(k, 1, near, near).wait_recv()
            onward(k, 2, (near + 2) % 4, near).wait_recv()
            onward(k, 0, s, far).wait_send()
            onward(k, 1, s, near).wait_send()
            onward(k, 2, far, near).wait_send()
        for k in range(4):
            attn_mail.finish(k, attn.at[k])
        if not self.ready:
            for k in range(2):
                wide_mail.finish(k, wide.at[k])
        for k in (4, 5):
            here, target, ahead = routes(k)

            @pl.when(here)
            def _(k=k, target=target, ahead=ahead):
                for slot, block in ahead:
                    relay_copy(k, slot, block, target).wait_send()

        def given(buf):
            def act(other, ob, os):
                place = buf.at[os, ob]
                remote(place, place, back_s.at[other], back_r.at[0], (0, 0)).wait_send()

            others(act)

        @pl.when(is_attn)
        def _():
            given(attn_in)

        @pl.when(is_wide)
        def _():
            given(wide_out)


def schulz_poly(xlow, gram, gram_low, poly, diag):
    size = xlow.shape[0]
    side = 256
    tiles = [slice(k, k + side) for k in range(0, size, side)]
    eye = lax.broadcasted_iota(jnp.int32, (side, side), 0) == lax.broadcasted_iota(
        jnp.int32, (side, side), 1
    )
    gram[...] = contract_last(xlow[...], xlow[...])
    down, along = [], []
    for i in tiles:
        for j in tiles:
            if i != j:
                gram_low[i, j] = gram[i, j].astype(BF16)
        block = gram[i, i]
        on_diag = jnp.where(eye, block, 0.0)
        down.append(jnp.sum(on_diag, axis=1, keepdims=True))
        along.append(jnp.sum(on_diag, axis=0, keepdims=True))
        gram_low[i, i] = jnp.where(eye, 0.0, block).astype(BF16)
    square = matmul(gram_low[...], gram_low[...])
    for i, left in zip(tiles, down):
        for j, right in zip(tiles, along):
            factor = (2.0315 * left - 4.775) + 2.0315 * right
            block = 2.0315 * square[i, j] + factor * gram[i, j]
            if i == j:
                value = jnp.sum(jnp.where(eye, 2.0315 * square[i, j], 0.0), axis=1, keepdims=True)
                diag[i] = value + (3.4445 + (2.0315 * left - 4.775) * left)
                block = jnp.where(eye, 0.0, block)
            poly[i, j] = block.astype(BF16)


def schulz_move(x32, xlow, poly, diag):
    wide = x32.shape[1]
    chunk = 768 if wide % 768 == 0 else 512
    for c in range(0, wide, chunk):
        moved = diag[...] * x32[:, c : c + chunk] + matmul(poly[...], xlow[:, c : c + chunk])
        x32[:, c : c + chunk] = moved
        xlow[:, c : c + chunk] = moved.astype(BF16)


def greet_peers(n, kinds):
    b, s, hi, lo, m = coords(n)
    peers = []
    if "seq" in kinds:
        peers += [(b, (s + k) % 4) for k in (1, 2, 3)]
    if "batch" in kinds:
        peers += [(((hi + d) % m) * 2 + lo, s) for d in range(1, m)]
        peers += [(hi * 2 + 1 - lo, s)]
    return peers


def greet_signal(n, kinds):
    b, s = lax.axis_index("batch"), lax.axis_index("seq")
    barrier = pltpu.get_barrier_semaphore()
    if "all" in kinds:
        me = s * n + b

        @pl.loop(1, SEQ * n)
        def _(k):
            other = (me + k) % (SEQ * n)
            pl.semaphore_signal(
                barrier, inc=1, device_id=(other % n, other // n), device_id_type=MESH
            )

        return
    for peer in greet_peers(n, kinds):
        pl.semaphore_signal(barrier, inc=1, device_id=peer, device_id_type=MESH)


def greet_wait(n, kinds):
    count = SEQ * n - 1 if "all" in kinds else len(greet_peers(n, kinds))
    pl.semaphore_wait(pltpu.get_barrier_semaphore(), count)


def greet(n, kinds):
    greet_signal(n, kinds)
    greet_wait(n, kinds)


def run_together(*live):
    live = list(live)
    while live:
        still = []
        for op in live:
            try:
                next(op)
                still.append(op)
            except StopIteration:
                pass
        live = still


def exchange(n, collective_id, name, *ops):
    ins = [a for op in ops for a in op.ins]
    outs = [o for op in ops for o in op.outs]
    scratch = [c for op in ops for c in op.scratch]
    kinds = {k for op in ops for k in op.peers}

    def kernel(*refs):
        in_refs, out_refs = refs[: len(ins)], refs[len(ins) : len(ins) + len(outs)]
        scratch_refs = refs[len(ins) + len(outs) :]
        greet(n, kinds)
        live = []
        i = o = c = 0
        for op in ops:
            ni, no, nc = len(op.ins), len(op.outs), len(op.scratch)
            live.append(
                op.run(*in_refs[i : i + ni], *out_refs[o : o + no], *scratch_refs[c : c + nc])
            )
            i, o, c = i + ni, o + no, c + nc
        run_together(*live)

    vmem = pl.BlockSpec(memory_space=pltpu.VMEM)
    return pl.pallas_call(
        kernel,
        out_shape=outs,
        in_specs=[vmem] * len(ins),
        out_specs=[vmem] * len(outs),
        scratch_shapes=scratch,
        compiler_params=pltpu.CompilerParams(
            collective_id=collective_id, has_side_effects=True, vmem_limit_bytes=60 * 2**20
        ),
        name=name,
    )(*ins)


def contract_last(left, right):
    return lax.dot_general(left, right, (((1,), (1,)), ((), ())), preferred_element_type=F32)


def contract_first(left, right):
    return lax.dot_general(left, right, (((0,), (0,)), ((), ())), preferred_element_type=F32)


def matmul(left, right):
    return jnp.dot(left, right, preferred_element_type=F32)


def exact_gelu(value_in):
    return jax.nn.gelu(value_in, approximate=False)


def normalize(hidden, gain_row):
    row_mean = jnp.mean(hidden, axis=-1, keepdims=True)
    centred = hidden - row_mean
    spread = lax.rsqrt(jnp.mean(centred * centred, axis=-1, keepdims=True) + norm_eps)
    scaled = centred * spread
    return (scaled * gain_row, scaled, spread)


def normalize_back(grad_in, scaled, spread, gain_row):
    weighted = grad_in * gain_row
    mean_first = jnp.mean(weighted, axis=-1, keepdims=True)
    second = jnp.mean(weighted * scaled, axis=-1, keepdims=True)
    return (
        spread * (weighted - mean_first - scaled * second),
        jnp.sum(grad_in * scaled, axis=0),
        jnp.sum(grad_in, axis=0),
    )


class RowGather:
    @staticmethod
    def scratch():
        return [pltpu.SemaphoreType.DMA((2, 3)), pltpu.SemaphoreType.DMA((2, 3))]

    def __init__(self, buf, ss, rs):
        self.buf, self.ss, self.rs = buf, ss, rs
        self.b, self.s = lax.axis_index("batch"), lax.axis_index("seq")
        self.far, self.near = (self.s + 2) % 4, self.s + 1 - 2 * (self.s % 2)
        self.diag = (self.near + 2) % 4

    def copy(self, r, step, block, device):
        place = self.buf.at[r, block]
        return remote(place, place, self.ss.at[r, step], self.rs.at[r, step], (self.b, device))

    def start(self, r):
        self.copy(r, 0, self.s, self.far).start()
        self.copy(r, 1, self.s, self.near).start()

    def wait_near(self, r):
        self.copy(r, 1, self.near, self.near).wait_recv()

    def pass_far(self, r):
        self.copy(r, 0, self.far, self.far).wait_recv()
        self.copy(r, 2, self.far, self.near).start()

    def wait_diag(self, r):
        self.copy(r, 2, self.diag, self.near).wait_recv()

    def finish(self, r):
        self.copy(r, 0, self.s, self.far).wait_send()
        self.copy(r, 1, self.s, self.near).wait_send()
        self.copy(r, 2, self.far, self.near).wait_send()


def gelu_parts(value):
    cdf = 0.5 * (1.0 + lax.erf(value * math.sqrt(0.5)))
    density = jnp.exp(-0.5 * value * value) * (1.0 / math.sqrt(2.0 * math.pi))
    return value * cdf, cdf + value * density


def row_sum(value):
    return jnp.sum(value, axis=0, keepdims=True)


class RowSwap:
    @staticmethod
    def scratch(shape):
        return [
            pltpu.VMEM(shape, BF16),
            pltpu.VMEM(shape, BF16),
            pltpu.SemaphoreType.DMA((2, 4)),
            pltpu.SemaphoreType.DMA((2, 4)),
        ]

    def __init__(self, src, dst, ss, rs):
        self.src, self.dst, self.ss, self.rs = src, dst, ss, rs
        self.b, self.s = lax.axis_index("batch"), lax.axis_index("seq")

    def copy(self, r, k):
        other = (self.s + k) % 4
        return remote(
            self.src.at[other, r], self.dst.at[self.s, r], self.ss.at[r, k], self.rs.at[r, k],
            (self.b, other),
        )

    def start(self, r):
        for k in (2, 3, 1):
            self.copy(r, k).start()
        self.dst[self.s, r] = self.src[self.s, r]

    def wait(self, r):
        for k in (2, 3, 1):
            self.copy(r, k).wait_recv()

    def finish(self, r):
        for k in (2, 3, 1):
            self.copy(r, k).wait_send()


def rounds(count):
    for _ in range(count):
        yield


def spaced(op, count):
    for _ in op:
        yield from rounds(count)


def step(op):
    try:
        next(op)
    except StopIteration:
        pass


def drain(op):
    for _ in op:
        pass


class DirectSum:
    peers = ("all",)

    def __init__(self, n, src):
        self.n = n
        self.scratch = [pltpu.VMEM(src.shape, F32)] + [pltpu.SemaphoreType.DMA((n,))] * 2

    def run(self, src, dst, arrived, ss, rs):
        n = self.n
        b, s = lax.axis_index("batch"), lax.axis_index("seq")
        copies = []
        for k in range(1, n):
            to = (b + k) % n
            copies.append(remote(src.at[to], arrived.at[k], ss.at[k], rs.at[k], (to, s)))
            copies[-1].start()
        yield
        total = src[b]
        for k, c in enumerate(copies):
            c.wait()
            total = total + arrived[k + 1]
        dst[...] = total


class BatchSum:
    peers = ("batch",)

    def __init__(self, n, src):
        self.n = n
        self.ins = [src]
        shape = src.shape[1:]
        self.outs = [jax.ShapeDtypeStruct(shape, F32)]
        m = n // 2
        self.scratch = [pltpu.VMEM((m,) + shape, BF16)] * 3 + [pltpu.SemaphoreType.DMA((m,))] * 4

    def run(self, src, dst, yrecv, zsend, zrecv, ys, yr, zs, zr):
        b, s, hi, lo, m = coords(self.n)
        pair = (hi * 2 + 1 - lo, s)
        first = {}
        for d in list(range(1, m)) + [0]:
            block = ((hi + d) % m) * 2 + 1 - lo
            first[d] = remote(src.at[block], yrecv.at[d], ys.at[d], yr.at[d], pair)
            first[d].start()
        yield
        second = []
        for d in range(1, m):
            h = (hi + d) % m
            first[d].wait_recv()
            zsend[d] = (src[h * 2 + lo].astype(F32) + yrecv[d].astype(F32)).astype(BF16)
            c = remote(zsend.at[d], zrecv.at[d], zs.at[d], zr.at[d], (h * 2 + lo, s))
            c.start()
            second.append(c)
            yield
        first[0].wait_recv()
        total = src[b].astype(F32) + yrecv[0].astype(F32)
        for d in range(1, m):
            second[d - 1].wait_recv()
            total = total + zrecv[d].astype(F32)
        dst[...] = total
        for c in list(first.values()) + second:
            c.wait_send()


class RowSum:
    @staticmethod
    def scratch(rows, shape):
        return [
            pltpu.VMEM((rows, 2) + shape, BF16),
            pltpu.VMEM((rows,) + shape, BF16),
            pltpu.VMEM((rows,) + shape, BF16),
            pltpu.SemaphoreType.DMA((rows, 3)),
            pltpu.SemaphoreType.DMA((rows, 3)),
        ]

    def __init__(self, src, near_in, far_out, far_in, ss, rs):
        self.src, self.near_in, self.far_out, self.far_in, self.ss, self.rs = (
            src, near_in, far_out, far_in, ss, rs,
        )
        self.b, self.s = lax.axis_index("batch"), lax.axis_index("seq")
        self.far, self.near = (self.s + 2) % 4, self.s + 1 - 2 * (self.s % 2)
        self.diag = (self.near + 2) % 4

    def beside(self, r, k):
        block = self.diag if k else self.near
        return remote(
            self.src.at[r, block], self.near_in.at[r, k], self.ss.at[r, k], self.rs.at[r, k],
            (self.b, self.near),
        )

    def across(self, r):
        return remote(
            self.far_out.at[r], self.far_in.at[r], self.ss.at[r, 2], self.rs.at[r, 2],
            (self.b, self.far),
        )

    def send_near(self, r):
        self.beside(r, 0).start()

    def send_diag(self, r):
        self.beside(r, 1).start()

    def cross(self, r):
        self.beside(r, 1).wait_recv()
        part = self.src[r, self.far].astype(F32) + self.near_in[r, 1].astype(F32)
        self.far_out[r] = part.astype(BF16)
        self.across(r).start()

    def total(self, r):
        self.beside(r, 0).wait_recv()
        part = self.src[r, self.s].astype(F32) + self.near_in[r, 0].astype(F32)
        self.across(r).wait_recv()
        return part + self.far_in[r].astype(F32)

    def finish(self, r):
        self.beside(r, 0).wait_send()
        self.beside(r, 1).wait_send()
        self.across(r).wait_send()


class Scratch:
    def __init__(self):
        self.names, self.shapes = [], []

    def add(self, **named):
        for name, shapes in named.items():
            one = not isinstance(shapes, list)
            shapes = [shapes] if one else shapes
            self.names.append((name, len(shapes), one))
            self.shapes += shapes

    def refs(self, refs):
        out, i = types.SimpleNamespace(), 0
        for name, count, one in self.names:
            setattr(out, name, refs[i] if one else refs[i : i + count])
            i += count
        return out


def layer(
    n, tokens, attn_weight, up_weight, down_weight, vec_own, pool_own, lengths, out_grad, up_moment, down_moment
):
    rows, span, width = tokens.shape
    quarter = width // SEQ
    span_all = span * SEQ
    own_rows = width // n
    local = rows * span
    aligned = own_rows % 16 == 0
    scale = HD**-0.5
    shape = jax.ShapeDtypeStruct
    full = (rows, SEQ, span, width)
    widths = (3 * quarter, quarter, width, width)
    low_ops = [GatherBatch(n, shape((own_rows, c), BF16), k == 0) for k, c in enumerate(widths)]
    low_ops = low_ops if aligned else []
    vec_op = GatherDirect(n, vec_own) if aligned else GatherBatch(n, vec_own)
    pool_op = GatherSeq(n, pool_own)
    out_op = GatherSeq(n, shape((width, quarter), BF16))
    sum_ops = [BatchSum(n, shape((n, own_rows, width), BF16)) for _ in range(2)]

    outs = [
        shape((rows, span, width), F32),
        shape((rows, width), F32),
        shape((rows, span, width), F32),
        shape((8, width), F32),
        shape((1, 3 * quarter), F32),
        shape(full, BF16),
    ]
    vmem = pl.BlockSpec(memory_space=pltpu.VMEM)
    anywhere = pl.BlockSpec(memory_space=pl.ANY)
    if aligned:
        outs += [shape((n, own_rows, c), BF16) for c in (3 * quarter, quarter)]
        outs += [shape((2, own_rows, width), BF16), shape((SEQ, n, own_rows, width), BF16)]
        out_specs = [vmem] * 9 + [anywhere]
    else:
        outs += [shape((width, c), BF16) for c in widths]
        out_specs = [vmem] * 10

    dma = pltpu.SemaphoreType.DMA
    sc = Scratch()
    if aligned:
        sc.add(
            lows=[pltpu.VMEM((own_rows, c), BF16) for c in widths],
            weights=[pltpu.VMEM(op.outs[0].shape, BF16) for op in low_ops],
            low_moves=[c for op in low_ops for c in op.scratch],
        )
    sc.add(vec_parts=pltpu.VMEM(vec_op.outs[0].shape, F32))
    sc.add(vec_move=vec_op.scratch)
    sc.add(vec=pltpu.VMEM((8, width), F32))
    sc.add(pool_parts=pltpu.VMEM(pool_op.outs[0].shape, F32))
    sc.add(pool_move=pool_op.scratch)
    sc.add(out_own=pltpu.VMEM((width, quarter), BF16))
    sc.add(out_parts=pltpu.VMEM((SEQ, width, quarter), BF16))
    sc.add(out_move=out_op.scratch)
    sc.add(w_out=pltpu.VMEM((width, width), BF16))
    sc.add(x_all=pltpu.VMEM(full, BF16))
    sc.add(x_gather=RowGather.scratch())
    sc.add(qkv=pltpu.VMEM((rows, span_all, 3 * quarter), BF16))
    sc.add(prob=pltpu.VMEM((rows, HEADS, span_all, span_all), F32))
    sc.add(swap=RowSwap.scratch((SEQ, rows, span, quarter)))
    sc.add(back_swap=RowSwap.scratch((SEQ, rows, span, quarter)))
    sc.add(context=pltpu.VMEM((rows, span, width), BF16))
    sc.add(normed=pltpu.VMEM((rows, span, width), F32))
    sc.add(scaled_one=pltpu.VMEM((rows, span, width), F32))
    sc.add(spread_one=pltpu.VMEM((rows, span, 1), F32))
    sc.add(y_all=pltpu.VMEM(full, BF16))
    sc.add(y_gather=RowGather.scratch())
    sc.add(slope=pltpu.VMEM(full, F32))
    sc.add(act=pltpu.VMEM(full, BF16))
    sc.add(z_sum=RowSum.scratch(rows, (span, width)))
    sc.add(dz_all=pltpu.VMEM(full, BF16))
    sc.add(dz_gather=RowGather.scratch())
    sc.add(du_all=pltpu.VMEM(full, BF16))
    sc.add(dy_sum=RowSum.scratch(rows, (span, width)))
    sc.add(pool_buf=pltpu.VMEM((SEQ, rows, width), F32))
    sc.add(pool_sems=[dma((3,)), dma((3,))])
    sc.add(a_quarters=pltpu.VMEM((SEQ, local, quarter), BF16))
    sc.add(out_part=pltpu.VMEM((1, SEQ, width, quarter), BF16))
    sc.add(out_sum=RowSum.scratch(1, (width, quarter)))
    if not aligned:
        sc.add(x_sum=RowSum.scratch(rows, (span, width)))
    sc.add(grad_qkv=pltpu.VMEM((rows, span_all, 3 * quarter), BF16))
    if aligned:
        sc.add(raw=dma((2 * SEQ + 1,)))
        sc.add(
            down_grad=pltpu.VMEM((n, own_rows, width), BF16),
            up_grad=pltpu.VMEM((n, own_rows, width), BF16),
            down_piece=pltpu.VMEM((own_rows, width), F32),
            up_piece=pltpu.VMEM((own_rows, width), F32),
            down_sum=sum_ops[0].scratch,
            up_sum=sum_ops[1].scratch,
        )
        sc.add(vec_low=pltpu.VMEM(vec_own.shape, F32))
        sc.add(wide_send=pltpu.VMEM((2, own_rows, width), BF16))
        sc.add(mail=OwnerMail.scratch(n, 2, (own_rows, width)))

    def kernel(
        tokens, attn_weight, up_weight, down_weight, vec_own, pool_own, lengths, out_grad, up_moment, down_moment,
        out_rows, pooled, second, vec_grad, bias_sums, part, grad_first, grad_second, *rest,
    ):
        if aligned:
            wide_bf, wide_in = rest[:2]
            rest = rest[2:]
        else:
            grad_up_out, grad_down_out = rest[:2]
            rest = rest[2:]
        at = sc.refs(rest)
        kinds = {"all"} if aligned else {"seq", "batch"}
        greet_signal(n, kinds)
        b, s = lax.axis_index("batch"), lax.axis_index("seq")
        x_all, y_all, dz_all, du_all = at.x_all, at.y_all, at.dz_all, at.du_all
        slope, act, prob, qkv = at.slope, at.act, at.prob, at.qkv
        normed, context, vec = at.normed, at.context, at.vec
        x_gather = RowGather(x_all, *at.x_gather)
        y_gather = RowGather(y_all, *at.y_gather)
        dz_gather = RowGather(dz_all, *at.dz_gather)
        swap, back_swap = RowSwap(*at.swap), RowSwap(*at.back_swap)
        z_sum, dy_sum = [RowSum(part, *refs) for refs in (at.z_sum, at.dy_sum)]
        out_sum = RowSum(at.out_part, *at.out_sum)
        far, near, diag = x_gather.far, x_gather.near, x_gather.diag

        def raw_block(k):
            return slope.at[k // SEQ, k % SEQ, pl.ds(0, own_rows)]

        def load_up(matrix):
            return [
                pltpu.make_async_copy(
                    matrix.at[:, pl.ds(k * width, width)], raw_block(SEQ + k), at.raw.at[SEQ + k]
                )
                for k in range(SEQ)
            ]

        def load_down(matrix, place):
            return pltpu.make_async_copy(
                matrix.at[pl.ds(s * own_rows, own_rows)], place, at.raw.at[2 * SEQ]
            )

        def raw_up(k):
            whole = jnp.concatenate([raw_block(SEQ + j)[...] for j in range(SEQ)], axis=1)
            return take_up(whole, n, k)

        if aligned:
            raws = [
                pltpu.make_async_copy(attn_weight.at[k], raw_block(k), at.raw.at[k]) for k in range(4)
            ]
            raws += load_up(up_weight)
            raws.append(load_down(down_weight, second.at[0, pl.ds(0, own_rows)]))
            for c in raws:
                c.start()
        for r in range(rows):
            x_all[r, s] = tokens[r].astype(BF16)
        if aligned:
            for c in raws[:4]:
                c.wait()
            for k in range(SEQ):

                @pl.when(s == k)
                def _(k=k):
                    block = [raw_block(j)[:, k * quarter : (k + 1) * quarter] for j in range(4)]
                    at.lows[0][...] = jnp.concatenate(block[:3], axis=1).astype(BF16)
                    at.lows[1][...] = block[3].astype(BF16)

            vec_low = at.vec_low
            vec_low[...] = vec_own[...].astype(BF16).astype(F32)
        else:
            vec_low = vec_own

        greet_wait(n, kinds)
        vec_move = vec_op.run(vec_low, at.vec_parts, *at.vec_move)
        pool_move = pool_op.run(pool_own, at.pool_parts, *at.pool_move)
        step(vec_move)
        if aligned:
            moves = [
                op.run(at.lows[k], at.weights[k], *at.low_moves[5 * k : 5 * k + 5])
                for k, op in enumerate(low_ops)
            ]
            step(moves[0])
            step(moves[1])
        step(pool_move)
        for r in range(rows):
            x_gather.start(r)
        if aligned:
            for c in raws[4:]:
                c.wait()
            for k in range(SEQ):

                @pl.when(s == k)
                def _(k=k):
                    at.lows[2][...] = raw_up(k).astype(BF16)

            at.lows[3][...] = second[0, :own_rows].astype(BF16)
            step(moves[0])
        x_gather.pass_far(0)
        if aligned:
            step(moves[0])
        step(pool_move)
        x_gather.pass_far(1)
        if aligned:
            step(moves[0])
            step(moves[2])
            step(moves[1])
        drain(vec_move)
        drain(pool_move)
        if aligned:
            whole = jnp.concatenate([at.vec_parts[k] for k in range(n)], axis=1)

            def here(make):
                return sum(jnp.where(s == k, make(k), 0.0) for k in range(SEQ))

            vec[0:6] = whole[2:8]
            vec[6:7] = here(
                lambda k: jnp.concatenate(
                    [
                        whole[8 + f // width : 9 + f // width, f % width : f % width + own_rows]
                        for f in ((j * SEQ + k) * own_rows for j in range(n))
                    ],
                    axis=1,
                )
            )
            blank = jnp.zeros((1, quarter), F32)
            vec[7:8] = here(
                lambda k: jnp.concatenate(
                    [
                        whole[0:1, k * quarter : (k + 1) * quarter],
                        blank,
                        whole[1:2, k * quarter : (k + 1) * quarter],
                        blank,
                    ],
                    axis=1,
                )
            )
        else:
            total = at.vec_parts[0]
            for k in range(1, n):
                total = total + at.vec_parts[k]
            vec[...] = total
        pool_whole = jnp.concatenate([at.pool_parts[k] for k in range(SEQ)], axis=1)

        if aligned:
            drain(moves[0])
            step(moves[3])

        def w_qkv():
            if aligned:
                return at.weights[0][...].reshape(width, 3 * quarter)
            return attn_weight[:, : 3 * quarter]

        def w_up():
            return at.weights[2][...].reshape(width, width) if aligned else up_weight[...]

        def w_down():
            return at.weights[3][...].reshape(width, width) if aligned else down_weight[...]

        out_move = out_op.run(at.out_own, at.out_parts, *at.out_move)

        def begin_out():
            if aligned:
                drain(moves[1])
                at.out_own[...] = at.weights[1][...].reshape(width, quarter)
            else:
                at.out_own[...] = attn_weight[:, 3 * quarter :]
            step(out_move)

        def turn(*ks):
            for k in ks:
                if aligned:
                    step(moves[k])

        bias = vec[7:8, : 3 * quarter]
        column = lax.broadcasted_iota(jnp.int32, (1, span_all), 1)

        def heads(r, h):
            return [
                qkv[r, :, k * quarter + h * HD : k * quarter + (h + 1) * HD] for k in range(3)
            ]

        for r in range(rows):
            x_gather.wait_near(r)
            x_gather.wait_diag(r)
            block = matmul(x_all[r].reshape(span_all, width), w_qkv()) + bias
            qkv[r] = block.astype(BF16)
            valid = column < lengths[r]
            mixed = []
            for h in range(HEADS):
                query, key, value = heads(r, h)
                scores = contract_last(query * jnp.bfloat16(scale), key)
                scores = jnp.where(valid, scores, -1e30)
                exponent = jnp.exp(scores - jnp.max(scores, axis=-1, keepdims=True))
                weight = exponent * (1.0 / jnp.sum(exponent, axis=-1, keepdims=True))
                prob[r, h] = weight
                mixed.append(matmul(weight.astype(BF16), value))
                if r == 0 and h == 1:
                    turn(1, 1)
                    begin_out()
                if r == 0 and h > 0:
                    turn(2)
                if r == 1 and h == 0:
                    turn(2)
                if r == 1 and h > 0:
                    turn(3)
            mixed = jnp.concatenate(mixed, axis=1).astype(BF16)
            for k in range(SEQ):
                at.swap[0][k, r] = mixed[k * span : (k + 1) * span]
            swap.start(r)
        step(out_move)
        turn(3)
        drain(out_move)
        w_out = at.w_out
        w_out[...] = jnp.concatenate([at.out_parts[k] for k in range(SEQ)], axis=1)
        gain_one, shift_one = vec[1:2], vec[2:3]
        for r in range(rows):
            swap.wait(r)
            context[r] = jnp.concatenate([at.swap[1][k, r] for k in range(SEQ)], axis=1)
            hidden = tokens[r] + (matmul(context[r], w_out[...]) + vec[0:1])
            centred = hidden - jnp.mean(hidden, axis=-1, keepdims=True)
            spread = lax.rsqrt(jnp.mean(centred * centred, axis=-1, keepdims=True) + norm_eps)
            scaled = centred * spread
            at.scaled_one[r] = scaled
            at.spread_one[r] = spread
            value = scaled * gain_one + shift_one
            normed[r] = value
            y_all[r, s] = value.astype(BF16)
            y_gather.start(r)

        if aligned:
            turn(3)
            drain(moves[2])
        gain_two, shift_two = vec[3:4], vec[4:5]
        bias_down, bias_up = vec[5:6], vec[6:7]

        def pair(ref, blocks):
            return jnp.concatenate([ref[i] for i in blocks], axis=0)

        def put(ref, blocks, value):
            for k, i in enumerate(blocks):
                ref[i] = value[k * span : (k + 1) * span].astype(ref.dtype)

        def rise(blocks):
            value, rate = gelu_parts(matmul(pair(y_all, blocks), w_up()) + bias_up)
            put(act, blocks, value)
            put(slope, blocks, rate)

        def fall(blocks):
            put(part, blocks, matmul(pair(act, blocks), w_down()))

        mine, beside = [[(r, k) for r in range(rows)] for k in (s, near)]
        rise(mine)
        for r in range(rows):
            y_gather.wait_near(r)
        rise(beside)
        turn(3)
        others = [[(r, diag), (r, far)] for r in range(rows)]
        for r in range(rows):
            y_gather.pass_far(r)
            y_gather.wait_diag(r)
            rise(others[r])
        if aligned:
            drain(moves[3])
        fall(beside)
        for r in range(rows):
            z_sum.send_near(r)
        for r in range(rows):
            fall(others[r])
            z_sum.send_diag(r)
            if r > 0:
                z_sum.cross(r - 1)
        fall(mine)
        z_sum.cross(rows - 1)

        position = s * span + lax.broadcasted_iota(jnp.int32, (span, 1), 0)
        grad_gain_two = grad_shift_two = grad_bias_down = jnp.zeros((1, width), F32)
        for r in range(rows):
            hidden = normed[r] + (z_sum.total(r) + bias_down)
            centred = hidden - jnp.mean(hidden, axis=-1, keepdims=True)
            spread_two = lax.rsqrt(jnp.mean(centred * centred, axis=-1, keepdims=True) + norm_eps)
            scaled = centred * spread_two
            output = scaled * gain_two + shift_two
            out_rows[r] = output
            live = (position < lengths[r]).astype(F32)
            length = jnp.full((1, 1), lengths[r], jnp.int32).astype(F32)
            at.pool_buf[s, r : r + 1] = row_sum(output * live) / length
            upstream = live * (out_grad[r] + pool_whole[r : r + 1] / length)
            weighted = upstream * gain_two
            mean_first = jnp.mean(weighted, axis=-1, keepdims=True)
            mean_second = jnp.mean(weighted * scaled, axis=-1, keepdims=True)
            grad = spread_two * (weighted - mean_first - scaled * mean_second)
            second[r] = grad
            low = grad.astype(BF16)
            dz_all[r, s] = low
            dz_gather.start(r)
            grad_gain_two += row_sum(upstream * scaled)
            grad_shift_two += row_sum(upstream)
            grad_bias_down += row_sum(low.astype(F32))

        def pool_copy(k, block, device):
            place = at.pool_buf.at[block]
            sems = at.pool_sems
            return remote(place, place, sems[0].at[k - 1], sems[1].at[k - 1], (b, device))

        for k in (1, 2, 3):
            pool_copy(k, s, (s + k) % 4).start()
        for r in range(rows):
            z_sum.finish(r)

        def backward(blocks):
            lift = contract_last(pair(dz_all, blocks), w_down())
            low = (lift * pair(slope, blocks)).astype(BF16)
            put(du_all, blocks, low)
            put(part, blocks, contract_last(low, w_up()))
            return row_sum(low.astype(F32))

        bias_grad = backward(mine)
        for r in range(rows):
            dz_gather.wait_near(r)
        bias_grad += backward(beside)
        for r in range(rows):
            dy_sum.send_near(r)
        for r in range(rows):
            dz_gather.pass_far(r)
            dz_gather.wait_diag(r)
            bias_grad += backward([(r, diag), (r, far)])
            dy_sum.send_diag(r)
            dy_sum.cross(r)

        flat = rows * span_all
        if aligned:
            down_move = sum_ops[0].run(at.down_grad, at.down_piece, *at.down_sum)
            up_move = sum_ops[1].run(at.up_grad, at.up_piece, *at.up_sum)
            mail = OwnerMail(n, owner_list(n)[4:], wide_in, *at.mail)
            wide_send = at.wide_send
            momenta = load_up(up_moment) + [load_down(down_moment, raw_block(0))]
            for c in momenta:
                c.start()
        whole = contract_first(act[...].reshape(flat, width), dz_all[...].reshape(flat, width))
        if aligned:
            at.down_grad[...] = whole.reshape(n, own_rows, width).astype(BF16)
            step(down_move)
        else:
            grad_down_out[...] = whole.astype(BF16)
        whole = contract_first(y_all[...].reshape(flat, width), du_all[...].reshape(flat, width))
        if aligned:
            at.up_grad[...] = whole.reshape(n, own_rows, width).astype(BF16)
            step(up_move)
        else:
            grad_up_out[...] = whole.astype(BF16)

        grad_gain_one = grad_shift_one = grad_bias_out = jnp.zeros((1, width), F32)
        for r in range(rows):
            grad = dy_sum.total(r) + second[r]
            scaled = at.scaled_one[r]
            weighted = grad * gain_one
            mean_first = jnp.mean(weighted, axis=-1, keepdims=True)
            mean_second = jnp.mean(weighted * scaled, axis=-1, keepdims=True)
            first = at.spread_one[r] * (weighted - mean_first - scaled * mean_second)
            second[r] = first
            low = first.astype(BF16)
            above = contract_last(low, w_out[...]).astype(BF16)
            for k in range(SEQ):
                columns = slice(k * quarter, (k + 1) * quarter)
                at.back_swap[0][k, r] = above[:, columns]
                at.a_quarters[k, r * span : (r + 1) * span] = low[:, columns]
            back_swap.start(r)
            grad_gain_one += row_sum(grad * scaled)
            grad_shift_one += row_sum(grad)
            grad_bias_out += row_sum(low.astype(F32))
        for k, value in enumerate(
            (
                grad_bias_out, grad_gain_one, grad_shift_one, grad_gain_two, grad_shift_two,
                grad_bias_down, bias_grad, jnp.zeros((1, width), F32),
            )
        ):
            vec_grad[k : k + 1] = value

        def new_momentum(k, piece, old):
            wide_bf[k] = piece[...].astype(BF16)
            wide_send[k] = (matrix_decay * old + wide_bf[k].astype(F32)).astype(BF16)
            mail.send(k, wide_send.at[k])

        flat_context = context[...].reshape(local, width)
        for k in range(SEQ):
            at.out_part[0, k] = contract_first(flat_context, at.a_quarters[k]).astype(BF16)
        out_sum.send_diag(0)
        out_sum.send_near(0)
        for r in range(rows):
            dy_sum.finish(r)
        sums = jnp.zeros((1, 3 * quarter), F32)
        for r in range(rows):
            back_swap.wait(r)
            arrived = jnp.concatenate([at.back_swap[1][k, r] for k in range(SEQ)], axis=0)
            query_grads, key_grads, value_grads = [], [], []
            for h in range(HEADS):
                query, key, value = heads(r, h)
                above = arrived[:, h * HD : (h + 1) * HD]
                weight = prob[r, h]
                prob_grad = contract_last(above, value)
                delta = jnp.sum(weight * prob_grad, axis=-1, keepdims=True)
                score_grad = (weight * (prob_grad - delta)).astype(BF16)
                query_grads.append(matmul(score_grad, key) * scale)
                key_grads.append(contract_first(query, score_grad) * scale)
                value_grads.append(contract_first(above, weight.astype(BF16)))
                if aligned and r == 0:
                    step(down_move)
                if r == 1 and h == 0:
                    out_sum.cross(0)
                if aligned and r == 1 and h > 0:
                    step(up_move)
                if not aligned and r > 0 and h == 2:
                    x_sum.cross(r - 1)
            turned = jnp.concatenate(key_grads + value_grads, axis=0).T
            block = jnp.concatenate(query_grads + [turned], axis=1).astype(BF16)
            at.grad_qkv[r] = block
            sums += row_sum(block.astype(F32))
            out = contract_last(block, w_qkv())
            for k in range(SEQ):
                part[r, k] = out[k * span : (k + 1) * span].astype(BF16)
            if not aligned:
                if r == 0:
                    x_sum = RowSum(part, *at.x_sum)
                x_sum.send_diag(r)
                x_sum.send_near(r)
        if aligned:
            step(up_move)
            drain(down_move)
            for c in momenta:
                c.wait()
            new_momentum(1, at.down_piece, raw_block(0)[...])
        bias_sums[...] = sums
        whole = contract_first(
            x_all[...].reshape(flat, width), at.grad_qkv[...].reshape(flat, 3 * quarter)
        )
        grad_first[...] = whole.astype(BF16).reshape(grad_first.shape)
        grad_second[...] = out_sum.total(0).astype(BF16).reshape(grad_second.shape)
        for k in (1, 2, 3):
            pool_copy(k, (s + 4 - k) % 4, (s + k) % 4).wait_recv()
        pool_buf = at.pool_buf
        pooled[...] = (pool_buf[0] + pool_buf[1]) + (pool_buf[2] + pool_buf[3])
        if aligned:
            mail.relay(1)
            drain(up_move)
            for k in range(SEQ):

                @pl.when(s == k)
                def _(k=k):
                    wide_bf[0] = at.up_piece[...].astype(BF16)
                    old = matrix_decay * raw_up(k) + wide_bf[0].astype(F32)
                    wide_send[0] = old.astype(BF16)

            mail.send(0, wide_send.at[0])
        else:
            x_sum.cross(rows - 1)
            for r in range(rows):
                second[r] = x_sum.total(r) + second[r]
                x_sum.finish(r)
        out_sum.finish(0)
        for k in (1, 2, 3):
            pool_copy(k, s, (s + k) % 4).wait_send()
        for r in range(rows):
            for op in (x_gather, swap, y_gather, dz_gather, back_swap):
                op.finish(r)
        if aligned:
            mail.relay(0)

            @pl.when(mail.mine[0] | mail.mine[1])
            def _():
                mail.collect()

            for k in range(2):
                mail.finish(k, wide_send.at[k])

    smem = pl.BlockSpec(memory_space=pltpu.SMEM)
    far_spec = anywhere if aligned else vmem
    return pl.pallas_call(
        kernel,
        out_shape=outs,
        in_specs=[vmem] + [far_spec] * 3 + [vmem] * 2 + [smem, vmem] + [anywhere] * 2,
        out_specs=out_specs,
        scratch_shapes=sc.shapes,
        compiler_params=pltpu.CompilerParams(
            collective_id=0, has_side_effects=True, vmem_limit_bytes=63 * 2**20
        ),
        name="layer",
    )(tokens, attn_weight, up_weight, down_weight, vec_own, pool_own, lengths, out_grad, up_moment, down_moment)


def join_up_parts(parts, n):
    hid_own = parts[0].shape[1] // n
    return jnp.concatenate(
        [parts[k][:, b * hid_own : (b + 1) * hid_own] for b in range(n) for k in range(SEQ)], axis=1
    )


def take_up(matrix, n, k):
    hid_own = matrix.shape[1] // n // SEQ
    return jnp.concatenate(
        [
            matrix[:, (b * SEQ + k) * hid_own : (b * SEQ + k + 1) * hid_own]
            for b in range(n)
        ],
        axis=1,
    )


def muon(n, grad_qkv, grad_out, wide_in, bias_sums, vec_grad, attn_moment, wide_bf, x_part, first_grad):
    rows, width = wide_in.shape[2:]
    quarter = width // SEQ
    hid_own = rows
    n_vec = 8 + SEQ
    shape = jax.ShapeDtypeStruct
    attn_op = GatherSeq(n, shape((4, rows, quarter), BF16))
    qkv_sum, out_sum = BatchSum(n, grad_qkv), BatchSum(n, grad_out)
    vec_sum = DirectSum(n, shape((n, n_vec, rows), F32))
    vec_op = GatherSeq(n, shape((n_vec, rows), F32))
    wide_op = GatherSeq(n, wide_bf)
    count, span = first_grad.shape[:2]
    main = Muon(n, shape((4, rows, quarter), BF16), wide_in=wide_in)
    outs = [attn_op.outs[0], wide_op.outs[0], shape((n_vec, rows), F32), shape(first_grad.shape, F32)]
    outs += main.outs
    groups = [
        [
            pltpu.VMEM((rows, 3 * quarter), F32),
            pltpu.VMEM((rows, quarter), F32),
            pltpu.VMEM((4, rows, quarter), BF16),
            pltpu.VMEM((4, rows, quarter), BF16),
            pltpu.VMEM((n, n_vec, rows), F32),
            pltpu.VMEM((n_vec, rows), F32),
            pltpu.VMEM((SEQ, n_vec, rows), F32),
        ]
    ] + [op.scratch for op in (attn_op, vec_sum, vec_op, main, qkv_sum, out_sum, wide_op)]
    groups.append(RowSum.scratch(count, (span, width)))

    def kernel(
        grad_qkv, grad_out, wide_in, bias_sums, vec_grad, attn_moment, wide_bf, x_part, first_grad,
        attn_all, wide_all, vec_total, input_grad, attn_orth, wide_orth, *rest,
    ):
        greet_signal(n, {"all"})
        parts, i = [], 0
        for group in groups:
            parts.append(rest[i : i + len(group)])
            i += len(group)
        qkv_piece, out_piece, attn_bf, attn_send, vec_local, vec_piece, vec_parts = parts[0]
        s = lax.axis_index("seq")
        main_move = main.run(attn_send, wide_in, attn_orth, wide_orth, *parts[4])
        step(main_move)
        main.prepare()
        greet_wait(n, {"all"})
        x_sum = RowSum(x_part, *parts[8])

        def inputs():
            for r in range(count):
                x_sum.send_diag(r)
                x_sum.send_near(r)
            yield
            for r in range(count):
                x_sum.cross(r)
            yield from rounds(8)
            for r in range(count):
                input_grad[r] = x_sum.total(r) + first_grad[r]
                x_sum.finish(r)

        def attention():
            ops = [
                qkv_sum.run(grad_qkv, qkv_piece, *parts[5]),
                out_sum.run(grad_out, out_piece, *parts[6]),
            ]
            for op in ops:
                step(op)
            yield from rounds(3)
            for _ in range(n // 2 - 1):
                for op in ops:
                    step(op)
            yield from rounds(3)
            for op in ops:
                drain(op)
            for j in range(3):
                attn_bf[j] = qkv_piece[:, j * quarter : (j + 1) * quarter].astype(BF16)
            attn_bf[3] = out_piece[...].astype(BF16)
            for k in range(SEQ):

                @pl.when(s == k)
                def _(k=k):
                    for j in range(4):
                        old = attn_moment[j, :, k * quarter : (k + 1) * quarter]
                        attn_send[j] = (matrix_decay * old + attn_bf[j].astype(F32)).astype(BF16)
            main.send_attn()
            yield
            main.attn_turn()
            yield from spaced(attn_op.run(attn_bf, attn_all, *parts[1]), 2)

        def vectors():
            def here(k, value):
                return jnp.where(s == k, value, 0.0)

            lines = [
                jnp.concatenate(
                    [here(k, bias_sums[:, j * quarter : (j + 1) * quarter]) for k in range(SEQ)], axis=1
                )
                for j in (0, 2)
            ]
            lines += [vec_grad[j : j + 1] for j in range(6)]
            hidden = vec_grad[6:7]
            pieces = [
                here(k, hidden[:, b * hid_own : (b + 1) * hid_own]) for b in range(n) for k in range(SEQ)
            ]
            each = n * SEQ // 4
            lines += [jnp.concatenate(pieces[j * each : (j + 1) * each], axis=1) for j in range(4)]
            whole = jnp.concatenate(lines, axis=0)
            for b in range(n):
                vec_local[b] = whole[:, b * rows : (b + 1) * rows]
            yield from spaced(vec_sum.run(vec_local, vec_piece, *parts[2]), 3)
            yield from spaced(vec_op.run(vec_piece, vec_parts, *parts[3]), 2)
            vec_total[...] = (vec_parts[0] + vec_parts[1]) + (vec_parts[2] + vec_parts[3])

        run_together(
            vectors(),
            attention(),
            inputs(),
            spaced(wide_op.run(wide_bf, wide_all, *parts[7]), 6),
            main_move,
        )

    vmem = pl.BlockSpec(memory_space=pltpu.VMEM)
    ins = (grad_qkv, grad_out, wide_in, bias_sums, vec_grad, attn_moment, wide_bf, x_part, first_grad)
    return pl.pallas_call(
        kernel,
        out_shape=outs,
        in_specs=[vmem] * 2 + [pl.BlockSpec(memory_space=pl.ANY)] + [vmem] * 6,
        out_specs=[vmem] * len(outs),
        scratch_shapes=[c for group in groups for c in group],
        compiler_params=pltpu.CompilerParams(
            collective_id=8, has_side_effects=True, vmem_limit_bytes=62 * 2**20
        ),
        name="muon",
    )(*ins)


def finish(
    n, out_rows, pool_sum, input_grad, attn_all, wide_all, attn_orth, wide_orth, vec_total,
    attn_weight, up_weight, down_weight, vectors, attn_moment, up_moment, down_moment, vector_moment,
    factors, vector_step,
):
    rows = wide_all.shape[2]
    quarter = attn_all.shape[3]

    def kernel(
        out_from, pool_sum, input_from, attn_all, wide_all, attn_orth, wide_orth, vec_total,
        attn_weight, up_weight, down_weight, vectors, attn_moment, up_moment, down_moment, vector_moment,
        out_to, pooled, input_to, attn_grad, up_grad, down_grad, vec_grad, attn_next, up_next, down_next, vec_next,
        attn_new, up_new, down_new, vec_new,
    ):
        out_to[...] = out_from[...]
        input_to[...] = input_from[...]
        s = lax.axis_index("seq")
        pooled[...] = sum(
            jnp.where(s == k, pool_sum[:, k * quarter : (k + 1) * quarter], 0.0) for k in range(SEQ)
        )
        for j in range(4):
            grad = jnp.concatenate([attn_all[k, j] for k in range(SEQ)], axis=1).astype(F32)
            attn_grad[j] = grad
            attn_next[j] = matrix_decay * attn_moment[j] + grad
            orth = jnp.concatenate([attn_orth[k, j] for k in range(SEQ)], axis=1).astype(F32)
            attn_new[j] = attn_weight[j] - factors[0] * orth
        grad = join_up_parts([wide_all[k, 0] for k in range(SEQ)], n).astype(F32)
        up_grad[...] = grad
        up_next[...] = matrix_decay * up_moment[...] + grad
        orth = join_up_parts([wide_orth[k, 0] for k in range(SEQ)], n).astype(F32)
        up_new[...] = up_weight[...] - factors[1] * orth
        for k in range(SEQ):
            part = pl.ds(k * rows, rows)
            grad = wide_all[k, 1].astype(F32)
            down_grad[part] = grad
            down_next[part] = matrix_decay * down_moment[part] + grad
            down_new[part] = down_weight[part] - factors[2] * wide_orth[k, 1].astype(F32)
        vec_grad[...] = vec_total[...]
        moved = vector_decay * vector_moment[...] + vec_total[...]
        vec_next[...] = moved
        vec_new[...] = vectors[...] - vector_step * moved

    vmem = pl.BlockSpec(memory_space=pltpu.VMEM)
    ins = (
        out_rows, pool_sum, input_grad, attn_all, wide_all, attn_orth, wide_orth, vec_total,
        attn_weight, up_weight, down_weight, vectors, attn_moment, up_moment, down_moment, vector_moment,
    )
    outs = [jax.ShapeDtypeStruct(a.shape, F32) for a in (attn_weight, up_weight, down_weight, vectors)] * 3
    tokens = jax.ShapeDtypeStruct(out_rows.shape, F32)
    outs = [tokens, jax.ShapeDtypeStruct((out_rows.shape[0], quarter), F32), tokens] + outs
    return pl.pallas_call(
        kernel,
        out_shape=outs,
        in_specs=[vmem] * len(ins),
        out_specs=[vmem] * len(outs),
        compiler_params=pltpu.CompilerParams(vmem_limit_bytes=60 * 2**20),
        name="finish",
    )(*ins)


def step_factor(rows_all, cols_all):
    return matrix_rate * math.sqrt(max(1.0, rows_all / cols_all))


def make_body(n):
    def body(
        layer_input,
        lengths,
        attn_weight,
        up_weight,
        down_weight,
        vectors,
        attn_moment,
        up_moment,
        down_moment,
        vector_moment,
        out_grad,
        pool_grad,
    ):
        rows, span, width = layer_input.shape
        own_rows = width // n
        quarter = width // SEQ
        hidden = up_weight.shape[1]
        hid_q = hidden // SEQ
        hid_own = hidden // n // SEQ
        seq_index = lax.axis_index("seq")

        def attn_quarter(stacked):
            part = lax.dynamic_index_in_dim(
                stacked.reshape(4, own_rows, SEQ, quarter), seq_index, 2, False
            )
            return part

        def up_quarter(matrix):
            return lax.dynamic_index_in_dim(
                matrix.reshape(own_rows, n, SEQ, hid_own), seq_index, 2, False
            ).reshape(own_rows, hid_q)

        def down_quarter(matrix):
            return lax.dynamic_index_in_dim(
                matrix.reshape(SEQ, hid_own, width), seq_index, 0, False
            )

        aligned = own_rows % 16 == 0
        if aligned:
            own = [attn_weight, up_weight, down_weight]
            vec_own = vectors
        else:
            attn_low = attn_quarter(attn_weight).astype(BF16).transpose(1, 0, 2).reshape(own_rows, width)
            up_low = up_quarter(up_weight).astype(BF16)
            down_low = down_quarter(down_weight).astype(BF16)
            vec_low = vectors.astype(BF16).astype(F32)
            placed = lax.dynamic_update_slice(
                jnp.zeros((vectors.shape[0], n, own_rows), F32),
                vec_low[:, None],
                (0, lax.axis_index("batch"), 0),
            ).reshape(-1, width)
            bias_up = lax.dynamic_index_in_dim(
                placed[8:].reshape(n, SEQ, hid_own), seq_index, 1, False
            ).reshape(1, hid_q)
            bias_qv = lax.dynamic_index_in_dim(
                placed[:2].reshape(2, SEQ, quarter), seq_index, 1, False
            )
            blank = jnp.zeros((quarter,), F32)
            bias_qkv = jnp.concatenate([bias_qv[0], blank, bias_qv[1], blank])[None]
            vec_own = jnp.concatenate([placed[2:8], bias_up, bias_qkv])
            own = exchange(
                n, 1, "gather_weights", *[GatherBatch(n, a) for a in (attn_low, up_low, down_low)]
            )
            own = [a.reshape(width, width) for a in own]
        out_rows, pool_sum, input_grad, vec_grad, bias_sums, x_part, *grads = layer(
            n, layer_input, *own, vec_own, pool_grad, lengths, out_grad, up_moment, down_moment
        )
        factors = [
            step_factor(width, width),
            step_factor(width, hidden),
            step_factor(hidden, width),
        ]
        vector_step = vector_rate / math.sqrt(rows * n)
        if aligned:
            grad_qkv, grad_out, wide_bf, wide_in = grads
            attn_all, wide_all, vec_total, input_grad, attn_orth, wide_orth = muon(
                n, grad_qkv, grad_out, wide_in, bias_sums, vec_grad, attn_moment, wide_bf, x_part, input_grad
            )
            return tuple(
                finish(
                    n, out_rows, pool_sum, input_grad, attn_all, wide_all, attn_orth, wide_orth, vec_total,
                    attn_weight, up_weight, down_weight, vectors,
                    attn_moment, up_moment, down_moment, vector_moment, factors, vector_step,
                )
            )
        pooled = lax.dynamic_slice_in_dim(pool_sum, seq_index * quarter, quarter, 1)
        qkv_piece, out_piece, up_piece, down_piece = exchange(
            n, 2, "sum_grads", *[BatchSum(n, a.reshape(n, own_rows, -1)) for a in grads]
        )
        attn_piece = jnp.concatenate([qkv_piece, out_piece], axis=1)
        bias_sums = bias_sums.reshape(3, quarter)

        vec_head = jnp.zeros((2, SEQ, quarter), F32)
        vec_head = lax.dynamic_update_slice(
            vec_head, bias_sums[jnp.array([0, 2])][:, None], (0, seq_index, 0)
        ).reshape(2, width)
        vec_mid = vec_grad[:6]
        grad_bias_up = vec_grad[6]
        vec_tail = lax.dynamic_update_slice(
            jnp.zeros((n, SEQ, hid_own), F32),
            grad_bias_up.reshape(n, 1, hid_own),
            (0, seq_index, 0),
        ).reshape(-1, width)
        vec_local = jnp.concatenate([vec_head, vec_mid, vec_tail])
        vec_local = vec_local.reshape(-1, n, own_rows).transpose(1, 0, 2)
        (vec_piece,) = exchange(n, 7, "sum_vectors", ScatterBatch(n, vec_local, F32))
        attn_bf = attn_piece.astype(BF16).reshape(own_rows, 4, quarter).transpose(1, 0, 2)
        wide_bf = jnp.stack([up_piece, down_piece]).astype(BF16)
        attn_send = (matrix_decay * attn_quarter(attn_moment) + attn_bf.astype(F32)).astype(BF16)
        wide_moment = jnp.stack([up_quarter(up_moment), down_quarter(down_moment)])
        wide_send = (matrix_decay * wide_moment + wide_bf.astype(F32)).astype(BF16)
        short = -own_rows % 16
        attn_send = jnp.pad(attn_send, ((0, 0), (0, short), (0, 0)))
        wide_send = jnp.pad(wide_send, ((0, 0), (0, short), (0, 0)))
        attn_all, wide_all, vec_parts, attn_orth, wide_orth = exchange(
            n,
            8,
            "muon",
            GatherSeq(n, attn_bf),
            GatherSeq(n, wide_bf),
            GatherSeq(n, vec_piece),
            Muon(n, attn_send, wide_send),
        )
        attn_orth = attn_orth[:, :, :own_rows]
        wide_orth = wide_orth[:, :, :own_rows]

        def join_attn(parts):
            return parts.astype(F32).transpose(1, 2, 0, 3).reshape(4, own_rows, width)

        def join_up(parts):
            return (
                parts.astype(F32)
                .reshape(SEQ, own_rows, n, hid_own)
                .transpose(1, 2, 0, 3)
                .reshape(own_rows, hidden)
            )

        def join_down(parts):
            return parts.astype(F32).reshape(SEQ * hid_own, width)

        attn_grad = join_attn(attn_all)
        up_grad, down_grad = join_up(wide_all[:, 0]), join_down(wide_all[:, 1])
        vector_grad = (vec_parts[0] + vec_parts[1]) + (vec_parts[2] + vec_parts[3])
        attn_next = matrix_decay * attn_moment + attn_grad
        up_next = matrix_decay * up_moment + up_grad
        down_next = matrix_decay * down_moment + down_grad

        attn_new = attn_weight - factors[0] * join_attn(attn_orth)
        up_new = up_weight - factors[1] * join_up(wide_orth[:, 0])
        down_new = down_weight - factors[2] * join_down(wide_orth[:, 1])
        vector_next = vector_decay * vector_moment + vector_grad
        vectors_new = vectors - vector_step * vector_next
        return (
            out_rows,
            pooled,
            input_grad,
            attn_grad,
            up_grad,
            down_grad,
            vector_grad,
            attn_next,
            up_next,
            down_next,
            vector_next,
            attn_new,
            up_new,
            down_new,
            vectors_new,
        )

    return body


def solution(mesh):
    placed = (
        P("batch", "seq", None),
        P("batch"),
        P(None, "batch", None),
        P("batch", None),
        P("batch", None),
        P(None, "batch"),
        P(None, "batch", None),
        P("batch", None),
        P("batch", None),
        P(None, "batch"),
        P("batch", "seq", None),
        P("batch", "seq"),
    )
    return jax.shard_map(
        make_body(mesh.shape["batch"]),
        mesh=mesh,
        in_specs=placed,
        out_specs=(
            P("batch", "seq", None),
            P("batch", "seq"),
            P("batch", "seq", None),
            P(None, "batch", None),
            P("batch", None),
            P("batch", None),
            P(None, "batch"),
            P(None, "batch", None),
            P("batch", None),
            P("batch", None),
            P(None, "batch"),
            P(None, "batch", None),
            P("batch", None),
            P("batch", None),
            P(None, "batch"),
        ),
        check_vma=False,
    )
```

```python
import math
import types

import jax
import jax.numpy as jnp
from jax import lax
from jax.experimental import pallas as pl
from jax.experimental.pallas import tpu as pltpu
from jax.sharding import PartitionSpec as P

H = 12
HD = 64
NS = 5
SEQ = 4
HEADS = H // SEQ

norm_eps = 1e-12
tiny_norm = 1e-07
matrix_decay = 0.95
vector_decay = 0.5
matrix_rate = 0.5
vector_rate = 0.03

MESH = pl.DeviceIdType.MESH
F32 = jnp.float32
BF16 = jnp.bfloat16


def coords(n):
    b = lax.axis_index("batch")
    s = lax.axis_index("seq")
    return b, s, b // 2, b % 2, n // 2


def remote(src, dst, send, recv, device):
    return pltpu.make_async_remote_copy(
        src_ref=src, dst_ref=dst, send_sem=send, recv_sem=recv, device_id=device, device_id_type=MESH
    )


class GatherBatch:
    peers = ("batch",)

    def __init__(self, n, src, eager=True):
        self.n = n
        self.eager = eager
        self.ins = [src]
        self.outs = [jax.ShapeDtypeStruct((n,) + src.shape, src.dtype)]
        m = n // 2
        self.scratch = [pltpu.SemaphoreType.DMA((m,))] * 4 + [pltpu.SemaphoreType.DMA]

    def run(self, src, dst, zs, zr, ys, yr, own):
        b, s, hi, lo, m = coords(self.n)
        local = pltpu.make_async_copy(src, dst.at[b], own)
        local.start()
        pair = (hi * 2 + 1 - lo, s)
        out = []
        for d in range(1, m):
            c = remote(src, dst.at[b], zs.at[d], zr.at[d], (((hi + d) % m) * 2 + lo, s))
            c.start()
            out.append(c)
        first = remote(src, dst.at[b], ys.at[0], yr.at[0], pair)
        if self.eager:
            first.start()
        yield
        passed = [first]
        for d in range(1, m):
            if d == 1 and not self.eager:
                first.start()
            out[d - 1].wait_recv()
            block = ((hi + m - d) % m) * 2 + lo
            c = remote(dst.at[block], dst.at[block], ys.at[d], yr.at[d], pair)
            c.start()
            passed.append(c)
            yield
        local.wait()
        for c in passed:
            c.wait()
        for c in out:
            c.wait_send()


class GatherDirect:
    peers = ("all",)

    def __init__(self, n, src):
        self.n = n
        self.ins = [src]
        self.outs = [jax.ShapeDtypeStruct((n,) + src.shape, src.dtype)]
        self.scratch = [pltpu.SemaphoreType.DMA((n,))] * 2 + [pltpu.SemaphoreType.DMA]

    def run(self, src, dst, ss, rs, own):
        n = self.n
        b, s = lax.axis_index("batch"), lax.axis_index("seq")
        local = pltpu.make_async_copy(src, dst.at[b], own)
        local.start()
        copies = [
            remote(src, dst.at[b], ss.at[k], rs.at[k], ((b + k) % n, s)) for k in range(1, n)
        ]
        for c in copies:
            c.start()
        yield
        local.wait()
        for c in copies:
            c.wait()


class ScatterBatch:
    peers = ("batch",)

    def __init__(self, n, src, wire=BF16):
        self.n = n
        self.wire = wire
        self.ins = [src]
        shape = src.shape[1:]
        self.outs = [jax.ShapeDtypeStruct(shape, F32)]
        m = n // 2
        self.scratch = [pltpu.VMEM((m,) + shape, wire)] * 4 + [pltpu.SemaphoreType.DMA((m,))] * 4

    def run(self, src, dst, ysend, yrecv, zsend, zrecv, ys, yr, zs, zr):
        b, s, hi, lo, m = coords(self.n)
        pair = (hi * 2 + 1 - lo, s)
        first = {}
        order = list(range(1, m)) + [0]
        for d in order:
            h = (hi + d) % m
            ysend[d] = src[h * 2 + 1 - lo].astype(self.wire)
            first[d] = remote(ysend.at[d], yrecv.at[d], ys.at[d], yr.at[d], pair)
            first[d].start()
        yield
        second = []
        for d in range(1, m):
            h = (hi + d) % m
            first[d].wait_recv()
            zsend[d] = (src[h * 2 + lo] + yrecv[d].astype(F32)).astype(self.wire)
            c = remote(zsend.at[d], zrecv.at[d], zs.at[d], zr.at[d], (h * 2 + lo, s))
            c.start()
            second.append(c)
            yield
        first[0].wait_recv()
        total = src[b] + yrecv[0].astype(F32)
        for d in range(1, m):
            second[d - 1].wait_recv()
            total = total + zrecv[d].astype(F32)
        dst[...] = total
        for c in list(first.values()) + second:
            c.wait_send()


class GatherSeq:
    peers = ("seq",)

    def __init__(self, n, src):
        self.ins = [src]
        self.outs = [jax.ShapeDtypeStruct((SEQ,) + src.shape, src.dtype)]
        self.scratch = [pltpu.SemaphoreType.DMA((3,))] * 2 + [pltpu.SemaphoreType.DMA]

    def run(self, src, dst, ss, rs, own):
        b, s = lax.axis_index("batch"), lax.axis_index("seq")
        far, near = (s + 2) % 4, s + 1 - 2 * (s % 2)
        across = remote(src, dst.at[s], ss.at[0], rs.at[0], (b, far))
        across.start()
        local = pltpu.make_async_copy(src, dst.at[s], own)
        local.start()
        beside = remote(src, dst.at[s], ss.at[1], rs.at[1], (b, near))
        beside.start()
        yield
        across.wait_recv()
        passed = remote(dst.at[far], dst.at[far], ss.at[2], rs.at[2], (b, near))
        passed.start()
        yield
        local.wait()
        beside.wait()
        passed.wait()
        across.wait_send()


def owner_list(n):
    return [(0, 2), (1, 0), (n - 2, 2), (n - 1, 0), (n // 4, 0), (n // 2 + 1, 2)]


class OwnerMail:
    @staticmethod
    def scratch(n, count, relayed=None):
        dma = pltpu.SemaphoreType.DMA
        base = [dma((count,)), dma((SEQ * n,)), dma]
        if relayed is not None:
            base += [pltpu.VMEM((count,) + relayed, BF16), dma((count,)), dma((count,))]
        return base

    def __init__(self, n, places, inbox, ss, rs, own, relayed=None, relay_s=None, relay_r=None):
        self.n, self.places, self.inbox, self.ss, self.rs, self.own = n, places, inbox, ss, rs, own
        self.relayed, self.relay_s, self.relay_r = relayed, relay_s, relay_r
        self.b, self.s = lax.axis_index("batch"), lax.axis_index("seq")
        self.me = self.s * n + self.b
        self.mine = [(self.b == ob) & (self.s == os) for ob, os in places]

    def slot(self, seq, block):
        if len(self.inbox.shape) == 4:
            return self.inbox.at[seq, block]
        rows = self.inbox.shape[1] // self.n
        return self.inbox.at[seq, pl.ds(pl.multiple_of(block * rows, rows), rows)]

    def indirect(self, k):
        ob, os = self.places[k]
        other_plane = self.b // 2 != ob // 2
        corner = (self.b % 2 != ob % 2) & (self.s // 2 != os // 2)
        column = (self.b % 2 == ob % 2) & (self.s // 2 == os // 2)
        return other_plane & corner, other_plane & column

    def copy(self, k, src):
        ob, os = self.places[k]
        place = self.slot(self.s, self.b)
        return remote(src, place, self.ss.at[k], self.rs.at[self.me], (ob, os))

    def aside(self, k, src):
        across = self.b + 1 - 2 * (self.b % 2)
        return remote(
            src, self.relayed.at[k], self.ss.at[k], self.relay_r.at[k], (across, (self.s + 2) % 4)
        )

    def pass_copy(self, k):
        block, seq = self.b + 1 - 2 * (self.b % 2), (self.s + 2) % 4
        place = self.slot(seq, block)
        return remote(
            self.relayed.at[k], place, self.relay_s.at[k], self.rs.at[seq * self.n + block], self.places[k]
        )

    def send(self, k, src):
        direct = jnp.logical_not(self.mine[k])
        if self.relayed is not None:
            by_relay, _ = self.indirect(k)
            direct = direct & jnp.logical_not(by_relay)

            @pl.when(by_relay)
            def _():
                self.aside(k, src).start()

        @pl.when(direct)
        def _():
            self.copy(k, src).start()

        @pl.when(self.mine[k])
        def _():
            pltpu.make_async_copy(src, self.slot(self.s, self.b), self.own).start()

    def relay(self, k):
        @pl.when(self.indirect(k)[1])
        def _():
            place = self.relayed.at[k]
            remote(place, place, self.relay_s.at[k], self.relay_r.at[k], (0, 0)).wait_recv()
            self.pass_copy(k).start()

    def collect(self):
        place = self.slot(self.s, self.b)
        pltpu.make_async_copy(place, place, self.own).wait()

        @pl.loop(1, SEQ * self.n)
        def _(k):
            other = (self.me + k) % (SEQ * self.n)
            place = self.slot(other // self.n, other % self.n)
            remote(place, place, self.ss.at[0], self.rs.at[other], (0, 0)).wait_recv()

    def finish(self, k, src):
        @pl.when(jnp.logical_not(self.mine[k]))
        def _():
            self.copy(k, src).wait_send()

        if self.relayed is not None:

            @pl.when(self.indirect(k)[1])
            def _():
                self.pass_copy(k).wait_send()


class Muon:
    peers = ("all",)

    def __init__(self, n, attn_piece, wide_piece=None, wide_in=None):
        self.n = n
        self.ready = wide_in is not None
        self.ins = [attn_piece, wide_in if self.ready else wide_piece]
        width = self.ins[1].shape[-1]
        size = wide_in.shape[1] if self.ready else n * wide_piece.shape[1]
        rows = size // n
        attn_shape = attn_piece.shape[1:]
        self.outs = [
            jax.ShapeDtypeStruct((SEQ, 4) + attn_shape, BF16),
            jax.ShapeDtypeStruct((SEQ, 2, rows, width), BF16),
        ]
        dma = pltpu.SemaphoreType.DMA
        self.scratch = [
            pltpu.VMEM((SEQ, n) + attn_shape, BF16),
            pltpu.VMEM((SEQ, size, width), BF16),
            pltpu.VMEM((2, n // 2, rows, width), BF16),
            pltpu.VMEM((size, SEQ * size), F32),
            pltpu.VMEM((size, SEQ * size), BF16),
            pltpu.VMEM((size, size), F32),
            pltpu.VMEM((size, size), BF16),
            pltpu.VMEM((size, size), BF16),
            pltpu.VMEM((size, 1), F32),
            pltpu.VMEM((1, 1), F32),
            dma((SEQ * n,)),
            dma((6,)),
            dma((2, n // 2)),
            dma((2, n // 2)),
            dma((6, 3)),
            dma((6, 3)),
            dma,
            dma((SEQ,)),
        ]
        self.scratch += OwnerMail.scratch(n, 4)
        if not self.ready:
            self.scratch += OwnerMail.scratch(n, 2) + [pltpu.VMEM((SEQ, size, width), BF16)]

    def run(
        self, attn, wide, attn_orth, wide_orth, attn_in, wide_out, relayed, x32, xlow, gram, gram_low, poly, diag,
        norm, back_s, back_r, relay_s, relay_r, seq_s, seq_r, own, loads, *mails,
    ):
        n = self.n
        b, s, hi, lo, m = coords(n)
        far, near = (s + 2) % 4, s + 1 - 2 * (s % 2)
        me = s * n + b
        size = x32.shape[0]
        width = wide.shape[-1]
        quarter = width // SEQ
        places = owner_list(n)
        attn_mail = OwnerMail(n, places[:4], attn_in, *mails[:3])
        wide_in = wide
        if not self.ready:
            wide_in = mails[6]
            wide_mail = OwnerMail(n, places[4:], wide_in, *mails[3:6])
        mine = [(b == ob) & (s == os) for ob, os in places]
        number = jnp.int32(0)
        for k in range(6):
            number = jnp.where(mine[k], jnp.int32(k), number)
        is_attn = mine[0] | mine[1] | mine[2] | mine[3]
        is_wide = mine[4] | mine[5]

        if not self.ready:
            for k in range(2):
                wide_mail.send(k, wide.at[k])
        def send_attn():
            for k in range(4):
                attn_mail.send(k, attn.at[k])

        if self.ready:
            self.send_attn = send_attn
        else:
            send_attn()

        if not self.ready:
            for _ in range(4):
                yield


        def result(k):
            return attn_orth.at[s, k] if k < 4 else wide_orth.at[s, k - 4]

        def others(act):
            @pl.loop(1, SEQ * n)
            def _(k):
                other = (me + k) % (SEQ * n)
                act(other, other % n, other // n)

        def give_attn():
            pltpu.make_async_copy(attn_in.at[s, b], attn_orth.at[s, number], own).start()

            def act(other, ob, os):
                remote(
                    attn_in.at[os, ob], attn_orth.at[os, number], back_s.at[other], back_r.at[number], (ob, os)
                ).start()

            others(act)

        piece = OwnerMail(n, places, wide_out, None, None, None).slot

        def give_wide(piece):
            index = number - 4
            pltpu.make_async_copy(piece(s, b), wide_orth.at[s, index], own).start()

            def act(other, ob, os):
                oh, ol = ob // 2, ob % 2
                up = hi < m // 2
                away = jnp.where(up, oh - hi, hi - oh)
                relay = (away > 0) & (os // 2 != s // 2)
                stop = jnp.where(ol == lo, os, (os + 2) % 4)
                src = piece(os, ob)

                @pl.when(relay)
                def _():
                    slot = jnp.maximum(away - 1, 0)
                    remote(
                        src, relayed.at[index, slot], back_s.at[other], relay_r.at[index, slot],
                        (hi * 2 + ol, stop),
                    ).start()

                @pl.when(jnp.logical_not(relay))
                def _():
                    remote(
                        src, wide_orth.at[os, index], back_s.at[other], back_r.at[number], (ob, os)
                    ).start()

            others(act)

        def prepare():
            @pl.when(is_wide)
            def _():
                if not self.ready:
                    wide_mail.collect()
                if width != size:
                    xlow[...] = jnp.zeros(xlow.shape, BF16)

            @pl.when(mine[4])
            def _():
                copies = [
                    pltpu.make_async_copy(
                        wide_in.at[k], xlow.at[:, pl.ds(k * size, width)], loads.at[k]
                    )
                    for k in range(SEQ)
                ]
                for c in copies:
                    c.start()
                for c in copies:
                    c.wait()

            @pl.when(mine[5])
            def _():
                copies = [
                    pltpu.make_async_copy(wide_in.at[k], wide_out.at[k], loads.at[k]) for k in range(SEQ)
                ]
                for c in copies:
                    c.start()
                for k, c in enumerate(copies):
                    c.wait()
                    xlow[:width, k * size : (k + 1) * size] = wide_out[k].T

        def attn_turn():
            @pl.when(is_attn)
            def _():
                attn_mail.collect()
                span = SEQ * quarter
                short, line = attn_in.shape[2:]
                whole = [attn_in[k].reshape(n * short, line) for k in range(SEQ)]
                for k in range(line // quarter):
                    block = [a[:, k * quarter : (k + 1) * quarter] for a in whole]
                    xlow[k * n * short : (k + 1) * n * short, :span] = jnp.concatenate(block, axis=1)
                square_x, square_low = x32.at[:, pl.ds(0, span)], xlow.at[:, pl.ds(0, span)]

                def turn(first):
                    schulz_poly(square_low, gram, gram_low, poly, diag, norm, first)
                    schulz_move(square_x, square_low, poly, diag, norm, first)

                turn(True)

                @pl.loop(1, NS)
                def _(k):
                    turn(False)

                for k in range(SEQ):
                    block = xlow[:, k * quarter : (k + 1) * quarter]
                    if line > quarter:
                        block = fold(block)
                    attn_in[k] = block.reshape(attn_in.shape[1:])
                give_attn()

        if not self.ready:
            prepare()
        else:
            self.prepare, self.attn_turn = prepare, attn_turn
            yield

        for turn in range(NS):

            @pl.when(is_wide)
            def _(turn=turn):
                schulz_poly(xlow, gram, gram_low, poly, diag, norm, turn == 0)

            yield

            @pl.when(is_wide)
            def _(turn=turn):
                schulz_move(x32, xlow, poly, diag, norm, turn == 0)

            yield

        @pl.when(is_wide)
        def _():
            @pl.when(mine[4])
            def _():
                rows = size // n

                def part(seq, block):
                    return xlow.at[
                        pl.ds(pl.multiple_of(block * rows, rows), rows),
                        pl.ds(pl.multiple_of(seq * size, 128), width),
                    ]

                give_wide(part)

            @pl.when(mine[5])
            def _():
                for k in range(SEQ):
                    wide_out[k] = xlow[:width, k * size : (k + 1) * size].T
                give_wide(piece)

        def routes(k):
            ob, os = places[k]
            oh, ol = ob // 2, ob % 2
            same_x = s // 2 == os // 2
            here = (hi == oh) & (((lo == ol) & jnp.logical_not(same_x)) | ((lo != ol) & same_x))
            target = jnp.where(lo == ol, s, far)
            ahead = range(oh + 1, m) if oh < m // 2 else range(oh - 1, -1, -1)
            return here, target, list(enumerate(ahead))

        def relay_copy(k, slot, block, target):
            return remote(
                relayed.at[k - 4, slot], wide_orth.at[target, k - 4], relay_s.at[k - 4, slot], back_r.at[k],
                (block * 2 + lo, target),
            )

        def onward(k, step, source, target):
            out = attn_orth.at[source, k] if k < 4 else wide_orth.at[source, k - 4]
            return remote(out, out, seq_s.at[k, step], seq_r.at[k, step], (b, target))

        if not self.ready:
            attn_turn()
        done = (0, 1, 2, 3, 4, 5)

        def returned(k):
            @pl.when(jnp.logical_not(mine[k]))
            def _():
                remote(result(k), result(k), seq_s.at[k, 0], back_r.at[k], (0, 0)).wait_recv()

            @pl.when(mine[k])
            def _():
                pltpu.make_async_copy(result(k), result(k), own).wait()

            onward(k, 0, s, far).start()
            onward(k, 1, s, near).start()

        def passed(k):
            onward(k, 0, far, far).wait_recv()
            onward(k, 2, far, near).start()

        for k in (4, 5):
            here, target, ahead = routes(k)

            @pl.when(here)
            def _(k=k, target=target, ahead=ahead):
                for slot, block in ahead:
                    place = relayed.at[k - 4, slot]
                    remote(place, place, relay_s.at[0, 0], relay_r.at[k - 4, slot], (0, 0)).wait_recv()
                    relay_copy(k, slot, block, target).start()

        for k in done[:4]:
            returned(k)
        for k in done[:4]:
            passed(k)
        for k in done[4:]:
            returned(k)
        for k in done[4:]:
            passed(k)
        for k in done:
            onward(k, 1, near, near).wait_recv()
            onward(k, 2, (near + 2) % 4, near).wait_recv()
            onward(k, 0, s, far).wait_send()
            onward(k, 1, s, near).wait_send()
            onward(k, 2, far, near).wait_send()
        for k in range(4):
            attn_mail.finish(k, attn.at[k])
        if not self.ready:
            for k in range(2):
                wide_mail.finish(k, wide.at[k])
        for k in (4, 5):
            here, target, ahead = routes(k)

            @pl.when(here)
            def _(k=k, target=target, ahead=ahead):
                for slot, block in ahead:
                    relay_copy(k, slot, block, target).wait_send()

        def given(buf):
            def act(other, ob, os):
                place = buf.at[os, ob] if len(buf.shape) == 4 else piece(os, ob)
                remote(place, place, back_s.at[other], back_r.at[0], (0, 0)).wait_send()

            others(act)

        @pl.when(is_attn)
        def _():
            given(attn_in)

        @pl.when(is_wide)
        def _():
            given(wide_out)


def schulz_poly(xlow, gram, gram_low, poly, diag, norm, first):
    size = xlow.shape[0]
    side = 256
    tiles = [slice(k, k + side) for k in range(0, size, side)]
    eye = lax.broadcasted_iota(jnp.int32, (side, side), 0) == lax.broadcasted_iota(
        jnp.int32, (side, side), 1
    )
    for j in tiles:
        gram[j.start :, j] = contract_last(xlow[j.start :, :], xlow[j, :])
    if first:
        total = jnp.zeros((1, 1), F32)
        for j in tiles:
            total = total + jnp.sum(jnp.where(eye, gram[j, j], 0.0), keepdims=True)
        inverse = 1.0 / (jnp.sqrt(total) + tiny_norm)
        norm[...] = inverse
        for j in tiles:
            gram[j.start :, j] = gram[j.start :, j] * (inverse * inverse)
    down, along = [], []
    for j in tiles:
        block = gram[j, j]
        on_diag = jnp.where(eye, block, 0.0)
        down.append(jnp.sum(on_diag, axis=1, keepdims=True))
        along.append(jnp.sum(on_diag, axis=0, keepdims=True))
        gram_low[j, j] = jnp.where(eye, 0.0, block).astype(BF16)
        for i in tiles:
            if i.start > j.start:
                block = gram[i, j]
                gram_low[i, j] = block.astype(BF16)
                gram_low[j, i] = block.T.astype(BF16)
    for j, right in zip(tiles, along):
        square = matmul(gram_low[j.start :, :], gram_low[:, j])
        for i, left in zip(tiles, down):
            if i.start < j.start:
                continue
            part = square[i.start - j.start : i.stop - j.start]
            factor = (2.0315 * left - 4.775) + 2.0315 * right
            block = 2.0315 * part + factor * gram[i, j]
            if i == j:
                value = jnp.sum(jnp.where(eye, 2.0315 * part, 0.0), axis=1, keepdims=True)
                diag[i] = value + (3.4445 + (2.0315 * left - 4.775) * left)
                poly[i, i] = jnp.where(eye, 0.0, block).astype(BF16)
            else:
                poly[i, j] = block.astype(BF16)
                poly[j, i] = block.T.astype(BF16)


def schulz_move(x32, xlow, poly, diag, norm, first):
    wide = x32.shape[1]
    chunk = 768 if wide % 768 == 0 else 512
    for c in range(0, wide, chunk):
        part = slice(c, c + chunk)
        if first:
            moved = (diag[...] * norm[...]) * xlow[:, part].astype(F32)
            moved = moved + matmul(poly[...], xlow[:, part]) * norm[...]
        else:
            moved = diag[...] * x32[:, part] + matmul(poly[...], xlow[:, part])
        x32[:, part] = moved
        xlow[:, part] = moved.astype(BF16)


def greet_peers(n, kinds):
    b, s, hi, lo, m = coords(n)
    peers = []
    if "seq" in kinds:
        peers += [(b, (s + k) % 4) for k in (1, 2, 3)]
    if "batch" in kinds:
        peers += [(((hi + d) % m) * 2 + lo, s) for d in range(1, m)]
        peers += [(hi * 2 + 1 - lo, s)]
    return peers


def greet_signal(n, kinds):
    b, s = lax.axis_index("batch"), lax.axis_index("seq")
    barrier = pltpu.get_barrier_semaphore()
    if "all" in kinds:
        me = s * n + b

        @pl.loop(1, SEQ * n)
        def _(k):
            other = (me + k) % (SEQ * n)
            pl.semaphore_signal(
                barrier, inc=1, device_id=(other % n, other // n), device_id_type=MESH
            )

        return
    for peer in greet_peers(n, kinds):
        pl.semaphore_signal(barrier, inc=1, device_id=peer, device_id_type=MESH)


def greet_wait(n, kinds):
    count = SEQ * n - 1 if "all" in kinds else len(greet_peers(n, kinds))
    pl.semaphore_wait(pltpu.get_barrier_semaphore(), count)


def greet(n, kinds):
    greet_signal(n, kinds)
    greet_wait(n, kinds)


def run_together(*live):
    live = list(live)
    while live:
        still = []
        for op in live:
            try:
                next(op)
                still.append(op)
            except StopIteration:
                pass
        live = still


def exchange(n, collective_id, name, *ops):
    ins = [a for op in ops for a in op.ins]
    outs = [o for op in ops for o in op.outs]
    scratch = [c for op in ops for c in op.scratch]
    kinds = {k for op in ops for k in op.peers}

    def kernel(*refs):
        in_refs, out_refs = refs[: len(ins)], refs[len(ins) : len(ins) + len(outs)]
        scratch_refs = refs[len(ins) + len(outs) :]
        greet(n, kinds)
        live = []
        i = o = c = 0
        for op in ops:
            ni, no, nc = len(op.ins), len(op.outs), len(op.scratch)
            live.append(
                op.run(*in_refs[i : i + ni], *out_refs[o : o + no], *scratch_refs[c : c + nc])
            )
            i, o, c = i + ni, o + no, c + nc
        run_together(*live)

    vmem = pl.BlockSpec(memory_space=pltpu.VMEM)
    return pl.pallas_call(
        kernel,
        out_shape=outs,
        in_specs=[vmem] * len(ins),
        out_specs=[vmem] * len(outs),
        scratch_shapes=scratch,
        compiler_params=pltpu.CompilerParams(
            collective_id=collective_id, has_side_effects=True, vmem_limit_bytes=60 * 2**20
        ),
        name=name,
    )(*ins)


def contract_last(left, right):
    return lax.dot_general(left, right, (((1,), (1,)), ((), ())), preferred_element_type=F32)


def contract_first(left, right):
    return lax.dot_general(left, right, (((0,), (0,)), ((), ())), preferred_element_type=F32)


def matmul(left, right):
    return jnp.dot(left, right, preferred_element_type=F32)


def exact_gelu(value_in):
    return jax.nn.gelu(value_in, approximate=False)


def normalize(hidden, gain_row):
    row_mean = jnp.mean(hidden, axis=-1, keepdims=True)
    centred = hidden - row_mean
    spread = lax.rsqrt(jnp.mean(centred * centred, axis=-1, keepdims=True) + norm_eps)
    scaled = centred * spread
    return (scaled * gain_row, scaled, spread)


def normalize_back(grad_in, scaled, spread, gain_row):
    weighted = grad_in * gain_row
    mean_first = jnp.mean(weighted, axis=-1, keepdims=True)
    second = jnp.mean(weighted * scaled, axis=-1, keepdims=True)
    return (
        spread * (weighted - mean_first - scaled * second),
        jnp.sum(grad_in * scaled, axis=0),
        jnp.sum(grad_in, axis=0),
    )


class RowGather:
    @staticmethod
    def scratch():
        return [pltpu.SemaphoreType.DMA((2, 3)), pltpu.SemaphoreType.DMA((2, 3))]

    def __init__(self, buf, ss, rs):
        self.buf, self.ss, self.rs = buf, ss, rs
        self.b, self.s = lax.axis_index("batch"), lax.axis_index("seq")
        self.far, self.near = (self.s + 2) % 4, self.s + 1 - 2 * (self.s % 2)
        self.diag = (self.near + 2) % 4

    def copy(self, r, step, block, device):
        place = self.buf.at[r, block]
        return remote(place, place, self.ss.at[r, step], self.rs.at[r, step], (self.b, device))

    def start(self, r):
        self.copy(r, 0, self.s, self.far).start()
        self.copy(r, 1, self.s, self.near).start()

    def wait_near(self, r):
        self.copy(r, 1, self.near, self.near).wait_recv()

    def pass_far(self, r):
        self.copy(r, 0, self.far, self.far).wait_recv()
        self.copy(r, 2, self.far, self.near).start()

    def wait_diag(self, r):
        self.copy(r, 2, self.diag, self.near).wait_recv()

    def finish(self, r):
        self.copy(r, 0, self.s, self.far).wait_send()
        self.copy(r, 1, self.s, self.near).wait_send()
        self.copy(r, 2, self.far, self.near).wait_send()


def gelu_parts(value):
    cdf = 0.5 * (1.0 + lax.erf(value * math.sqrt(0.5)))
    density = jnp.exp(-0.5 * value * value) * (1.0 / math.sqrt(2.0 * math.pi))
    return value * cdf, cdf + value * density


def row_sum(value):
    return jnp.sum(value, axis=0, keepdims=True)


class RowSwap:
    @staticmethod
    def scratch(shape):
        return [
            pltpu.VMEM(shape, BF16),
            pltpu.VMEM(shape, BF16),
            pltpu.SemaphoreType.DMA((2, 4)),
            pltpu.SemaphoreType.DMA((2, 4)),
        ]

    def __init__(self, src, dst, ss, rs):
        self.src, self.dst, self.ss, self.rs = src, dst, ss, rs
        self.b, self.s = lax.axis_index("batch"), lax.axis_index("seq")

    def copy(self, r, k):
        other = (self.s + k) % 4
        return remote(
            self.src.at[other, r], self.dst.at[self.s, r], self.ss.at[r, k], self.rs.at[r, k],
            (self.b, other),
        )

    def start(self, r):
        for k in (2, 3, 1):
            self.copy(r, k).start()
        self.dst[self.s, r] = self.src[self.s, r]

    def wait(self, r):
        for k in (2, 3, 1):
            self.copy(r, k).wait_recv()

    def finish(self, r):
        for k in (2, 3, 1):
            self.copy(r, k).wait_send()


def fold(value):
    half = value.shape[0] // 2
    return jnp.concatenate([value[:half], value[half:]], axis=1)


def unfold(value):
    half = value.shape[1] // 2
    return jnp.concatenate([value[:, :half], value[:, half:]], axis=0)


def rounds(count):
    for _ in range(count):
        yield


def spaced(op, count):
    for _ in op:
        yield from rounds(count)


def step(op):
    try:
        next(op)
    except StopIteration:
        pass


def drain(op):
    for _ in op:
        pass


class DirectSum:
    peers = ("all",)

    def __init__(self, n, src):
        self.n = n
        self.scratch = [pltpu.VMEM(src.shape, F32)] + [pltpu.SemaphoreType.DMA((n,))] * 2

    def run(self, src, dst, arrived, ss, rs):
        n = self.n
        b, s = lax.axis_index("batch"), lax.axis_index("seq")
        copies = []
        for k in range(1, n):
            to = (b + k) % n
            copies.append(remote(src.at[to], arrived.at[k], ss.at[k], rs.at[k], (to, s)))
            copies[-1].start()
        yield
        total = src[b]
        for k, c in enumerate(copies):
            c.wait()
            total = total + arrived[k + 1]
        dst[...] = total


class BatchSum:
    peers = ("batch",)

    def __init__(self, n, src):
        self.n = n
        self.ins = [src]
        shape = src.shape[1:]
        self.outs = [jax.ShapeDtypeStruct(shape, F32)]
        m = n // 2
        self.scratch = [pltpu.VMEM((m,) + shape, BF16)] * 3 + [pltpu.SemaphoreType.DMA((m,))] * 4

    def run(self, src, dst, yrecv, zsend, zrecv, ys, yr, zs, zr):
        b, s, hi, lo, m = coords(self.n)
        pair = (hi * 2 + 1 - lo, s)
        first = {}
        for d in list(range(1, m)) + [0]:
            block = ((hi + d) % m) * 2 + 1 - lo
            first[d] = remote(src.at[block], yrecv.at[d], ys.at[d], yr.at[d], pair)
            first[d].start()
        yield
        second = []
        for d in range(1, m):
            h = (hi + d) % m
            first[d].wait_recv()
            zsend[d] = (src[h * 2 + lo].astype(F32) + yrecv[d].astype(F32)).astype(BF16)
            c = remote(zsend.at[d], zrecv.at[d], zs.at[d], zr.at[d], (h * 2 + lo, s))
            c.start()
            second.append(c)
            yield
        first[0].wait_recv()
        total = src[b].astype(F32) + yrecv[0].astype(F32)
        for d in range(1, m):
            second[d - 1].wait_recv()
            total = total + zrecv[d].astype(F32)
        dst[...] = total
        for c in list(first.values()) + second:
            c.wait_send()


class RowSum:
    @staticmethod
    def scratch(rows, shape):
        return [
            pltpu.VMEM((rows, 2) + shape, BF16),
            pltpu.VMEM((rows,) + shape, BF16),
            pltpu.VMEM((rows,) + shape, BF16),
            pltpu.SemaphoreType.DMA((rows, 3)),
            pltpu.SemaphoreType.DMA((rows, 3)),
        ]

    def __init__(self, src, near_in, far_out, far_in, ss, rs):
        self.src, self.near_in, self.far_out, self.far_in, self.ss, self.rs = (
            src, near_in, far_out, far_in, ss, rs,
        )
        self.b, self.s = lax.axis_index("batch"), lax.axis_index("seq")
        self.far, self.near = (self.s + 2) % 4, self.s + 1 - 2 * (self.s % 2)
        self.diag = (self.near + 2) % 4

    def beside(self, r, k):
        block = self.diag if k else self.near
        return remote(
            self.src.at[r, block], self.near_in.at[r, k], self.ss.at[r, k], self.rs.at[r, k],
            (self.b, self.near),
        )

    def across(self, r):
        return remote(
            self.far_out.at[r], self.far_in.at[r], self.ss.at[r, 2], self.rs.at[r, 2],
            (self.b, self.far),
        )

    def send_near(self, r):
        self.beside(r, 0).start()

    def send_diag(self, r):
        self.beside(r, 1).start()

    def cross(self, r):
        self.beside(r, 1).wait_recv()
        part = self.src[r, self.far].astype(F32) + self.near_in[r, 1].astype(F32)
        self.far_out[r] = part.astype(BF16)
        self.across(r).start()

    def total(self, r):
        self.beside(r, 0).wait_recv()
        part = self.src[r, self.s].astype(F32) + self.near_in[r, 0].astype(F32)
        self.across(r).wait_recv()
        return part + self.far_in[r].astype(F32)

    def finish(self, r):
        self.beside(r, 0).wait_send()
        self.beside(r, 1).wait_send()
        self.across(r).wait_send()


class Scratch:
    def __init__(self):
        self.names, self.shapes = [], []

    def add(self, **named):
        for name, shapes in named.items():
            one = not isinstance(shapes, list)
            shapes = [shapes] if one else shapes
            self.names.append((name, len(shapes), one))
            self.shapes += shapes

    def refs(self, refs):
        out, i = types.SimpleNamespace(), 0
        for name, count, one in self.names:
            setattr(out, name, refs[i] if one else refs[i : i + count])
            i += count
        return out


def layer(
    n, tokens, attn_weight, up_weight, down_weight, vec_own, pool_own, lengths, out_grad, up_moment, down_moment
):
    rows, span, width = tokens.shape
    quarter = width // SEQ
    span_all = span * SEQ
    own_rows = width // n
    local = rows * span
    aligned = own_rows % 16 == 0
    scale = HD**-0.5
    shape = jax.ShapeDtypeStruct
    full = (rows, SEQ, span, width)
    widths = (3 * quarter, quarter, width, width)
    low_ops = [GatherBatch(n, shape((own_rows, c), BF16), k == 0) for k, c in enumerate(widths)]
    low_ops = low_ops if aligned else []
    vec_op = GatherDirect(n, vec_own) if aligned else GatherBatch(n, vec_own)
    pool_op = GatherSeq(n, pool_own)
    out_op = GatherSeq(n, shape((width, quarter), BF16))
    sum_ops = [BatchSum(n, shape((n, own_rows, width), BF16)) for _ in range(2)]

    outs = [
        shape((rows, span, width), F32),
        shape((rows, width), F32),
        shape((rows, span, width), F32),
        shape((8, width), F32),
        shape((1, 3 * quarter), F32),
        shape(full, BF16),
    ]
    vmem = pl.BlockSpec(memory_space=pltpu.VMEM)
    anywhere = pl.BlockSpec(memory_space=pl.ANY)
    if aligned:
        outs += [shape((n, own_rows, width), BF16)]
        outs += [shape((2, own_rows, width), BF16), shape((SEQ, width, width), BF16)]
        out_specs = [vmem] * 8 + [anywhere]
    else:
        outs += [shape((width, width), BF16)] * 3
        out_specs = [vmem] * 9

    dma = pltpu.SemaphoreType.DMA
    sc = Scratch()
    if aligned:
        sc.add(
            lows=[pltpu.VMEM((own_rows, c), BF16) for c in widths],
            weights=[pltpu.VMEM(op.outs[0].shape, BF16) for op in low_ops],
            low_moves=[c for op in low_ops for c in op.scratch],
        )
    sc.add(vec_parts=pltpu.VMEM(vec_op.outs[0].shape, F32))
    sc.add(vec_move=vec_op.scratch)
    sc.add(vec=pltpu.VMEM((8, width), F32))
    sc.add(pool_parts=pltpu.VMEM(pool_op.outs[0].shape, F32))
    sc.add(pool_move=pool_op.scratch)
    sc.add(out_own=pltpu.VMEM((width, quarter), BF16))
    sc.add(out_parts=pltpu.VMEM((SEQ, width, quarter), BF16))
    sc.add(out_move=out_op.scratch)
    sc.add(w_out=pltpu.VMEM((width, width), BF16))
    sc.add(x_all=pltpu.VMEM(full, BF16))
    sc.add(x_gather=RowGather.scratch())
    sc.add(qkv=pltpu.VMEM((rows, span_all, 3 * quarter), BF16))
    sc.add(prob=pltpu.VMEM((rows, HEADS, span_all, span_all), F32))
    sc.add(swap=RowSwap.scratch((SEQ, rows, span, quarter)))
    sc.add(back_swap=RowSwap.scratch((SEQ, rows, span, quarter)))
    sc.add(context=pltpu.VMEM((rows, span, width), BF16))
    sc.add(normed=pltpu.VMEM((rows, span, width), F32))
    sc.add(scaled_one=pltpu.VMEM((rows, span, width), F32))
    sc.add(spread_one=pltpu.VMEM((rows, span, 1), F32))
    sc.add(y_all=pltpu.VMEM(full, BF16))
    sc.add(y_gather=RowGather.scratch())
    sc.add(slope=pltpu.VMEM(full, F32))
    sc.add(act=pltpu.VMEM(full, BF16))
    sc.add(z_sum=RowSum.scratch(rows, (span, width)))
    sc.add(dz_all=pltpu.VMEM(full, BF16))
    sc.add(dz_gather=RowGather.scratch())
    sc.add(du_all=pltpu.VMEM(full, BF16))
    sc.add(dy_sum=RowSum.scratch(rows, (span, width)))
    sc.add(pool_buf=pltpu.VMEM((SEQ, rows, width), F32))
    sc.add(pool_sems=[dma((3,)), dma((3,))])
    sc.add(a_quarters=pltpu.VMEM((SEQ, local, quarter), BF16))
    sc.add(out_part=pltpu.VMEM((1, SEQ, width, quarter), BF16))
    sc.add(out_sum=RowSum.scratch(1, (width, quarter)))
    if not aligned:
        sc.add(x_sum=RowSum.scratch(rows, (span, width)))
    sc.add(grad_qkv=pltpu.VMEM((rows, span_all, 3 * quarter), BF16))
    if aligned:
        sc.add(raw=dma((2 * SEQ + 1,)))
        sc.add(
            down_grad=pltpu.VMEM((n, own_rows, width), BF16),
            up_grad=pltpu.VMEM((n, own_rows, width), BF16),
            down_piece=pltpu.VMEM((own_rows, width), F32),
            up_piece=pltpu.VMEM((own_rows, width), F32),
            down_sum=sum_ops[0].scratch,
            up_sum=sum_ops[1].scratch,
        )
        sc.add(vec_low=pltpu.VMEM(vec_own.shape, F32))
        sc.add(wide_send=pltpu.VMEM((2, own_rows, width), BF16))
        sc.add(mail=OwnerMail.scratch(n, 2, (own_rows, width)))

    def kernel(
        tokens, attn_weight, up_weight, down_weight, vec_own, pool_own, lengths, out_grad, up_moment, down_moment,
        out_rows, pooled, second, vec_grad, bias_sums, part, grad_attn, *rest,
    ):
        if aligned:
            wide_bf, wide_in = rest[:2]
            rest = rest[2:]
        else:
            grad_up_out, grad_down_out = rest[:2]
            rest = rest[2:]
        at = sc.refs(rest)
        kinds = {"all"} if aligned else {"seq", "batch"}
        greet_signal(n, kinds)
        b, s = lax.axis_index("batch"), lax.axis_index("seq")
        x_all, y_all, dz_all, du_all = at.x_all, at.y_all, at.dz_all, at.du_all
        slope, act, prob, qkv = at.slope, at.act, at.prob, at.qkv
        normed, context, vec = at.normed, at.context, at.vec
        x_gather = RowGather(x_all, *at.x_gather)
        y_gather = RowGather(y_all, *at.y_gather)
        dz_gather = RowGather(dz_all, *at.dz_gather)
        swap, back_swap = RowSwap(*at.swap), RowSwap(*at.back_swap)
        z_sum, dy_sum = [RowSum(part, *refs) for refs in (at.z_sum, at.dy_sum)]
        out_sum = RowSum(at.out_part, *at.out_sum)
        far, near, diag = x_gather.far, x_gather.near, x_gather.diag

        def raw_block(k):
            return slope.at[k // SEQ, k % SEQ, pl.ds(0, own_rows)]

        def load_up(matrix):
            return [
                pltpu.make_async_copy(
                    matrix.at[:, pl.ds(k * width, width)], raw_block(SEQ + k), at.raw.at[SEQ + k]
                )
                for k in range(SEQ)
            ]

        def load_down(matrix, place):
            return pltpu.make_async_copy(
                matrix.at[pl.ds(s * own_rows, own_rows)], place, at.raw.at[2 * SEQ]
            )

        def raw_up(k):
            whole = jnp.concatenate([raw_block(SEQ + j)[...] for j in range(SEQ)], axis=1)
            return take_up(whole, n, k)

        if aligned:
            raws = [
                pltpu.make_async_copy(attn_weight.at[k], raw_block(k), at.raw.at[k]) for k in range(4)
            ]
            raws += load_up(up_weight)
            raws.append(load_down(down_weight, second.at[0, pl.ds(0, own_rows)]))
            for c in raws:
                c.start()
        for r in range(rows):
            x_all[r, s] = tokens[r].astype(BF16)
        if aligned:
            for c in raws[:4]:
                c.wait()
            for k in range(SEQ):

                @pl.when(s == k)
                def _(k=k):
                    block = [raw_block(j)[:, k * quarter : (k + 1) * quarter] for j in range(4)]
                    at.lows[0][...] = jnp.concatenate(block[:3], axis=1).astype(BF16)
                    at.lows[1][...] = block[3].astype(BF16)

            vec_low = at.vec_low
            vec_low[...] = vec_own[...].astype(BF16).astype(F32)
        else:
            vec_low = vec_own

        greet_wait(n, kinds)
        vec_move = vec_op.run(vec_low, at.vec_parts, *at.vec_move)
        pool_move = pool_op.run(pool_own, at.pool_parts, *at.pool_move)
        step(vec_move)
        if aligned:
            moves = [
                op.run(at.lows[k], at.weights[k], *at.low_moves[5 * k : 5 * k + 5])
                for k, op in enumerate(low_ops)
            ]
            step(moves[0])
        step(pool_move)
        for r in range(rows):
            x_gather.start(r)
        if aligned:
            for c in raws[4:]:
                c.wait()
            for k in range(SEQ):

                @pl.when(s == k)
                def _(k=k):
                    at.lows[2][...] = raw_up(k).astype(BF16)

            at.lows[3][...] = second[0, :own_rows].astype(BF16)
            step(moves[0])
        x_gather.pass_far(0)
        if aligned:
            step(moves[0])
        step(pool_move)
        x_gather.pass_far(1)
        if aligned:
            step(moves[0])
            step(moves[1])
            step(moves[2])
        drain(vec_move)
        drain(pool_move)
        if aligned:
            whole = jnp.concatenate([at.vec_parts[k] for k in range(n)], axis=1)

            def here(make):
                return sum(jnp.where(s == k, make(k), 0.0) for k in range(SEQ))

            vec[0:6] = whole[2:8]
            vec[6:7] = here(
                lambda k: jnp.concatenate(
                    [
                        whole[8 + f // width : 9 + f // width, f % width : f % width + own_rows]
                        for f in ((j * SEQ + k) * own_rows for j in range(n))
                    ],
                    axis=1,
                )
            )
            blank = jnp.zeros((1, quarter), F32)
            vec[7:8] = here(
                lambda k: jnp.concatenate(
                    [
                        whole[0:1, k * quarter : (k + 1) * quarter],
                        blank,
                        whole[1:2, k * quarter : (k + 1) * quarter],
                        blank,
                    ],
                    axis=1,
                )
            )
        else:
            total = at.vec_parts[0]
            for k in range(1, n):
                total = total + at.vec_parts[k]
            vec[...] = total
        pool_whole = jnp.concatenate([at.pool_parts[k] for k in range(SEQ)], axis=1)

        if aligned:
            drain(moves[0])
            step(moves[3])

        def w_qkv():
            if aligned:
                return at.weights[0][...].reshape(width, 3 * quarter)
            return attn_weight[:, : 3 * quarter]

        def w_up():
            return at.weights[2][...].reshape(width, width) if aligned else up_weight[...]

        def w_down():
            return at.weights[3][...].reshape(width, width) if aligned else down_weight[...]

        out_move = out_op.run(at.out_own, at.out_parts, *at.out_move)

        def begin_out():
            if aligned:
                drain(moves[1])
                at.out_own[...] = at.weights[1][...].reshape(width, quarter)
            else:
                at.out_own[...] = attn_weight[:, 3 * quarter :]
            step(out_move)

        def turn(*ks):
            for k in ks:
                if aligned:
                    step(moves[k])

        bias = vec[7:8, : 3 * quarter]
        column = lax.broadcasted_iota(jnp.int32, (1, span_all), 1)

        def heads(r, h):
            return [
                qkv[r, :, k * quarter + h * HD : k * quarter + (h + 1) * HD] for k in range(3)
            ]

        for r in range(rows):
            x_gather.wait_near(r)
            x_gather.wait_diag(r)
            block = matmul(x_all[r].reshape(span_all, width), w_qkv()) + bias
            qkv[r] = block.astype(BF16)
            valid = column < lengths[r]
            mixed = []
            for h in range(HEADS):
                query, key, value = heads(r, h)
                scores = contract_last(query * jnp.bfloat16(scale), key)
                scores = jnp.where(valid, scores, -1e30)
                exponent = jnp.exp(scores - jnp.max(scores, axis=-1, keepdims=True))
                weight = exponent * (1.0 / jnp.sum(exponent, axis=-1, keepdims=True))
                prob[r, h] = weight
                mixed.append(matmul(weight.astype(BF16), value))
                if r == 0 and h == 0:
                    turn(1, 1, 1)
                if r == 0 and h == 1:
                    begin_out()
                if r == 0 and h > 0:
                    turn(2)
                if r == 1 and h == 0:
                    turn(2)
                if r == 1 and h > 0:
                    turn(3)
            mixed = jnp.concatenate(mixed, axis=1).astype(BF16)
            for k in range(SEQ):
                at.swap[0][k, r] = mixed[k * span : (k + 1) * span]
            swap.start(r)
        step(out_move)
        turn(3)
        drain(out_move)
        w_out = at.w_out
        w_out[...] = jnp.concatenate([at.out_parts[k] for k in range(SEQ)], axis=1)
        gain_one, shift_one = vec[1:2], vec[2:3]
        for r in range(rows):
            swap.wait(r)
            context[r] = jnp.concatenate([at.swap[1][k, r] for k in range(SEQ)], axis=1)
            hidden = tokens[r] + (matmul(context[r], w_out[...]) + vec[0:1])
            centred = hidden - jnp.mean(hidden, axis=-1, keepdims=True)
            spread = lax.rsqrt(jnp.mean(centred * centred, axis=-1, keepdims=True) + norm_eps)
            scaled = centred * spread
            at.scaled_one[r] = scaled
            at.spread_one[r] = spread
            value = scaled * gain_one + shift_one
            normed[r] = value
            y_all[r, s] = value.astype(BF16)
            y_gather.start(r)

        if aligned:
            turn(3)
            drain(moves[2])
        gain_two, shift_two = vec[3:4], vec[4:5]
        bias_down, bias_up = vec[5:6], vec[6:7]

        def pair(ref, blocks):
            return jnp.concatenate([ref[i] for i in blocks], axis=0)

        def put(ref, blocks, value):
            for k, i in enumerate(blocks):
                ref[i] = value[k * span : (k + 1) * span].astype(ref.dtype)

        def rise(blocks):
            value, rate = gelu_parts(matmul(pair(y_all, blocks), w_up()) + bias_up)
            put(act, blocks, value)
            put(slope, blocks, rate)

        def fall(blocks):
            put(part, blocks, matmul(pair(act, blocks), w_down()))

        mine, beside = [[(r, k) for r in range(rows)] for k in (s, near)]
        rise(mine)
        for r in range(rows):
            y_gather.wait_near(r)
        rise(beside)
        turn(3)
        others = [[(r, diag), (r, far)] for r in range(rows)]
        for r in range(rows):
            y_gather.pass_far(r)
            y_gather.wait_diag(r)
            rise(others[r])
        if aligned:
            drain(moves[3])
        fall(beside)
        for r in range(rows):
            z_sum.send_near(r)
        for r in range(rows):
            fall(others[r])
            z_sum.send_diag(r)
            if r > 0:
                z_sum.cross(r - 1)
        fall(mine)
        z_sum.cross(rows - 1)

        position = s * span + lax.broadcasted_iota(jnp.int32, (span, 1), 0)
        grad_gain_two = grad_shift_two = grad_bias_down = jnp.zeros((1, width), F32)
        for r in range(rows):
            hidden = normed[r] + (z_sum.total(r) + bias_down)
            centred = hidden - jnp.mean(hidden, axis=-1, keepdims=True)
            spread_two = lax.rsqrt(jnp.mean(centred * centred, axis=-1, keepdims=True) + norm_eps)
            scaled = centred * spread_two
            output = scaled * gain_two + shift_two
            out_rows[r] = output
            live = (position < lengths[r]).astype(F32)
            length = jnp.full((1, 1), lengths[r], jnp.int32).astype(F32)
            at.pool_buf[s, r : r + 1] = row_sum(output * live) / length
            upstream = live * (out_grad[r] + pool_whole[r : r + 1] / length)
            weighted = upstream * gain_two
            mean_first = jnp.mean(weighted, axis=-1, keepdims=True)
            mean_second = jnp.mean(weighted * scaled, axis=-1, keepdims=True)
            grad = spread_two * (weighted - mean_first - scaled * mean_second)
            second[r] = grad
            low = grad.astype(BF16)
            dz_all[r, s] = low
            dz_gather.start(r)
            grad_gain_two += row_sum(upstream * scaled)
            grad_shift_two += row_sum(upstream)
            grad_bias_down += row_sum(low.astype(F32))

        def pool_copy(k, block, device):
            place = at.pool_buf.at[block]
            sems = at.pool_sems
            return remote(place, place, sems[0].at[k - 1], sems[1].at[k - 1], (b, device))

        for k in (1, 2, 3):
            pool_copy(k, s, (s + k) % 4).start()
        for r in range(rows):
            z_sum.finish(r)

        def backward(blocks):
            lift = contract_last(pair(dz_all, blocks), w_down())
            low = (lift * pair(slope, blocks)).astype(BF16)
            put(du_all, blocks, low)
            put(part, blocks, contract_last(low, w_up()))
            return row_sum(low.astype(F32))

        bias_grad = backward(mine)
        for r in range(rows):
            dz_gather.wait_near(r)
        bias_grad += backward(beside)
        for r in range(rows):
            dy_sum.send_near(r)
        for r in range(rows):
            dz_gather.pass_far(r)
            dz_gather.wait_diag(r)
            bias_grad += backward([(r, diag), (r, far)])
            dy_sum.send_diag(r)
            dy_sum.cross(r)

        flat = rows * span_all
        if aligned:
            down_move = sum_ops[0].run(at.down_grad, at.down_piece, *at.down_sum)
            up_move = sum_ops[1].run(at.up_grad, at.up_piece, *at.up_sum)
            mail = OwnerMail(n, owner_list(n)[4:], wide_in, *at.mail)
            wide_send = at.wide_send
            momenta = load_up(up_moment) + [load_down(down_moment, raw_block(0))]
            for c in momenta:
                c.start()
        whole = contract_first(act[...].reshape(flat, width), dz_all[...].reshape(flat, width))
        if aligned:
            at.down_grad[...] = whole.reshape(n, own_rows, width).astype(BF16)
            step(down_move)
        else:
            grad_down_out[...] = whole.astype(BF16)
        whole = contract_first(y_all[...].reshape(flat, width), du_all[...].reshape(flat, width))
        if aligned:
            at.up_grad[...] = whole.reshape(n, own_rows, width).astype(BF16)
            step(up_move)
        else:
            grad_up_out[...] = whole.astype(BF16)

        grad_gain_one = grad_shift_one = grad_bias_out = jnp.zeros((1, width), F32)
        for r in range(rows):
            grad = dy_sum.total(r) + second[r]
            scaled = at.scaled_one[r]
            weighted = grad * gain_one
            mean_first = jnp.mean(weighted, axis=-1, keepdims=True)
            mean_second = jnp.mean(weighted * scaled, axis=-1, keepdims=True)
            first = at.spread_one[r] * (weighted - mean_first - scaled * mean_second)
            second[r] = first
            low = first.astype(BF16)
            above = contract_last(low, w_out[...]).astype(BF16)
            for k in range(SEQ):
                columns = slice(k * quarter, (k + 1) * quarter)
                at.back_swap[0][k, r] = above[:, columns]
                at.a_quarters[k, r * span : (r + 1) * span] = low[:, columns]
            back_swap.start(r)
            grad_gain_one += row_sum(grad * scaled)
            grad_shift_one += row_sum(grad)
            grad_bias_out += row_sum(low.astype(F32))
        for k, value in enumerate(
            (
                grad_bias_out, grad_gain_one, grad_shift_one, grad_gain_two, grad_shift_two,
                grad_bias_down, bias_grad, jnp.zeros((1, width), F32),
            )
        ):
            vec_grad[k : k + 1] = value

        def new_momentum(k, piece, old):
            wide_bf[k] = piece[...].astype(BF16)
            wide_send[k] = (matrix_decay * old + wide_bf[k].astype(F32)).astype(BF16)
            mail.send(k, wide_send.at[k])

        flat_context = context[...].reshape(local, width)
        for k in range(SEQ):
            at.out_part[0, k] = contract_first(flat_context, at.a_quarters[k]).astype(BF16)
        out_sum.send_diag(0)
        out_sum.send_near(0)
        for r in range(rows):
            dy_sum.finish(r)
        sums = jnp.zeros((1, 3 * quarter), F32)
        for r in range(rows):
            back_swap.wait(r)
            arrived = jnp.concatenate([at.back_swap[1][k, r] for k in range(SEQ)], axis=0)
            query_grads, key_grads, value_grads = [], [], []
            for h in range(HEADS):
                query, key, value = heads(r, h)
                above = arrived[:, h * HD : (h + 1) * HD]
                weight = prob[r, h]
                prob_grad = contract_last(above, value)
                delta = jnp.sum(weight * prob_grad, axis=-1, keepdims=True)
                score_grad = (weight * (prob_grad - delta)).astype(BF16)
                query_grads.append(matmul(score_grad, key) * scale)
                key_grads.append(contract_first(query, score_grad) * scale)
                value_grads.append(contract_first(above, weight.astype(BF16)))
                if aligned and r == 0:
                    step(down_move)
                if r == 1 and h == 0:
                    out_sum.cross(0)
                if aligned and r == 1 and h > 0:
                    step(up_move)
                if not aligned and r > 0 and h == 2:
                    x_sum.cross(r - 1)
            turned = jnp.concatenate(key_grads + value_grads, axis=0).T
            block = jnp.concatenate(query_grads + [turned], axis=1).astype(BF16)
            at.grad_qkv[r] = block
            sums += row_sum(block.astype(F32))
            out = contract_last(block, w_qkv())
            for k in range(SEQ):
                part[r, k] = out[k * span : (k + 1) * span].astype(BF16)
            if not aligned:
                if r == 0:
                    x_sum = RowSum(part, *at.x_sum)
                x_sum.send_diag(r)
                x_sum.send_near(r)
        if aligned:
            step(up_move)
            drain(down_move)
            for c in momenta:
                c.wait()
            new_momentum(1, at.down_piece, raw_block(0)[...])
        bias_sums[...] = sums
        whole = contract_first(
            x_all[...].reshape(flat, width), at.grad_qkv[...].reshape(flat, 3 * quarter)
        )
        whole = jnp.concatenate([whole, out_sum.total(0)], axis=1)
        grad_attn[...] = whole.astype(BF16).reshape(grad_attn.shape)
        for k in (1, 2, 3):
            pool_copy(k, (s + 4 - k) % 4, (s + k) % 4).wait_recv()
        pool_buf = at.pool_buf
        pooled[...] = (pool_buf[0] + pool_buf[1]) + (pool_buf[2] + pool_buf[3])
        if aligned:
            mail.relay(1)
            drain(up_move)
            for k in range(SEQ):

                @pl.when(s == k)
                def _(k=k):
                    wide_bf[0] = at.up_piece[...].astype(BF16)
                    old = matrix_decay * raw_up(k) + wide_bf[0].astype(F32)
                    wide_send[0] = old.astype(BF16)

            mail.send(0, wide_send.at[0])
        else:
            x_sum.cross(rows - 1)
            for r in range(rows):
                second[r] = x_sum.total(r) + second[r]
                x_sum.finish(r)
        out_sum.finish(0)
        for k in (1, 2, 3):
            pool_copy(k, s, (s + k) % 4).wait_send()
        for r in range(rows):
            for op in (x_gather, swap, y_gather, dz_gather, back_swap):
                op.finish(r)
        if aligned:
            mail.relay(0)

            @pl.when(mail.mine[0] | mail.mine[1])
            def _():
                mail.collect()

            for k in range(2):
                mail.finish(k, wide_send.at[k])

    smem = pl.BlockSpec(memory_space=pltpu.SMEM)
    far_spec = anywhere if aligned else vmem
    return pl.pallas_call(
        kernel,
        out_shape=outs,
        in_specs=[vmem] + [far_spec] * 3 + [vmem] * 2 + [smem, vmem] + [anywhere] * 2,
        out_specs=out_specs,
        scratch_shapes=sc.shapes,
        compiler_params=pltpu.CompilerParams(
            collective_id=0, has_side_effects=True, vmem_limit_bytes=63 * 2**20
        ),
        name="layer",
    )(tokens, attn_weight, up_weight, down_weight, vec_own, pool_own, lengths, out_grad, up_moment, down_moment)


def join_up_parts(parts, n):
    hid_own = parts[0].shape[1] // n
    return jnp.concatenate(
        [parts[k][:, b * hid_own : (b + 1) * hid_own] for b in range(n) for k in range(SEQ)], axis=1
    )


def take_up(matrix, n, k):
    hid_own = matrix.shape[1] // n // SEQ
    return jnp.concatenate(
        [
            matrix[:, (b * SEQ + k) * hid_own : (b * SEQ + k + 1) * hid_own]
            for b in range(n)
        ],
        axis=1,
    )


def muon(n, grad_attn, wide_in, bias_sums, vec_grad, attn_moment, wide_bf, x_part, first_grad):
    rows, width = wide_bf.shape[1:]
    quarter = width // SEQ
    hid_own = rows
    n_vec = 8 + SEQ
    shape = jax.ShapeDtypeStruct
    attn_shape = (4, rows // 2, 2 * quarter)
    attn_op = GatherSeq(n, shape(attn_shape, BF16))
    attn_sum = BatchSum(n, grad_attn)
    vec_sum = DirectSum(n, shape((n, n_vec, rows), F32))
    vec_op = GatherSeq(n, shape((n_vec, rows), F32))
    wide_op = GatherSeq(n, wide_bf)
    count, span = first_grad.shape[:2]
    main = Muon(n, shape(attn_shape, BF16), wide_in=wide_in)
    outs = [attn_op.outs[0], wide_op.outs[0], shape((n_vec, rows), F32), shape(first_grad.shape, F32)]
    outs += main.outs
    groups = [
        [
            pltpu.VMEM((rows, width), F32),
            pltpu.VMEM(attn_shape, BF16),
            pltpu.VMEM(attn_shape, BF16),
            pltpu.VMEM((n, n_vec, rows), F32),
            pltpu.VMEM((n_vec, rows), F32),
            pltpu.VMEM((SEQ, n_vec, rows), F32),
        ]
    ] + [op.scratch for op in (attn_op, vec_sum, vec_op, main, attn_sum, wide_op)]
    groups.append(RowSum.scratch(count, (span, width)))

    def kernel(
        grad_attn, wide_in, bias_sums, vec_grad, attn_moment, wide_bf, x_part, first_grad,
        attn_all, wide_all, vec_total, input_grad, attn_orth, wide_orth, *rest,
    ):
        greet_signal(n, {"all"})
        parts, i = [], 0
        for group in groups:
            parts.append(rest[i : i + len(group)])
            i += len(group)
        attn_piece, attn_bf, attn_send, vec_local, vec_piece, vec_parts = parts[0]
        s = lax.axis_index("seq")
        main_move = main.run(attn_send, wide_in, attn_orth, wide_orth, *parts[4])
        step(main_move)
        main.prepare()
        greet_wait(n, {"all"})
        x_sum = RowSum(x_part, *parts[7])

        def inputs():
            for r in range(count):
                x_sum.send_diag(r)
                x_sum.send_near(r)
            yield
            for r in range(count):
                x_sum.cross(r)
            yield from rounds(8)
            for r in range(count):
                input_grad[r] = x_sum.total(r) + first_grad[r]
                x_sum.finish(r)

        def attention():
            moving = attn_sum.run(grad_attn, attn_piece, *parts[5])
            step(moving)
            yield from rounds(3)
            for _ in range(n // 2 - 1):
                step(moving)
            yield from rounds(3)
            drain(moving)
            for j in range(4):
                attn_bf[j] = fold(attn_piece[:, j * quarter : (j + 1) * quarter]).astype(BF16)
            for k in range(SEQ):

                @pl.when(s == k)
                def _(k=k):
                    for j in range(4):
                        old = fold(attn_moment[j, :, k * quarter : (k + 1) * quarter])
                        attn_send[j] = (matrix_decay * old + attn_bf[j].astype(F32)).astype(BF16)
            main.send_attn()
            yield
            main.attn_turn()
            yield from spaced(attn_op.run(attn_bf, attn_all, *parts[1]), 2)

        def vectors():
            def here(k, value):
                return jnp.where(s == k, value, 0.0)

            lines = [
                jnp.concatenate(
                    [here(k, bias_sums[:, j * quarter : (j + 1) * quarter]) for k in range(SEQ)], axis=1
                )
                for j in (0, 2)
            ]
            lines += [vec_grad[j : j + 1] for j in range(6)]
            hidden = vec_grad[6:7]
            pieces = [
                here(k, hidden[:, b * hid_own : (b + 1) * hid_own]) for b in range(n) for k in range(SEQ)
            ]
            each = n * SEQ // 4
            lines += [jnp.concatenate(pieces[j * each : (j + 1) * each], axis=1) for j in range(4)]
            whole = jnp.concatenate(lines, axis=0)
            for b in range(n):
                vec_local[b] = whole[:, b * rows : (b + 1) * rows]
            yield from spaced(vec_sum.run(vec_local, vec_piece, *parts[2]), 3)
            yield from spaced(vec_op.run(vec_piece, vec_parts, *parts[3]), 2)
            vec_total[...] = (vec_parts[0] + vec_parts[1]) + (vec_parts[2] + vec_parts[3])

        run_together(
            vectors(),
            attention(),
            inputs(),
            spaced(wide_op.run(wide_bf, wide_all, *parts[6]), 6),
            main_move,
        )

    vmem = pl.BlockSpec(memory_space=pltpu.VMEM)
    ins = (grad_attn, wide_in, bias_sums, vec_grad, attn_moment, wide_bf, x_part, first_grad)
    return pl.pallas_call(
        kernel,
        out_shape=outs,
        in_specs=[vmem, pl.BlockSpec(memory_space=pl.ANY)] + [vmem] * 6,
        out_specs=[vmem] * len(outs),
        scratch_shapes=[c for group in groups for c in group],
        compiler_params=pltpu.CompilerParams(
            collective_id=8, has_side_effects=True, vmem_limit_bytes=62 * 2**20
        ),
        name="muon",
    )(*ins)


def finish(
    n, out_rows, pool_sum, input_grad, attn_all, wide_all, attn_orth, wide_orth, vec_total,
    attn_weight, up_weight, down_weight, vectors, attn_moment, up_moment, down_moment, vector_moment,
    factors, vector_step,
):
    rows = wide_all.shape[2]
    quarter = wide_all.shape[3] // SEQ
    shape = jax.ShapeDtypeStruct
    ins = (
        attn_all, attn_moment, wide_all, up_moment, down_moment, out_rows, input_grad, pool_sum, vec_total,
        vectors, vector_moment, attn_orth, attn_weight, wide_orth, up_weight, down_weight,
    )
    token, pool = shape(out_rows.shape, F32), shape((out_rows.shape[0], quarter), F32)
    attn, up, down, vec = [shape(a.shape, F32) for a in (attn_weight, up_weight, down_weight, vectors)]
    outs = [token, pool, token] + [attn, up, down, vec] * 3
    direct = {0: 5, 2: 6}
    held = [k for k in range(len(outs)) if k not in direct]

    def kernel(*refs):
        far_in, far_out = refs[: len(ins)], refs[len(ins) : len(ins) + len(outs)]
        refs = refs[len(ins) + len(outs) :]
        near_in = refs[: len(ins)]
        near_out = dict(zip(held, refs[len(ins) :]))
        near_out.update({k: near_in[j] for k, j in direct.items()})
        in_sem, out_sem = refs[-2:]
        arriving = [
            pltpu.make_async_copy(a, b, in_sem.at[k]) for k, (a, b) in enumerate(zip(far_in, near_in))
        ]
        leaving = [
            pltpu.make_async_copy(near_out[k], far_out[k], out_sem.at[k]) for k in range(len(outs))
        ]
        for c in arriving:
            c.start()
        (
            attn_all, attn_moment, wide_all, up_moment, down_moment, _, _, pool_sum, vec_total,
            vectors, vector_moment, attn_orth, attn_weight, wide_orth, up_weight, down_weight,
        ) = near_in
        (
            _, pooled, _, attn_grad, up_grad, down_grad, vec_grad, attn_next, up_next, down_next, vec_next,
            attn_new, up_new, down_new, vec_new,
        ) = [near_out[k] for k in range(len(outs))]

        def wait(*ks):
            for k in ks:
                arriving[k].wait()

        def leave(*ks):
            for k in ks:
                leaving[k].start()

        def attn_of(parts, j):
            return jnp.concatenate([unfold(parts[k, j]) for k in range(SEQ)], axis=1).astype(F32)

        wait(0, 1)
        for j in range(4):
            grad = attn_of(attn_all, j)
            attn_grad[j] = grad
            attn_next[j] = matrix_decay * attn_moment[j] + grad
        leave(3, 7)
        wait(2, 3)
        grad = join_up_parts([wide_all[k, 0] for k in range(SEQ)], n).astype(F32)
        up_grad[...] = grad
        up_next[...] = matrix_decay * up_moment[...] + grad
        leave(4, 8)
        wait(4)
        for k in range(SEQ):
            part = pl.ds(k * rows, rows)
            grad = wide_all[k, 1].astype(F32)
            down_grad[part] = grad
            down_next[part] = matrix_decay * down_moment[part] + grad
        leave(5, 9)
        wait(5)
        leave(0)
        wait(6)
        leave(2)
        wait(7, 8, 9, 10)
        s = lax.axis_index("seq")
        pooled[...] = sum(
            jnp.where(s == k, pool_sum[:, k * quarter : (k + 1) * quarter], 0.0) for k in range(SEQ)
        )
        vec_grad[...] = vec_total[...]
        moved = vector_decay * vector_moment[...] + vec_total[...]
        vec_next[...] = moved
        vec_new[...] = vectors[...] - vector_step * moved
        leave(1, 6, 10, 14)
        wait(11, 12)
        for j in range(4):
            attn_new[j] = attn_weight[j] - factors[0] * attn_of(attn_orth, j)
        leave(11)
        wait(13, 14)
        orth = join_up_parts([wide_orth[k, 0] for k in range(SEQ)], n).astype(F32)
        up_new[...] = up_weight[...] - factors[1] * orth
        leave(12)
        wait(15)
        for k in range(SEQ):
            part = pl.ds(k * rows, rows)
            down_new[part] = down_weight[part] - factors[2] * wide_orth[k, 1].astype(F32)
        leave(13)
        for c in leaving:
            c.wait()

    anywhere = pl.BlockSpec(memory_space=pl.ANY)
    return pl.pallas_call(
        kernel,
        out_shape=outs,
        in_specs=[anywhere] * len(ins),
        out_specs=[anywhere] * len(outs),
        scratch_shapes=[pltpu.VMEM(a.shape, a.dtype) for a in ins]
        + [pltpu.VMEM(outs[k].shape, F32) for k in held]
        + [pltpu.SemaphoreType.DMA((len(ins),)), pltpu.SemaphoreType.DMA((len(outs),))],
        compiler_params=pltpu.CompilerParams(vmem_limit_bytes=60 * 2**20),
        name="finish",
    )(*ins)


def step_factor(rows_all, cols_all):
    return matrix_rate * math.sqrt(max(1.0, rows_all / cols_all))


def make_body(n):
    def body(
        layer_input,
        lengths,
        attn_weight,
        up_weight,
        down_weight,
        vectors,
        attn_moment,
        up_moment,
        down_moment,
        vector_moment,
        out_grad,
        pool_grad,
    ):
        rows, span, width = layer_input.shape
        own_rows = width // n
        quarter = width // SEQ
        hidden = up_weight.shape[1]
        hid_q = hidden // SEQ
        hid_own = hidden // n // SEQ
        seq_index = lax.axis_index("seq")

        def attn_quarter(stacked):
            part = lax.dynamic_index_in_dim(
                stacked.reshape(4, own_rows, SEQ, quarter), seq_index, 2, False
            )
            return part

        def up_quarter(matrix):
            return lax.dynamic_index_in_dim(
                matrix.reshape(own_rows, n, SEQ, hid_own), seq_index, 2, False
            ).reshape(own_rows, hid_q)

        def down_quarter(matrix):
            return lax.dynamic_index_in_dim(
                matrix.reshape(SEQ, hid_own, width), seq_index, 0, False
            )

        aligned = own_rows % 16 == 0
        if aligned:
            own = [attn_weight, up_weight, down_weight]
            vec_own = vectors
        else:
            attn_low = attn_quarter(attn_weight).astype(BF16).transpose(1, 0, 2).reshape(own_rows, width)
            up_low = up_quarter(up_weight).astype(BF16)
            down_low = down_quarter(down_weight).astype(BF16)
            vec_low = vectors.astype(BF16).astype(F32)
            placed = lax.dynamic_update_slice(
                jnp.zeros((vectors.shape[0], n, own_rows), F32),
                vec_low[:, None],
                (0, lax.axis_index("batch"), 0),
            ).reshape(-1, width)
            bias_up = lax.dynamic_index_in_dim(
                placed[8:].reshape(n, SEQ, hid_own), seq_index, 1, False
            ).reshape(1, hid_q)
            bias_qv = lax.dynamic_index_in_dim(
                placed[:2].reshape(2, SEQ, quarter), seq_index, 1, False
            )
            blank = jnp.zeros((quarter,), F32)
            bias_qkv = jnp.concatenate([bias_qv[0], blank, bias_qv[1], blank])[None]
            vec_own = jnp.concatenate([placed[2:8], bias_up, bias_qkv])
            own = exchange(
                n, 1, "gather_weights", *[GatherBatch(n, a) for a in (attn_low, up_low, down_low)]
            )
            own = [a.reshape(width, width) for a in own]
        out_rows, pool_sum, input_grad, vec_grad, bias_sums, x_part, *grads = layer(
            n, layer_input, *own, vec_own, pool_grad, lengths, out_grad, up_moment, down_moment
        )
        factors = [
            step_factor(width, width),
            step_factor(width, hidden),
            step_factor(hidden, width),
        ]
        vector_step = vector_rate / math.sqrt(rows * n)
        if aligned:
            grad_attn, wide_bf, wide_in = grads
            attn_all, wide_all, vec_total, input_grad, attn_orth, wide_orth = muon(
                n, grad_attn, wide_in, bias_sums, vec_grad, attn_moment, wide_bf, x_part, input_grad
            )
            return tuple(
                finish(
                    n, out_rows, pool_sum, input_grad, attn_all, wide_all, attn_orth, wide_orth, vec_total,
                    attn_weight, up_weight, down_weight, vectors,
                    attn_moment, up_moment, down_moment, vector_moment, factors, vector_step,
                )
            )
        pooled = lax.dynamic_slice_in_dim(pool_sum, seq_index * quarter, quarter, 1)
        attn_piece, up_piece, down_piece = exchange(
            n, 2, "sum_grads", *[BatchSum(n, a.reshape(n, own_rows, width)) for a in grads]
        )
        bias_sums = bias_sums.reshape(3, quarter)

        vec_head = jnp.zeros((2, SEQ, quarter), F32)
        vec_head = lax.dynamic_update_slice(
            vec_head, bias_sums[jnp.array([0, 2])][:, None], (0, seq_index, 0)
        ).reshape(2, width)
        vec_mid = vec_grad[:6]
        grad_bias_up = vec_grad[6]
        vec_tail = lax.dynamic_update_slice(
            jnp.zeros((n, SEQ, hid_own), F32),
            grad_bias_up.reshape(n, 1, hid_own),
            (0, seq_index, 0),
        ).reshape(-1, width)
        vec_local = jnp.concatenate([vec_head, vec_mid, vec_tail])
        vec_local = vec_local.reshape(-1, n, own_rows).transpose(1, 0, 2)
        (vec_piece,) = exchange(n, 7, "sum_vectors", ScatterBatch(n, vec_local, F32))
        attn_bf = attn_piece.astype(BF16).reshape(own_rows, 4, quarter).transpose(1, 0, 2)
        wide_bf = jnp.stack([up_piece, down_piece]).astype(BF16)
        attn_send = (matrix_decay * attn_quarter(attn_moment) + attn_bf.astype(F32)).astype(BF16)
        wide_moment = jnp.stack([up_quarter(up_moment), down_quarter(down_moment)])
        wide_send = (matrix_decay * wide_moment + wide_bf.astype(F32)).astype(BF16)
        short = -own_rows % 16
        attn_send = jnp.pad(attn_send, ((0, 0), (0, short), (0, 0)))
        wide_send = jnp.pad(wide_send, ((0, 0), (0, short), (0, 0)))
        attn_all, wide_all, vec_parts, attn_orth, wide_orth = exchange(
            n,
            8,
            "muon",
            GatherSeq(n, attn_bf),
            GatherSeq(n, wide_bf),
            GatherSeq(n, vec_piece),
            Muon(n, attn_send, wide_send),
        )
        attn_orth = attn_orth[:, :, :own_rows]
        wide_orth = wide_orth[:, :, :own_rows]

        def join_attn(parts):
            return parts.astype(F32).transpose(1, 2, 0, 3).reshape(4, own_rows, width)

        def join_up(parts):
            return (
                parts.astype(F32)
                .reshape(SEQ, own_rows, n, hid_own)
                .transpose(1, 2, 0, 3)
                .reshape(own_rows, hidden)
            )

        def join_down(parts):
            return parts.astype(F32).reshape(SEQ * hid_own, width)

        attn_grad = join_attn(attn_all)
        up_grad, down_grad = join_up(wide_all[:, 0]), join_down(wide_all[:, 1])
        vector_grad = (vec_parts[0] + vec_parts[1]) + (vec_parts[2] + vec_parts[3])
        attn_next = matrix_decay * attn_moment + attn_grad
        up_next = matrix_decay * up_moment + up_grad
        down_next = matrix_decay * down_moment + down_grad

        attn_new = attn_weight - factors[0] * join_attn(attn_orth)
        up_new = up_weight - factors[1] * join_up(wide_orth[:, 0])
        down_new = down_weight - factors[2] * join_down(wide_orth[:, 1])
        vector_next = vector_decay * vector_moment + vector_grad
        vectors_new = vectors - vector_step * vector_next
        return (
            out_rows,
            pooled,
            input_grad,
            attn_grad,
            up_grad,
            down_grad,
            vector_grad,
            attn_next,
            up_next,
            down_next,
            vector_next,
            attn_new,
            up_new,
            down_new,
            vectors_new,
        )

    return body


def solution(mesh):
    placed = (
        P("batch", "seq", None),
        P("batch"),
        P(None, "batch", None),
        P("batch", None),
        P("batch", None),
        P(None, "batch"),
        P(None, "batch", None),
        P("batch", None),
        P("batch", None),
        P(None, "batch"),
        P("batch", "seq", None),
        P("batch", "seq"),
    )
    return jax.shard_map(
        make_body(mesh.shape["batch"]),
        mesh=mesh,
        in_specs=placed,
        out_specs=(
            P("batch", "seq", None),
            P("batch", "seq"),
            P("batch", "seq", None),
            P(None, "batch", None),
            P("batch", None),
            P("batch", None),
            P(None, "batch"),
            P(None, "batch", None),
            P("batch", None),
            P("batch", None),
            P(None, "batch"),
            P(None, "batch", None),
            P("batch", None),
            P("batch", None),
            P(None, "batch"),
        ),
        check_vma=False,
    )
```

```python
import math
import types

import jax
import jax.numpy as jnp
from jax import lax
from jax.experimental import pallas as pl
from jax.experimental.pallas import tpu as pltpu
from jax.sharding import PartitionSpec as P

H = 12
HD = 64
NS = 5
SEQ = 4
HEADS = H // SEQ

norm_eps = 1e-12
tiny_norm = 1e-07
matrix_decay = 0.95
vector_decay = 0.5
matrix_rate = 0.5
vector_rate = 0.03

MESH = pl.DeviceIdType.MESH
F32 = jnp.float32
BF16 = jnp.bfloat16


def coords(n):
    b = lax.axis_index("batch")
    s = lax.axis_index("seq")
    return b, s, b // 2, b % 2, n // 2


def remote(src, dst, send, recv, device):
    return pltpu.make_async_remote_copy(
        src_ref=src, dst_ref=dst, send_sem=send, recv_sem=recv, device_id=device, device_id_type=MESH
    )


class GatherBatch:
    peers = ("batch",)

    def __init__(self, n, src, eager=True):
        self.n = n
        self.eager = eager
        self.ins = [src]
        self.outs = [jax.ShapeDtypeStruct((n,) + src.shape, src.dtype)]
        m = n // 2
        self.scratch = [pltpu.SemaphoreType.DMA((2, m))] * 4 + [pltpu.SemaphoreType.DMA]

    def run(self, src, dst, zs, zr, ys, yr, own):
        b, s, hi, lo, m = coords(self.n)
        pair = (hi * 2 + 1 - lo, s)
        local = pltpu.make_async_copy(src, dst.at[b], own)
        local.start()

        def exists(way, d):
            return hi >= d if way == 0 else hi + d < m

        def ahead(way):
            return hi + 1 < m if way == 0 else hi >= 1

        def block_of(way, d):
            place = jnp.clip(hi - d if way == 0 else hi + d, 0, m - 1)
            return place * 2 + lo

        def along(way, d, ref):
            place = jnp.clip(hi + 1 if way == 0 else hi - 1, 0, m - 1)
            return remote(
                ref, dst.at[block_of(way, d)], zs.at[way, d], zr.at[way, d + 1], (place * 2 + lo, s)
            )

        def aside(way, d):
            place = dst.at[block_of(way, d)]
            return remote(place, place, ys.at[way, d], yr.at[way, d], pair)

        first = remote(src, dst.at[b], ys.at[0, 0], yr.at[0, 0], pair)
        for way in (0, 1):

            @pl.when(ahead(way))
            def _(way=way):
                along(way, 0, src).start()

        if not self.eager:
            yield
        first.start()
        yield
        for d in range(1, m):
            for way in (0, 1):

                @pl.when(exists(way, d))
                def _(way=way, d=d):
                    place = dst.at[block_of(way, d)]
                    remote(place, place, zs.at[way, d], zr.at[way, d], pair).wait_recv()
                    if d < m - 1:

                        @pl.when(ahead(way))
                        def _():
                            along(way, d, place).start()

                    aside(way, d).start()

            yield
        local.wait()
        first.wait()
        for d in range(m):
            for way in (0, 1):
                if d > 0:

                    @pl.when(exists(way, d))
                    def _(way=way, d=d):
                        aside(way, d).wait()

                if d < m - 1:

                    @pl.when(exists(way, d) & ahead(way))
                    def _(way=way, d=d):
                        along(way, d, dst.at[block_of(way, d)]).wait_send()


class GatherDirect:
    peers = ("all",)

    def __init__(self, n, src):
        self.n = n
        self.ins = [src]
        self.outs = [jax.ShapeDtypeStruct((n,) + src.shape, src.dtype)]
        self.scratch = [pltpu.SemaphoreType.DMA((n,))] * 2 + [pltpu.SemaphoreType.DMA]

    def run(self, src, dst, ss, rs, own):
        n = self.n
        b, s = lax.axis_index("batch"), lax.axis_index("seq")
        local = pltpu.make_async_copy(src, dst.at[b], own)
        local.start()
        copies = [
            remote(src, dst.at[b], ss.at[k], rs.at[k], ((b + k) % n, s)) for k in range(1, n)
        ]
        for c in copies:
            c.start()
        yield
        local.wait()
        for c in copies:
            c.wait()


class ScatterBatch:
    peers = ("batch",)

    def __init__(self, n, src, wire=BF16):
        self.n = n
        self.wire = wire
        self.ins = [src]
        shape = src.shape[1:]
        self.outs = [jax.ShapeDtypeStruct(shape, F32)]
        m = n // 2
        self.scratch = [pltpu.VMEM((m,) + shape, wire)] * 4 + [pltpu.SemaphoreType.DMA((m,))] * 4

    def run(self, src, dst, ysend, yrecv, zsend, zrecv, ys, yr, zs, zr):
        b, s, hi, lo, m = coords(self.n)
        pair = (hi * 2 + 1 - lo, s)
        first = {}
        order = list(range(1, m)) + [0]
        for d in order:
            h = (hi + d) % m
            ysend[d] = src[h * 2 + 1 - lo].astype(self.wire)
            first[d] = remote(ysend.at[d], yrecv.at[d], ys.at[d], yr.at[d], pair)
            first[d].start()
        yield
        second = []
        for d in range(1, m):
            h = (hi + d) % m
            first[d].wait_recv()
            zsend[d] = (src[h * 2 + lo] + yrecv[d].astype(F32)).astype(self.wire)
            c = remote(zsend.at[d], zrecv.at[d], zs.at[d], zr.at[d], (h * 2 + lo, s))
            c.start()
            second.append(c)
            yield
        first[0].wait_recv()
        total = src[b] + yrecv[0].astype(F32)
        for d in range(1, m):
            second[d - 1].wait_recv()
            total = total + zrecv[d].astype(F32)
        dst[...] = total
        for c in list(first.values()) + second:
            c.wait_send()


class GatherSeq:
    peers = ("seq",)

    def __init__(self, n, src):
        self.ins = [src]
        self.outs = [jax.ShapeDtypeStruct((SEQ,) + src.shape, src.dtype)]
        self.scratch = [pltpu.SemaphoreType.DMA((3,))] * 2 + [pltpu.SemaphoreType.DMA]

    def run(self, src, dst, ss, rs, own):
        b, s = lax.axis_index("batch"), lax.axis_index("seq")
        far, near = (s + 2) % 4, s + 1 - 2 * (s % 2)
        across = remote(src, dst.at[s], ss.at[0], rs.at[0], (b, far))
        across.start()
        local = pltpu.make_async_copy(src, dst.at[s], own)
        local.start()
        beside = remote(src, dst.at[s], ss.at[1], rs.at[1], (b, near))
        beside.start()
        yield
        across.wait_recv()
        passed = remote(dst.at[far], dst.at[far], ss.at[2], rs.at[2], (b, near))
        passed.start()
        yield
        local.wait()
        beside.wait()
        passed.wait()
        across.wait_send()


def owner_list(n):
    return [(0, 2), (1, 0), (n - 2, 2), (n - 1, 0), (n // 4, 0), (n // 2 + 1, 2)]


class OwnerMail:
    @staticmethod
    def scratch(n, count, relayed=None):
        dma = pltpu.SemaphoreType.DMA
        base = [dma((count,)), dma((SEQ * n,)), dma]
        if relayed is not None:
            base += [pltpu.VMEM((count,) + relayed, BF16), dma((count,)), dma((count,))]
        return base

    def __init__(self, n, places, inbox, ss, rs, own, relayed=None, relay_s=None, relay_r=None):
        self.n, self.places, self.inbox, self.ss, self.rs, self.own = n, places, inbox, ss, rs, own
        self.relayed, self.relay_s, self.relay_r = relayed, relay_s, relay_r
        self.b, self.s = lax.axis_index("batch"), lax.axis_index("seq")
        self.me = self.s * n + self.b
        self.mine = [(self.b == ob) & (self.s == os) for ob, os in places]

    def slot(self, seq, block):
        if len(self.inbox.shape) == 4:
            return self.inbox.at[seq, block]
        rows = self.inbox.shape[1] // self.n
        return self.inbox.at[seq, pl.ds(pl.multiple_of(block * rows, rows), rows)]

    def indirect(self, k):
        ob, os = self.places[k]
        other_plane = self.b // 2 != ob // 2
        corner = (self.b % 2 != ob % 2) & (self.s // 2 != os // 2)
        column = (self.b % 2 == ob % 2) & (self.s // 2 == os // 2)
        return other_plane & corner, other_plane & column

    def copy(self, k, src):
        ob, os = self.places[k]
        place = self.slot(self.s, self.b)
        return remote(src, place, self.ss.at[k], self.rs.at[self.me], (ob, os))

    def aside(self, k, src):
        across = self.b + 1 - 2 * (self.b % 2)
        return remote(
            src, self.relayed.at[k], self.ss.at[k], self.relay_r.at[k], (across, (self.s + 2) % 4)
        )

    def pass_copy(self, k):
        block, seq = self.b + 1 - 2 * (self.b % 2), (self.s + 2) % 4
        place = self.slot(seq, block)
        return remote(
            self.relayed.at[k], place, self.relay_s.at[k], self.rs.at[seq * self.n + block], self.places[k]
        )

    def send(self, k, src):
        direct = jnp.logical_not(self.mine[k])
        if self.relayed is not None:
            by_relay, _ = self.indirect(k)
            direct = direct & jnp.logical_not(by_relay)

            @pl.when(by_relay)
            def _():
                self.aside(k, src).start()

        @pl.when(direct)
        def _():
            self.copy(k, src).start()

        @pl.when(self.mine[k])
        def _():
            pltpu.make_async_copy(src, self.slot(self.s, self.b), self.own).start()

    def relay(self, k):
        @pl.when(self.indirect(k)[1])
        def _():
            place = self.relayed.at[k]
            remote(place, place, self.relay_s.at[k], self.relay_r.at[k], (0, 0)).wait_recv()
            self.pass_copy(k).start()

    def collect(self):
        place = self.slot(self.s, self.b)
        pltpu.make_async_copy(place, place, self.own).wait()

        @pl.loop(1, SEQ * self.n)
        def _(k):
            other = (self.me + k) % (SEQ * self.n)
            place = self.slot(other // self.n, other % self.n)
            remote(place, place, self.ss.at[0], self.rs.at[other], (0, 0)).wait_recv()

    def finish(self, k, src):
        @pl.when(jnp.logical_not(self.mine[k]))
        def _():
            self.copy(k, src).wait_send()

        if self.relayed is not None:

            @pl.when(self.indirect(k)[1])
            def _():
                self.pass_copy(k).wait_send()


class Muon:
    peers = ("all",)

    def __init__(self, n, attn_piece, wide_piece=None, wide_in=None):
        self.n = n
        self.ready = wide_in is not None
        self.ins = [attn_piece, wide_in if self.ready else wide_piece]
        width = self.ins[1].shape[-1]
        size = wide_in.shape[1] if self.ready else n * wide_piece.shape[1]
        rows = size // n
        attn_shape = attn_piece.shape[1:]
        self.outs = [
            jax.ShapeDtypeStruct((SEQ, 4) + attn_shape, BF16),
            jax.ShapeDtypeStruct((SEQ, 2, rows, width), BF16),
        ]
        dma = pltpu.SemaphoreType.DMA
        self.scratch = [
            pltpu.VMEM((SEQ, n) + attn_shape, BF16),
            pltpu.VMEM((SEQ, size, width), BF16),
            pltpu.VMEM((2, n // 2, rows, width), BF16),
            pltpu.VMEM((size, SEQ * size), F32),
            pltpu.VMEM((size, SEQ * size), BF16),
            pltpu.VMEM((size, size), F32),
            pltpu.VMEM((size, size), BF16),
            pltpu.VMEM((size, size), BF16),
            pltpu.VMEM((size, 1), F32),
            pltpu.VMEM((1, 1), F32),
            dma((SEQ * n,)),
            dma((6,)),
            dma((2, n // 2)),
            dma((2, n // 2)),
            dma((6, 3)),
            dma((6, 3)),
            dma,
            dma((SEQ,)),
        ]
        self.scratch += OwnerMail.scratch(n, 4)
        if not self.ready:
            self.scratch += OwnerMail.scratch(n, 2) + [pltpu.VMEM((SEQ, size, width), BF16)]

    def run(
        self, attn, wide, attn_orth, wide_orth, attn_in, wide_out, relayed, x32, xlow, gram, gram_low, poly, diag,
        norm, back_s, back_r, relay_s, relay_r, seq_s, seq_r, own, loads, *mails,
    ):
        n = self.n
        b, s, hi, lo, m = coords(n)
        far, near = (s + 2) % 4, s + 1 - 2 * (s % 2)
        me = s * n + b
        size = x32.shape[0]
        width = wide.shape[-1]
        quarter = width // SEQ
        places = owner_list(n)
        attn_mail = OwnerMail(n, places[:4], attn_in, *mails[:3])
        wide_in = wide
        if not self.ready:
            wide_in = mails[6]
            wide_mail = OwnerMail(n, places[4:], wide_in, *mails[3:6])
        mine = [(b == ob) & (s == os) for ob, os in places]
        number = jnp.int32(0)
        for k in range(6):
            number = jnp.where(mine[k], jnp.int32(k), number)
        is_attn = mine[0] | mine[1] | mine[2] | mine[3]
        is_wide = mine[4] | mine[5]

        if not self.ready:
            for k in range(2):
                wide_mail.send(k, wide.at[k])
        def send_attn():
            for k in range(4):
                attn_mail.send(k, attn.at[k])

        if self.ready:
            self.send_attn = send_attn
        else:
            send_attn()

        if not self.ready:
            for _ in range(4):
                yield


        def result(k):
            return attn_orth.at[s, k] if k < 4 else wide_orth.at[s, k - 4]

        def others(act):
            @pl.loop(1, SEQ * n)
            def _(k):
                other = (me + k) % (SEQ * n)
                act(other, other % n, other // n)

        def give_attn():
            pltpu.make_async_copy(attn_in.at[s, b], attn_orth.at[s, number], own).start()

            def act(other, ob, os):
                remote(
                    attn_in.at[os, ob], attn_orth.at[os, number], back_s.at[other], back_r.at[number], (ob, os)
                ).start()

            others(act)

        piece = OwnerMail(n, places, wide_out, None, None, None).slot

        def give_wide(piece):
            index = number - 4
            pltpu.make_async_copy(piece(s, b), wide_orth.at[s, index], own).start()

            def act(other, ob, os):
                oh, ol = ob // 2, ob % 2
                up = hi < m // 2
                away = jnp.where(up, oh - hi, hi - oh)
                relay = (away > 0) & (os // 2 != s // 2)
                stop = jnp.where(ol == lo, os, (os + 2) % 4)
                src = piece(os, ob)

                @pl.when(relay)
                def _():
                    slot = jnp.maximum(away - 1, 0)
                    remote(
                        src, relayed.at[index, slot], back_s.at[other], relay_r.at[index, slot],
                        (hi * 2 + ol, stop),
                    ).start()

                @pl.when(jnp.logical_not(relay))
                def _():
                    remote(
                        src, wide_orth.at[os, index], back_s.at[other], back_r.at[number], (ob, os)
                    ).start()

            others(act)

        def prepare():
            @pl.when(is_wide)
            def _():
                if not self.ready:
                    wide_mail.collect()
                if width != size:
                    xlow[...] = jnp.zeros(xlow.shape, BF16)

            @pl.when(mine[4])
            def _():
                copies = [
                    pltpu.make_async_copy(
                        wide_in.at[k], xlow.at[:, pl.ds(k * size, width)], loads.at[k]
                    )
                    for k in range(SEQ)
                ]
                for c in copies:
                    c.start()
                for c in copies:
                    c.wait()

            @pl.when(mine[5])
            def _():
                copies = [
                    pltpu.make_async_copy(wide_in.at[k], wide_out.at[k], loads.at[k]) for k in range(SEQ)
                ]
                for c in copies:
                    c.start()
                for k, c in enumerate(copies):
                    c.wait()
                    xlow[:width, k * size : (k + 1) * size] = wide_out[k].T

        def attn_turn():
            @pl.when(is_attn)
            def _():
                attn_mail.collect()
                span = SEQ * quarter
                short, line = attn_in.shape[2:]
                whole = [attn_in[k].reshape(n * short, line) for k in range(SEQ)]
                for k in range(line // quarter):
                    block = [a[:, k * quarter : (k + 1) * quarter] for a in whole]
                    xlow[k * n * short : (k + 1) * n * short, :span] = jnp.concatenate(block, axis=1)
                square_x, square_low = x32.at[:, pl.ds(0, span)], xlow.at[:, pl.ds(0, span)]

                def turn(first):
                    schulz_poly(square_low, gram, gram_low, poly, diag, norm, first)
                    schulz_move(square_x, square_low, poly, diag, norm, first)

                turn(True)

                @pl.loop(1, NS)
                def _(k):
                    turn(False)

                for k in range(SEQ):
                    block = xlow[:, k * quarter : (k + 1) * quarter]
                    if line > quarter:
                        block = fold(block)
                    attn_in[k] = block.reshape(attn_in.shape[1:])
                give_attn()

        if not self.ready:
            prepare()
        else:
            self.prepare, self.attn_turn = prepare, attn_turn
            yield

        for turn in range(NS):

            @pl.when(is_wide)
            def _(turn=turn):
                schulz_poly(xlow, gram, gram_low, poly, diag, norm, turn == 0)

            yield

            @pl.when(is_wide)
            def _(turn=turn):
                schulz_move(x32, xlow, poly, diag, norm, turn == 0)

            yield

        @pl.when(is_wide)
        def _():
            @pl.when(mine[4])
            def _():
                rows = size // n

                def part(seq, block):
                    return xlow.at[
                        pl.ds(pl.multiple_of(block * rows, rows), rows),
                        pl.ds(pl.multiple_of(seq * size, 128), width),
                    ]

                give_wide(part)

            @pl.when(mine[5])
            def _():
                for k in range(SEQ):
                    wide_out[k] = xlow[:width, k * size : (k + 1) * size].T
                give_wide(piece)

        def routes(k):
            ob, os = places[k]
            oh, ol = ob // 2, ob % 2
            same_x = s // 2 == os // 2
            here = (hi == oh) & (((lo == ol) & jnp.logical_not(same_x)) | ((lo != ol) & same_x))
            target = jnp.where(lo == ol, s, far)
            ahead = range(oh + 1, m) if oh < m // 2 else range(oh - 1, -1, -1)
            return here, target, list(enumerate(ahead))

        def relay_copy(k, slot, block, target):
            return remote(
                relayed.at[k - 4, slot], wide_orth.at[target, k - 4], relay_s.at[k - 4, slot], back_r.at[k],
                (block * 2 + lo, target),
            )

        def onward(k, step, source, target):
            out = attn_orth.at[source, k] if k < 4 else wide_orth.at[source, k - 4]
            return remote(out, out, seq_s.at[k, step], seq_r.at[k, step], (b, target))

        if not self.ready:
            attn_turn()
        done = (0, 1, 2, 3, 4, 5)

        def returned(k):
            @pl.when(jnp.logical_not(mine[k]))
            def _():
                remote(result(k), result(k), seq_s.at[k, 0], back_r.at[k], (0, 0)).wait_recv()

            @pl.when(mine[k])
            def _():
                pltpu.make_async_copy(result(k), result(k), own).wait()

            onward(k, 0, s, far).start()
            onward(k, 1, s, near).start()

        def passed(k):
            onward(k, 0, far, far).wait_recv()
            onward(k, 2, far, near).start()

        for k in (4, 5):
            here, target, ahead = routes(k)

            @pl.when(here)
            def _(k=k, target=target, ahead=ahead):
                for slot, block in ahead:
                    place = relayed.at[k - 4, slot]
                    remote(place, place, relay_s.at[0, 0], relay_r.at[k - 4, slot], (0, 0)).wait_recv()
                    relay_copy(k, slot, block, target).start()

        for k in done[:4]:
            returned(k)
        for k in done[:4]:
            passed(k)
        for k in done[4:]:
            returned(k)
        for k in done[4:]:
            passed(k)
        for k in done:
            onward(k, 1, near, near).wait_recv()
            onward(k, 2, (near + 2) % 4, near).wait_recv()
            onward(k, 0, s, far).wait_send()
            onward(k, 1, s, near).wait_send()
            onward(k, 2, far, near).wait_send()
        for k in range(4):
            attn_mail.finish(k, attn.at[k])
        if not self.ready:
            for k in range(2):
                wide_mail.finish(k, wide.at[k])
        for k in (4, 5):
            here, target, ahead = routes(k)

            @pl.when(here)
            def _(k=k, target=target, ahead=ahead):
                for slot, block in ahead:
                    relay_copy(k, slot, block, target).wait_send()

        def given(buf):
            def act(other, ob, os):
                place = buf.at[os, ob] if len(buf.shape) == 4 else piece(os, ob)
                remote(place, place, back_s.at[other], back_r.at[0], (0, 0)).wait_send()

            others(act)

        @pl.when(is_attn)
        def _():
            given(attn_in)

        @pl.when(is_wide)
        def _():
            given(wide_out)


def schulz_poly(xlow, gram, gram_low, poly, diag, norm, first):
    size = xlow.shape[0]
    side = 256
    tiles = [slice(k, k + side) for k in range(0, size, side)]
    eye = lax.broadcasted_iota(jnp.int32, (side, side), 0) == lax.broadcasted_iota(
        jnp.int32, (side, side), 1
    )
    for j in tiles:
        gram[j.start :, j] = contract_last(xlow[j.start :, :], xlow[j, :])
    if first:
        total = jnp.zeros((1, 1), F32)
        for j in tiles:
            total = total + jnp.sum(jnp.where(eye, gram[j, j], 0.0), keepdims=True)
        inverse = 1.0 / (jnp.sqrt(total) + tiny_norm)
        norm[...] = inverse
        for j in tiles:
            gram[j.start :, j] = gram[j.start :, j] * (inverse * inverse)
    down, along = [], []
    for j in tiles:
        block = gram[j, j]
        on_diag = jnp.where(eye, block, 0.0)
        down.append(jnp.sum(on_diag, axis=1, keepdims=True))
        along.append(jnp.sum(on_diag, axis=0, keepdims=True))
        gram_low[j, j] = jnp.where(eye, 0.0, block).astype(BF16)
        for i in tiles:
            if i.start > j.start:
                block = gram[i, j]
                gram_low[i, j] = block.astype(BF16)
                gram_low[j, i] = block.T.astype(BF16)
    for j, right in zip(tiles, along):
        square = matmul(gram_low[j.start :, :], gram_low[:, j])
        for i, left in zip(tiles, down):
            if i.start < j.start:
                continue
            part = square[i.start - j.start : i.stop - j.start]
            factor = (2.0315 * left - 4.775) + 2.0315 * right
            block = 2.0315 * part + factor * gram[i, j]
            if i == j:
                value = jnp.sum(jnp.where(eye, 2.0315 * part, 0.0), axis=1, keepdims=True)
                diag[i] = value + (3.4445 + (2.0315 * left - 4.775) * left)
                poly[i, i] = jnp.where(eye, 0.0, block).astype(BF16)
            else:
                poly[i, j] = block.astype(BF16)
                poly[j, i] = block.T.astype(BF16)


def schulz_move(x32, xlow, poly, diag, norm, first):
    wide = x32.shape[1]
    chunk = 768 if wide % 768 == 0 else 512
    for c in range(0, wide, chunk):
        part = slice(c, c + chunk)
        if first:
            moved = (diag[...] * norm[...]) * xlow[:, part].astype(F32)
            moved = moved + matmul(poly[...], xlow[:, part]) * norm[...]
        else:
            moved = diag[...] * x32[:, part] + matmul(poly[...], xlow[:, part])
        x32[:, part] = moved
        xlow[:, part] = moved.astype(BF16)


def greet_peers(n, kinds):
    b, s, hi, lo, m = coords(n)
    peers = []
    if "seq" in kinds:
        peers += [(b, (s + k) % 4) for k in (1, 2, 3)]
    if "batch" in kinds:
        peers += [(((hi + d) % m) * 2 + lo, s) for d in range(1, m)]
        peers += [(hi * 2 + 1 - lo, s)]
    return peers


def greet_signal(n, kinds):
    b, s = lax.axis_index("batch"), lax.axis_index("seq")
    barrier = pltpu.get_barrier_semaphore()
    if "all" in kinds:
        me = s * n + b

        @pl.loop(1, SEQ * n)
        def _(k):
            other = (me + k) % (SEQ * n)
            pl.semaphore_signal(
                barrier, inc=1, device_id=(other % n, other // n), device_id_type=MESH
            )

        return
    for peer in greet_peers(n, kinds):
        pl.semaphore_signal(barrier, inc=1, device_id=peer, device_id_type=MESH)


def greet_wait(n, kinds):
    count = SEQ * n - 1 if "all" in kinds else len(greet_peers(n, kinds))
    pl.semaphore_wait(pltpu.get_barrier_semaphore(), count)


def greet(n, kinds):
    greet_signal(n, kinds)
    greet_wait(n, kinds)


def run_together(*live):
    live = list(live)
    while live:
        still = []
        for op in live:
            try:
                next(op)
                still.append(op)
            except StopIteration:
                pass
        live = still


def exchange(n, collective_id, name, *ops):
    ins = [a for op in ops for a in op.ins]
    outs = [o for op in ops for o in op.outs]
    scratch = [c for op in ops for c in op.scratch]
    kinds = {k for op in ops for k in op.peers}

    def kernel(*refs):
        in_refs, out_refs = refs[: len(ins)], refs[len(ins) : len(ins) + len(outs)]
        scratch_refs = refs[len(ins) + len(outs) :]
        greet(n, kinds)
        live = []
        i = o = c = 0
        for op in ops:
            ni, no, nc = len(op.ins), len(op.outs), len(op.scratch)
            live.append(
                op.run(*in_refs[i : i + ni], *out_refs[o : o + no], *scratch_refs[c : c + nc])
            )
            i, o, c = i + ni, o + no, c + nc
        run_together(*live)

    vmem = pl.BlockSpec(memory_space=pltpu.VMEM)
    return pl.pallas_call(
        kernel,
        out_shape=outs,
        in_specs=[vmem] * len(ins),
        out_specs=[vmem] * len(outs),
        scratch_shapes=scratch,
        compiler_params=pltpu.CompilerParams(
            collective_id=collective_id, has_side_effects=True, vmem_limit_bytes=60 * 2**20
        ),
        name=name,
    )(*ins)


def contract_last(left, right):
    return lax.dot_general(left, right, (((1,), (1,)), ((), ())), preferred_element_type=F32)


def contract_first(left, right):
    return lax.dot_general(left, right, (((0,), (0,)), ((), ())), preferred_element_type=F32)


def matmul(left, right):
    return jnp.dot(left, right, preferred_element_type=F32)


def exact_gelu(value_in):
    return jax.nn.gelu(value_in, approximate=False)


def normalize(hidden, gain_row):
    row_mean = jnp.mean(hidden, axis=-1, keepdims=True)
    centred = hidden - row_mean
    spread = lax.rsqrt(jnp.mean(centred * centred, axis=-1, keepdims=True) + norm_eps)
    scaled = centred * spread
    return (scaled * gain_row, scaled, spread)


def normalize_back(grad_in, scaled, spread, gain_row):
    weighted = grad_in * gain_row
    mean_first = jnp.mean(weighted, axis=-1, keepdims=True)
    second = jnp.mean(weighted * scaled, axis=-1, keepdims=True)
    return (
        spread * (weighted - mean_first - scaled * second),
        jnp.sum(grad_in * scaled, axis=0),
        jnp.sum(grad_in, axis=0),
    )


class RowGather:
    @staticmethod
    def scratch():
        return [pltpu.SemaphoreType.DMA((2, 3)), pltpu.SemaphoreType.DMA((2, 3))]

    def __init__(self, buf, ss, rs):
        self.buf, self.ss, self.rs = buf, ss, rs
        self.b, self.s = lax.axis_index("batch"), lax.axis_index("seq")
        self.far, self.near = (self.s + 2) % 4, self.s + 1 - 2 * (self.s % 2)
        self.diag = (self.near + 2) % 4

    def copy(self, r, step, block, device):
        place = self.buf.at[r, block]
        return remote(place, place, self.ss.at[r, step], self.rs.at[r, step], (self.b, device))

    def start(self, r):
        self.copy(r, 0, self.s, self.far).start()
        self.copy(r, 1, self.s, self.near).start()

    def wait_near(self, r):
        self.copy(r, 1, self.near, self.near).wait_recv()

    def pass_far(self, r):
        self.copy(r, 0, self.far, self.far).wait_recv()
        self.copy(r, 2, self.far, self.near).start()

    def wait_diag(self, r):
        self.copy(r, 2, self.diag, self.near).wait_recv()

    def finish(self, r):
        self.copy(r, 0, self.s, self.far).wait_send()
        self.copy(r, 1, self.s, self.near).wait_send()
        self.copy(r, 2, self.far, self.near).wait_send()


def gelu_parts(value):
    cdf = 0.5 * (1.0 + lax.erf(value * math.sqrt(0.5)))
    density = jnp.exp(-0.5 * value * value) * (1.0 / math.sqrt(2.0 * math.pi))
    return value * cdf, cdf + value * density


def row_sum(value):
    return jnp.sum(value, axis=0, keepdims=True)


class RowSwap:
    @staticmethod
    def scratch(shape):
        return [
            pltpu.VMEM(shape, BF16),
            pltpu.VMEM(shape, BF16),
            pltpu.SemaphoreType.DMA((2, 4)),
            pltpu.SemaphoreType.DMA((2, 4)),
        ]

    def __init__(self, src, dst, ss, rs):
        self.src, self.dst, self.ss, self.rs = src, dst, ss, rs
        self.b, self.s = lax.axis_index("batch"), lax.axis_index("seq")

    def copy(self, r, k):
        other = (self.s + k) % 4
        return remote(
            self.src.at[other, r], self.dst.at[self.s, r], self.ss.at[r, k], self.rs.at[r, k],
            (self.b, other),
        )

    def start(self, r):
        for k in (2, 3, 1):
            self.copy(r, k).start()
        self.dst[self.s, r] = self.src[self.s, r]

    def wait(self, r):
        for k in (2, 3, 1):
            self.copy(r, k).wait_recv()

    def finish(self, r):
        for k in (2, 3, 1):
            self.copy(r, k).wait_send()


def fold(value):
    half = value.shape[0] // 2
    return jnp.concatenate([value[:half], value[half:]], axis=1)


def unfold(value):
    half = value.shape[1] // 2
    return jnp.concatenate([value[:, :half], value[:, half:]], axis=0)


def rounds(count):
    for _ in range(count):
        yield


def spaced(op, count):
    for _ in op:
        yield from rounds(count)


def step(op):
    try:
        next(op)
    except StopIteration:
        pass


def drain(op):
    for _ in op:
        pass


class DirectSum:
    peers = ("all",)

    def __init__(self, n, src):
        self.n = n
        self.scratch = [pltpu.VMEM(src.shape, F32)] + [pltpu.SemaphoreType.DMA((n,))] * 2

    def run(self, src, dst, arrived, ss, rs):
        n = self.n
        b, s = lax.axis_index("batch"), lax.axis_index("seq")
        copies = []
        for k in range(1, n):
            to = (b + k) % n
            copies.append(remote(src.at[to], arrived.at[k], ss.at[k], rs.at[k], (to, s)))
            copies[-1].start()
        yield
        total = src[b]
        for k, c in enumerate(copies):
            c.wait()
            total = total + arrived[k + 1]
        dst[...] = total


class BatchSum:
    peers = ("batch",)

    def __init__(self, n, src):
        self.n = n
        self.ins = [src]
        shape = src.shape[1:]
        self.outs = [jax.ShapeDtypeStruct(shape, F32)]
        m = n // 2
        self.scratch = [pltpu.VMEM((m,) + shape, BF16)] * 3 + [pltpu.SemaphoreType.DMA((m,))] * 4

    def run(self, src, dst, yrecv, zsend, zrecv, ys, yr, zs, zr):
        b, s, hi, lo, m = coords(self.n)
        pair = (hi * 2 + 1 - lo, s)
        first = {}
        for d in list(range(1, m)) + [0]:
            block = ((hi + d) % m) * 2 + 1 - lo
            first[d] = remote(src.at[block], yrecv.at[d], ys.at[d], yr.at[d], pair)
            first[d].start()
        yield
        second = []
        for d in range(1, m):
            h = (hi + d) % m
            first[d].wait_recv()
            zsend[d] = (src[h * 2 + lo].astype(F32) + yrecv[d].astype(F32)).astype(BF16)
            c = remote(zsend.at[d], zrecv.at[d], zs.at[d], zr.at[d], (h * 2 + lo, s))
            c.start()
            second.append(c)
            yield
        first[0].wait_recv()
        total = src[b].astype(F32) + yrecv[0].astype(F32)
        for d in range(1, m):
            second[d - 1].wait_recv()
            total = total + zrecv[d].astype(F32)
        dst[...] = total
        for c in list(first.values()) + second:
            c.wait_send()


class RowSum:
    @staticmethod
    def scratch(rows, shape):
        return [
            pltpu.VMEM((rows, 2) + shape, BF16),
            pltpu.VMEM((rows,) + shape, BF16),
            pltpu.VMEM((rows,) + shape, BF16),
            pltpu.SemaphoreType.DMA((rows, 3)),
            pltpu.SemaphoreType.DMA((rows, 3)),
        ]

    def __init__(self, src, near_in, far_out, far_in, ss, rs):
        self.src, self.near_in, self.far_out, self.far_in, self.ss, self.rs = (
            src, near_in, far_out, far_in, ss, rs,
        )
        self.b, self.s = lax.axis_index("batch"), lax.axis_index("seq")
        self.far, self.near = (self.s + 2) % 4, self.s + 1 - 2 * (self.s % 2)
        self.diag = (self.near + 2) % 4

    def beside(self, r, k):
        block = self.diag if k else self.near
        return remote(
            self.src.at[r, block], self.near_in.at[r, k], self.ss.at[r, k], self.rs.at[r, k],
            (self.b, self.near),
        )

    def across(self, r):
        return remote(
            self.far_out.at[r], self.far_in.at[r], self.ss.at[r, 2], self.rs.at[r, 2],
            (self.b, self.far),
        )

    def send_near(self, r):
        self.beside(r, 0).start()

    def send_diag(self, r):
        self.beside(r, 1).start()

    def cross(self, r):
        self.beside(r, 1).wait_recv()
        part = self.src[r, self.far].astype(F32) + self.near_in[r, 1].astype(F32)
        self.far_out[r] = part.astype(BF16)
        self.across(r).start()

    def total(self, r):
        self.beside(r, 0).wait_recv()
        part = self.src[r, self.s].astype(F32) + self.near_in[r, 0].astype(F32)
        self.across(r).wait_recv()
        return part + self.far_in[r].astype(F32)

    def finish(self, r):
        self.beside(r, 0).wait_send()
        self.beside(r, 1).wait_send()
        self.across(r).wait_send()


class Scratch:
    def __init__(self):
        self.names, self.shapes = [], []

    def add(self, **named):
        for name, shapes in named.items():
            one = not isinstance(shapes, list)
            shapes = [shapes] if one else shapes
            self.names.append((name, len(shapes), one))
            self.shapes += shapes

    def refs(self, refs):
        out, i = types.SimpleNamespace(), 0
        for name, count, one in self.names:
            setattr(out, name, refs[i] if one else refs[i : i + count])
            i += count
        return out


def layer(
    n, tokens, attn_weight, up_weight, down_weight, vec_own, pool_own, lengths, out_grad, up_moment, down_moment
):
    rows, span, width = tokens.shape
    quarter = width // SEQ
    span_all = span * SEQ
    own_rows = width // n
    local = rows * span
    aligned = own_rows % 16 == 0
    scale = HD**-0.5
    shape = jax.ShapeDtypeStruct
    full = (rows, SEQ, span, width)
    widths = (3 * quarter, quarter, width, width)
    low_ops = [GatherBatch(n, shape((own_rows, c), BF16), k < 2) for k, c in enumerate(widths)]
    low_ops = low_ops if aligned else []
    vec_op = GatherDirect(n, vec_own) if aligned else GatherBatch(n, vec_own)
    pool_op = GatherSeq(n, pool_own)
    out_op = GatherSeq(n, shape((width, quarter), BF16))
    sum_ops = [BatchSum(n, shape((n, own_rows, width), BF16)) for _ in range(2)]

    outs = [
        shape((rows, span, width), F32),
        shape((rows, width), F32),
        shape((rows, span, width), F32),
        shape((8, width), F32),
        shape((1, 3 * quarter), F32),
        shape(full, BF16),
    ]
    vmem = pl.BlockSpec(memory_space=pltpu.VMEM)
    anywhere = pl.BlockSpec(memory_space=pl.ANY)
    if aligned:
        outs += [shape((n, own_rows, width), BF16)]
        outs += [shape((2, own_rows, width), BF16), shape((SEQ, width, width), BF16)]
        out_specs = [anywhere, vmem, anywhere, vmem, vmem, anywhere, anywhere, vmem, anywhere]
    else:
        outs += [shape((width, width), BF16)] * 3
        out_specs = [vmem] * 9

    dma = pltpu.SemaphoreType.DMA
    sc = Scratch()
    if aligned:
        sc.add(
            lows=[pltpu.VMEM((own_rows, c), BF16) for c in widths],
            weights=[pltpu.VMEM(op.outs[0].shape, BF16) for op in low_ops],
            low_moves=[c for op in low_ops for c in op.scratch],
        )
    sc.add(vec_parts=pltpu.VMEM(vec_op.outs[0].shape, F32))
    sc.add(vec_move=vec_op.scratch)
    sc.add(vec=pltpu.VMEM((8, width), F32))
    sc.add(pool_parts=pltpu.VMEM(pool_op.outs[0].shape, F32))
    sc.add(pool_move=pool_op.scratch)
    sc.add(out_own=pltpu.VMEM((width, quarter), BF16))
    sc.add(out_parts=pltpu.VMEM((SEQ, width, quarter), BF16))
    sc.add(out_move=out_op.scratch)
    sc.add(w_out=pltpu.VMEM((width, width), BF16))
    sc.add(x_all=pltpu.VMEM(full, BF16))
    sc.add(x_gather=RowGather.scratch())
    sc.add(qkv=pltpu.VMEM((rows, span_all, 3 * quarter), BF16))
    sc.add(prob=pltpu.VMEM((rows, HEADS, span_all, span_all), F32))
    sc.add(swap=RowSwap.scratch((SEQ, rows, span, quarter)))
    sc.add(back_swap=RowSwap.scratch((SEQ, rows, span, quarter)))
    sc.add(context=pltpu.VMEM((rows, span, width), BF16))
    sc.add(normed=pltpu.VMEM((rows, span, width), F32))
    sc.add(scaled_one=pltpu.VMEM((rows, span, width), F32))
    sc.add(spread_one=pltpu.VMEM((rows, span, 1), F32))
    sc.add(y_all=pltpu.VMEM(full, BF16))
    sc.add(y_gather=RowGather.scratch())
    sc.add(slope=pltpu.VMEM(full, F32))
    sc.add(act=pltpu.VMEM(full, BF16))
    sc.add(z_sum=RowSum.scratch(rows, (span, width)))
    sc.add(dz_all=pltpu.VMEM(full, BF16))
    sc.add(dz_gather=RowGather.scratch())
    sc.add(du_all=pltpu.VMEM(full, BF16))
    sc.add(dy_sum=RowSum.scratch(rows, (span, width)))
    sc.add(pool_buf=pltpu.VMEM((SEQ, rows, width), F32))
    sc.add(pool_sems=[dma((3,)), dma((3,))])
    sc.add(a_quarters=pltpu.VMEM((SEQ, local, quarter), BF16))
    sc.add(out_part=pltpu.VMEM((1, SEQ, width, quarter), BF16))
    sc.add(out_sum=RowSum.scratch(1, (width, quarter)))
    if not aligned:
        sc.add(x_sum=RowSum.scratch(rows, (span, width)))
    sc.add(grad_qkv=pltpu.VMEM((rows, span_all, 3 * quarter), BF16))
    if aligned:
        sc.add(early=[pltpu.VMEM(outs[k].shape, outs[k].dtype) for k in (0, 2, 5, 6)])
        sc.add(early_sems=dma((4,)))
        sc.add(raw=dma((2 * SEQ + 1,)))
        sc.add(
            down_grad=pltpu.VMEM((n, own_rows, width), BF16),
            up_grad=pltpu.VMEM((n, own_rows, width), BF16),
            down_piece=pltpu.VMEM((own_rows, width), F32),
            up_piece=pltpu.VMEM((own_rows, width), F32),
            down_sum=sum_ops[0].scratch,
            up_sum=sum_ops[1].scratch,
        )
        sc.add(vec_low=pltpu.VMEM(vec_own.shape, F32))
        sc.add(wide_send=pltpu.VMEM((2, own_rows, width), BF16))
        sc.add(mail=OwnerMail.scratch(n, 2, (own_rows, width)))

    def kernel(
        tokens, attn_weight, up_weight, down_weight, vec_own, pool_own, lengths, out_grad, up_moment, down_moment,
        out_rows, pooled, second, vec_grad, bias_sums, part, grad_attn, *rest,
    ):
        if aligned:
            wide_bf, wide_in = rest[:2]
            rest = rest[2:]
        else:
            grad_up_out, grad_down_out = rest[:2]
            rest = rest[2:]
        at = sc.refs(rest)
        if aligned:
            leaving = [
                pltpu.make_async_copy(a, b, at.early_sems.at[k])
                for k, (a, b) in enumerate(zip(at.early, (out_rows, second, part, grad_attn)))
            ]
            out_rows, second, part, grad_attn = at.early
        kinds = {"all"} if aligned else {"seq", "batch"}
        greet_signal(n, kinds)
        b, s = lax.axis_index("batch"), lax.axis_index("seq")
        x_all, y_all, dz_all, du_all = at.x_all, at.y_all, at.dz_all, at.du_all
        slope, act, prob, qkv = at.slope, at.act, at.prob, at.qkv
        normed, context, vec = at.normed, at.context, at.vec
        x_gather = RowGather(x_all, *at.x_gather)
        y_gather = RowGather(y_all, *at.y_gather)
        dz_gather = RowGather(dz_all, *at.dz_gather)
        swap, back_swap = RowSwap(*at.swap), RowSwap(*at.back_swap)
        z_sum, dy_sum = [RowSum(part, *refs) for refs in (at.z_sum, at.dy_sum)]
        out_sum = RowSum(at.out_part, *at.out_sum)
        far, near, diag = x_gather.far, x_gather.near, x_gather.diag

        def raw_block(k):
            return slope.at[k // SEQ, k % SEQ, pl.ds(0, own_rows)]

        def load_up(matrix):
            return [
                pltpu.make_async_copy(
                    matrix.at[:, pl.ds(k * width, width)], raw_block(SEQ + k), at.raw.at[SEQ + k]
                )
                for k in range(SEQ)
            ]

        def load_down(matrix, place):
            return pltpu.make_async_copy(
                matrix.at[pl.ds(s * own_rows, own_rows)], place, at.raw.at[2 * SEQ]
            )

        def raw_up(k):
            whole = jnp.concatenate([raw_block(SEQ + j)[...] for j in range(SEQ)], axis=1)
            return take_up(whole, n, k)

        if aligned:
            raws = [
                pltpu.make_async_copy(attn_weight.at[k], raw_block(k), at.raw.at[k]) for k in range(4)
            ]
            raws += load_up(up_weight)
            raws.append(load_down(down_weight, second.at[0, pl.ds(0, own_rows)]))
            for c in raws:
                c.start()
        for r in range(rows):
            x_all[r, s] = tokens[r].astype(BF16)
        if aligned:
            for c in raws[:4]:
                c.wait()
            for k in range(SEQ):

                @pl.when(s == k)
                def _(k=k):
                    block = [raw_block(j)[:, k * quarter : (k + 1) * quarter] for j in range(4)]
                    at.lows[0][...] = jnp.concatenate(block[:3], axis=1).astype(BF16)
                    at.lows[1][...] = block[3].astype(BF16)

            vec_low = at.vec_low
            vec_low[...] = vec_own[...].astype(BF16).astype(F32)
        else:
            vec_low = vec_own

        greet_wait(n, kinds)
        vec_move = vec_op.run(vec_low, at.vec_parts, *at.vec_move)
        pool_move = pool_op.run(pool_own, at.pool_parts, *at.pool_move)
        step(vec_move)
        if aligned:
            moves = [
                op.run(at.lows[k], at.weights[k], *at.low_moves[5 * k : 5 * k + 5])
                for k, op in enumerate(low_ops)
            ]
            step(moves[0])
        step(pool_move)
        for r in range(rows):
            x_gather.start(r)
        if aligned:
            for c in raws[4:]:
                c.wait()
            for k in range(SEQ):

                @pl.when(s == k)
                def _(k=k):
                    at.lows[2][...] = raw_up(k).astype(BF16)

            at.lows[3][...] = second[0, :own_rows].astype(BF16)
            step(moves[0])
        x_gather.pass_far(0)
        if aligned:
            step(moves[0])
        step(pool_move)
        x_gather.pass_far(1)
        if aligned:
            step(moves[0])
            step(moves[1])
            step(moves[2])
        drain(vec_move)
        drain(pool_move)
        if aligned:
            whole = jnp.concatenate([at.vec_parts[k] for k in range(n)], axis=1)

            def here(make):
                return sum(jnp.where(s == k, make(k), 0.0) for k in range(SEQ))

            vec[0:6] = whole[2:8]
            vec[6:7] = here(
                lambda k: jnp.concatenate(
                    [
                        whole[8 + f // width : 9 + f // width, f % width : f % width + own_rows]
                        for f in ((j * SEQ + k) * own_rows for j in range(n))
                    ],
                    axis=1,
                )
            )
            blank = jnp.zeros((1, quarter), F32)
            vec[7:8] = here(
                lambda k: jnp.concatenate(
                    [
                        whole[0:1, k * quarter : (k + 1) * quarter],
                        blank,
                        whole[1:2, k * quarter : (k + 1) * quarter],
                        blank,
                    ],
                    axis=1,
                )
            )
        else:
            total = at.vec_parts[0]
            for k in range(1, n):
                total = total + at.vec_parts[k]
            vec[...] = total
        pool_whole = jnp.concatenate([at.pool_parts[k] for k in range(SEQ)], axis=1)

        if aligned:
            drain(moves[0])
            step(moves[1])
            step(moves[2])
            step(moves[3])

        def w_qkv():
            if aligned:
                return at.weights[0][...].reshape(width, 3 * quarter)
            return attn_weight[:, : 3 * quarter]

        def w_up():
            return at.weights[2][...].reshape(width, width) if aligned else up_weight[...]

        def w_down():
            return at.weights[3][...].reshape(width, width) if aligned else down_weight[...]

        out_move = out_op.run(at.out_own, at.out_parts, *at.out_move)

        def begin_out():
            if aligned:
                drain(moves[1])
                at.out_own[...] = at.weights[1][...].reshape(width, quarter)
            else:
                at.out_own[...] = attn_weight[:, 3 * quarter :]
            step(out_move)

        def turn(*ks):
            for k in ks:
                if aligned:
                    step(moves[k])

        bias = vec[7:8, : 3 * quarter]
        column = lax.broadcasted_iota(jnp.int32, (1, span_all), 1)

        def heads(r, h):
            return [
                qkv[r, :, k * quarter + h * HD : k * quarter + (h + 1) * HD] for k in range(3)
            ]

        for r in range(rows):
            x_gather.wait_near(r)
            x_gather.wait_diag(r)
            block = matmul(x_all[r].reshape(span_all, width), w_qkv()) + bias
            qkv[r] = block.astype(BF16)
            valid = column < lengths[r]
            if r == 0:
                turn(1)
            mixed = []
            for h in range(HEADS):
                query, key, value = heads(r, h)
                scores = contract_last(query * jnp.bfloat16(scale), key)
                scores = jnp.where(valid, scores, -1e30)
                exponent = jnp.exp(scores - jnp.max(scores, axis=-1, keepdims=True))
                weight = exponent * (1.0 / jnp.sum(exponent, axis=-1, keepdims=True))
                prob[r, h] = weight
                mixed.append(matmul(weight.astype(BF16), value))
                if r == 0 and h == 0:
                    turn(1, 3, 2)
                if r == 0 and h == 1:
                    begin_out()
                    turn(2)
                if r == 0 and h == 2:
                    turn(2)
                if r == 1:
                    turn(3)
            mixed = jnp.concatenate(mixed, axis=1).astype(BF16)
            for k in range(SEQ):
                at.swap[0][k, r] = mixed[k * span : (k + 1) * span]
            swap.start(r)
        step(out_move)
        drain(out_move)
        w_out = at.w_out
        w_out[...] = jnp.concatenate([at.out_parts[k] for k in range(SEQ)], axis=1)
        gain_one, shift_one = vec[1:2], vec[2:3]
        for r in range(rows):
            swap.wait(r)
            context[r] = jnp.concatenate([at.swap[1][k, r] for k in range(SEQ)], axis=1)
            hidden = tokens[r] + (matmul(context[r], w_out[...]) + vec[0:1])
            centred = hidden - jnp.mean(hidden, axis=-1, keepdims=True)
            spread = lax.rsqrt(jnp.mean(centred * centred, axis=-1, keepdims=True) + norm_eps)
            scaled = centred * spread
            at.scaled_one[r] = scaled
            at.spread_one[r] = spread
            value = scaled * gain_one + shift_one
            normed[r] = value
            y_all[r, s] = value.astype(BF16)
            y_gather.start(r)

        if aligned:
            drain(moves[2])
        gain_two, shift_two = vec[3:4], vec[4:5]
        bias_down, bias_up = vec[5:6], vec[6:7]

        def pair(ref, blocks):
            return jnp.concatenate([ref[i] for i in blocks], axis=0)

        def put(ref, blocks, value):
            for k, i in enumerate(blocks):
                ref[i] = value[k * span : (k + 1) * span].astype(ref.dtype)

        def rise(blocks):
            value, rate = gelu_parts(matmul(pair(y_all, blocks), w_up()) + bias_up)
            put(act, blocks, value)
            put(slope, blocks, rate)

        def fall(blocks):
            put(part, blocks, matmul(pair(act, blocks), w_down()))

        mine, beside = [[(r, k) for r in range(rows)] for k in (s, near)]
        rise(mine)
        for r in range(rows):
            y_gather.wait_near(r)
        rise(beside)
        if aligned:
            drain(moves[3])
        fall(beside)
        for r in range(rows):
            z_sum.send_near(r)
        for r in range(rows):
            y_gather.pass_far(r)
            y_gather.wait_diag(r)
            rise([(r, diag), (r, far)])
            fall([(r, diag), (r, far)])
            z_sum.send_diag(r)
            if r == 0:
                fall(mine)
            z_sum.cross(r)

        position = s * span + lax.broadcasted_iota(jnp.int32, (span, 1), 0)
        grad_gain_two = grad_shift_two = grad_bias_down = jnp.zeros((1, width), F32)
        for r in range(rows):
            hidden = normed[r] + (z_sum.total(r) + bias_down)
            centred = hidden - jnp.mean(hidden, axis=-1, keepdims=True)
            spread_two = lax.rsqrt(jnp.mean(centred * centred, axis=-1, keepdims=True) + norm_eps)
            scaled = centred * spread_two
            output = scaled * gain_two + shift_two
            out_rows[r] = output
            live = (position < lengths[r]).astype(F32)
            length = jnp.full((1, 1), lengths[r], jnp.int32).astype(F32)
            at.pool_buf[s, r : r + 1] = row_sum(output * live) / length
            upstream = live * (out_grad[r] + pool_whole[r : r + 1] / length)
            weighted = upstream * gain_two
            mean_first = jnp.mean(weighted, axis=-1, keepdims=True)
            mean_second = jnp.mean(weighted * scaled, axis=-1, keepdims=True)
            grad = spread_two * (weighted - mean_first - scaled * mean_second)
            second[r] = grad
            low = grad.astype(BF16)
            dz_all[r, s] = low
            dz_gather.start(r)
            grad_gain_two += row_sum(upstream * scaled)
            grad_shift_two += row_sum(upstream)
            grad_bias_down += row_sum(low.astype(F32))

        if aligned:
            leaving[0].start()

        def pool_copy(k, block, device):
            place = at.pool_buf.at[block]
            sems = at.pool_sems
            return remote(place, place, sems[0].at[k - 1], sems[1].at[k - 1], (b, device))

        for k in (1, 2, 3):
            pool_copy(k, s, (s + k) % 4).start()
        for r in range(rows):
            z_sum.finish(r)

        def backward(blocks):
            lift = contract_last(pair(dz_all, blocks), w_down())
            low = (lift * pair(slope, blocks)).astype(BF16)
            put(du_all, blocks, low)
            put(part, blocks, contract_last(low, w_up()))
            return row_sum(low.astype(F32))

        bias_grad = backward(mine)
        for r in range(rows):
            dz_gather.wait_near(r)
        bias_grad += backward(beside)
        for r in range(rows):
            dy_sum.send_near(r)
        for r in range(rows):
            dz_gather.pass_far(r)
            dz_gather.wait_diag(r)
            bias_grad += backward([(r, diag), (r, far)])
            dy_sum.send_diag(r)
            dy_sum.cross(r)

        flat = rows * span_all
        if aligned:
            down_move = sum_ops[0].run(at.down_grad, at.down_piece, *at.down_sum)
            up_move = sum_ops[1].run(at.up_grad, at.up_piece, *at.up_sum)
            mail = OwnerMail(n, owner_list(n)[4:], wide_in, *at.mail)
            wide_send = at.wide_send
            momenta = load_up(up_moment) + [load_down(down_moment, raw_block(0))]
            for c in momenta:
                c.start()
        whole = contract_first(act[...].reshape(flat, width), dz_all[...].reshape(flat, width))
        if aligned:
            at.down_grad[...] = whole.reshape(n, own_rows, width).astype(BF16)
            step(down_move)
        else:
            grad_down_out[...] = whole.astype(BF16)
        whole = contract_first(y_all[...].reshape(flat, width), du_all[...].reshape(flat, width))
        if aligned:
            at.up_grad[...] = whole.reshape(n, own_rows, width).astype(BF16)
            step(up_move)
        else:
            grad_up_out[...] = whole.astype(BF16)

        grad_gain_one = grad_shift_one = grad_bias_out = jnp.zeros((1, width), F32)
        for r in range(rows):
            grad = dy_sum.total(r) + second[r]
            scaled = at.scaled_one[r]
            weighted = grad * gain_one
            mean_first = jnp.mean(weighted, axis=-1, keepdims=True)
            mean_second = jnp.mean(weighted * scaled, axis=-1, keepdims=True)
            first = at.spread_one[r] * (weighted - mean_first - scaled * mean_second)
            second[r] = first
            low = first.astype(BF16)
            above = contract_last(low, w_out[...]).astype(BF16)
            for k in range(SEQ):
                columns = slice(k * quarter, (k + 1) * quarter)
                at.back_swap[0][k, r] = above[:, columns]
                at.a_quarters[k, r * span : (r + 1) * span] = low[:, columns]
            back_swap.start(r)
            grad_gain_one += row_sum(grad * scaled)
            grad_shift_one += row_sum(grad)
            grad_bias_out += row_sum(low.astype(F32))
        for k, value in enumerate(
            (
                grad_bias_out, grad_gain_one, grad_shift_one, grad_gain_two, grad_shift_two,
                grad_bias_down, bias_grad, jnp.zeros((1, width), F32),
            )
        ):
            vec_grad[k : k + 1] = value

        def new_momentum(k, piece, old):
            wide_bf[k] = piece[...].astype(BF16)
            wide_send[k] = (matrix_decay * old + wide_bf[k].astype(F32)).astype(BF16)
            mail.send(k, wide_send.at[k])

        flat_context = context[...].reshape(local, width)
        for k in range(SEQ):
            at.out_part[0, k] = contract_first(flat_context, at.a_quarters[k]).astype(BF16)
        out_sum.send_diag(0)
        out_sum.send_near(0)
        for r in range(rows):
            dy_sum.finish(r)
        sums = jnp.zeros((1, 3 * quarter), F32)
        for r in range(rows):
            back_swap.wait(r)
            arrived = jnp.concatenate([at.back_swap[1][k, r] for k in range(SEQ)], axis=0)
            query_grads, key_grads, value_grads = [], [], []
            for h in range(HEADS):
                query, key, value = heads(r, h)
                above = arrived[:, h * HD : (h + 1) * HD]
                weight = prob[r, h]
                prob_grad = contract_last(above, value)
                delta = jnp.sum(weight * prob_grad, axis=-1, keepdims=True)
                score_grad = (weight * (prob_grad - delta)).astype(BF16)
                query_grads.append(matmul(score_grad, key) * scale)
                key_grads.append(contract_first(query, score_grad) * scale)
                value_grads.append(contract_first(above, weight.astype(BF16)))
                if aligned and r == 0:
                    step(down_move)
                if r == 1 and h == 0:
                    out_sum.cross(0)
                if aligned and r == 1 and h > 0:
                    step(up_move)
                if not aligned and r > 0 and h == 2:
                    x_sum.cross(r - 1)
            turned = jnp.concatenate(key_grads + value_grads, axis=0).T
            block = jnp.concatenate(query_grads + [turned], axis=1).astype(BF16)
            at.grad_qkv[r] = block
            sums += row_sum(block.astype(F32))
            out = contract_last(block, w_qkv())
            for k in range(SEQ):
                part[r, k] = out[k * span : (k + 1) * span].astype(BF16)
            if not aligned:
                if r == 0:
                    x_sum = RowSum(part, *at.x_sum)
                x_sum.send_diag(r)
                x_sum.send_near(r)
        if aligned:
            step(up_move)
            drain(down_move)
            for c in momenta:
                c.wait()
            new_momentum(1, at.down_piece, raw_block(0)[...])
        bias_sums[...] = sums
        if aligned:
            leaving[1].start()
            leaving[2].start()
        whole = contract_first(
            x_all[...].reshape(flat, width), at.grad_qkv[...].reshape(flat, 3 * quarter)
        )
        whole = jnp.concatenate([whole, out_sum.total(0)], axis=1)
        grad_attn[...] = whole.astype(BF16).reshape(grad_attn.shape)
        if aligned:
            leaving[3].start()
        for k in (1, 2, 3):
            pool_copy(k, (s + 4 - k) % 4, (s + k) % 4).wait_recv()
        pool_buf = at.pool_buf
        pooled[...] = (pool_buf[0] + pool_buf[1]) + (pool_buf[2] + pool_buf[3])
        if aligned:
            mail.relay(1)
            drain(up_move)
            for k in range(SEQ):

                @pl.when(s == k)
                def _(k=k):
                    wide_bf[0] = at.up_piece[...].astype(BF16)
                    old = matrix_decay * raw_up(k) + wide_bf[0].astype(F32)
                    wide_send[0] = old.astype(BF16)

            mail.send(0, wide_send.at[0])
        else:
            x_sum.cross(rows - 1)
            for r in range(rows):
                second[r] = x_sum.total(r) + second[r]
                x_sum.finish(r)
        out_sum.finish(0)
        for k in (1, 2, 3):
            pool_copy(k, s, (s + k) % 4).wait_send()
        for r in range(rows):
            for op in (x_gather, swap, y_gather, dz_gather, back_swap):
                op.finish(r)
        if aligned:
            mail.relay(0)

            @pl.when(mail.mine[0] | mail.mine[1])
            def _():
                mail.collect()

            for k in range(2):
                mail.finish(k, wide_send.at[k])
            for c in leaving:
                c.wait()

    smem = pl.BlockSpec(memory_space=pltpu.SMEM)
    far_spec = anywhere if aligned else vmem
    return pl.pallas_call(
        kernel,
        out_shape=outs,
        in_specs=[vmem] + [far_spec] * 3 + [vmem] * 2 + [smem, vmem] + [anywhere] * 2,
        out_specs=out_specs,
        scratch_shapes=sc.shapes,
        compiler_params=pltpu.CompilerParams(
            collective_id=0, has_side_effects=True, vmem_limit_bytes=63 * 2**20
        ),
        name="layer",
    )(tokens, attn_weight, up_weight, down_weight, vec_own, pool_own, lengths, out_grad, up_moment, down_moment)


def join_up_parts(parts, n):
    hid_own = parts[0].shape[1] // n
    return jnp.concatenate(
        [parts[k][:, b * hid_own : (b + 1) * hid_own] for b in range(n) for k in range(SEQ)], axis=1
    )


def take_up(matrix, n, k):
    hid_own = matrix.shape[1] // n // SEQ
    return jnp.concatenate(
        [
            matrix[:, (b * SEQ + k) * hid_own : (b * SEQ + k + 1) * hid_own]
            for b in range(n)
        ],
        axis=1,
    )


def muon(n, grad_attn, wide_in, bias_sums, vec_grad, attn_moment, wide_bf, x_part, first_grad):
    rows, width = wide_bf.shape[1:]
    quarter = width // SEQ
    hid_own = rows
    n_vec = 8 + SEQ
    shape = jax.ShapeDtypeStruct
    attn_shape = (4, rows // 2, 2 * quarter)
    attn_op = GatherSeq(n, shape(attn_shape, BF16))
    attn_sum = BatchSum(n, grad_attn)
    vec_sum = DirectSum(n, shape((n, n_vec, rows), F32))
    vec_op = GatherSeq(n, shape((n_vec, rows), F32))
    wide_op = GatherSeq(n, wide_bf)
    count, span = first_grad.shape[:2]
    main = Muon(n, shape(attn_shape, BF16), wide_in=wide_in)
    outs = [attn_op.outs[0], wide_op.outs[0], shape((n_vec, rows), F32), shape(first_grad.shape, F32)]
    outs += main.outs
    groups = [
        [
            pltpu.VMEM((rows, width), F32),
            pltpu.VMEM(attn_shape, BF16),
            pltpu.VMEM(attn_shape, BF16),
            pltpu.VMEM((n, n_vec, rows), F32),
            pltpu.VMEM((n_vec, rows), F32),
            pltpu.VMEM((SEQ, n_vec, rows), F32),
        ]
    ] + [op.scratch for op in (attn_op, vec_sum, vec_op, main, attn_sum, wide_op)]
    groups.append(RowSum.scratch(count, (span, width)))
    late = (attn_moment, x_part, first_grad)
    groups.append([pltpu.VMEM(a.shape, a.dtype) for a in late] + [pltpu.SemaphoreType.DMA((3,))])

    def kernel(
        grad_attn, wide_in, bias_sums, vec_grad, attn_moment, wide_bf, x_part, first_grad,
        attn_all, wide_all, vec_total, input_grad, attn_orth, wide_orth, *rest,
    ):
        greet_signal(n, {"all"})
        parts, i = [], 0
        for group in groups:
            parts.append(rest[i : i + len(group)])
            i += len(group)
        attn_piece, attn_bf, attn_send, vec_local, vec_piece, vec_parts = parts[0]
        s = lax.axis_index("seq")
        arriving = [
            pltpu.make_async_copy(a, b, parts[8][3].at[k])
            for k, (a, b) in enumerate(zip((attn_moment, x_part, first_grad), parts[8][:3]))
        ]
        attn_moment, x_part, first_grad = parts[8][:3]
        for c in arriving:
            c.start()
        main_move = main.run(attn_send, wide_in, attn_orth, wide_orth, *parts[4])
        step(main_move)
        main.prepare()
        greet_wait(n, {"all"})
        x_sum = RowSum(x_part, *parts[7])

        def inputs():
            arriving[1].wait()
            arriving[2].wait()
            for r in range(count):
                x_sum.send_diag(r)
                x_sum.send_near(r)
            yield
            for r in range(count):
                x_sum.cross(r)
            yield from rounds(8)
            for r in range(count):
                input_grad[r] = x_sum.total(r) + first_grad[r]
                x_sum.finish(r)

        def attention():
            moving = attn_sum.run(grad_attn, attn_piece, *parts[5])
            step(moving)
            yield from rounds(3)
            for _ in range(n // 2 - 1):
                step(moving)
            yield from rounds(3)
            drain(moving)
            arriving[0].wait()
            for j in range(4):
                attn_bf[j] = fold(attn_piece[:, j * quarter : (j + 1) * quarter]).astype(BF16)
            for k in range(SEQ):

                @pl.when(s == k)
                def _(k=k):
                    for j in range(4):
                        old = fold(attn_moment[j, :, k * quarter : (k + 1) * quarter])
                        attn_send[j] = (matrix_decay * old + attn_bf[j].astype(F32)).astype(BF16)
            main.send_attn()
            yield
            main.attn_turn()
            yield from spaced(attn_op.run(attn_bf, attn_all, *parts[1]), 2)

        def vectors():
            def here(k, value):
                return jnp.where(s == k, value, 0.0)

            lines = [
                jnp.concatenate(
                    [here(k, bias_sums[:, j * quarter : (j + 1) * quarter]) for k in range(SEQ)], axis=1
                )
                for j in (0, 2)
            ]
            lines += [vec_grad[j : j + 1] for j in range(6)]
            hidden = vec_grad[6:7]
            pieces = [
                here(k, hidden[:, b * hid_own : (b + 1) * hid_own]) for b in range(n) for k in range(SEQ)
            ]
            each = n * SEQ // 4
            lines += [jnp.concatenate(pieces[j * each : (j + 1) * each], axis=1) for j in range(4)]
            whole = jnp.concatenate(lines, axis=0)
            for b in range(n):
                vec_local[b] = whole[:, b * rows : (b + 1) * rows]
            yield from spaced(vec_sum.run(vec_local, vec_piece, *parts[2]), 3)
            yield from spaced(vec_op.run(vec_piece, vec_parts, *parts[3]), 2)
            vec_total[...] = (vec_parts[0] + vec_parts[1]) + (vec_parts[2] + vec_parts[3])

        run_together(
            vectors(),
            attention(),
            inputs(),
            spaced(wide_op.run(wide_bf, wide_all, *parts[6]), 6),
            main_move,
        )

    vmem = pl.BlockSpec(memory_space=pltpu.VMEM)
    far = pl.BlockSpec(memory_space=pl.ANY)
    ins = (grad_attn, wide_in, bias_sums, vec_grad, attn_moment, wide_bf, x_part, first_grad)
    return pl.pallas_call(
        kernel,
        out_shape=outs,
        in_specs=[vmem, far, vmem, vmem, far, vmem, far, far],
        out_specs=[vmem] * len(outs),
        scratch_shapes=[c for group in groups for c in group],
        compiler_params=pltpu.CompilerParams(
            collective_id=8, has_side_effects=True, vmem_limit_bytes=62 * 2**20
        ),
        name="muon",
    )(*ins)


def finish(
    n, out_rows, pool_sum, input_grad, attn_all, wide_all, attn_orth, wide_orth, vec_total,
    attn_weight, up_weight, down_weight, vectors, attn_moment, up_moment, down_moment, vector_moment,
    factors, vector_step,
):
    rows = wide_all.shape[2]
    quarter = wide_all.shape[3] // SEQ
    shape = jax.ShapeDtypeStruct
    ins = (
        attn_all, attn_moment, wide_all, up_moment, down_moment, out_rows, input_grad, pool_sum, vec_total,
        vectors, vector_moment, attn_orth, attn_weight, wide_orth, up_weight, down_weight,
    )
    token, pool = shape(out_rows.shape, F32), shape((out_rows.shape[0], quarter), F32)
    attn, up, down, vec = [shape(a.shape, F32) for a in (attn_weight, up_weight, down_weight, vectors)]
    outs = [token, pool, token] + [attn, up, down, vec] * 3
    direct = {0: 5, 2: 6}
    held = [k for k in range(len(outs)) if k not in direct]

    def kernel(*refs):
        far_in, far_out = refs[: len(ins)], refs[len(ins) : len(ins) + len(outs)]
        refs = refs[len(ins) + len(outs) :]
        near_in = refs[: len(ins)]
        near_out = dict(zip(held, refs[len(ins) :]))
        near_out.update({k: near_in[j] for k, j in direct.items()})
        in_sem, out_sem = refs[-2:]
        arriving = [
            pltpu.make_async_copy(a, b, in_sem.at[k]) for k, (a, b) in enumerate(zip(far_in, near_in))
        ]
        leaving = [
            pltpu.make_async_copy(near_out[k], far_out[k], out_sem.at[k]) for k in range(len(outs))
        ]
        for c in arriving:
            c.start()
        (
            attn_all, attn_moment, wide_all, up_moment, down_moment, _, _, pool_sum, vec_total,
            vectors, vector_moment, attn_orth, attn_weight, wide_orth, up_weight, down_weight,
        ) = near_in
        (
            _, pooled, _, attn_grad, up_grad, down_grad, vec_grad, attn_next, up_next, down_next, vec_next,
            attn_new, up_new, down_new, vec_new,
        ) = [near_out[k] for k in range(len(outs))]

        def wait(*ks):
            for k in ks:
                arriving[k].wait()

        def leave(*ks):
            for k in ks:
                leaving[k].start()

        def attn_of(parts, j):
            return jnp.concatenate([unfold(parts[k, j]) for k in range(SEQ)], axis=1).astype(F32)

        wait(0, 1)
        for j in range(4):
            grad = attn_of(attn_all, j)
            attn_grad[j] = grad
            attn_next[j] = matrix_decay * attn_moment[j] + grad
        leave(3, 7)
        wait(2, 3)
        grad = join_up_parts([wide_all[k, 0] for k in range(SEQ)], n).astype(F32)
        up_grad[...] = grad
        up_next[...] = matrix_decay * up_moment[...] + grad
        leave(4, 8)
        wait(4)
        for k in range(SEQ):
            part = pl.ds(k * rows, rows)
            grad = wide_all[k, 1].astype(F32)
            down_grad[part] = grad
            down_next[part] = matrix_decay * down_moment[part] + grad
        leave(5, 9)
        wait(5)
        leave(0)
        wait(6)
        leave(2)
        wait(7, 8, 9, 10)
        s = lax.axis_index("seq")
        pooled[...] = sum(
            jnp.where(s == k, pool_sum[:, k * quarter : (k + 1) * quarter], 0.0) for k in range(SEQ)
        )
        vec_grad[...] = vec_total[...]
        moved = vector_decay * vector_moment[...] + vec_total[...]
        vec_next[...] = moved
        vec_new[...] = vectors[...] - vector_step * moved
        leave(1, 6, 10, 14)
        wait(11, 12)
        for j in range(4):
            attn_new[j] = attn_weight[j] - factors[0] * attn_of(attn_orth, j)
        leave(11)
        wait(13, 14)
        orth = join_up_parts([wide_orth[k, 0] for k in range(SEQ)], n).astype(F32)
        up_new[...] = up_weight[...] - factors[1] * orth
        leave(12)
        wait(15)
        for k in range(SEQ):
            part = pl.ds(k * rows, rows)
            down_new[part] = down_weight[part] - factors[2] * wide_orth[k, 1].astype(F32)
        leave(13)
        for c in leaving:
            c.wait()

    anywhere = pl.BlockSpec(memory_space=pl.ANY)
    return pl.pallas_call(
        kernel,
        out_shape=outs,
        in_specs=[anywhere] * len(ins),
        out_specs=[anywhere] * len(outs),
        scratch_shapes=[pltpu.VMEM(a.shape, a.dtype) for a in ins]
        + [pltpu.VMEM(outs[k].shape, F32) for k in held]
        + [pltpu.SemaphoreType.DMA((len(ins),)), pltpu.SemaphoreType.DMA((len(outs),))],
        compiler_params=pltpu.CompilerParams(vmem_limit_bytes=60 * 2**20),
        name="finish",
    )(*ins)


def step_factor(rows_all, cols_all):
    return matrix_rate * math.sqrt(max(1.0, rows_all / cols_all))


def make_body(n):
    def body(
        layer_input,
        lengths,
        attn_weight,
        up_weight,
        down_weight,
        vectors,
        attn_moment,
        up_moment,
        down_moment,
        vector_moment,
        out_grad,
        pool_grad,
    ):
        rows, span, width = layer_input.shape
        own_rows = width // n
        quarter = width // SEQ
        hidden = up_weight.shape[1]
        hid_q = hidden // SEQ
        hid_own = hidden // n // SEQ
        seq_index = lax.axis_index("seq")

        def attn_quarter(stacked):
            part = lax.dynamic_index_in_dim(
                stacked.reshape(4, own_rows, SEQ, quarter), seq_index, 2, False
            )
            return part

        def up_quarter(matrix):
            return lax.dynamic_index_in_dim(
                matrix.reshape(own_rows, n, SEQ, hid_own), seq_index, 2, False
            ).reshape(own_rows, hid_q)

        def down_quarter(matrix):
            return lax.dynamic_index_in_dim(
                matrix.reshape(SEQ, hid_own, width), seq_index, 0, False
            )

        aligned = own_rows % 16 == 0
        if aligned:
            own = [attn_weight, up_weight, down_weight]
            vec_own = vectors
        else:
            attn_low = attn_quarter(attn_weight).astype(BF16).transpose(1, 0, 2).reshape(own_rows, width)
            up_low = up_quarter(up_weight).astype(BF16)
            down_low = down_quarter(down_weight).astype(BF16)
            vec_low = vectors.astype(BF16).astype(F32)
            placed = lax.dynamic_update_slice(
                jnp.zeros((vectors.shape[0], n, own_rows), F32),
                vec_low[:, None],
                (0, lax.axis_index("batch"), 0),
            ).reshape(-1, width)
            bias_up = lax.dynamic_index_in_dim(
                placed[8:].reshape(n, SEQ, hid_own), seq_index, 1, False
            ).reshape(1, hid_q)
            bias_qv = lax.dynamic_index_in_dim(
                placed[:2].reshape(2, SEQ, quarter), seq_index, 1, False
            )
            blank = jnp.zeros((quarter,), F32)
            bias_qkv = jnp.concatenate([bias_qv[0], blank, bias_qv[1], blank])[None]
            vec_own = jnp.concatenate([placed[2:8], bias_up, bias_qkv])
            own = exchange(
                n, 1, "gather_weights", *[GatherBatch(n, a) for a in (attn_low, up_low, down_low)]
            )
            own = [a.reshape(width, width) for a in own]
        out_rows, pool_sum, input_grad, vec_grad, bias_sums, x_part, *grads = layer(
            n, layer_input, *own, vec_own, pool_grad, lengths, out_grad, up_moment, down_moment
        )
        factors = [
            step_factor(width, width),
            step_factor(width, hidden),
            step_factor(hidden, width),
        ]
        vector_step = vector_rate / math.sqrt(rows * n)
        if aligned:
            grad_attn, wide_bf, wide_in = grads
            attn_all, wide_all, vec_total, input_grad, attn_orth, wide_orth = muon(
                n, grad_attn, wide_in, bias_sums, vec_grad, attn_moment, wide_bf, x_part, input_grad
            )
            return tuple(
                finish(
                    n, out_rows, pool_sum, input_grad, attn_all, wide_all, attn_orth, wide_orth, vec_total,
                    attn_weight, up_weight, down_weight, vectors,
                    attn_moment, up_moment, down_moment, vector_moment, factors, vector_step,
                )
            )
        pooled = lax.dynamic_slice_in_dim(pool_sum, seq_index * quarter, quarter, 1)
        attn_piece, up_piece, down_piece = exchange(
            n, 2, "sum_grads", *[BatchSum(n, a.reshape(n, own_rows, width)) for a in grads]
        )
        bias_sums = bias_sums.reshape(3, quarter)

        vec_head = jnp.zeros((2, SEQ, quarter), F32)
        vec_head = lax.dynamic_update_slice(
            vec_head, bias_sums[jnp.array([0, 2])][:, None], (0, seq_index, 0)
        ).reshape(2, width)
        vec_mid = vec_grad[:6]
        grad_bias_up = vec_grad[6]
        vec_tail = lax.dynamic_update_slice(
            jnp.zeros((n, SEQ, hid_own), F32),
            grad_bias_up.reshape(n, 1, hid_own),
            (0, seq_index, 0),
        ).reshape(-1, width)
        vec_local = jnp.concatenate([vec_head, vec_mid, vec_tail])
        vec_local = vec_local.reshape(-1, n, own_rows).transpose(1, 0, 2)
        (vec_piece,) = exchange(n, 7, "sum_vectors", ScatterBatch(n, vec_local, F32))
        attn_bf = attn_piece.astype(BF16).reshape(own_rows, 4, quarter).transpose(1, 0, 2)
        wide_bf = jnp.stack([up_piece, down_piece]).astype(BF16)
        attn_send = (matrix_decay * attn_quarter(attn_moment) + attn_bf.astype(F32)).astype(BF16)
        wide_moment = jnp.stack([up_quarter(up_moment), down_quarter(down_moment)])
        wide_send = (matrix_decay * wide_moment + wide_bf.astype(F32)).astype(BF16)
        short = -own_rows % 16
        attn_send = jnp.pad(attn_send, ((0, 0), (0, short), (0, 0)))
        wide_send = jnp.pad(wide_send, ((0, 0), (0, short), (0, 0)))
        attn_all, wide_all, vec_parts, attn_orth, wide_orth = exchange(
            n,
            8,
            "muon",
            GatherSeq(n, attn_bf),
            GatherSeq(n, wide_bf),
            GatherSeq(n, vec_piece),
            Muon(n, attn_send, wide_send),
        )
        attn_orth = attn_orth[:, :, :own_rows]
        wide_orth = wide_orth[:, :, :own_rows]

        def join_attn(parts):
            return parts.astype(F32).transpose(1, 2, 0, 3).reshape(4, own_rows, width)

        def join_up(parts):
            return (
                parts.astype(F32)
                .reshape(SEQ, own_rows, n, hid_own)
                .transpose(1, 2, 0, 3)
                .reshape(own_rows, hidden)
            )

        def join_down(parts):
            return parts.astype(F32).reshape(SEQ * hid_own, width)

        attn_grad = join_attn(attn_all)
        up_grad, down_grad = join_up(wide_all[:, 0]), join_down(wide_all[:, 1])
        vector_grad = (vec_parts[0] + vec_parts[1]) + (vec_parts[2] + vec_parts[3])
        attn_next = matrix_decay * attn_moment + attn_grad
        up_next = matrix_decay * up_moment + up_grad
        down_next = matrix_decay * down_moment + down_grad

        attn_new = attn_weight - factors[0] * join_attn(attn_orth)
        up_new = up_weight - factors[1] * join_up(wide_orth[:, 0])
        down_new = down_weight - factors[2] * join_down(wide_orth[:, 1])
        vector_next = vector_decay * vector_moment + vector_grad
        vectors_new = vectors - vector_step * vector_next
        return (
            out_rows,
            pooled,
            input_grad,
            attn_grad,
            up_grad,
            down_grad,
            vector_grad,
            attn_next,
            up_next,
            down_next,
            vector_next,
            attn_new,
            up_new,
            down_new,
            vectors_new,
        )

    return body


def solution(mesh):
    placed = (
        P("batch", "seq", None),
        P("batch"),
        P(None, "batch", None),
        P("batch", None),
        P("batch", None),
        P(None, "batch"),
        P(None, "batch", None),
        P("batch", None),
        P("batch", None),
        P(None, "batch"),
        P("batch", "seq", None),
        P("batch", "seq"),
    )
    return jax.shard_map(
        make_body(mesh.shape["batch"]),
        mesh=mesh,
        in_specs=placed,
        out_specs=(
            P("batch", "seq", None),
            P("batch", "seq"),
            P("batch", "seq", None),
            P(None, "batch", None),
            P("batch", None),
            P("batch", None),
            P(None, "batch"),
            P(None, "batch", None),
            P("batch", None),
            P("batch", None),
            P(None, "batch"),
            P(None, "batch", None),
            P("batch", None),
            P("batch", None),
            P(None, "batch"),
        ),
        check_vma=False,
    )
```

```python
import math
import types

import jax
import jax.numpy as jnp
from jax import lax
from jax.experimental import pallas as pl
from jax.experimental.pallas import tpu as pltpu
from jax.sharding import PartitionSpec as P

H = 12
HD = 64
NS = 5
SEQ = 4
HEADS = H // SEQ

norm_eps = 1e-12
tiny_norm = 1e-07
matrix_decay = 0.95
vector_decay = 0.5
matrix_rate = 0.5
vector_rate = 0.03

MESH = pl.DeviceIdType.MESH
F32 = jnp.float32
BF16 = jnp.bfloat16


def coords(n):
    b = lax.axis_index("batch")
    s = lax.axis_index("seq")
    return b, s, b // 2, b % 2, n // 2


def remote(src, dst, send, recv, device):
    return pltpu.make_async_remote_copy(
        src_ref=src, dst_ref=dst, send_sem=send, recv_sem=recv, device_id=device, device_id_type=MESH
    )


class GatherBatch:
    peers = ("batch",)

    def __init__(self, n, src, eager=True):
        self.n = n
        self.eager = eager
        self.ins = [src]
        self.outs = [jax.ShapeDtypeStruct((n,) + src.shape, src.dtype)]
        m = n // 2
        self.scratch = [pltpu.SemaphoreType.DMA((2, m))] * 4 + [pltpu.SemaphoreType.DMA]

    def run(self, src, dst, zs, zr, ys, yr, own):
        b, s, hi, lo, m = coords(self.n)
        pair = (hi * 2 + 1 - lo, s)
        local = pltpu.make_async_copy(src, dst.at[b], own)
        local.start()

        def exists(way, d):
            return hi >= d if way == 0 else hi + d < m

        def ahead(way):
            return hi + 1 < m if way == 0 else hi >= 1

        def block_of(way, d):
            place = jnp.clip(hi - d if way == 0 else hi + d, 0, m - 1)
            return place * 2 + lo

        def along(way, d, ref):
            place = jnp.clip(hi + 1 if way == 0 else hi - 1, 0, m - 1)
            return remote(
                ref, dst.at[block_of(way, d)], zs.at[way, d], zr.at[way, d + 1], (place * 2 + lo, s)
            )

        def aside(way, d):
            place = dst.at[block_of(way, d)]
            return remote(place, place, ys.at[way, d], yr.at[way, d], pair)

        first = remote(src, dst.at[b], ys.at[0, 0], yr.at[0, 0], pair)
        for way in (0, 1):

            @pl.when(ahead(way))
            def _(way=way):
                along(way, 0, src).start()

        if not self.eager:
            yield
        first.start()
        yield
        for d in range(1, m):
            for way in (0, 1):

                @pl.when(exists(way, d))
                def _(way=way, d=d):
                    place = dst.at[block_of(way, d)]
                    remote(place, place, zs.at[way, d], zr.at[way, d], pair).wait_recv()
                    if d < m - 1:

                        @pl.when(ahead(way))
                        def _():
                            along(way, d, place).start()

                    aside(way, d).start()

            yield
        local.wait()
        first.wait()
        for d in range(m):
            for way in (0, 1):
                if d > 0:

                    @pl.when(exists(way, d))
                    def _(way=way, d=d):
                        aside(way, d).wait()

                if d < m - 1:

                    @pl.when(exists(way, d) & ahead(way))
                    def _(way=way, d=d):
                        along(way, d, dst.at[block_of(way, d)]).wait_send()


class GatherDirect:
    peers = ("all",)

    def __init__(self, n, src):
        self.n = n
        self.ins = [src]
        self.outs = [jax.ShapeDtypeStruct((n,) + src.shape, src.dtype)]
        self.scratch = [pltpu.SemaphoreType.DMA((n,))] * 2 + [pltpu.SemaphoreType.DMA]

    def run(self, src, dst, ss, rs, own):
        n = self.n
        b, s = lax.axis_index("batch"), lax.axis_index("seq")
        local = pltpu.make_async_copy(src, dst.at[b], own)
        local.start()
        copies = [
            remote(src, dst.at[b], ss.at[k], rs.at[k], ((b + k) % n, s)) for k in range(1, n)
        ]
        for c in copies:
            c.start()
        yield
        local.wait()
        for c in copies:
            c.wait()


class ScatterBatch:
    peers = ("batch",)

    def __init__(self, n, src, wire=BF16):
        self.n = n
        self.wire = wire
        self.ins = [src]
        shape = src.shape[1:]
        self.outs = [jax.ShapeDtypeStruct(shape, F32)]
        m = n // 2
        self.scratch = [pltpu.VMEM((m,) + shape, wire)] * 4 + [pltpu.SemaphoreType.DMA((m,))] * 4

    def run(self, src, dst, ysend, yrecv, zsend, zrecv, ys, yr, zs, zr):
        b, s, hi, lo, m = coords(self.n)
        pair = (hi * 2 + 1 - lo, s)
        first = {}
        order = list(range(1, m)) + [0]
        for d in order:
            h = (hi + d) % m
            ysend[d] = src[h * 2 + 1 - lo].astype(self.wire)
            first[d] = remote(ysend.at[d], yrecv.at[d], ys.at[d], yr.at[d], pair)
            first[d].start()
        yield
        second = []
        for d in range(1, m):
            h = (hi + d) % m
            first[d].wait_recv()
            zsend[d] = (src[h * 2 + lo] + yrecv[d].astype(F32)).astype(self.wire)
            c = remote(zsend.at[d], zrecv.at[d], zs.at[d], zr.at[d], (h * 2 + lo, s))
            c.start()
            second.append(c)
            yield
        first[0].wait_recv()
        total = src[b] + yrecv[0].astype(F32)
        for d in range(1, m):
            second[d - 1].wait_recv()
            total = total + zrecv[d].astype(F32)
        dst[...] = total
        for c in list(first.values()) + second:
            c.wait_send()


class GatherSeq:
    peers = ("seq",)

    def __init__(self, n, src):
        self.ins = [src]
        self.outs = [jax.ShapeDtypeStruct((SEQ,) + src.shape, src.dtype)]
        self.scratch = [pltpu.SemaphoreType.DMA((3,))] * 2 + [pltpu.SemaphoreType.DMA]

    def run(self, src, dst, ss, rs, own):
        b, s = lax.axis_index("batch"), lax.axis_index("seq")
        far, near = (s + 2) % 4, s + 1 - 2 * (s % 2)
        across = remote(src, dst.at[s], ss.at[0], rs.at[0], (b, far))
        across.start()
        local = pltpu.make_async_copy(src, dst.at[s], own)
        local.start()
        beside = remote(src, dst.at[s], ss.at[1], rs.at[1], (b, near))
        beside.start()
        yield
        across.wait_recv()
        passed = remote(dst.at[far], dst.at[far], ss.at[2], rs.at[2], (b, near))
        passed.start()
        yield
        local.wait()
        beside.wait()
        passed.wait()
        across.wait_send()


def owner_list(n):
    return [(0, 2), (1, 0), (n - 2, 2), (n - 1, 0), (n // 4, 0), (n // 2 + 1, 2)]


class OwnerMail:
    @staticmethod
    def scratch(n, count, relayed=None):
        dma = pltpu.SemaphoreType.DMA
        base = [dma((count,)), dma((SEQ * n,)), dma]
        if relayed is not None:
            base += [pltpu.VMEM((count, 2) + relayed, BF16), dma((count, 2)), dma((count, 2))]
        return base

    def __init__(self, n, places, inbox, ss, rs, own, relayed=None, relay_s=None, relay_r=None):
        self.n, self.places, self.inbox, self.ss, self.rs, self.own = n, places, inbox, ss, rs, own
        self.relayed, self.relay_s, self.relay_r = relayed, relay_s, relay_r
        self.b, self.s = lax.axis_index("batch"), lax.axis_index("seq")
        self.me = self.s * n + self.b
        self.mine = [(self.b == ob) & (self.s == os) for ob, os in places]

    def slot(self, seq, block):
        if len(self.inbox.shape) == 4:
            return self.inbox.at[seq, block]
        rows = self.inbox.shape[1] // self.n
        return self.inbox.at[seq, pl.ds(pl.multiple_of(block * rows, rows), rows)]

    def indirect(self, k):
        ob, os = self.places[k]
        hi, oh = self.b // 2, ob // 2
        light = hi < oh if oh < self.n // 4 else hi > oh
        same_lo, same_x = self.b % 2 == ob % 2, self.s // 2 == os // 2
        other_lo, other_x = jnp.logical_not(same_lo), jnp.logical_not(same_x)
        away = hi != oh
        column = away & same_lo & same_x
        return (away & other_lo & other_x, light & other_lo & same_x), (column, column & light)

    def copy(self, k, src):
        ob, os = self.places[k]
        place = self.slot(self.s, self.b)
        return remote(src, place, self.ss.at[k], self.rs.at[self.me], (ob, os))

    def aside(self, k, slot, src):
        across = self.b + 1 - 2 * (self.b % 2)
        seq = self.s if slot else (self.s + 2) % 4
        return remote(
            src, self.relayed.at[k, slot], self.ss.at[k], self.relay_r.at[k, slot], (across, seq)
        )

    def pass_copy(self, k, slot):
        block, seq = self.b + 1 - 2 * (self.b % 2), self.s if slot else (self.s + 2) % 4
        return remote(
            self.relayed.at[k, slot], self.slot(seq, block), self.relay_s.at[k, slot],
            self.rs.at[seq * self.n + block], self.places[k],
        )

    def send(self, k, src):
        direct = jnp.logical_not(self.mine[k])
        if self.relayed is not None:
            for slot, by_relay in enumerate(self.indirect(k)[0]):
                direct = direct & jnp.logical_not(by_relay)

                @pl.when(by_relay)
                def _(slot=slot):
                    self.aside(k, slot, src).start()

        @pl.when(direct)
        def _():
            self.copy(k, src).start()

        @pl.when(self.mine[k])
        def _():
            pltpu.make_async_copy(src, self.slot(self.s, self.b), self.own).start()

    def relay(self, k):
        for slot, here in enumerate(self.indirect(k)[1]):

            @pl.when(here)
            def _(slot=slot):
                place = self.relayed.at[k, slot]
                remote(
                    place, place, self.relay_s.at[k, slot], self.relay_r.at[k, slot], (0, 0)
                ).wait_recv()
                self.pass_copy(k, slot).start()

    def collect(self):
        place = self.slot(self.s, self.b)
        pltpu.make_async_copy(place, place, self.own).wait()

        @pl.loop(1, SEQ * self.n)
        def _(k):
            other = (self.me + k) % (SEQ * self.n)
            place = self.slot(other // self.n, other % self.n)
            remote(place, place, self.ss.at[0], self.rs.at[other], (0, 0)).wait_recv()

    def finish(self, k, src):
        @pl.when(jnp.logical_not(self.mine[k]))
        def _():
            self.copy(k, src).wait_send()

        if self.relayed is not None:

            for slot, here in enumerate(self.indirect(k)[1]):

                @pl.when(here)
                def _(slot=slot):
                    self.pass_copy(k, slot).wait_send()


class Muon:
    peers = ("all",)

    def __init__(self, n, attn_piece, wide_piece=None, wide_in=None):
        self.n = n
        self.ready = wide_in is not None
        self.ins = [attn_piece, wide_in if self.ready else wide_piece]
        width = self.ins[1].shape[-1]
        size = wide_in.shape[1] if self.ready else n * wide_piece.shape[1]
        rows = size // n
        attn_shape = attn_piece.shape[1:]
        self.outs = [
            jax.ShapeDtypeStruct((SEQ, 4) + attn_shape, BF16),
            jax.ShapeDtypeStruct((SEQ, 2, rows, width), BF16),
        ]
        dma = pltpu.SemaphoreType.DMA
        self.scratch = [
            pltpu.VMEM((SEQ, n) + attn_shape, BF16),
            pltpu.VMEM((SEQ, size, width), BF16),
            pltpu.VMEM((2, n // 2, rows, width), BF16),
            pltpu.VMEM((size, SEQ * size), F32),
            pltpu.VMEM((size, SEQ * size), BF16),
            pltpu.VMEM((size, size), F32),
            pltpu.VMEM((size, size), BF16),
            pltpu.VMEM((size, size), BF16),
            pltpu.VMEM((size, 1), F32),
            pltpu.VMEM((1, 1), F32),
            dma((SEQ * n,)),
            dma((6,)),
            dma((2, n // 2)),
            dma((2, n // 2)),
            dma((6, 3)),
            dma((6, 3)),
            dma,
            dma((SEQ,)),
        ]
        self.scratch += OwnerMail.scratch(n, 4)
        if not self.ready:
            self.scratch += OwnerMail.scratch(n, 2) + [pltpu.VMEM((SEQ, size, width), BF16)]

    def run(
        self, attn, wide, attn_orth, wide_orth, attn_in, wide_out, relayed, x32, xlow, gram, gram_low, poly, diag,
        norm, back_s, back_r, relay_s, relay_r, seq_s, seq_r, own, loads, *mails,
    ):
        n = self.n
        b, s, hi, lo, m = coords(n)
        far, near = (s + 2) % 4, s + 1 - 2 * (s % 2)
        me = s * n + b
        size = x32.shape[0]
        width = wide.shape[-1]
        quarter = width // SEQ
        places = owner_list(n)
        attn_mail = OwnerMail(n, places[:4], attn_in, *mails[:3])
        wide_in = wide
        if not self.ready:
            wide_in = mails[6]
            wide_mail = OwnerMail(n, places[4:], wide_in, *mails[3:6])
        mine = [(b == ob) & (s == os) for ob, os in places]
        number = jnp.int32(0)
        for k in range(6):
            number = jnp.where(mine[k], jnp.int32(k), number)
        is_attn = mine[0] | mine[1] | mine[2] | mine[3]
        is_wide = mine[4] | mine[5]

        if not self.ready:
            for k in range(2):
                wide_mail.send(k, wide.at[k])
        def send_attn():
            for k in range(4):
                attn_mail.send(k, attn.at[k])

        if self.ready:
            self.send_attn = send_attn
        else:
            send_attn()

        if not self.ready:
            for _ in range(4):
                yield


        def result(k):
            return attn_orth.at[s, k] if k < 4 else wide_orth.at[s, k - 4]

        def others(act):
            @pl.loop(1, SEQ * n)
            def _(k):
                other = (me + 9 * k) % (SEQ * n)
                act(other, other % n, other // n)

        def give_attn():
            pltpu.make_async_copy(attn_in.at[s, b], attn_orth.at[s, number], own).start()

            def act(other, ob, os):
                remote(
                    attn_in.at[os, ob], attn_orth.at[os, number], back_s.at[other], back_r.at[number], (ob, os)
                ).start()

            others(act)

        piece = OwnerMail(n, places, wide_out, None, None, None).slot

        def give_wide(piece):
            index = number - 4
            pltpu.make_async_copy(piece(s, b), wide_orth.at[s, index], own).start()

            def act(other, ob, os):
                oh, ol = ob // 2, ob % 2
                up = hi < m // 2
                away = jnp.where(up, oh - hi, hi - oh)
                relay = (away > 0) & (os // 2 != s // 2)
                stop = jnp.where(ol == lo, os, (os + 2) % 4)
                src = piece(os, ob)

                @pl.when(relay)
                def _():
                    slot = jnp.maximum(away - 1, 0)
                    remote(
                        src, relayed.at[index, slot], back_s.at[other], relay_r.at[index, slot],
                        (hi * 2 + ol, stop),
                    ).start()

                @pl.when(jnp.logical_not(relay))
                def _():
                    remote(
                        src, wide_orth.at[os, index], back_s.at[other], back_r.at[number], (ob, os)
                    ).start()

            others(act)

        def prepare():
            @pl.when(is_wide)
            def _():
                if not self.ready:
                    wide_mail.collect()
                if width != size:
                    xlow[...] = jnp.zeros(xlow.shape, BF16)

            @pl.when(mine[4])
            def _():
                copies = [
                    pltpu.make_async_copy(
                        wide_in.at[k], xlow.at[:, pl.ds(k * size, width)], loads.at[k]
                    )
                    for k in range(SEQ)
                ]
                for c in copies:
                    c.start()
                for c in copies:
                    c.wait()

            @pl.when(mine[5])
            def _():
                copies = [
                    pltpu.make_async_copy(wide_in.at[k], wide_out.at[k], loads.at[k]) for k in range(SEQ)
                ]
                for c in copies:
                    c.start()
                for k, c in enumerate(copies):
                    c.wait()
                    xlow[:width, k * size : (k + 1) * size] = wide_out[k].T

        def attn_turn():
            @pl.when(is_attn)
            def _():
                attn_mail.collect()
                span = SEQ * quarter
                short, line = attn_in.shape[2:]
                whole = [attn_in[k].reshape(n * short, line) for k in range(SEQ)]
                for k in range(line // quarter):
                    block = [a[:, k * quarter : (k + 1) * quarter] for a in whole]
                    xlow[k * n * short : (k + 1) * n * short, :span] = jnp.concatenate(block, axis=1)
                square_x, square_low = x32.at[:, pl.ds(0, span)], xlow.at[:, pl.ds(0, span)]

                def turn(first):
                    schulz_poly(square_low, gram, gram_low, poly, diag, norm, first)
                    schulz_move(square_x, square_low, poly, diag, norm, first)

                turn(True)

                @pl.loop(1, NS)
                def _(k):
                    turn(False)

                for k in range(SEQ):
                    block = xlow[:, k * quarter : (k + 1) * quarter]
                    if line > quarter:
                        block = fold(block)
                    attn_in[k] = block.reshape(attn_in.shape[1:])
                give_attn()

        if not self.ready:
            prepare()
        else:
            self.prepare, self.attn_turn = prepare, attn_turn
            yield

        for turn in range(NS):

            @pl.when(is_wide)
            def _(turn=turn):
                schulz_poly(xlow, gram, gram_low, poly, diag, norm, turn == 0)

            yield

            @pl.when(is_wide)
            def _(turn=turn):
                schulz_move(x32, xlow, poly, diag, norm, turn == 0)

            yield

        @pl.when(is_wide)
        def _():
            @pl.when(mine[4])
            def _():
                rows = size // n

                def part(seq, block):
                    return xlow.at[
                        pl.ds(pl.multiple_of(block * rows, rows), rows),
                        pl.ds(pl.multiple_of(seq * size, 128), width),
                    ]

                give_wide(part)

            @pl.when(mine[5])
            def _():
                for k in range(SEQ):
                    wide_out[k] = xlow[:width, k * size : (k + 1) * size].T
                give_wide(piece)

        def routes(k):
            ob, os = places[k]
            oh, ol = ob // 2, ob % 2
            same_x = s // 2 == os // 2
            here = (hi == oh) & (((lo == ol) & jnp.logical_not(same_x)) | ((lo != ol) & same_x))
            target = jnp.where(lo == ol, s, far)
            ahead = range(oh + 1, m) if oh < m // 2 else range(oh - 1, -1, -1)
            return here, target, list(enumerate(ahead))

        def relay_copy(k, slot, block, target):
            return remote(
                relayed.at[k - 4, slot], wide_orth.at[target, k - 4], relay_s.at[k - 4, slot], back_r.at[k],
                (block * 2 + lo, target),
            )

        def onward(k, step, source, target):
            out = attn_orth.at[source, k] if k < 4 else wide_orth.at[source, k - 4]
            return remote(out, out, seq_s.at[k, step], seq_r.at[k, step], (b, target))

        if not self.ready:
            attn_turn()
        done = (0, 1, 2, 3, 4, 5)

        def returned(k):
            @pl.when(jnp.logical_not(mine[k]))
            def _():
                remote(result(k), result(k), seq_s.at[k, 0], back_r.at[k], (0, 0)).wait_recv()

            @pl.when(mine[k])
            def _():
                pltpu.make_async_copy(result(k), result(k), own).wait()

            onward(k, 0, s, far).start()
            onward(k, 1, s, near).start()

        def passed(k):
            onward(k, 0, far, far).wait_recv()
            onward(k, 2, far, near).start()

        for k in (4, 5):
            here, target, ahead = routes(k)

            @pl.when(here)
            def _(k=k, target=target, ahead=ahead):
                for slot, block in ahead:
                    place = relayed.at[k - 4, slot]
                    remote(place, place, relay_s.at[0, 0], relay_r.at[k - 4, slot], (0, 0)).wait_recv()
                    relay_copy(k, slot, block, target).start()

        for k in done[:4]:
            returned(k)
        for k in done[4:]:
            returned(k)
        for k in done:
            passed(k)
        for k in done:
            onward(k, 1, near, near).wait_recv()
            onward(k, 2, (near + 2) % 4, near).wait_recv()
            onward(k, 0, s, far).wait_send()
            onward(k, 1, s, near).wait_send()
            onward(k, 2, far, near).wait_send()
        for k in range(4):
            attn_mail.finish(k, attn.at[k])
        if not self.ready:
            for k in range(2):
                wide_mail.finish(k, wide.at[k])
        for k in (4, 5):
            here, target, ahead = routes(k)

            @pl.when(here)
            def _(k=k, target=target, ahead=ahead):
                for slot, block in ahead:
                    relay_copy(k, slot, block, target).wait_send()

        def given(buf):
            def act(other, ob, os):
                place = buf.at[os, ob] if len(buf.shape) == 4 else piece(os, ob)
                remote(place, place, back_s.at[other], back_r.at[0], (0, 0)).wait_send()

            others(act)

        @pl.when(is_attn)
        def _():
            given(attn_in)

        @pl.when(is_wide)
        def _():
            given(wide_out)


def schulz_poly(xlow, gram, gram_low, poly, diag, norm, first):
    size = xlow.shape[0]
    side = 256
    tiles = [slice(k, k + side) for k in range(0, size, side)]
    eye = lax.broadcasted_iota(jnp.int32, (side, side), 0) == lax.broadcasted_iota(
        jnp.int32, (side, side), 1
    )
    for j in tiles:
        gram[j.start :, j] = contract_last(xlow[j.start :, :], xlow[j, :])
    if first:
        total = jnp.zeros((1, 1), F32)
        for j in tiles:
            total = total + jnp.sum(jnp.where(eye, gram[j, j], 0.0), keepdims=True)
        inverse = 1.0 / (jnp.sqrt(total) + tiny_norm)
        norm[...] = inverse
        for j in tiles:
            gram[j.start :, j] = gram[j.start :, j] * (inverse * inverse)
    down, along = [], []
    for j in tiles:
        block = gram[j, j]
        on_diag = jnp.where(eye, block, 0.0)
        down.append(jnp.sum(on_diag, axis=1, keepdims=True))
        along.append(jnp.sum(on_diag, axis=0, keepdims=True))
        gram_low[j, j] = jnp.where(eye, 0.0, block).astype(BF16)
        for i in tiles:
            if i.start > j.start:
                block = gram[i, j]
                gram_low[i, j] = block.astype(BF16)
                gram_low[j, i] = block.T.astype(BF16)
    for j, right in zip(tiles, along):
        square = matmul(gram_low[j.start :, :], gram_low[:, j])
        for i, left in zip(tiles, down):
            if i.start < j.start:
                continue
            part = square[i.start - j.start : i.stop - j.start]
            factor = (2.0315 * left - 4.775) + 2.0315 * right
            block = 2.0315 * part + factor * gram[i, j]
            if i == j:
                value = jnp.sum(jnp.where(eye, 2.0315 * part, 0.0), axis=1, keepdims=True)
                diag[i] = value + (3.4445 + (2.0315 * left - 4.775) * left)
                poly[i, i] = jnp.where(eye, 0.0, block).astype(BF16)
            else:
                poly[i, j] = block.astype(BF16)
                poly[j, i] = block.T.astype(BF16)


def schulz_move(x32, xlow, poly, diag, norm, first):
    wide = x32.shape[1]
    chunk = 768 if wide % 768 == 0 else 512
    for c in range(0, wide, chunk):
        part = slice(c, c + chunk)
        if first:
            moved = (diag[...] * norm[...]) * xlow[:, part].astype(F32)
            moved = moved + matmul(poly[...], xlow[:, part]) * norm[...]
        else:
            moved = diag[...] * x32[:, part] + matmul(poly[...], xlow[:, part])
        x32[:, part] = moved
        xlow[:, part] = moved.astype(BF16)


def greet_peers(n, kinds):
    b, s, hi, lo, m = coords(n)
    peers = []
    if "seq" in kinds:
        peers += [(b, (s + k) % 4) for k in (1, 2, 3)]
    if "batch" in kinds:
        peers += [(((hi + d) % m) * 2 + lo, s) for d in range(1, m)]
        peers += [(hi * 2 + 1 - lo, s)]
    return peers


def greet_signal(n, kinds):
    b, s = lax.axis_index("batch"), lax.axis_index("seq")
    barrier = pltpu.get_barrier_semaphore()
    if "all" in kinds:
        me = s * n + b

        @pl.loop(1, SEQ * n)
        def _(k):
            other = (me + k) % (SEQ * n)
            pl.semaphore_signal(
                barrier, inc=1, device_id=(other % n, other // n), device_id_type=MESH
            )

        return
    for peer in greet_peers(n, kinds):
        pl.semaphore_signal(barrier, inc=1, device_id=peer, device_id_type=MESH)


def greet_wait(n, kinds):
    count = SEQ * n - 1 if "all" in kinds else len(greet_peers(n, kinds))
    pl.semaphore_wait(pltpu.get_barrier_semaphore(), count)


def greet(n, kinds):
    greet_signal(n, kinds)
    greet_wait(n, kinds)


def run_together(*live):
    live = list(live)
    while live:
        still = []
        for op in live:
            try:
                next(op)
                still.append(op)
            except StopIteration:
                pass
        live = still


def exchange(n, collective_id, name, *ops):
    ins = [a for op in ops for a in op.ins]
    outs = [o for op in ops for o in op.outs]
    scratch = [c for op in ops for c in op.scratch]
    kinds = {k for op in ops for k in op.peers}

    def kernel(*refs):
        in_refs, out_refs = refs[: len(ins)], refs[len(ins) : len(ins) + len(outs)]
        scratch_refs = refs[len(ins) + len(outs) :]
        greet(n, kinds)
        live = []
        i = o = c = 0
        for op in ops:
            ni, no, nc = len(op.ins), len(op.outs), len(op.scratch)
            live.append(
                op.run(*in_refs[i : i + ni], *out_refs[o : o + no], *scratch_refs[c : c + nc])
            )
            i, o, c = i + ni, o + no, c + nc
        run_together(*live)

    vmem = pl.BlockSpec(memory_space=pltpu.VMEM)
    return pl.pallas_call(
        kernel,
        out_shape=outs,
        in_specs=[vmem] * len(ins),
        out_specs=[vmem] * len(outs),
        scratch_shapes=scratch,
        compiler_params=pltpu.CompilerParams(
            collective_id=collective_id, has_side_effects=True, vmem_limit_bytes=60 * 2**20
        ),
        name=name,
    )(*ins)


def contract_last(left, right):
    return lax.dot_general(left, right, (((1,), (1,)), ((), ())), preferred_element_type=F32)


def contract_first(left, right):
    return lax.dot_general(left, right, (((0,), (0,)), ((), ())), preferred_element_type=F32)


def matmul(left, right):
    return jnp.dot(left, right, preferred_element_type=F32)


def exact_gelu(value_in):
    return jax.nn.gelu(value_in, approximate=False)


def normalize(hidden, gain_row):
    row_mean = jnp.mean(hidden, axis=-1, keepdims=True)
    centred = hidden - row_mean
    spread = lax.rsqrt(jnp.mean(centred * centred, axis=-1, keepdims=True) + norm_eps)
    scaled = centred * spread
    return (scaled * gain_row, scaled, spread)


def normalize_back(grad_in, scaled, spread, gain_row):
    weighted = grad_in * gain_row
    mean_first = jnp.mean(weighted, axis=-1, keepdims=True)
    second = jnp.mean(weighted * scaled, axis=-1, keepdims=True)
    return (
        spread * (weighted - mean_first - scaled * second),
        jnp.sum(grad_in * scaled, axis=0),
        jnp.sum(grad_in, axis=0),
    )


class RowGather:
    @staticmethod
    def scratch():
        return [pltpu.SemaphoreType.DMA((2, 3)), pltpu.SemaphoreType.DMA((2, 3))]

    def __init__(self, buf, ss, rs):
        self.buf, self.ss, self.rs = buf, ss, rs
        self.b, self.s = lax.axis_index("batch"), lax.axis_index("seq")
        self.far, self.near = (self.s + 2) % 4, self.s + 1 - 2 * (self.s % 2)
        self.diag = (self.near + 2) % 4

    def copy(self, r, step, block, device):
        place = self.buf.at[r, block]
        return remote(place, place, self.ss.at[r, step], self.rs.at[r, step], (self.b, device))

    def start(self, r):
        self.copy(r, 0, self.s, self.far).start()
        self.copy(r, 1, self.s, self.near).start()

    def wait_near(self, r):
        self.copy(r, 1, self.near, self.near).wait_recv()

    def pass_far(self, r):
        self.copy(r, 0, self.far, self.far).wait_recv()
        self.copy(r, 2, self.far, self.near).start()

    def wait_diag(self, r):
        self.copy(r, 2, self.diag, self.near).wait_recv()

    def finish(self, r):
        self.copy(r, 0, self.s, self.far).wait_send()
        self.copy(r, 1, self.s, self.near).wait_send()
        self.copy(r, 2, self.far, self.near).wait_send()


def gelu_parts(value):
    cdf = 0.5 * (1.0 + lax.erf(value * math.sqrt(0.5)))
    density = jnp.exp(-0.5 * value * value) * (1.0 / math.sqrt(2.0 * math.pi))
    return value * cdf, cdf + value * density


def row_sum(value):
    return jnp.sum(value, axis=0, keepdims=True)


class RowSwap:
    @staticmethod
    def scratch(shape):
        return [
            pltpu.VMEM(shape, BF16),
            pltpu.VMEM(shape, BF16),
            pltpu.SemaphoreType.DMA((2, 4)),
            pltpu.SemaphoreType.DMA((2, 4)),
        ]

    def __init__(self, src, dst, ss, rs):
        self.src, self.dst, self.ss, self.rs = src, dst, ss, rs
        self.b, self.s = lax.axis_index("batch"), lax.axis_index("seq")

    def copy(self, r, k):
        other = (self.s + k) % 4
        return remote(
            self.src.at[other, r], self.dst.at[self.s, r], self.ss.at[r, k], self.rs.at[r, k],
            (self.b, other),
        )

    def start(self, r):
        for k in (2, 3, 1):
            self.copy(r, k).start()
        self.dst[self.s, r] = self.src[self.s, r]

    def wait(self, r):
        for k in (2, 3, 1):
            self.copy(r, k).wait_recv()

    def finish(self, r):
        for k in (2, 3, 1):
            self.copy(r, k).wait_send()


def fold(value):
    half = value.shape[0] // 2
    return jnp.concatenate([value[:half], value[half:]], axis=1)


def unfold(value):
    half = value.shape[1] // 2
    return jnp.concatenate([value[:, :half], value[:, half:]], axis=0)


def rounds(count):
    for _ in range(count):
        yield


def spaced(op, count):
    for _ in op:
        yield from rounds(count)


def step(op):
    try:
        next(op)
    except StopIteration:
        pass


def drain(op):
    for _ in op:
        pass


class DirectSum:
    peers = ("all",)

    def __init__(self, n, src):
        self.n = n
        self.scratch = [pltpu.VMEM(src.shape, F32)] + [pltpu.SemaphoreType.DMA((n,))] * 2

    def run(self, src, dst, arrived, ss, rs):
        n = self.n
        b, s = lax.axis_index("batch"), lax.axis_index("seq")
        copies = []
        for k in range(1, n):
            to = (b + k) % n
            copies.append(remote(src.at[to], arrived.at[k], ss.at[k], rs.at[k], (to, s)))
            copies[-1].start()
        yield
        total = src[b]
        for k, c in enumerate(copies):
            c.wait()
            total = total + arrived[k + 1]
        dst[...] = total


class BatchSum:
    peers = ("batch",)

    def __init__(self, n, src):
        self.n = n
        self.ins = [src]
        shape = src.shape[1:]
        self.outs = [jax.ShapeDtypeStruct(shape, F32)]
        m = n // 2
        self.scratch = [pltpu.VMEM((m,) + shape, BF16)] * 3 + [pltpu.SemaphoreType.DMA((m,))] * 4

    def run(self, src, dst, yrecv, zsend, zrecv, ys, yr, zs, zr):
        b, s, hi, lo, m = coords(self.n)
        pair = (hi * 2 + 1 - lo, s)
        first = {}
        for d in list(range(1, m)) + [0]:
            block = ((hi + d) % m) * 2 + 1 - lo
            first[d] = remote(src.at[block], yrecv.at[d], ys.at[d], yr.at[d], pair)
            first[d].start()
        yield
        second = []
        for d in range(1, m):
            h = (hi + d) % m
            first[d].wait_recv()
            zsend[d] = (src[h * 2 + lo].astype(F32) + yrecv[d].astype(F32)).astype(BF16)
            c = remote(zsend.at[d], zrecv.at[d], zs.at[d], zr.at[d], (h * 2 + lo, s))
            c.start()
            second.append(c)
            yield
        first[0].wait_recv()
        total = src[b].astype(F32) + yrecv[0].astype(F32)
        for d in range(1, m):
            second[d - 1].wait_recv()
            total = total + zrecv[d].astype(F32)
        dst[...] = total
        for c in list(first.values()) + second:
            c.wait_send()


class RowSum:
    @staticmethod
    def scratch(rows, shape):
        return [
            pltpu.VMEM((rows, 2) + shape, BF16),
            pltpu.VMEM((rows,) + shape, BF16),
            pltpu.VMEM((rows,) + shape, BF16),
            pltpu.SemaphoreType.DMA((rows, 3)),
            pltpu.SemaphoreType.DMA((rows, 3)),
        ]

    def __init__(self, src, near_in, far_out, far_in, ss, rs):
        self.src, self.near_in, self.far_out, self.far_in, self.ss, self.rs = (
            src, near_in, far_out, far_in, ss, rs,
        )
        self.b, self.s = lax.axis_index("batch"), lax.axis_index("seq")
        self.far, self.near = (self.s + 2) % 4, self.s + 1 - 2 * (self.s % 2)
        self.diag = (self.near + 2) % 4

    def beside(self, r, k):
        block = self.diag if k else self.near
        return remote(
            self.src.at[r, block], self.near_in.at[r, k], self.ss.at[r, k], self.rs.at[r, k],
            (self.b, self.near),
        )

    def across(self, r):
        return remote(
            self.far_out.at[r], self.far_in.at[r], self.ss.at[r, 2], self.rs.at[r, 2],
            (self.b, self.far),
        )

    def send_near(self, r):
        self.beside(r, 0).start()

    def send_diag(self, r):
        self.beside(r, 1).start()

    def cross(self, r):
        self.beside(r, 1).wait_recv()
        part = self.src[r, self.far].astype(F32) + self.near_in[r, 1].astype(F32)
        self.far_out[r] = part.astype(BF16)
        self.across(r).start()

    def total(self, r):
        self.beside(r, 0).wait_recv()
        part = self.src[r, self.s].astype(F32) + self.near_in[r, 0].astype(F32)
        self.across(r).wait_recv()
        return part + self.far_in[r].astype(F32)

    def finish(self, r):
        self.beside(r, 0).wait_send()
        self.beside(r, 1).wait_send()
        self.across(r).wait_send()


class Scratch:
    def __init__(self):
        self.names, self.shapes = [], []

    def add(self, **named):
        for name, shapes in named.items():
            one = not isinstance(shapes, list)
            shapes = [shapes] if one else shapes
            self.names.append((name, len(shapes), one))
            self.shapes += shapes

    def refs(self, refs):
        out, i = types.SimpleNamespace(), 0
        for name, count, one in self.names:
            setattr(out, name, refs[i] if one else refs[i : i + count])
            i += count
        return out


def layer(
    n, tokens, attn_weight, up_weight, down_weight, vec_own, pool_own, lengths, out_grad, up_moment, down_moment
):
    rows, span, width = tokens.shape
    quarter = width // SEQ
    span_all = span * SEQ
    own_rows = width // n
    local = rows * span
    aligned = own_rows % 16 == 0
    scale = HD**-0.5
    shape = jax.ShapeDtypeStruct
    full = (rows, SEQ, span, width)
    widths = (3 * quarter, quarter, width, width)
    low_ops = [GatherBatch(n, shape((own_rows, c), BF16), k < 2) for k, c in enumerate(widths)]
    low_ops = low_ops if aligned else []
    vec_op = GatherDirect(n, vec_own) if aligned else GatherBatch(n, vec_own)
    pool_op = GatherSeq(n, pool_own)
    out_op = GatherSeq(n, shape((width, quarter), BF16))
    sum_ops = [BatchSum(n, shape((n, own_rows, width), BF16)) for _ in range(2)]

    outs = [
        shape((rows, span, width), F32),
        shape((rows, width), F32),
        shape((rows, span, width), F32),
        shape((8, width), F32),
        shape((1, 3 * quarter), F32),
        shape(full, BF16),
    ]
    vmem = pl.BlockSpec(memory_space=pltpu.VMEM)
    anywhere = pl.BlockSpec(memory_space=pl.ANY)
    if aligned:
        outs += [shape((n, own_rows, width), BF16)]
        outs += [shape((2, own_rows, width), BF16), shape((SEQ, width, width), BF16)]
        out_specs = [anywhere, vmem, anywhere, vmem, vmem, anywhere, anywhere, vmem, anywhere]
    else:
        outs += [shape((width, width), BF16)] * 3
        out_specs = [vmem] * 9

    dma = pltpu.SemaphoreType.DMA
    sc = Scratch()
    if aligned:
        sc.add(
            lows=[pltpu.VMEM((own_rows, c), BF16) for c in widths],
            weights=[pltpu.VMEM(op.outs[0].shape, BF16) for op in low_ops],
            low_moves=[c for op in low_ops for c in op.scratch],
        )
    sc.add(vec_parts=pltpu.VMEM(vec_op.outs[0].shape, F32))
    sc.add(vec_move=vec_op.scratch)
    sc.add(vec=pltpu.VMEM((8, width), F32))
    sc.add(pool_parts=pltpu.VMEM(pool_op.outs[0].shape, F32))
    sc.add(pool_move=pool_op.scratch)
    sc.add(out_own=pltpu.VMEM((width, quarter), BF16))
    sc.add(out_parts=pltpu.VMEM((SEQ, width, quarter), BF16))
    sc.add(out_move=out_op.scratch)
    sc.add(w_out=pltpu.VMEM((width, width), BF16))
    sc.add(x_all=pltpu.VMEM(full, BF16))
    sc.add(x_gather=RowGather.scratch())
    sc.add(qkv=pltpu.VMEM((rows, span_all, 3 * quarter), BF16))
    sc.add(prob=pltpu.VMEM((rows, HEADS, span_all, span_all), F32))
    sc.add(swap=RowSwap.scratch((SEQ, rows, span, quarter)))
    sc.add(back_swap=RowSwap.scratch((SEQ, rows, span, quarter)))
    sc.add(context=pltpu.VMEM((rows, span, width), BF16))
    sc.add(normed=pltpu.VMEM((rows, span, width), F32))
    sc.add(scaled_one=pltpu.VMEM((rows, span, width), F32))
    sc.add(spread_one=pltpu.VMEM((rows, span, 1), F32))
    sc.add(y_all=pltpu.VMEM(full, BF16))
    sc.add(y_gather=RowGather.scratch())
    sc.add(slope=pltpu.VMEM(full, F32))
    sc.add(act=pltpu.VMEM(full, BF16))
    sc.add(z_sum=RowSum.scratch(rows, (span, width)))
    sc.add(dz_all=pltpu.VMEM(full, BF16))
    sc.add(dz_gather=RowGather.scratch())
    sc.add(du_all=pltpu.VMEM(full, BF16))
    sc.add(dy_sum=RowSum.scratch(rows, (span, width)))
    sc.add(pool_buf=pltpu.VMEM((SEQ, rows, width), F32))
    sc.add(pool_sems=[dma((3,)), dma((3,))])
    sc.add(a_quarters=pltpu.VMEM((SEQ, local, quarter), BF16))
    sc.add(out_part=pltpu.VMEM((1, SEQ, width, quarter), BF16))
    sc.add(out_sum=RowSum.scratch(1, (width, quarter)))
    if not aligned:
        sc.add(x_sum=RowSum.scratch(rows, (span, width)))
    sc.add(grad_qkv=pltpu.VMEM((rows, span_all, 3 * quarter), BF16))
    if aligned:
        sc.add(early=[pltpu.VMEM(outs[k].shape, outs[k].dtype) for k in (0, 2, 5, 6)])
        sc.add(early_sems=dma((4,)))
        sc.add(raw=dma((2 * SEQ + 1,)))
        sc.add(
            down_grad=pltpu.VMEM((n, own_rows, width), BF16),
            up_grad=pltpu.VMEM((n, own_rows, width), BF16),
            down_piece=pltpu.VMEM((own_rows, width), F32),
            up_piece=pltpu.VMEM((own_rows, width), F32),
            down_sum=sum_ops[0].scratch,
            up_sum=sum_ops[1].scratch,
        )
        sc.add(vec_low=pltpu.VMEM(vec_own.shape, F32))
        sc.add(wide_send=pltpu.VMEM((2, own_rows, width), BF16))
        sc.add(mail=OwnerMail.scratch(n, 2, (own_rows, width)))

    def kernel(
        tokens, attn_weight, up_weight, down_weight, vec_own, pool_own, lengths, out_grad, up_moment, down_moment,
        out_rows, pooled, second, vec_grad, bias_sums, part, grad_attn, *rest,
    ):
        if aligned:
            wide_bf, wide_in = rest[:2]
            rest = rest[2:]
        else:
            grad_up_out, grad_down_out = rest[:2]
            rest = rest[2:]
        at = sc.refs(rest)
        if aligned:
            leaving = [
                pltpu.make_async_copy(a, b, at.early_sems.at[k])
                for k, (a, b) in enumerate(zip(at.early, (out_rows, second, part, grad_attn)))
            ]
            out_rows, second, part, grad_attn = at.early
        kinds = {"all"} if aligned else {"seq", "batch"}
        greet_signal(n, kinds)
        b, s = lax.axis_index("batch"), lax.axis_index("seq")
        x_all, y_all, dz_all, du_all = at.x_all, at.y_all, at.dz_all, at.du_all
        slope, act, prob, qkv = at.slope, at.act, at.prob, at.qkv
        normed, context, vec = at.normed, at.context, at.vec
        x_gather = RowGather(x_all, *at.x_gather)
        y_gather = RowGather(y_all, *at.y_gather)
        dz_gather = RowGather(dz_all, *at.dz_gather)
        swap, back_swap = RowSwap(*at.swap), RowSwap(*at.back_swap)
        z_sum, dy_sum = [RowSum(part, *refs) for refs in (at.z_sum, at.dy_sum)]
        out_sum = RowSum(at.out_part, *at.out_sum)
        far, near, diag = x_gather.far, x_gather.near, x_gather.diag

        def raw_block(k):
            return slope.at[k // SEQ, k % SEQ, pl.ds(0, own_rows)]

        def load_up(matrix):
            return [
                pltpu.make_async_copy(
                    matrix.at[:, pl.ds(k * width, width)], raw_block(SEQ + k), at.raw.at[SEQ + k]
                )
                for k in range(SEQ)
            ]

        def load_down(matrix, place):
            return pltpu.make_async_copy(
                matrix.at[pl.ds(s * own_rows, own_rows)], place, at.raw.at[2 * SEQ]
            )

        def raw_up(k):
            whole = jnp.concatenate([raw_block(SEQ + j)[...] for j in range(SEQ)], axis=1)
            return take_up(whole, n, k)

        if aligned:
            raws = [
                pltpu.make_async_copy(attn_weight.at[k], raw_block(k), at.raw.at[k]) for k in range(4)
            ]
            raws += load_up(up_weight)
            raws.append(load_down(down_weight, second.at[0, pl.ds(0, own_rows)]))
            for c in raws:
                c.start()
        for r in range(rows):
            x_all[r, s] = tokens[r].astype(BF16)
        if aligned:
            for c in raws[:4]:
                c.wait()
            for k in range(SEQ):

                @pl.when(s == k)
                def _(k=k):
                    block = [raw_block(j)[:, k * quarter : (k + 1) * quarter] for j in range(4)]
                    at.lows[0][...] = jnp.concatenate(block[:3], axis=1).astype(BF16)
                    at.lows[1][...] = block[3].astype(BF16)

            vec_low = at.vec_low
            vec_low[...] = vec_own[...].astype(BF16).astype(F32)
        else:
            vec_low = vec_own

        greet_wait(n, kinds)
        vec_move = vec_op.run(vec_low, at.vec_parts, *at.vec_move)
        pool_move = pool_op.run(pool_own, at.pool_parts, *at.pool_move)
        step(vec_move)
        if aligned:
            moves = [
                op.run(at.lows[k], at.weights[k], *at.low_moves[5 * k : 5 * k + 5])
                for k, op in enumerate(low_ops)
            ]
            step(moves[0])
        step(pool_move)
        for r in range(rows):
            x_gather.start(r)
        if aligned:
            for c in raws[4:]:
                c.wait()
            for k in range(SEQ):

                @pl.when(s == k)
                def _(k=k):
                    at.lows[2][...] = raw_up(k).astype(BF16)

            at.lows[3][...] = second[0, :own_rows].astype(BF16)
            step(moves[0])
        x_gather.pass_far(0)
        if aligned:
            step(moves[0])
        step(pool_move)
        x_gather.pass_far(1)
        if aligned:
            step(moves[0])
            step(moves[1])
            step(moves[2])
        drain(vec_move)
        drain(pool_move)
        if aligned:
            whole = jnp.concatenate([at.vec_parts[k] for k in range(n)], axis=1)

            def here(make):
                return sum(jnp.where(s == k, make(k), 0.0) for k in range(SEQ))

            vec[0:6] = whole[2:8]
            vec[6:7] = here(
                lambda k: jnp.concatenate(
                    [
                        whole[8 + f // width : 9 + f // width, f % width : f % width + own_rows]
                        for f in ((j * SEQ + k) * own_rows for j in range(n))
                    ],
                    axis=1,
                )
            )
            blank = jnp.zeros((1, quarter), F32)
            vec[7:8] = here(
                lambda k: jnp.concatenate(
                    [
                        whole[0:1, k * quarter : (k + 1) * quarter],
                        blank,
                        whole[1:2, k * quarter : (k + 1) * quarter],
                        blank,
                    ],
                    axis=1,
                )
            )
        else:
            total = at.vec_parts[0]
            for k in range(1, n):
                total = total + at.vec_parts[k]
            vec[...] = total
        pool_whole = jnp.concatenate([at.pool_parts[k] for k in range(SEQ)], axis=1)

        if aligned:
            drain(moves[0])
            step(moves[1])
            step(moves[2])
            step(moves[3])

        def w_qkv():
            if aligned:
                return at.weights[0][...].reshape(width, 3 * quarter)
            return attn_weight[:, : 3 * quarter]

        def w_up():
            return at.weights[2][...].reshape(width, width) if aligned else up_weight[...]

        def w_down():
            return at.weights[3][...].reshape(width, width) if aligned else down_weight[...]

        out_move = out_op.run(at.out_own, at.out_parts, *at.out_move)

        def begin_out():
            if aligned:
                drain(moves[1])
                at.out_own[...] = at.weights[1][...].reshape(width, quarter)
            else:
                at.out_own[...] = attn_weight[:, 3 * quarter :]
            step(out_move)

        def turn(*ks):
            for k in ks:
                if aligned:
                    step(moves[k])

        bias = vec[7:8, : 3 * quarter]
        column = lax.broadcasted_iota(jnp.int32, (1, span_all), 1)

        def heads(r, h):
            return [
                qkv[r, :, k * quarter + h * HD : k * quarter + (h + 1) * HD] for k in range(3)
            ]

        for r in range(rows):
            x_gather.wait_near(r)
            x_gather.wait_diag(r)
            block = matmul(x_all[r].reshape(span_all, width), w_qkv()) + bias
            qkv[r] = block.astype(BF16)
            valid = column < lengths[r]
            if r == 0:
                turn(1)
            mixed = []
            for h in range(HEADS):
                query, key, value = heads(r, h)
                scores = contract_last(query * jnp.bfloat16(scale), key)
                scores = jnp.where(valid, scores, -1e30)
                exponent = jnp.exp(scores - jnp.max(scores, axis=-1, keepdims=True))
                weight = exponent * (1.0 / jnp.sum(exponent, axis=-1, keepdims=True))
                prob[r, h] = weight
                mixed.append(matmul(weight.astype(BF16), value))
                if r == 0 and h == 0:
                    turn(1, 3, 2)
                if r == 0 and h == 1:
                    begin_out()
                    turn(2)
                if r == 0 and h == 2:
                    turn(2)
                if r == 1:
                    turn(3)
            mixed = jnp.concatenate(mixed, axis=1).astype(BF16)
            for k in range(SEQ):
                at.swap[0][k, r] = mixed[k * span : (k + 1) * span]
            swap.start(r)
        step(out_move)
        drain(out_move)
        w_out = at.w_out
        w_out[...] = jnp.concatenate([at.out_parts[k] for k in range(SEQ)], axis=1)
        gain_one, shift_one = vec[1:2], vec[2:3]
        for r in range(rows):
            swap.wait(r)
            context[r] = jnp.concatenate([at.swap[1][k, r] for k in range(SEQ)], axis=1)
            hidden = tokens[r] + (matmul(context[r], w_out[...]) + vec[0:1])
            centred = hidden - jnp.mean(hidden, axis=-1, keepdims=True)
            spread = lax.rsqrt(jnp.mean(centred * centred, axis=-1, keepdims=True) + norm_eps)
            scaled = centred * spread
            at.scaled_one[r] = scaled
            at.spread_one[r] = spread
            value = scaled * gain_one + shift_one
            normed[r] = value
            y_all[r, s] = value.astype(BF16)
            y_gather.start(r)

        if aligned:
            drain(moves[2])
        gain_two, shift_two = vec[3:4], vec[4:5]
        bias_down, bias_up = vec[5:6], vec[6:7]

        def pair(ref, blocks):
            return jnp.concatenate([ref[i] for i in blocks], axis=0)

        def put(ref, blocks, value):
            for k, i in enumerate(blocks):
                ref[i] = value[k * span : (k + 1) * span].astype(ref.dtype)

        def rise(blocks):
            value, rate = gelu_parts(matmul(pair(y_all, blocks), w_up()) + bias_up)
            put(act, blocks, value)
            put(slope, blocks, rate)

        def fall(blocks):
            put(part, blocks, matmul(pair(act, blocks), w_down()))

        mine, beside = [[(r, k) for r in range(rows)] for k in (s, near)]
        rise(mine)
        for r in range(rows):
            y_gather.wait_near(r)
        rise(beside)
        if aligned:
            drain(moves[3])
        fall(beside)
        for r in range(rows):
            z_sum.send_near(r)
        for r in range(rows):
            y_gather.pass_far(r)
            y_gather.wait_diag(r)
            rise([(r, diag), (r, far)])
            fall([(r, diag), (r, far)])
            z_sum.send_diag(r)
            if r == 0:
                fall(mine)
            z_sum.cross(r)

        position = s * span + lax.broadcasted_iota(jnp.int32, (span, 1), 0)
        grad_gain_two = grad_shift_two = grad_bias_down = jnp.zeros((1, width), F32)
        for r in range(rows):
            hidden = normed[r] + (z_sum.total(r) + bias_down)
            centred = hidden - jnp.mean(hidden, axis=-1, keepdims=True)
            spread_two = lax.rsqrt(jnp.mean(centred * centred, axis=-1, keepdims=True) + norm_eps)
            scaled = centred * spread_two
            output = scaled * gain_two + shift_two
            out_rows[r] = output
            live = (position < lengths[r]).astype(F32)
            length = jnp.full((1, 1), lengths[r], jnp.int32).astype(F32)
            at.pool_buf[s, r : r + 1] = row_sum(output * live) / length
            upstream = live * (out_grad[r] + pool_whole[r : r + 1] / length)
            weighted = upstream * gain_two
            mean_first = jnp.mean(weighted, axis=-1, keepdims=True)
            mean_second = jnp.mean(weighted * scaled, axis=-1, keepdims=True)
            grad = spread_two * (weighted - mean_first - scaled * mean_second)
            second[r] = grad
            low = grad.astype(BF16)
            dz_all[r, s] = low
            dz_gather.start(r)
            grad_gain_two += row_sum(upstream * scaled)
            grad_shift_two += row_sum(upstream)
            grad_bias_down += row_sum(low.astype(F32))

        if aligned:
            leaving[0].start()

        def pool_copy(k, block, device):
            place = at.pool_buf.at[block]
            sems = at.pool_sems
            return remote(place, place, sems[0].at[k - 1], sems[1].at[k - 1], (b, device))

        for k in (1, 2, 3):
            pool_copy(k, s, (s + k) % 4).start()
        for r in range(rows):
            z_sum.finish(r)

        def backward(blocks):
            lift = contract_last(pair(dz_all, blocks), w_down())
            low = (lift * pair(slope, blocks)).astype(BF16)
            put(du_all, blocks, low)
            put(part, blocks, contract_last(low, w_up()))
            return row_sum(low.astype(F32))

        bias_grad = backward(mine)
        for r in range(rows):
            dz_gather.wait_near(r)
        bias_grad += backward(beside)
        for r in range(rows):
            dy_sum.send_near(r)
        for r in range(rows):
            dz_gather.pass_far(r)
            dz_gather.wait_diag(r)
            bias_grad += backward([(r, diag), (r, far)])
            dy_sum.send_diag(r)
            dy_sum.cross(r)

        flat = rows * span_all
        if aligned:
            down_move = sum_ops[0].run(at.down_grad, at.down_piece, *at.down_sum)
            up_move = sum_ops[1].run(at.up_grad, at.up_piece, *at.up_sum)
            mail = OwnerMail(n, owner_list(n)[4:], wide_in, *at.mail)
            wide_send = at.wide_send
            momenta = load_up(up_moment) + [load_down(down_moment, raw_block(0))]
            for c in momenta:
                c.start()
        whole = contract_first(act[...].reshape(flat, width), dz_all[...].reshape(flat, width))
        if aligned:
            at.down_grad[...] = whole.reshape(n, own_rows, width).astype(BF16)
            step(down_move)
        else:
            grad_down_out[...] = whole.astype(BF16)
        whole = contract_first(y_all[...].reshape(flat, width), du_all[...].reshape(flat, width))
        if aligned:
            at.up_grad[...] = whole.reshape(n, own_rows, width).astype(BF16)
            step(up_move)
        else:
            grad_up_out[...] = whole.astype(BF16)

        grad_gain_one = grad_shift_one = grad_bias_out = jnp.zeros((1, width), F32)
        for r in range(rows):
            grad = dy_sum.total(r) + second[r]
            scaled = at.scaled_one[r]
            weighted = grad * gain_one
            mean_first = jnp.mean(weighted, axis=-1, keepdims=True)
            mean_second = jnp.mean(weighted * scaled, axis=-1, keepdims=True)
            first = at.spread_one[r] * (weighted - mean_first - scaled * mean_second)
            second[r] = first
            low = first.astype(BF16)
            above = contract_last(low, w_out[...]).astype(BF16)
            for k in range(SEQ):
                columns = slice(k * quarter, (k + 1) * quarter)
                at.back_swap[0][k, r] = above[:, columns]
                at.a_quarters[k, r * span : (r + 1) * span] = low[:, columns]
            back_swap.start(r)
            grad_gain_one += row_sum(grad * scaled)
            grad_shift_one += row_sum(grad)
            grad_bias_out += row_sum(low.astype(F32))
        for k, value in enumerate(
            (
                grad_bias_out, grad_gain_one, grad_shift_one, grad_gain_two, grad_shift_two,
                grad_bias_down, bias_grad, jnp.zeros((1, width), F32),
            )
        ):
            vec_grad[k : k + 1] = value

        def new_momentum(k, piece, old):
            wide_bf[k] = piece[...].astype(BF16)
            wide_send[k] = (matrix_decay * old + wide_bf[k].astype(F32)).astype(BF16)
            mail.send(k, wide_send.at[k])

        flat_context = context[...].reshape(local, width)
        for k in range(SEQ):
            at.out_part[0, k] = contract_first(flat_context, at.a_quarters[k]).astype(BF16)
        out_sum.send_diag(0)
        out_sum.send_near(0)
        for r in range(rows):
            dy_sum.finish(r)
        sums = jnp.zeros((1, 3 * quarter), F32)
        for r in range(rows):
            back_swap.wait(r)
            arrived = jnp.concatenate([at.back_swap[1][k, r] for k in range(SEQ)], axis=0)
            query_grads, key_grads, value_grads = [], [], []
            for h in range(HEADS):
                query, key, value = heads(r, h)
                above = arrived[:, h * HD : (h + 1) * HD]
                weight = prob[r, h]
                prob_grad = contract_last(above, value)
                delta = jnp.sum(weight * prob_grad, axis=-1, keepdims=True)
                score_grad = (weight * (prob_grad - delta)).astype(BF16)
                query_grads.append(matmul(score_grad, key) * scale)
                key_grads.append(contract_first(query, score_grad) * scale)
                value_grads.append(contract_first(above, weight.astype(BF16)))
                if aligned and r == 0:
                    step(down_move)
                if r == 1 and h == 0:
                    out_sum.cross(0)
                if aligned and r == 1 and h > 0:
                    step(up_move)
                if not aligned and r > 0 and h == 2:
                    x_sum.cross(r - 1)
            turned = jnp.concatenate(key_grads + value_grads, axis=0).T
            block = jnp.concatenate(query_grads + [turned], axis=1).astype(BF16)
            at.grad_qkv[r] = block
            sums += row_sum(block.astype(F32))
            out = contract_last(block, w_qkv())
            for k in range(SEQ):
                part[r, k] = out[k * span : (k + 1) * span].astype(BF16)
            if not aligned:
                if r == 0:
                    x_sum = RowSum(part, *at.x_sum)
                x_sum.send_diag(r)
                x_sum.send_near(r)
        if aligned:
            step(up_move)
            drain(down_move)
            for c in momenta:
                c.wait()
            new_momentum(1, at.down_piece, raw_block(0)[...])
        bias_sums[...] = sums
        if aligned:
            leaving[1].start()
            leaving[2].start()
        whole = contract_first(
            x_all[...].reshape(flat, width), at.grad_qkv[...].reshape(flat, 3 * quarter)
        )
        whole = jnp.concatenate([whole, out_sum.total(0)], axis=1)
        grad_attn[...] = whole.astype(BF16).reshape(grad_attn.shape)
        if aligned:
            leaving[3].start()
        for k in (1, 2, 3):
            pool_copy(k, (s + 4 - k) % 4, (s + k) % 4).wait_recv()
        pool_buf = at.pool_buf
        pooled[...] = (pool_buf[0] + pool_buf[1]) + (pool_buf[2] + pool_buf[3])
        if aligned:
            mail.relay(1)
            drain(up_move)
            for k in range(SEQ):

                @pl.when(s == k)
                def _(k=k):
                    wide_bf[0] = at.up_piece[...].astype(BF16)
                    old = matrix_decay * raw_up(k) + wide_bf[0].astype(F32)
                    wide_send[0] = old.astype(BF16)

            mail.send(0, wide_send.at[0])
        else:
            x_sum.cross(rows - 1)
            for r in range(rows):
                second[r] = x_sum.total(r) + second[r]
                x_sum.finish(r)
        out_sum.finish(0)
        for k in (1, 2, 3):
            pool_copy(k, s, (s + k) % 4).wait_send()
        for r in range(rows):
            for op in (x_gather, swap, y_gather, dz_gather, back_swap):
                op.finish(r)
        if aligned:
            mail.relay(0)

            @pl.when(mail.mine[0] | mail.mine[1])
            def _():
                mail.collect()

            for k in range(2):
                mail.finish(k, wide_send.at[k])
            for c in leaving:
                c.wait()

    smem = pl.BlockSpec(memory_space=pltpu.SMEM)
    far_spec = anywhere if aligned else vmem
    return pl.pallas_call(
        kernel,
        out_shape=outs,
        in_specs=[vmem] + [far_spec] * 3 + [vmem] * 2 + [smem, vmem] + [anywhere] * 2,
        out_specs=out_specs,
        scratch_shapes=sc.shapes,
        compiler_params=pltpu.CompilerParams(
            collective_id=0, has_side_effects=True, vmem_limit_bytes=63 * 2**20
        ),
        name="layer",
    )(tokens, attn_weight, up_weight, down_weight, vec_own, pool_own, lengths, out_grad, up_moment, down_moment)


def join_up_parts(parts, n):
    hid_own = parts[0].shape[1] // n
    return jnp.concatenate(
        [parts[k][:, b * hid_own : (b + 1) * hid_own] for b in range(n) for k in range(SEQ)], axis=1
    )


def take_up(matrix, n, k):
    hid_own = matrix.shape[1] // n // SEQ
    return jnp.concatenate(
        [
            matrix[:, (b * SEQ + k) * hid_own : (b * SEQ + k + 1) * hid_own]
            for b in range(n)
        ],
        axis=1,
    )


def muon(n, grad_attn, wide_in, bias_sums, vec_grad, attn_moment, wide_bf, x_part, first_grad):
    rows, width = wide_bf.shape[1:]
    quarter = width // SEQ
    hid_own = rows
    n_vec = 8 + SEQ
    shape = jax.ShapeDtypeStruct
    attn_shape = (4, rows // 2, 2 * quarter)
    attn_op = GatherSeq(n, shape(attn_shape, BF16))
    attn_sum = BatchSum(n, grad_attn)
    vec_sum = DirectSum(n, shape((n, n_vec, rows), F32))
    vec_op = GatherSeq(n, shape((n_vec, rows), F32))
    wide_op = GatherSeq(n, wide_bf)
    count, span = first_grad.shape[:2]
    main = Muon(n, shape(attn_shape, BF16), wide_in=wide_in)
    outs = [attn_op.outs[0], wide_op.outs[0], shape((n_vec, rows), F32), shape(first_grad.shape, F32)]
    outs += main.outs
    groups = [
        [
            pltpu.VMEM((rows, width), F32),
            pltpu.VMEM(attn_shape, BF16),
            pltpu.VMEM(attn_shape, BF16),
            pltpu.VMEM((n, n_vec, rows), F32),
            pltpu.VMEM((n_vec, rows), F32),
            pltpu.VMEM((SEQ, n_vec, rows), F32),
        ]
    ] + [op.scratch for op in (attn_op, vec_sum, vec_op, main, attn_sum, wide_op)]
    groups.append(RowSum.scratch(count, (span, width)))
    late = (attn_moment, x_part, first_grad)
    groups.append([pltpu.VMEM(a.shape, a.dtype) for a in late] + [pltpu.SemaphoreType.DMA((3,))])

    def kernel(
        grad_attn, wide_in, bias_sums, vec_grad, attn_moment, wide_bf, x_part, first_grad,
        attn_all, wide_all, vec_total, input_grad, attn_orth, wide_orth, *rest,
    ):
        greet_signal(n, {"all"})
        parts, i = [], 0
        for group in groups:
            parts.append(rest[i : i + len(group)])
            i += len(group)
        attn_piece, attn_bf, attn_send, vec_local, vec_piece, vec_parts = parts[0]
        s = lax.axis_index("seq")
        arriving = [
            pltpu.make_async_copy(a, b, parts[8][3].at[k])
            for k, (a, b) in enumerate(zip((attn_moment, x_part, first_grad), parts[8][:3]))
        ]
        attn_moment, x_part, first_grad = parts[8][:3]
        for c in arriving:
            c.start()
        main_move = main.run(attn_send, wide_in, attn_orth, wide_orth, *parts[4])
        step(main_move)
        main.prepare()
        greet_wait(n, {"all"})
        x_sum = RowSum(x_part, *parts[7])

        def inputs():
            arriving[1].wait()
            arriving[2].wait()
            for r in range(count):
                x_sum.send_diag(r)
                x_sum.send_near(r)
            yield
            for r in range(count):
                x_sum.cross(r)
            yield from rounds(8)
            for r in range(count):
                input_grad[r] = x_sum.total(r) + first_grad[r]
                x_sum.finish(r)

        def attention():
            moving = attn_sum.run(grad_attn, attn_piece, *parts[5])
            step(moving)
            yield from rounds(3)
            for _ in range(n // 2 - 1):
                step(moving)
            yield from rounds(3)
            drain(moving)
            arriving[0].wait()
            for j in range(4):
                attn_bf[j] = fold(attn_piece[:, j * quarter : (j + 1) * quarter]).astype(BF16)
            for k in range(SEQ):

                @pl.when(s == k)
                def _(k=k):
                    for j in range(4):
                        old = fold(attn_moment[j, :, k * quarter : (k + 1) * quarter])
                        attn_send[j] = (matrix_decay * old + attn_bf[j].astype(F32)).astype(BF16)
            main.send_attn()
            yield
            main.attn_turn()
            yield from spaced(attn_op.run(attn_bf, attn_all, *parts[1]), 2)

        def vectors():
            def here(k, value):
                return jnp.where(s == k, value, 0.0)

            lines = [
                jnp.concatenate(
                    [here(k, bias_sums[:, j * quarter : (j + 1) * quarter]) for k in range(SEQ)], axis=1
                )
                for j in (0, 2)
            ]
            lines += [vec_grad[j : j + 1] for j in range(6)]
            hidden = vec_grad[6:7]
            pieces = [
                here(k, hidden[:, b * hid_own : (b + 1) * hid_own]) for b in range(n) for k in range(SEQ)
            ]
            each = n * SEQ // 4
            lines += [jnp.concatenate(pieces[j * each : (j + 1) * each], axis=1) for j in range(4)]
            whole = jnp.concatenate(lines, axis=0)
            for b in range(n):
                vec_local[b] = whole[:, b * rows : (b + 1) * rows]
            yield from spaced(vec_sum.run(vec_local, vec_piece, *parts[2]), 3)
            yield from spaced(vec_op.run(vec_piece, vec_parts, *parts[3]), 2)
            vec_total[...] = (vec_parts[0] + vec_parts[1]) + (vec_parts[2] + vec_parts[3])

        run_together(
            vectors(),
            attention(),
            inputs(),
            spaced(wide_op.run(wide_bf, wide_all, *parts[6]), 6),
            main_move,
        )

    vmem = pl.BlockSpec(memory_space=pltpu.VMEM)
    far = pl.BlockSpec(memory_space=pl.ANY)
    ins = (grad_attn, wide_in, bias_sums, vec_grad, attn_moment, wide_bf, x_part, first_grad)
    return pl.pallas_call(
        kernel,
        out_shape=outs,
        in_specs=[vmem, far, vmem, vmem, far, vmem, far, far],
        out_specs=[vmem] * len(outs),
        scratch_shapes=[c for group in groups for c in group],
        compiler_params=pltpu.CompilerParams(
            collective_id=8, has_side_effects=True, vmem_limit_bytes=62 * 2**20
        ),
        name="muon",
    )(*ins)


def finish(
    n, out_rows, pool_sum, input_grad, attn_all, wide_all, attn_orth, wide_orth, vec_total,
    attn_weight, up_weight, down_weight, vectors, attn_moment, up_moment, down_moment, vector_moment,
    factors, vector_step,
):
    rows = wide_all.shape[2]
    quarter = wide_all.shape[3] // SEQ
    shape = jax.ShapeDtypeStruct
    ins = (
        attn_all, attn_moment, wide_all, up_moment, down_moment, out_rows, input_grad, pool_sum, vec_total,
        vectors, vector_moment, attn_orth, attn_weight, wide_orth, up_weight, down_weight,
    )
    token, pool = shape(out_rows.shape, F32), shape((out_rows.shape[0], quarter), F32)
    attn, up, down, vec = [shape(a.shape, F32) for a in (attn_weight, up_weight, down_weight, vectors)]
    outs = [token, pool, token] + [attn, up, down, vec] * 3
    direct = {0: 5, 2: 6}
    held = [k for k in range(len(outs)) if k not in direct]

    def kernel(*refs):
        far_in, far_out = refs[: len(ins)], refs[len(ins) : len(ins) + len(outs)]
        refs = refs[len(ins) + len(outs) :]
        near_in = refs[: len(ins)]
        near_out = dict(zip(held, refs[len(ins) :]))
        near_out.update({k: near_in[j] for k, j in direct.items()})
        in_sem, out_sem = refs[-2:]
        arriving = [
            pltpu.make_async_copy(a, b, in_sem.at[k]) for k, (a, b) in enumerate(zip(far_in, near_in))
        ]
        leaving = [
            pltpu.make_async_copy(near_out[k], far_out[k], out_sem.at[k]) for k in range(len(outs))
        ]
        for c in arriving:
            c.start()
        (
            attn_all, attn_moment, wide_all, up_moment, down_moment, _, _, pool_sum, vec_total,
            vectors, vector_moment, attn_orth, attn_weight, wide_orth, up_weight, down_weight,
        ) = near_in
        (
            _, pooled, _, attn_grad, up_grad, down_grad, vec_grad, attn_next, up_next, down_next, vec_next,
            attn_new, up_new, down_new, vec_new,
        ) = [near_out[k] for k in range(len(outs))]

        def wait(*ks):
            for k in ks:
                arriving[k].wait()

        def leave(*ks):
            for k in ks:
                leaving[k].start()

        def attn_of(parts, j):
            return jnp.concatenate([unfold(parts[k, j]) for k in range(SEQ)], axis=1).astype(F32)

        wait(0, 1)
        for j in range(4):
            grad = attn_of(attn_all, j)
            attn_grad[j] = grad
            attn_next[j] = matrix_decay * attn_moment[j] + grad
        leave(3, 7)
        wait(2, 3)
        grad = join_up_parts([wide_all[k, 0] for k in range(SEQ)], n).astype(F32)
        up_grad[...] = grad
        up_next[...] = matrix_decay * up_moment[...] + grad
        leave(4, 8)
        wait(4)
        for k in range(SEQ):
            part = pl.ds(k * rows, rows)
            grad = wide_all[k, 1].astype(F32)
            down_grad[part] = grad
            down_next[part] = matrix_decay * down_moment[part] + grad
        leave(5, 9)
        wait(5)
        leave(0)
        wait(6)
        leave(2)
        wait(7, 8, 9, 10)
        s = lax.axis_index("seq")
        pooled[...] = sum(
            jnp.where(s == k, pool_sum[:, k * quarter : (k + 1) * quarter], 0.0) for k in range(SEQ)
        )
        vec_grad[...] = vec_total[...]
        moved = vector_decay * vector_moment[...] + vec_total[...]
        vec_next[...] = moved
        vec_new[...] = vectors[...] - vector_step * moved
        leave(1, 6, 10, 14)
        wait(11, 12)
        for j in range(4):
            attn_new[j] = attn_weight[j] - factors[0] * attn_of(attn_orth, j)
        leave(11)
        wait(13, 14)
        orth = join_up_parts([wide_orth[k, 0] for k in range(SEQ)], n).astype(F32)
        up_new[...] = up_weight[...] - factors[1] * orth
        leave(12)
        wait(15)
        for k in range(SEQ):
            part = pl.ds(k * rows, rows)
            down_new[part] = down_weight[part] - factors[2] * wide_orth[k, 1].astype(F32)
        leave(13)
        for c in leaving:
            c.wait()

    anywhere = pl.BlockSpec(memory_space=pl.ANY)
    return pl.pallas_call(
        kernel,
        out_shape=outs,
        in_specs=[anywhere] * len(ins),
        out_specs=[anywhere] * len(outs),
        scratch_shapes=[pltpu.VMEM(a.shape, a.dtype) for a in ins]
        + [pltpu.VMEM(outs[k].shape, F32) for k in held]
        + [pltpu.SemaphoreType.DMA((len(ins),)), pltpu.SemaphoreType.DMA((len(outs),))],
        compiler_params=pltpu.CompilerParams(vmem_limit_bytes=60 * 2**20),
        name="finish",
    )(*ins)


def step_factor(rows_all, cols_all):
    return matrix_rate * math.sqrt(max(1.0, rows_all / cols_all))


def make_body(n):
    def body(
        layer_input,
        lengths,
        attn_weight,
        up_weight,
        down_weight,
        vectors,
        attn_moment,
        up_moment,
        down_moment,
        vector_moment,
        out_grad,
        pool_grad,
    ):
        rows, span, width = layer_input.shape
        own_rows = width // n
        quarter = width // SEQ
        hidden = up_weight.shape[1]
        hid_q = hidden // SEQ
        hid_own = hidden // n // SEQ
        seq_index = lax.axis_index("seq")

        def attn_quarter(stacked):
            part = lax.dynamic_index_in_dim(
                stacked.reshape(4, own_rows, SEQ, quarter), seq_index, 2, False
            )
            return part

        def up_quarter(matrix):
            return lax.dynamic_index_in_dim(
                matrix.reshape(own_rows, n, SEQ, hid_own), seq_index, 2, False
            ).reshape(own_rows, hid_q)

        def down_quarter(matrix):
            return lax.dynamic_index_in_dim(
                matrix.reshape(SEQ, hid_own, width), seq_index, 0, False
            )

        aligned = own_rows % 16 == 0
        if aligned:
            own = [attn_weight, up_weight, down_weight]
            vec_own = vectors
        else:
            attn_low = attn_quarter(attn_weight).astype(BF16).transpose(1, 0, 2).reshape(own_rows, width)
            up_low = up_quarter(up_weight).astype(BF16)
            down_low = down_quarter(down_weight).astype(BF16)
            vec_low = vectors.astype(BF16).astype(F32)
            placed = lax.dynamic_update_slice(
                jnp.zeros((vectors.shape[0], n, own_rows), F32),
                vec_low[:, None],
                (0, lax.axis_index("batch"), 0),
            ).reshape(-1, width)
            bias_up = lax.dynamic_index_in_dim(
                placed[8:].reshape(n, SEQ, hid_own), seq_index, 1, False
            ).reshape(1, hid_q)
            bias_qv = lax.dynamic_index_in_dim(
                placed[:2].reshape(2, SEQ, quarter), seq_index, 1, False
            )
            blank = jnp.zeros((quarter,), F32)
            bias_qkv = jnp.concatenate([bias_qv[0], blank, bias_qv[1], blank])[None]
            vec_own = jnp.concatenate([placed[2:8], bias_up, bias_qkv])
            own = exchange(
                n, 1, "gather_weights", *[GatherBatch(n, a) for a in (attn_low, up_low, down_low)]
            )
            own = [a.reshape(width, width) for a in own]
        out_rows, pool_sum, input_grad, vec_grad, bias_sums, x_part, *grads = layer(
            n, layer_input, *own, vec_own, pool_grad, lengths, out_grad, up_moment, down_moment
        )
        factors = [
            step_factor(width, width),
            step_factor(width, hidden),
            step_factor(hidden, width),
        ]
        vector_step = vector_rate / math.sqrt(rows * n)
        if aligned:
            grad_attn, wide_bf, wide_in = grads
            attn_all, wide_all, vec_total, input_grad, attn_orth, wide_orth = muon(
                n, grad_attn, wide_in, bias_sums, vec_grad, attn_moment, wide_bf, x_part, input_grad
            )
            return tuple(
                finish(
                    n, out_rows, pool_sum, input_grad, attn_all, wide_all, attn_orth, wide_orth, vec_total,
                    attn_weight, up_weight, down_weight, vectors,
                    attn_moment, up_moment, down_moment, vector_moment, factors, vector_step,
                )
            )
        pooled = lax.dynamic_slice_in_dim(pool_sum, seq_index * quarter, quarter, 1)
        attn_piece, up_piece, down_piece = exchange(
            n, 2, "sum_grads", *[BatchSum(n, a.reshape(n, own_rows, width)) for a in grads]
        )
        bias_sums = bias_sums.reshape(3, quarter)

        vec_head = jnp.zeros((2, SEQ, quarter), F32)
        vec_head = lax.dynamic_update_slice(
            vec_head, bias_sums[jnp.array([0, 2])][:, None], (0, seq_index, 0)
        ).reshape(2, width)
        vec_mid = vec_grad[:6]
        grad_bias_up = vec_grad[6]
        vec_tail = lax.dynamic_update_slice(
            jnp.zeros((n, SEQ, hid_own), F32),
            grad_bias_up.reshape(n, 1, hid_own),
            (0, seq_index, 0),
        ).reshape(-1, width)
        vec_local = jnp.concatenate([vec_head, vec_mid, vec_tail])
        vec_local = vec_local.reshape(-1, n, own_rows).transpose(1, 0, 2)
        (vec_piece,) = exchange(n, 7, "sum_vectors", ScatterBatch(n, vec_local, F32))
        attn_bf = attn_piece.astype(BF16).reshape(own_rows, 4, quarter).transpose(1, 0, 2)
        wide_bf = jnp.stack([up_piece, down_piece]).astype(BF16)
        attn_send = (matrix_decay * attn_quarter(attn_moment) + attn_bf.astype(F32)).astype(BF16)
        wide_moment = jnp.stack([up_quarter(up_moment), down_quarter(down_moment)])
        wide_send = (matrix_decay * wide_moment + wide_bf.astype(F32)).astype(BF16)
        short = -own_rows % 16
        attn_send = jnp.pad(attn_send, ((0, 0), (0, short), (0, 0)))
        wide_send = jnp.pad(wide_send, ((0, 0), (0, short), (0, 0)))
        attn_all, wide_all, vec_parts, attn_orth, wide_orth = exchange(
            n,
            8,
            "muon",
            GatherSeq(n, attn_bf),
            GatherSeq(n, wide_bf),
            GatherSeq(n, vec_piece),
            Muon(n, attn_send, wide_send),
        )
        attn_orth = attn_orth[:, :, :own_rows]
        wide_orth = wide_orth[:, :, :own_rows]

        def join_attn(parts):
            return parts.astype(F32).transpose(1, 2, 0, 3).reshape(4, own_rows, width)

        def join_up(parts):
            return (
                parts.astype(F32)
                .reshape(SEQ, own_rows, n, hid_own)
                .transpose(1, 2, 0, 3)
                .reshape(own_rows, hidden)
            )

        def join_down(parts):
            return parts.astype(F32).reshape(SEQ * hid_own, width)

        attn_grad = join_attn(attn_all)
        up_grad, down_grad = join_up(wide_all[:, 0]), join_down(wide_all[:, 1])
        vector_grad = (vec_parts[0] + vec_parts[1]) + (vec_parts[2] + vec_parts[3])
        attn_next = matrix_decay * attn_moment + attn_grad
        up_next = matrix_decay * up_moment + up_grad
        down_next = matrix_decay * down_moment + down_grad

        attn_new = attn_weight - factors[0] * join_attn(attn_orth)
        up_new = up_weight - factors[1] * join_up(wide_orth[:, 0])
        down_new = down_weight - factors[2] * join_down(wide_orth[:, 1])
        vector_next = vector_decay * vector_moment + vector_grad
        vectors_new = vectors - vector_step * vector_next
        return (
            out_rows,
            pooled,
            input_grad,
            attn_grad,
            up_grad,
            down_grad,
            vector_grad,
            attn_next,
            up_next,
            down_next,
            vector_next,
            attn_new,
            up_new,
            down_new,
            vectors_new,
        )

    return body


def solution(mesh):
    placed = (
        P("batch", "seq", None),
        P("batch"),
        P(None, "batch", None),
        P("batch", None),
        P("batch", None),
        P(None, "batch"),
        P(None, "batch", None),
        P("batch", None),
        P("batch", None),
        P(None, "batch"),
        P("batch", "seq", None),
        P("batch", "seq"),
    )
    return jax.shard_map(
        make_body(mesh.shape["batch"]),
        mesh=mesh,
        in_specs=placed,
        out_specs=(
            P("batch", "seq", None),
            P("batch", "seq"),
            P("batch", "seq", None),
            P(None, "batch", None),
            P("batch", None),
            P("batch", None),
            P(None, "batch"),
            P(None, "batch", None),
            P("batch", None),
            P("batch", None),
            P(None, "batch"),
            P(None, "batch", None),
            P("batch", None),
            P("batch", None),
            P(None, "batch"),
        ),
        check_vma=False,
    )
```

```python
import math
import types

import jax
import jax.numpy as jnp
from jax import lax
from jax.experimental import pallas as pl
from jax.experimental.pallas import tpu as pltpu
from jax.sharding import PartitionSpec as P

H = 12
HD = 64
NS = 5
SEQ = 4
HEADS = H // SEQ

norm_eps = 1e-12
tiny_norm = 1e-07
matrix_decay = 0.95
vector_decay = 0.5
matrix_rate = 0.5
vector_rate = 0.03

MESH = pl.DeviceIdType.MESH
F32 = jnp.float32
BF16 = jnp.bfloat16


def coords(n):
    b = lax.axis_index("batch")
    s = lax.axis_index("seq")
    return b, s, b // 2, b % 2, n // 2


def remote(src, dst, send, recv, device):
    return pltpu.make_async_remote_copy(
        src_ref=src, dst_ref=dst, send_sem=send, recv_sem=recv, device_id=device, device_id_type=MESH
    )


class GatherBatch:
    peers = ("batch",)

    def __init__(self, n, src, eager=True):
        self.n = n
        self.eager = eager
        self.ins = [src]
        self.outs = [jax.ShapeDtypeStruct((n,) + src.shape, src.dtype)]
        m = n // 2
        self.scratch = [pltpu.SemaphoreType.DMA((2, m))] * 4 + [pltpu.SemaphoreType.DMA]

    def run(self, src, dst, zs, zr, ys, yr, own):
        b, s, hi, lo, m = coords(self.n)
        pair = (hi * 2 + 1 - lo, s)
        local = pltpu.make_async_copy(src, dst.at[b], own)
        local.start()

        def exists(way, d):
            return hi >= d if way == 0 else hi + d < m

        def ahead(way):
            return hi + 1 < m if way == 0 else hi >= 1

        def block_of(way, d):
            place = jnp.clip(hi - d if way == 0 else hi + d, 0, m - 1)
            return place * 2 + lo

        def along(way, d, ref):
            place = jnp.clip(hi + 1 if way == 0 else hi - 1, 0, m - 1)
            return remote(
                ref, dst.at[block_of(way, d)], zs.at[way, d], zr.at[way, d + 1], (place * 2 + lo, s)
            )

        def aside(way, d):
            place = dst.at[block_of(way, d)]
            return remote(place, place, ys.at[way, d], yr.at[way, d], pair)

        first = remote(src, dst.at[b], ys.at[0, 0], yr.at[0, 0], pair)
        for way in (0, 1):

            @pl.when(ahead(way))
            def _(way=way):
                along(way, 0, src).start()

        if not self.eager:
            yield
        first.start()
        yield
        for d in range(1, m):
            for way in (0, 1):

                @pl.when(exists(way, d))
                def _(way=way, d=d):
                    place = dst.at[block_of(way, d)]
                    remote(place, place, zs.at[way, d], zr.at[way, d], pair).wait_recv()
                    if d < m - 1:

                        @pl.when(ahead(way))
                        def _():
                            along(way, d, place).start()

                    aside(way, d).start()

            yield
        local.wait()
        first.wait()
        for d in range(m):
            for way in (0, 1):
                if d > 0:

                    @pl.when(exists(way, d))
                    def _(way=way, d=d):
                        aside(way, d).wait()

                if d < m - 1:

                    @pl.when(exists(way, d) & ahead(way))
                    def _(way=way, d=d):
                        along(way, d, dst.at[block_of(way, d)]).wait_send()


class GatherDirect:
    peers = ("all",)

    def __init__(self, n, src):
        self.n = n
        self.ins = [src]
        self.outs = [jax.ShapeDtypeStruct((n,) + src.shape, src.dtype)]
        self.scratch = [pltpu.SemaphoreType.DMA((n,))] * 2 + [pltpu.SemaphoreType.DMA]

    def run(self, src, dst, ss, rs, own):
        n = self.n
        b, s = lax.axis_index("batch"), lax.axis_index("seq")
        local = pltpu.make_async_copy(src, dst.at[b], own)
        local.start()
        copies = [
            remote(src, dst.at[b], ss.at[k], rs.at[k], ((b + k) % n, s)) for k in range(1, n)
        ]
        for c in copies:
            c.start()
        yield
        local.wait()
        for c in copies:
            c.wait()


class ScatterBatch:
    peers = ("batch",)

    def __init__(self, n, src, wire=BF16):
        self.n = n
        self.wire = wire
        self.ins = [src]
        shape = src.shape[1:]
        self.outs = [jax.ShapeDtypeStruct(shape, F32)]
        m = n // 2
        self.scratch = [pltpu.VMEM((m,) + shape, wire)] * 4 + [pltpu.SemaphoreType.DMA((m,))] * 4

    def run(self, src, dst, ysend, yrecv, zsend, zrecv, ys, yr, zs, zr):
        b, s, hi, lo, m = coords(self.n)
        pair = (hi * 2 + 1 - lo, s)
        first = {}
        order = list(range(1, m)) + [0]
        for d in order:
            h = (hi + d) % m
            ysend[d] = src[h * 2 + 1 - lo].astype(self.wire)
            first[d] = remote(ysend.at[d], yrecv.at[d], ys.at[d], yr.at[d], pair)
            first[d].start()
        yield
        second = []
        for d in range(1, m):
            h = (hi + d) % m
            first[d].wait_recv()
            zsend[d] = (src[h * 2 + lo] + yrecv[d].astype(F32)).astype(self.wire)
            c = remote(zsend.at[d], zrecv.at[d], zs.at[d], zr.at[d], (h * 2 + lo, s))
            c.start()
            second.append(c)
            yield
        first[0].wait_recv()
        total = src[b] + yrecv[0].astype(F32)
        for d in range(1, m):
            second[d - 1].wait_recv()
            total = total + zrecv[d].astype(F32)
        dst[...] = total
        for c in list(first.values()) + second:
            c.wait_send()


class GatherSeq:
    peers = ("seq",)

    def __init__(self, n, src):
        self.ins = [src]
        self.outs = [jax.ShapeDtypeStruct((SEQ,) + src.shape, src.dtype)]
        self.scratch = [pltpu.SemaphoreType.DMA((3,))] * 2 + [pltpu.SemaphoreType.DMA]

    def run(self, src, dst, ss, rs, own):
        b, s = lax.axis_index("batch"), lax.axis_index("seq")
        far, near = (s + 2) % 4, s + 1 - 2 * (s % 2)
        across = remote(src, dst.at[s], ss.at[0], rs.at[0], (b, far))
        across.start()
        local = pltpu.make_async_copy(src, dst.at[s], own)
        local.start()
        beside = remote(src, dst.at[s], ss.at[1], rs.at[1], (b, near))
        beside.start()
        yield
        across.wait_recv()
        passed = remote(dst.at[far], dst.at[far], ss.at[2], rs.at[2], (b, near))
        passed.start()
        yield
        local.wait()
        beside.wait()
        passed.wait()
        across.wait_send()


def owner_list(n):
    return [(0, 2), (1, 0), (n - 2, 2), (n - 1, 0), (n // 4, 0), (n // 2 + 1, 2)]


class OwnerMail:
    @staticmethod
    def scratch(n, count, relayed=None):
        dma = pltpu.SemaphoreType.DMA
        base = [dma((count,)), dma((SEQ * n,)), dma]
        if relayed is not None:
            base += [pltpu.VMEM((count, 2) + relayed, BF16), dma((count, 2)), dma((count, 2))]
        return base

    def __init__(self, n, places, inbox, ss, rs, own, relayed=None, relay_s=None, relay_r=None):
        self.n, self.places, self.inbox, self.ss, self.rs, self.own = n, places, inbox, ss, rs, own
        self.relayed, self.relay_s, self.relay_r = relayed, relay_s, relay_r
        self.b, self.s = lax.axis_index("batch"), lax.axis_index("seq")
        self.me = self.s * n + self.b
        self.mine = [(self.b == ob) & (self.s == os) for ob, os in places]

    def slot(self, seq, block):
        if len(self.inbox.shape) == 4:
            return self.inbox.at[seq, block]
        rows = self.inbox.shape[1] // self.n
        return self.inbox.at[seq, pl.ds(pl.multiple_of(block * rows, rows), rows)]

    def indirect(self, k):
        ob, os = self.places[k]
        hi, oh = self.b // 2, ob // 2
        light = hi < oh if oh < self.n // 4 else hi > oh
        same_lo, same_x = self.b % 2 == ob % 2, self.s // 2 == os // 2
        other_lo, other_x = jnp.logical_not(same_lo), jnp.logical_not(same_x)
        away = hi != oh
        column = away & same_lo & same_x
        return (away & other_lo & other_x, light & other_lo & same_x), (column, column & light)

    def copy(self, k, src):
        ob, os = self.places[k]
        place = self.slot(self.s, self.b)
        return remote(src, place, self.ss.at[k], self.rs.at[self.me], (ob, os))

    def aside(self, k, slot, src):
        across = self.b + 1 - 2 * (self.b % 2)
        seq = self.s if slot else (self.s + 2) % 4
        return remote(
            src, self.relayed.at[k, slot], self.ss.at[k], self.relay_r.at[k, slot], (across, seq)
        )

    def pass_copy(self, k, slot):
        block, seq = self.b + 1 - 2 * (self.b % 2), self.s if slot else (self.s + 2) % 4
        return remote(
            self.relayed.at[k, slot], self.slot(seq, block), self.relay_s.at[k, slot],
            self.rs.at[seq * self.n + block], self.places[k],
        )

    def send(self, k, src):
        direct = jnp.logical_not(self.mine[k])
        if self.relayed is not None:
            for slot, by_relay in enumerate(self.indirect(k)[0]):
                direct = direct & jnp.logical_not(by_relay)

                @pl.when(by_relay)
                def _(slot=slot):
                    self.aside(k, slot, src).start()

        @pl.when(direct)
        def _():
            self.copy(k, src).start()

        @pl.when(self.mine[k])
        def _():
            pltpu.make_async_copy(src, self.slot(self.s, self.b), self.own).start()

    def relay(self, k):
        for slot, here in enumerate(self.indirect(k)[1]):

            @pl.when(here)
            def _(slot=slot):
                place = self.relayed.at[k, slot]
                remote(
                    place, place, self.relay_s.at[k, slot], self.relay_r.at[k, slot], (0, 0)
                ).wait_recv()
                self.pass_copy(k, slot).start()

    def collect(self):
        place = self.slot(self.s, self.b)
        pltpu.make_async_copy(place, place, self.own).wait()

        @pl.loop(1, SEQ * self.n)
        def _(k):
            other = (self.me + k) % (SEQ * self.n)
            place = self.slot(other // self.n, other % self.n)
            remote(place, place, self.ss.at[0], self.rs.at[other], (0, 0)).wait_recv()

    def finish(self, k, src):
        @pl.when(jnp.logical_not(self.mine[k]))
        def _():
            self.copy(k, src).wait_send()

        if self.relayed is not None:

            for slot, here in enumerate(self.indirect(k)[1]):

                @pl.when(here)
                def _(slot=slot):
                    self.pass_copy(k, slot).wait_send()


class Muon:
    peers = ("all",)

    def __init__(self, n, attn_piece, wide_piece=None, wide_in=None):
        self.n = n
        self.ready = wide_in is not None
        self.ins = [attn_piece, wide_in if self.ready else wide_piece]
        width = self.ins[1].shape[-1]
        size = wide_in.shape[1] if self.ready else n * wide_piece.shape[1]
        rows = size // n
        attn_shape = attn_piece.shape[1:]
        self.outs = [
            jax.ShapeDtypeStruct((SEQ, 4) + attn_shape, BF16),
            jax.ShapeDtypeStruct((SEQ, 2, rows, width), BF16),
        ]
        dma = pltpu.SemaphoreType.DMA
        self.scratch = [
            pltpu.VMEM((SEQ, n) + attn_shape, BF16),
            pltpu.VMEM((SEQ, size, width), BF16),
            pltpu.VMEM((2, n // 2, rows, width), BF16),
            pltpu.VMEM((size, SEQ * size), F32),
            pltpu.VMEM((size, SEQ * size), BF16),
            pltpu.VMEM((size, size), F32),
            pltpu.VMEM((size, size), BF16),
            pltpu.VMEM((size, size), BF16),
            pltpu.VMEM((size, 1), F32),
            pltpu.VMEM((1, 1), F32),
            dma((SEQ * n,)),
            dma((6,)),
            dma((2, n // 2)),
            dma((2, n // 2)),
            dma((6, 3)),
            dma((6, 3)),
            dma,
            dma((SEQ,)),
        ]
        self.scratch += OwnerMail.scratch(n, 4)
        if not self.ready:
            self.scratch += OwnerMail.scratch(n, 2) + [pltpu.VMEM((SEQ, size, width), BF16)]

    def run(
        self, attn, wide, attn_orth, wide_orth, attn_in, wide_out, relayed, x32, xlow, gram, gram_low, poly, diag,
        norm, back_s, back_r, relay_s, relay_r, seq_s, seq_r, own, loads, *mails,
    ):
        n = self.n
        b, s, hi, lo, m = coords(n)
        far, near = (s + 2) % 4, s + 1 - 2 * (s % 2)
        me = s * n + b
        size = x32.shape[0]
        width = wide.shape[-1]
        quarter = width // SEQ
        places = owner_list(n)
        attn_mail = OwnerMail(n, places[:4], attn_in, *mails[:3])
        wide_in = wide
        if not self.ready:
            wide_in = mails[6]
            wide_mail = OwnerMail(n, places[4:], wide_in, *mails[3:6])
        mine = [(b == ob) & (s == os) for ob, os in places]
        number = jnp.int32(0)
        for k in range(6):
            number = jnp.where(mine[k], jnp.int32(k), number)
        is_attn = mine[0] | mine[1] | mine[2] | mine[3]
        is_wide = mine[4] | mine[5]

        if not self.ready:
            for k in range(2):
                wide_mail.send(k, wide.at[k])
        def send_attn():
            for k in range(4):
                attn_mail.send(k, attn.at[k])

        if self.ready:
            self.send_attn = send_attn
        else:
            send_attn()

        if not self.ready:
            for _ in range(4):
                yield


        def result(k):
            return attn_orth.at[s, k] if k < 4 else wide_orth.at[s, k - 4]

        def others(act):
            @pl.loop(1, SEQ * n)
            def _(k):
                other = (me + 9 * k) % (SEQ * n)
                act(other, other % n, other // n)

        def give_attn():
            pltpu.make_async_copy(attn_in.at[s, b], attn_orth.at[s, number], own).start()

            def act(other, ob, os):
                remote(
                    attn_in.at[os, ob], attn_orth.at[os, number], back_s.at[other], back_r.at[number], (ob, os)
                ).start()

            others(act)

        piece = OwnerMail(n, places, wide_out, None, None, None).slot

        def give_wide(piece):
            index = number - 4
            pltpu.make_async_copy(piece(s, b), wide_orth.at[s, index], own).start()

            def act(other, ob, os):
                oh, ol = ob // 2, ob % 2
                up = hi < m // 2
                away = jnp.where(up, oh - hi, hi - oh)
                relay = (away > 0) & (os // 2 != s // 2)
                stop = jnp.where(ol == lo, os, (os + 2) % 4)
                src = piece(os, ob)

                @pl.when(relay)
                def _():
                    slot = jnp.maximum(away - 1, 0)
                    remote(
                        src, relayed.at[index, slot], back_s.at[other], relay_r.at[index, slot],
                        (hi * 2 + ol, stop),
                    ).start()

                @pl.when(jnp.logical_not(relay))
                def _():
                    remote(
                        src, wide_orth.at[os, index], back_s.at[other], back_r.at[number], (ob, os)
                    ).start()

            others(act)

        def prepare():
            @pl.when(is_wide)
            def _():
                if not self.ready:
                    wide_mail.collect()
                if width != size:
                    xlow[...] = jnp.zeros(xlow.shape, BF16)

            @pl.when(mine[4])
            def _():
                copies = [
                    pltpu.make_async_copy(
                        wide_in.at[k], xlow.at[:, pl.ds(k * size, width)], loads.at[k]
                    )
                    for k in range(SEQ)
                ]
                for c in copies:
                    c.start()
                for c in copies:
                    c.wait()

            @pl.when(mine[5])
            def _():
                copies = [
                    pltpu.make_async_copy(wide_in.at[k], wide_out.at[k], loads.at[k]) for k in range(SEQ)
                ]
                for c in copies:
                    c.start()
                for k, c in enumerate(copies):
                    c.wait()
                    xlow[:width, k * size : (k + 1) * size] = wide_out[k].T

        def attn_turn():
            @pl.when(is_attn)
            def _():
                attn_mail.collect()
                span = SEQ * quarter
                short, line = attn_in.shape[2:]
                whole = [attn_in[k].reshape(n * short, line) for k in range(SEQ)]
                for k in range(line // quarter):
                    block = [a[:, k * quarter : (k + 1) * quarter] for a in whole]
                    xlow[k * n * short : (k + 1) * n * short, :span] = jnp.concatenate(block, axis=1)
                square_x, square_low = x32.at[:, pl.ds(0, span)], xlow.at[:, pl.ds(0, span)]

                def turn(first):
                    schulz_poly(square_low, gram, gram_low, poly, diag, norm, first)
                    schulz_move(square_x, square_low, poly, diag, norm, first)

                turn(True)

                @pl.loop(1, NS)
                def _(k):
                    turn(False)

                for k in range(SEQ):
                    block = xlow[:, k * quarter : (k + 1) * quarter]
                    if line > quarter:
                        block = fold(block)
                    attn_in[k] = block.reshape(attn_in.shape[1:])
                give_attn()

        if not self.ready:
            prepare()
        else:
            self.prepare, self.attn_turn = prepare, attn_turn
            yield

        for turn in range(NS):

            @pl.when(is_wide)
            def _(turn=turn):
                schulz_poly(xlow, gram, gram_low, poly, diag, norm, turn == 0)

            yield

            @pl.when(is_wide)
            def _(turn=turn):
                schulz_move(x32, xlow, poly, diag, norm, turn == 0)

            yield

        @pl.when(is_wide)
        def _():
            @pl.when(mine[4])
            def _():
                rows = size // n

                def part(seq, block):
                    return xlow.at[
                        pl.ds(pl.multiple_of(block * rows, rows), rows),
                        pl.ds(pl.multiple_of(seq * size, 128), width),
                    ]

                give_wide(part)

            @pl.when(mine[5])
            def _():
                for k in range(SEQ):
                    wide_out[k] = xlow[:width, k * size : (k + 1) * size].T
                give_wide(piece)

        def routes(k):
            ob, os = places[k]
            oh, ol = ob // 2, ob % 2
            same_x = s // 2 == os // 2
            here = (hi == oh) & (((lo == ol) & jnp.logical_not(same_x)) | ((lo != ol) & same_x))
            target = jnp.where(lo == ol, s, far)
            ahead = range(oh + 1, m) if oh < m // 2 else range(oh - 1, -1, -1)
            return here, target, list(enumerate(ahead))

        def relay_copy(k, slot, block, target):
            return remote(
                relayed.at[k - 4, slot], wide_orth.at[target, k - 4], relay_s.at[k - 4, slot], back_r.at[k],
                (block * 2 + lo, target),
            )

        def onward(k, step, source, target):
            out = attn_orth.at[source, k] if k < 4 else wide_orth.at[source, k - 4]
            return remote(out, out, seq_s.at[k, step], seq_r.at[k, step], (b, target))

        if not self.ready:
            attn_turn()
        done = (0, 1, 2, 3, 4, 5)

        def returned(k):
            @pl.when(jnp.logical_not(mine[k]))
            def _():
                remote(result(k), result(k), seq_s.at[k, 0], back_r.at[k], (0, 0)).wait_recv()

            @pl.when(mine[k])
            def _():
                pltpu.make_async_copy(result(k), result(k), own).wait()

            onward(k, 0, s, far).start()
            onward(k, 1, s, near).start()

        def passed(k):
            onward(k, 0, far, far).wait_recv()
            onward(k, 2, far, near).start()

        for k in (4, 5):
            here, target, ahead = routes(k)

            @pl.when(here)
            def _(k=k, target=target, ahead=ahead):
                for slot, block in ahead:
                    place = relayed.at[k - 4, slot]
                    remote(place, place, relay_s.at[0, 0], relay_r.at[k - 4, slot], (0, 0)).wait_recv()
                    relay_copy(k, slot, block, target).start()

        for k in done[:4]:
            returned(k)
        for k in done[4:]:
            returned(k)
        for k in done:
            passed(k)
        for k in done:
            onward(k, 1, near, near).wait_recv()
            onward(k, 2, (near + 2) % 4, near).wait_recv()
            onward(k, 0, s, far).wait_send()
            onward(k, 1, s, near).wait_send()
            onward(k, 2, far, near).wait_send()
        for k in range(4):
            attn_mail.finish(k, attn.at[k])
        if not self.ready:
            for k in range(2):
                wide_mail.finish(k, wide.at[k])
        for k in (4, 5):
            here, target, ahead = routes(k)

            @pl.when(here)
            def _(k=k, target=target, ahead=ahead):
                for slot, block in ahead:
                    relay_copy(k, slot, block, target).wait_send()

        def given(buf):
            def act(other, ob, os):
                place = buf.at[os, ob] if len(buf.shape) == 4 else piece(os, ob)
                remote(place, place, back_s.at[other], back_r.at[0], (0, 0)).wait_send()

            others(act)

        @pl.when(is_attn)
        def _():
            given(attn_in)

        @pl.when(is_wide)
        def _():
            given(wide_out)


def schulz_poly(xlow, gram, gram_low, poly, diag, norm, first):
    size = xlow.shape[0]
    side = 256
    tiles = [slice(k, k + side) for k in range(0, size, side)]
    eye = lax.broadcasted_iota(jnp.int32, (side, side), 0) == lax.broadcasted_iota(
        jnp.int32, (side, side), 1
    )
    for j in tiles:
        gram[j.start :, j] = contract_last(xlow[j.start :, :], xlow[j, :])
    if first:
        total = jnp.zeros((1, 1), F32)
        for j in tiles:
            total = total + jnp.sum(jnp.where(eye, gram[j, j], 0.0), keepdims=True)
        inverse = 1.0 / (jnp.sqrt(total) + tiny_norm)
        norm[...] = inverse
        for j in tiles:
            gram[j.start :, j] = gram[j.start :, j] * (inverse * inverse)
    down, along = [], []
    for j in tiles:
        block = gram[j, j]
        on_diag = jnp.where(eye, block, 0.0)
        down.append(jnp.sum(on_diag, axis=1, keepdims=True))
        along.append(jnp.sum(on_diag, axis=0, keepdims=True))
        gram_low[j, j] = jnp.where(eye, 0.0, block).astype(BF16)
        for i in tiles:
            if i.start > j.start:
                block = gram[i, j]
                gram_low[i, j] = block.astype(BF16)
                gram_low[j, i] = block.T.astype(BF16)
    for j, right in zip(tiles, along):
        square = matmul(gram_low[j.start :, :], gram_low[:, j])
        for i, left in zip(tiles, down):
            if i.start < j.start:
                continue
            part = square[i.start - j.start : i.stop - j.start]
            factor = (2.0315 * left - 4.775) + 2.0315 * right
            block = 2.0315 * part + factor * gram[i, j]
            if i == j:
                value = jnp.sum(jnp.where(eye, 2.0315 * part, 0.0), axis=1, keepdims=True)
                diag[i] = value + (3.4445 + (2.0315 * left - 4.775) * left)
                poly[i, i] = jnp.where(eye, 0.0, block).astype(BF16)
            else:
                poly[i, j] = block.astype(BF16)
                poly[j, i] = block.T.astype(BF16)


def schulz_move(x32, xlow, poly, diag, norm, first):
    wide = x32.shape[1]
    chunk = 768 if wide % 768 == 0 else 512
    for c in range(0, wide, chunk):
        part = slice(c, c + chunk)
        if first:
            moved = (diag[...] * norm[...]) * xlow[:, part].astype(F32)
            moved = moved + matmul(poly[...], xlow[:, part]) * norm[...]
        else:
            moved = diag[...] * x32[:, part] + matmul(poly[...], xlow[:, part])
        x32[:, part] = moved
        xlow[:, part] = moved.astype(BF16)


def greet_peers(n, kinds):
    b, s, hi, lo, m = coords(n)
    peers = []
    if "seq" in kinds:
        peers += [(b, (s + k) % 4) for k in (1, 2, 3)]
    if "batch" in kinds:
        peers += [(((hi + d) % m) * 2 + lo, s) for d in range(1, m)]
        peers += [(hi * 2 + 1 - lo, s)]
    return peers


def greet_signal(n, kinds):
    b, s = lax.axis_index("batch"), lax.axis_index("seq")
    barrier = pltpu.get_barrier_semaphore()
    if "all" in kinds:
        me = s * n + b

        @pl.loop(1, SEQ * n)
        def _(k):
            other = (me + k) % (SEQ * n)
            pl.semaphore_signal(
                barrier, inc=1, device_id=(other % n, other // n), device_id_type=MESH
            )

        return
    for peer in greet_peers(n, kinds):
        pl.semaphore_signal(barrier, inc=1, device_id=peer, device_id_type=MESH)


def greet_wait(n, kinds):
    count = SEQ * n - 1 if "all" in kinds else len(greet_peers(n, kinds))
    pl.semaphore_wait(pltpu.get_barrier_semaphore(), count)


def greet(n, kinds):
    greet_signal(n, kinds)
    greet_wait(n, kinds)


def run_together(*live):
    live = list(live)
    while live:
        still = []
        for op in live:
            try:
                next(op)
                still.append(op)
            except StopIteration:
                pass
        live = still


def exchange(n, collective_id, name, *ops):
    ins = [a for op in ops for a in op.ins]
    outs = [o for op in ops for o in op.outs]
    scratch = [c for op in ops for c in op.scratch]
    kinds = {k for op in ops for k in op.peers}

    def kernel(*refs):
        in_refs, out_refs = refs[: len(ins)], refs[len(ins) : len(ins) + len(outs)]
        scratch_refs = refs[len(ins) + len(outs) :]
        greet(n, kinds)
        live = []
        i = o = c = 0
        for op in ops:
            ni, no, nc = len(op.ins), len(op.outs), len(op.scratch)
            live.append(
                op.run(*in_refs[i : i + ni], *out_refs[o : o + no], *scratch_refs[c : c + nc])
            )
            i, o, c = i + ni, o + no, c + nc
        run_together(*live)

    vmem = pl.BlockSpec(memory_space=pltpu.VMEM)
    return pl.pallas_call(
        kernel,
        out_shape=outs,
        in_specs=[vmem] * len(ins),
        out_specs=[vmem] * len(outs),
        scratch_shapes=scratch,
        compiler_params=pltpu.CompilerParams(
            collective_id=collective_id, has_side_effects=True, vmem_limit_bytes=60 * 2**20
        ),
        name=name,
    )(*ins)


def contract_last(left, right):
    return lax.dot_general(left, right, (((1,), (1,)), ((), ())), preferred_element_type=F32)


def contract_first(left, right):
    return lax.dot_general(left, right, (((0,), (0,)), ((), ())), preferred_element_type=F32)


def matmul(left, right):
    return jnp.dot(left, right, preferred_element_type=F32)


def exact_gelu(value_in):
    return jax.nn.gelu(value_in, approximate=False)


def normalize(hidden, gain_row):
    row_mean = jnp.mean(hidden, axis=-1, keepdims=True)
    centred = hidden - row_mean
    spread = lax.rsqrt(jnp.mean(centred * centred, axis=-1, keepdims=True) + norm_eps)
    scaled = centred * spread
    return (scaled * gain_row, scaled, spread)


def normalize_back(grad_in, scaled, spread, gain_row):
    weighted = grad_in * gain_row
    mean_first = jnp.mean(weighted, axis=-1, keepdims=True)
    second = jnp.mean(weighted * scaled, axis=-1, keepdims=True)
    return (
        spread * (weighted - mean_first - scaled * second),
        jnp.sum(grad_in * scaled, axis=0),
        jnp.sum(grad_in, axis=0),
    )


class RowGather:
    @staticmethod
    def scratch():
        return [pltpu.SemaphoreType.DMA((2, 3)), pltpu.SemaphoreType.DMA((2, 3))]

    def __init__(self, buf, ss, rs):
        self.buf, self.ss, self.rs = buf, ss, rs
        self.b, self.s = lax.axis_index("batch"), lax.axis_index("seq")
        self.far, self.near = (self.s + 2) % 4, self.s + 1 - 2 * (self.s % 2)
        self.diag = (self.near + 2) % 4

    def copy(self, r, step, block, device):
        place = self.buf.at[r, block]
        return remote(place, place, self.ss.at[r, step], self.rs.at[r, step], (self.b, device))

    def start(self, r):
        self.copy(r, 0, self.s, self.far).start()
        self.copy(r, 1, self.s, self.near).start()

    def wait_near(self, r):
        self.copy(r, 1, self.near, self.near).wait_recv()

    def pass_far(self, r):
        self.copy(r, 0, self.far, self.far).wait_recv()
        self.copy(r, 2, self.far, self.near).start()

    def wait_diag(self, r):
        self.copy(r, 2, self.diag, self.near).wait_recv()

    def finish(self, r):
        self.copy(r, 0, self.s, self.far).wait_send()
        self.copy(r, 1, self.s, self.near).wait_send()
        self.copy(r, 2, self.far, self.near).wait_send()


def gelu_parts(value):
    cdf = 0.5 * (1.0 + lax.erf(value * math.sqrt(0.5)))
    density = jnp.exp(-0.5 * value * value) * (1.0 / math.sqrt(2.0 * math.pi))
    return value * cdf, cdf + value * density


def row_sum(value):
    return jnp.sum(value, axis=0, keepdims=True)


class RowSwap:
    @staticmethod
    def scratch(shape):
        return [
            pltpu.VMEM(shape, BF16),
            pltpu.VMEM(shape, BF16),
            pltpu.SemaphoreType.DMA((2, 4)),
            pltpu.SemaphoreType.DMA((2, 4)),
        ]

    def __init__(self, src, dst, ss, rs):
        self.src, self.dst, self.ss, self.rs = src, dst, ss, rs
        self.b, self.s = lax.axis_index("batch"), lax.axis_index("seq")

    def copy(self, r, k):
        other = (self.s + k) % 4
        return remote(
            self.src.at[other, r], self.dst.at[self.s, r], self.ss.at[r, k], self.rs.at[r, k],
            (self.b, other),
        )

    def start(self, r):
        for k in (2, 3, 1):
            self.copy(r, k).start()
        self.dst[self.s, r] = self.src[self.s, r]

    def wait(self, r):
        for k in (2, 3, 1):
            self.copy(r, k).wait_recv()

    def finish(self, r):
        for k in (2, 3, 1):
            self.copy(r, k).wait_send()


def fold(value):
    half = value.shape[0] // 2
    return jnp.concatenate([value[:half], value[half:]], axis=1)


def unfold(value):
    half = value.shape[1] // 2
    return jnp.concatenate([value[:, :half], value[:, half:]], axis=0)


def rounds(count):
    for _ in range(count):
        yield


def spaced(op, count):
    for _ in op:
        yield from rounds(count)


def step(op):
    try:
        next(op)
    except StopIteration:
        pass


def drain(op):
    for _ in op:
        pass


class DirectSum:
    peers = ("all",)

    def __init__(self, n, src):
        self.n = n
        self.scratch = [pltpu.VMEM(src.shape, F32)] + [pltpu.SemaphoreType.DMA((n,))] * 2

    def run(self, src, dst, arrived, ss, rs):
        n = self.n
        b, s = lax.axis_index("batch"), lax.axis_index("seq")
        copies = []
        for k in range(1, n):
            to = (b + k) % n
            copies.append(remote(src.at[to], arrived.at[k], ss.at[k], rs.at[k], (to, s)))
            copies[-1].start()
        yield
        total = src[b]
        for k, c in enumerate(copies):
            c.wait()
            total = total + arrived[k + 1]
        dst[...] = total


class BatchSum:
    peers = ("batch",)

    def __init__(self, n, src):
        self.n = n
        self.ins = [src]
        shape = src.shape[1:]
        self.outs = [jax.ShapeDtypeStruct(shape, F32)]
        m = n // 2
        self.scratch = [pltpu.VMEM((m,) + shape, BF16)] * 3 + [pltpu.SemaphoreType.DMA((m,))] * 4

    def run(self, src, dst, yrecv, zsend, zrecv, ys, yr, zs, zr):
        b, s, hi, lo, m = coords(self.n)
        pair = (hi * 2 + 1 - lo, s)
        first = {}
        for d in list(range(1, m)) + [0]:
            block = ((hi + d) % m) * 2 + 1 - lo
            first[d] = remote(src.at[block], yrecv.at[d], ys.at[d], yr.at[d], pair)
            first[d].start()
        yield
        second = []
        for d in range(1, m):
            h = (hi + d) % m
            first[d].wait_recv()
            zsend[d] = (src[h * 2 + lo].astype(F32) + yrecv[d].astype(F32)).astype(BF16)
            c = remote(zsend.at[d], zrecv.at[d], zs.at[d], zr.at[d], (h * 2 + lo, s))
            c.start()
            second.append(c)
            yield
        first[0].wait_recv()
        total = src[b].astype(F32) + yrecv[0].astype(F32)
        for d in range(1, m):
            second[d - 1].wait_recv()
            total = total + zrecv[d].astype(F32)
        dst[...] = total
        for c in list(first.values()) + second:
            c.wait_send()


class RowSum:
    @staticmethod
    def scratch(rows, shape):
        return [
            pltpu.VMEM((rows, 2) + shape, BF16),
            pltpu.VMEM((rows,) + shape, BF16),
            pltpu.VMEM((rows,) + shape, BF16),
            pltpu.SemaphoreType.DMA((rows, 3)),
            pltpu.SemaphoreType.DMA((rows, 3)),
        ]

    def __init__(self, src, near_in, far_out, far_in, ss, rs):
        self.src, self.near_in, self.far_out, self.far_in, self.ss, self.rs = (
            src, near_in, far_out, far_in, ss, rs,
        )
        self.b, self.s = lax.axis_index("batch"), lax.axis_index("seq")
        self.far, self.near = (self.s + 2) % 4, self.s + 1 - 2 * (self.s % 2)
        self.diag = (self.near + 2) % 4

    def beside(self, r, k):
        block = self.diag if k else self.near
        return remote(
            self.src.at[r, block], self.near_in.at[r, k], self.ss.at[r, k], self.rs.at[r, k],
            (self.b, self.near),
        )

    def across(self, r):
        return remote(
            self.far_out.at[r], self.far_in.at[r], self.ss.at[r, 2], self.rs.at[r, 2],
            (self.b, self.far),
        )

    def send_near(self, r):
        self.beside(r, 0).start()

    def send_diag(self, r):
        self.beside(r, 1).start()

    def cross(self, r):
        self.beside(r, 1).wait_recv()
        part = self.src[r, self.far].astype(F32) + self.near_in[r, 1].astype(F32)
        self.far_out[r] = part.astype(BF16)
        self.across(r).start()

    def total(self, r):
        self.beside(r, 0).wait_recv()
        part = self.src[r, self.s].astype(F32) + self.near_in[r, 0].astype(F32)
        self.across(r).wait_recv()
        return part + self.far_in[r].astype(F32)

    def finish(self, r):
        self.beside(r, 0).wait_send()
        self.beside(r, 1).wait_send()
        self.across(r).wait_send()


class Scratch:
    def __init__(self):
        self.names, self.shapes = [], []

    def add(self, **named):
        for name, shapes in named.items():
            one = not isinstance(shapes, list)
            shapes = [shapes] if one else shapes
            self.names.append((name, len(shapes), one))
            self.shapes += shapes

    def refs(self, refs):
        out, i = types.SimpleNamespace(), 0
        for name, count, one in self.names:
            setattr(out, name, refs[i] if one else refs[i : i + count])
            i += count
        return out


def layer(
    n, tokens, attn_weight, up_weight, down_weight, vec_own, pool_own, lengths, out_grad, up_moment, down_moment
):
    rows, span, width = tokens.shape
    quarter = width // SEQ
    span_all = span * SEQ
    own_rows = width // n
    local = rows * span
    aligned = own_rows % 16 == 0
    scale = HD**-0.5
    shape = jax.ShapeDtypeStruct
    full = (rows, SEQ, span, width)
    widths = (3 * quarter, quarter, width, width)
    low_ops = [GatherBatch(n, shape((own_rows, c), BF16), k < 2) for k, c in enumerate(widths)]
    low_ops = low_ops if aligned else []
    vec_op = GatherDirect(n, vec_own) if aligned else GatherBatch(n, vec_own)
    pool_op = GatherSeq(n, pool_own)
    out_op = GatherSeq(n, shape((width, quarter), BF16))
    sum_ops = [BatchSum(n, shape((n, own_rows, width), BF16)) for _ in range(2)]

    outs = [
        shape((rows, span, width), F32),
        shape((rows, width), F32),
        shape((rows, span, width), F32),
        shape((8, width), F32),
        shape((1, 3 * quarter), F32),
        shape(full, BF16),
    ]
    vmem = pl.BlockSpec(memory_space=pltpu.VMEM)
    anywhere = pl.BlockSpec(memory_space=pl.ANY)
    if aligned:
        outs += [shape((n, own_rows, width), BF16)]
        outs += [shape((2, own_rows, width), BF16), shape((SEQ, width, width), BF16)]
        out_specs = [anywhere, vmem, anywhere, vmem, vmem, anywhere, anywhere, vmem, anywhere]
    else:
        outs += [shape((width, width), BF16)] * 3
        out_specs = [vmem] * 9

    dma = pltpu.SemaphoreType.DMA
    sc = Scratch()
    if aligned:
        sc.add(
            lows=[pltpu.VMEM((own_rows, c), BF16) for c in widths],
            weights=[pltpu.VMEM(op.outs[0].shape, BF16) for op in low_ops],
            low_moves=[c for op in low_ops for c in op.scratch],
        )
    sc.add(vec_parts=pltpu.VMEM(vec_op.outs[0].shape, F32))
    sc.add(vec_move=vec_op.scratch)
    sc.add(vec=pltpu.VMEM((8, width), F32))
    sc.add(pool_parts=pltpu.VMEM(pool_op.outs[0].shape, F32))
    sc.add(pool_move=pool_op.scratch)
    sc.add(out_own=pltpu.VMEM((width, quarter), BF16))
    sc.add(out_parts=pltpu.VMEM((SEQ, width, quarter), BF16))
    sc.add(out_move=out_op.scratch)
    sc.add(w_out=pltpu.VMEM((width, width), BF16))
    sc.add(x_all=pltpu.VMEM(full, BF16))
    sc.add(x_gather=RowGather.scratch())
    sc.add(qkv=pltpu.VMEM((rows, span_all, 3 * quarter), BF16))
    sc.add(prob=pltpu.VMEM((rows, HEADS, span_all, span_all), F32))
    sc.add(swap=RowSwap.scratch((SEQ, rows, span, quarter)))
    sc.add(back_swap=RowSwap.scratch((SEQ, rows, span, quarter)))
    sc.add(context=pltpu.VMEM((rows, span, width), BF16))
    sc.add(normed=pltpu.VMEM((rows, span, width), F32))
    sc.add(scaled_one=pltpu.VMEM((rows, span, width), F32))
    sc.add(spread_one=pltpu.VMEM((rows, span, 1), F32))
    sc.add(y_all=pltpu.VMEM(full, BF16))
    sc.add(y_gather=RowGather.scratch())
    sc.add(slope=pltpu.VMEM(full, F32))
    sc.add(act=pltpu.VMEM(full, BF16))
    sc.add(z_sum=RowSum.scratch(rows, (span, width)))
    sc.add(dz_all=pltpu.VMEM(full, BF16))
    sc.add(dz_gather=RowGather.scratch())
    sc.add(du_all=pltpu.VMEM(full, BF16))
    sc.add(dy_sum=RowSum.scratch(rows, (span, width)))
    sc.add(pool_buf=pltpu.VMEM((SEQ, rows, width), F32))
    sc.add(pool_sems=[dma((3,)), dma((3,))])
    sc.add(a_quarters=pltpu.VMEM((SEQ, local, quarter), BF16))
    sc.add(out_part=pltpu.VMEM((1, SEQ, width, quarter), BF16))
    sc.add(out_sum=RowSum.scratch(1, (width, quarter)))
    if not aligned:
        sc.add(x_sum=RowSum.scratch(rows, (span, width)))
    sc.add(grad_qkv=pltpu.VMEM((rows, span_all, 3 * quarter), BF16))
    if aligned:
        sc.add(early=[pltpu.VMEM(outs[k].shape, outs[k].dtype) for k in (0, 2, 5, 6)])
        sc.add(early_sems=dma((4,)))
        sc.add(raw=dma((2 * SEQ + 1,)))
        sc.add(
            down_grad=pltpu.VMEM((n, own_rows, width), BF16),
            up_grad=pltpu.VMEM((n, own_rows, width), BF16),
            down_piece=pltpu.VMEM((own_rows, width), F32),
            up_piece=pltpu.VMEM((own_rows, width), F32),
            down_sum=sum_ops[0].scratch,
            up_sum=sum_ops[1].scratch,
        )
        sc.add(vec_low=pltpu.VMEM(vec_own.shape, F32))
        sc.add(wide_send=pltpu.VMEM((2, own_rows, width), BF16))
        sc.add(mail=OwnerMail.scratch(n, 2, (own_rows, width)))

    def kernel(
        tokens, attn_weight, up_weight, down_weight, vec_own, pool_own, lengths, out_grad, up_moment, down_moment,
        out_rows, pooled, second, vec_grad, bias_sums, part, grad_attn, *rest,
    ):
        if aligned:
            wide_bf, wide_in = rest[:2]
            rest = rest[2:]
        else:
            grad_up_out, grad_down_out = rest[:2]
            rest = rest[2:]
        at = sc.refs(rest)
        if aligned:
            leaving = [
                pltpu.make_async_copy(a, b, at.early_sems.at[k])
                for k, (a, b) in enumerate(zip(at.early, (out_rows, second, part, grad_attn)))
            ]
            out_rows, second, part, grad_attn = at.early
        kinds = {"all"} if aligned else {"seq", "batch"}
        greet_signal(n, kinds)
        b, s = lax.axis_index("batch"), lax.axis_index("seq")
        x_all, y_all, dz_all, du_all = at.x_all, at.y_all, at.dz_all, at.du_all
        slope, act, prob, qkv = at.slope, at.act, at.prob, at.qkv
        normed, context, vec = at.normed, at.context, at.vec
        x_gather = RowGather(x_all, *at.x_gather)
        y_gather = RowGather(y_all, *at.y_gather)
        dz_gather = RowGather(dz_all, *at.dz_gather)
        swap, back_swap = RowSwap(*at.swap), RowSwap(*at.back_swap)
        z_sum, dy_sum = [RowSum(part, *refs) for refs in (at.z_sum, at.dy_sum)]
        out_sum = RowSum(at.out_part, *at.out_sum)
        far, near, diag = x_gather.far, x_gather.near, x_gather.diag

        def raw_block(k):
            return slope.at[k // SEQ, k % SEQ, pl.ds(0, own_rows)]

        def load_up(matrix):
            return [
                pltpu.make_async_copy(
                    matrix.at[:, pl.ds(k * width, width)], raw_block(SEQ + k), at.raw.at[SEQ + k]
                )
                for k in range(SEQ)
            ]

        def load_down(matrix, place):
            return pltpu.make_async_copy(
                matrix.at[pl.ds(s * own_rows, own_rows)], place, at.raw.at[2 * SEQ]
            )

        def raw_up(k):
            whole = jnp.concatenate([raw_block(SEQ + j)[...] for j in range(SEQ)], axis=1)
            return take_up(whole, n, k)

        if aligned:
            raws = [
                pltpu.make_async_copy(attn_weight.at[k], raw_block(k), at.raw.at[k]) for k in range(4)
            ]
            raws += load_up(up_weight)
            raws.append(load_down(down_weight, second.at[0, pl.ds(0, own_rows)]))
            for c in raws:
                c.start()
        for r in range(rows):
            x_all[r, s] = tokens[r].astype(BF16)
        if aligned:
            for c in raws[:4]:
                c.wait()
            for k in range(SEQ):

                @pl.when(s == k)
                def _(k=k):
                    block = [raw_block(j)[:, k * quarter : (k + 1) * quarter] for j in range(4)]
                    at.lows[0][...] = jnp.concatenate(block[:3], axis=1).astype(BF16)
                    at.lows[1][...] = block[3].astype(BF16)

            vec_low = at.vec_low
            vec_low[...] = vec_own[...].astype(BF16).astype(F32)
        else:
            vec_low = vec_own

        greet_wait(n, kinds)
        vec_move = vec_op.run(vec_low, at.vec_parts, *at.vec_move)
        pool_move = pool_op.run(pool_own, at.pool_parts, *at.pool_move)
        step(vec_move)
        if aligned:
            moves = [
                op.run(at.lows[k], at.weights[k], *at.low_moves[5 * k : 5 * k + 5])
                for k, op in enumerate(low_ops)
            ]
            step(moves[0])
        step(pool_move)
        for r in range(rows):
            x_gather.start(r)
        if aligned:
            for c in raws[4:]:
                c.wait()
            for k in range(SEQ):

                @pl.when(s == k)
                def _(k=k):
                    at.lows[2][...] = raw_up(k).astype(BF16)

            at.lows[3][...] = second[0, :own_rows].astype(BF16)
            step(moves[0])
        x_gather.pass_far(0)
        if aligned:
            step(moves[0])
        step(pool_move)
        x_gather.pass_far(1)
        if aligned:
            step(moves[0])
            step(moves[1])
            step(moves[2])
        drain(vec_move)
        drain(pool_move)
        if aligned:
            whole = jnp.concatenate([at.vec_parts[k] for k in range(n)], axis=1)

            def here(make):
                return sum(jnp.where(s == k, make(k), 0.0) for k in range(SEQ))

            vec[0:6] = whole[2:8]
            vec[6:7] = here(
                lambda k: jnp.concatenate(
                    [
                        whole[8 + f // width : 9 + f // width, f % width : f % width + own_rows]
                        for f in ((j * SEQ + k) * own_rows for j in range(n))
                    ],
                    axis=1,
                )
            )
            blank = jnp.zeros((1, quarter), F32)
            vec[7:8] = here(
                lambda k: jnp.concatenate(
                    [
                        whole[0:1, k * quarter : (k + 1) * quarter],
                        blank,
                        whole[1:2, k * quarter : (k + 1) * quarter],
                        blank,
                    ],
                    axis=1,
                )
            )
        else:
            total = at.vec_parts[0]
            for k in range(1, n):
                total = total + at.vec_parts[k]
            vec[...] = total
        pool_whole = jnp.concatenate([at.pool_parts[k] for k in range(SEQ)], axis=1)

        if aligned:
            drain(moves[0])
            step(moves[1])
            step(moves[2])
            step(moves[3])

        def w_qkv():
            if aligned:
                return at.weights[0][...].reshape(width, 3 * quarter)
            return attn_weight[:, : 3 * quarter]

        def w_up():
            return at.weights[2][...].reshape(width, width) if aligned else up_weight[...]

        def w_down():
            return at.weights[3][...].reshape(width, width) if aligned else down_weight[...]

        out_move = out_op.run(at.out_own, at.out_parts, *at.out_move)

        def begin_out():
            if aligned:
                drain(moves[1])
                at.out_own[...] = at.weights[1][...].reshape(width, quarter)
            else:
                at.out_own[...] = attn_weight[:, 3 * quarter :]
            step(out_move)

        def turn(*ks):
            for k in ks:
                if aligned:
                    step(moves[k])

        bias = vec[7:8, : 3 * quarter]
        column = lax.broadcasted_iota(jnp.int32, (1, span_all), 1)

        def heads(r, h):
            return [
                qkv[r, :, k * quarter + h * HD : k * quarter + (h + 1) * HD] for k in range(3)
            ]

        for r in range(rows):
            x_gather.wait_near(r)
            x_gather.wait_diag(r)
            block = matmul(x_all[r].reshape(span_all, width), w_qkv()) + bias
            qkv[r] = block.astype(BF16)
            valid = column < lengths[r]
            if r == 0:
                turn(1)
            mixed = []
            for h in range(HEADS):
                query, key, value = heads(r, h)
                scores = contract_last(query * jnp.bfloat16(scale), key)
                scores = jnp.where(valid, scores, -1e30)
                exponent = jnp.exp(scores - jnp.max(scores, axis=-1, keepdims=True))
                weight = exponent * (1.0 / jnp.sum(exponent, axis=-1, keepdims=True))
                prob[r, h] = weight
                mixed.append(matmul(weight.astype(BF16), value))
                if r == 0 and h == 0:
                    turn(1, 3, 2)
                if r == 0 and h == 1:
                    begin_out()
                    turn(2)
                if r == 0 and h == 2:
                    turn(2)
                if r == 1:
                    turn(3)
            mixed = jnp.concatenate(mixed, axis=1).astype(BF16)
            for k in range(SEQ):
                at.swap[0][k, r] = mixed[k * span : (k + 1) * span]
            swap.start(r)
        step(out_move)
        drain(out_move)
        w_out = at.w_out
        w_out[...] = jnp.concatenate([at.out_parts[k] for k in range(SEQ)], axis=1)
        gain_one, shift_one = vec[1:2], vec[2:3]
        for r in range(rows):
            swap.wait(r)
            context[r] = jnp.concatenate([at.swap[1][k, r] for k in range(SEQ)], axis=1)
            hidden = tokens[r] + (matmul(context[r], w_out[...]) + vec[0:1])
            centred = hidden - jnp.mean(hidden, axis=-1, keepdims=True)
            spread = lax.rsqrt(jnp.mean(centred * centred, axis=-1, keepdims=True) + norm_eps)
            scaled = centred * spread
            at.scaled_one[r] = scaled
            at.spread_one[r] = spread
            value = scaled * gain_one + shift_one
            normed[r] = value
            y_all[r, s] = value.astype(BF16)
            y_gather.start(r)

        if aligned:
            drain(moves[2])
        gain_two, shift_two = vec[3:4], vec[4:5]
        bias_down, bias_up = vec[5:6], vec[6:7]

        def pair(ref, blocks):
            return jnp.concatenate([ref[i] for i in blocks], axis=0)

        def put(ref, blocks, value):
            for k, i in enumerate(blocks):
                ref[i] = value[k * span : (k + 1) * span].astype(ref.dtype)

        def rise(blocks):
            value, rate = gelu_parts(matmul(pair(y_all, blocks), w_up()) + bias_up)
            put(act, blocks, value)
            put(slope, blocks, rate)

        def fall(blocks):
            put(part, blocks, matmul(pair(act, blocks), w_down()))

        mine, beside = [[(r, k) for r in range(rows)] for k in (s, near)]
        rise(mine)
        for r in range(rows):
            y_gather.wait_near(r)
        rise(beside)
        if aligned:
            drain(moves[3])
        fall(beside)
        for r in range(rows):
            z_sum.send_near(r)
        for r in range(rows):
            y_gather.pass_far(r)
            y_gather.wait_diag(r)
            rise([(r, diag), (r, far)])
            fall([(r, diag), (r, far)])
            z_sum.send_diag(r)
            if r == 0:
                fall(mine)
            z_sum.cross(r)

        position = s * span + lax.broadcasted_iota(jnp.int32, (span, 1), 0)
        grad_gain_two = grad_shift_two = grad_bias_down = jnp.zeros((1, width), F32)
        for r in range(rows):
            hidden = normed[r] + (z_sum.total(r) + bias_down)
            centred = hidden - jnp.mean(hidden, axis=-1, keepdims=True)
            spread_two = lax.rsqrt(jnp.mean(centred * centred, axis=-1, keepdims=True) + norm_eps)
            scaled = centred * spread_two
            output = scaled * gain_two + shift_two
            out_rows[r] = output
            live = (position < lengths[r]).astype(F32)
            length = jnp.full((1, 1), lengths[r], jnp.int32).astype(F32)
            at.pool_buf[s, r : r + 1] = row_sum(output * live) / length
            upstream = live * (out_grad[r] + pool_whole[r : r + 1] / length)
            weighted = upstream * gain_two
            mean_first = jnp.mean(weighted, axis=-1, keepdims=True)
            mean_second = jnp.mean(weighted * scaled, axis=-1, keepdims=True)
            grad = spread_two * (weighted - mean_first - scaled * mean_second)
            second[r] = grad
            low = grad.astype(BF16)
            dz_all[r, s] = low
            dz_gather.start(r)
            grad_gain_two += row_sum(upstream * scaled)
            grad_shift_two += row_sum(upstream)
            grad_bias_down += row_sum(low.astype(F32))

        if aligned:
            leaving[0].start()

        def pool_copy(k, block, device):
            place = at.pool_buf.at[block]
            sems = at.pool_sems
            return remote(place, place, sems[0].at[k - 1], sems[1].at[k - 1], (b, device))

        for k in (1, 2, 3):
            pool_copy(k, s, (s + k) % 4).start()
        for r in range(rows):
            z_sum.finish(r)

        def backward(blocks):
            lift = contract_last(pair(dz_all, blocks), w_down())
            low = (lift * pair(slope, blocks)).astype(BF16)
            put(du_all, blocks, low)
            put(part, blocks, contract_last(low, w_up()))
            return row_sum(low.astype(F32))

        bias_grad = backward(mine)
        for r in range(rows):
            dz_gather.wait_near(r)
        bias_grad += backward(beside)
        for r in range(rows):
            dy_sum.send_near(r)
        for r in range(rows):
            dz_gather.pass_far(r)
            dz_gather.wait_diag(r)
            bias_grad += backward([(r, diag), (r, far)])
            dy_sum.send_diag(r)
            dy_sum.cross(r)

        flat = rows * span_all
        if aligned:
            down_move = sum_ops[0].run(at.down_grad, at.down_piece, *at.down_sum)
            up_move = sum_ops[1].run(at.up_grad, at.up_piece, *at.up_sum)
            mail = OwnerMail(n, owner_list(n)[4:], wide_in, *at.mail)
            wide_send = at.wide_send
            momenta = load_up(up_moment) + [load_down(down_moment, raw_block(0))]
            for c in momenta:
                c.start()
        whole = contract_first(act[...].reshape(flat, width), dz_all[...].reshape(flat, width))
        if aligned:
            at.down_grad[...] = whole.reshape(n, own_rows, width).astype(BF16)
            step(down_move)
        else:
            grad_down_out[...] = whole.astype(BF16)
        whole = contract_first(y_all[...].reshape(flat, width), du_all[...].reshape(flat, width))
        if aligned:
            at.up_grad[...] = whole.reshape(n, own_rows, width).astype(BF16)
            step(up_move)
        else:
            grad_up_out[...] = whole.astype(BF16)

        grad_gain_one = grad_shift_one = grad_bias_out = jnp.zeros((1, width), F32)
        for r in range(rows):
            grad = dy_sum.total(r) + second[r]
            scaled = at.scaled_one[r]
            weighted = grad * gain_one
            mean_first = jnp.mean(weighted, axis=-1, keepdims=True)
            mean_second = jnp.mean(weighted * scaled, axis=-1, keepdims=True)
            first = at.spread_one[r] * (weighted - mean_first - scaled * mean_second)
            second[r] = first
            low = first.astype(BF16)
            above = contract_last(low, w_out[...]).astype(BF16)
            for k in range(SEQ):
                columns = slice(k * quarter, (k + 1) * quarter)
                at.back_swap[0][k, r] = above[:, columns]
                at.a_quarters[k, r * span : (r + 1) * span] = low[:, columns]
            back_swap.start(r)
            grad_gain_one += row_sum(grad * scaled)
            grad_shift_one += row_sum(grad)
            grad_bias_out += row_sum(low.astype(F32))
        for k, value in enumerate(
            (
                grad_bias_out, grad_gain_one, grad_shift_one, grad_gain_two, grad_shift_two,
                grad_bias_down, bias_grad, jnp.zeros((1, width), F32),
            )
        ):
            vec_grad[k : k + 1] = value

        def new_momentum(k, piece, old):
            wide_bf[k] = piece[...].astype(BF16)
            wide_send[k] = (matrix_decay * old + wide_bf[k].astype(F32)).astype(BF16)
            mail.send(k, wide_send.at[k])

        flat_context = context[...].reshape(local, width)
        for k in range(SEQ):
            at.out_part[0, k] = contract_first(flat_context, at.a_quarters[k]).astype(BF16)
        out_sum.send_diag(0)
        out_sum.send_near(0)
        for r in range(rows):
            dy_sum.finish(r)
        sums = jnp.zeros((1, 3 * quarter), F32)
        for r in range(rows):
            back_swap.wait(r)
            arrived = jnp.concatenate([at.back_swap[1][k, r] for k in range(SEQ)], axis=0)
            query_grads, key_grads, value_grads = [], [], []
            for h in range(HEADS):
                query, key, value = heads(r, h)
                above = arrived[:, h * HD : (h + 1) * HD]
                weight = prob[r, h]
                prob_grad = contract_last(above, value)
                delta = jnp.sum(weight * prob_grad, axis=-1, keepdims=True)
                score_grad = (weight * (prob_grad - delta)).astype(BF16)
                query_grads.append(matmul(score_grad, key) * scale)
                key_grads.append(contract_first(query, score_grad) * scale)
                value_grads.append(contract_first(above, weight.astype(BF16)))
                if aligned and r == 0:
                    step(down_move)
                if r == 1 and h == 0:
                    out_sum.cross(0)
                if aligned and r == 1 and h > 0:
                    step(up_move)
                if not aligned and r > 0 and h == 2:
                    x_sum.cross(r - 1)
            turned = jnp.concatenate(key_grads + value_grads, axis=0).T
            block = jnp.concatenate(query_grads + [turned], axis=1).astype(BF16)
            at.grad_qkv[r] = block
            sums += row_sum(block.astype(F32))
            out = contract_last(block, w_qkv())
            for k in range(SEQ):
                part[r, k] = out[k * span : (k + 1) * span].astype(BF16)
            if not aligned:
                if r == 0:
                    x_sum = RowSum(part, *at.x_sum)
                x_sum.send_diag(r)
                x_sum.send_near(r)
        if aligned:
            step(up_move)
            drain(down_move)
            for c in momenta:
                c.wait()
            new_momentum(1, at.down_piece, raw_block(0)[...])
        bias_sums[...] = sums
        if aligned:
            leaving[1].start()
            leaving[2].start()
        whole = contract_first(
            x_all[...].reshape(flat, width), at.grad_qkv[...].reshape(flat, 3 * quarter)
        )
        whole = jnp.concatenate([whole, out_sum.total(0)], axis=1)
        grad_attn[...] = whole.astype(BF16).reshape(grad_attn.shape)
        if aligned:
            leaving[3].start()
        for k in (1, 2, 3):
            pool_copy(k, (s + 4 - k) % 4, (s + k) % 4).wait_recv()
        pool_buf = at.pool_buf
        pooled[...] = (pool_buf[0] + pool_buf[1]) + (pool_buf[2] + pool_buf[3])
        if aligned:
            mail.relay(1)
            drain(up_move)
            for k in range(SEQ):

                @pl.when(s == k)
                def _(k=k):
                    wide_bf[0] = at.up_piece[...].astype(BF16)
                    old = matrix_decay * raw_up(k) + wide_bf[0].astype(F32)
                    wide_send[0] = old.astype(BF16)

            mail.send(0, wide_send.at[0])
        else:
            x_sum.cross(rows - 1)
            for r in range(rows):
                second[r] = x_sum.total(r) + second[r]
                x_sum.finish(r)
        out_sum.finish(0)
        for k in (1, 2, 3):
            pool_copy(k, s, (s + k) % 4).wait_send()
        for r in range(rows):
            for op in (x_gather, swap, y_gather, dz_gather, back_swap):
                op.finish(r)
        if aligned:
            mail.relay(0)

            @pl.when(mail.mine[0] | mail.mine[1])
            def _():
                mail.collect()

            for k in range(2):
                mail.finish(k, wide_send.at[k])
            for c in leaving:
                c.wait()

    smem = pl.BlockSpec(memory_space=pltpu.SMEM)
    far_spec = anywhere if aligned else vmem
    return pl.pallas_call(
        kernel,
        out_shape=outs,
        in_specs=[vmem] + [far_spec] * 3 + [vmem] * 2 + [smem, vmem] + [anywhere] * 2,
        out_specs=out_specs,
        scratch_shapes=sc.shapes,
        compiler_params=pltpu.CompilerParams(
            collective_id=0, has_side_effects=True, vmem_limit_bytes=63 * 2**20
        ),
        name="layer",
    )(tokens, attn_weight, up_weight, down_weight, vec_own, pool_own, lengths, out_grad, up_moment, down_moment)


def join_up_parts(parts, n):
    hid_own = parts[0].shape[1] // n
    return jnp.concatenate(
        [parts[k][:, b * hid_own : (b + 1) * hid_own] for b in range(n) for k in range(SEQ)], axis=1
    )


def take_up(matrix, n, k):
    hid_own = matrix.shape[1] // n // SEQ
    return jnp.concatenate(
        [
            matrix[:, (b * SEQ + k) * hid_own : (b * SEQ + k + 1) * hid_own]
            for b in range(n)
        ],
        axis=1,
    )


def muon(n, grad_attn, wide_in, bias_sums, vec_grad, attn_moment, wide_bf, x_part, first_grad):
    rows, width = wide_bf.shape[1:]
    quarter = width // SEQ
    hid_own = rows
    n_vec = 8 + SEQ
    shape = jax.ShapeDtypeStruct
    attn_shape = (4, rows // 2, 2 * quarter)
    attn_op = GatherSeq(n, shape(attn_shape, BF16))
    attn_sum = BatchSum(n, grad_attn)
    vec_sum = DirectSum(n, shape((n, n_vec, rows), F32))
    vec_op = GatherSeq(n, shape((n_vec, rows), F32))
    wide_op = GatherSeq(n, wide_bf)
    count, span = first_grad.shape[:2]
    main = Muon(n, shape(attn_shape, BF16), wide_in=wide_in)
    outs = [attn_op.outs[0], wide_op.outs[0], shape((n_vec, rows), F32), shape(first_grad.shape, F32)]
    outs += main.outs
    groups = [
        [
            pltpu.VMEM((rows, width), F32),
            pltpu.VMEM(attn_shape, BF16),
            pltpu.VMEM(attn_shape, BF16),
            pltpu.VMEM((n, n_vec, rows), F32),
            pltpu.VMEM((n_vec, rows), F32),
            pltpu.VMEM((SEQ, n_vec, rows), F32),
        ]
    ] + [op.scratch for op in (attn_op, vec_sum, vec_op, main, attn_sum, wide_op)]
    groups.append(RowSum.scratch(count, (span, width)))
    late = (attn_moment, x_part, first_grad)
    groups.append([pltpu.VMEM(a.shape, a.dtype) for a in late] + [pltpu.SemaphoreType.DMA((3,))])

    def kernel(
        grad_attn, wide_in, bias_sums, vec_grad, attn_moment, wide_bf, x_part, first_grad,
        attn_all, wide_all, vec_total, input_grad, attn_orth, wide_orth, *rest,
    ):
        greet_signal(n, {"all"})
        parts, i = [], 0
        for group in groups:
            parts.append(rest[i : i + len(group)])
            i += len(group)
        attn_piece, attn_bf, attn_send, vec_local, vec_piece, vec_parts = parts[0]
        s = lax.axis_index("seq")
        arriving = [
            pltpu.make_async_copy(a, b, parts[8][3].at[k])
            for k, (a, b) in enumerate(zip((attn_moment, x_part, first_grad), parts[8][:3]))
        ]
        attn_moment, x_part, first_grad = parts[8][:3]
        for c in arriving:
            c.start()
        main_move = main.run(attn_send, wide_in, attn_orth, wide_orth, *parts[4])
        step(main_move)
        main.prepare()
        greet_wait(n, {"all"})
        x_sum = RowSum(x_part, *parts[7])

        def inputs():
            arriving[1].wait()
            arriving[2].wait()
            for r in range(count):
                x_sum.send_diag(r)
                x_sum.send_near(r)
            yield
            for r in range(count):
                x_sum.cross(r)
            yield from rounds(8)
            for r in range(count):
                input_grad[r] = x_sum.total(r) + first_grad[r]
                x_sum.finish(r)

        def attention():
            moving = attn_sum.run(grad_attn, attn_piece, *parts[5])
            step(moving)
            yield from rounds(3)
            for _ in range(n // 2 - 1):
                step(moving)
            yield from rounds(3)
            drain(moving)
            arriving[0].wait()
            for j in range(4):
                attn_bf[j] = fold(attn_piece[:, j * quarter : (j + 1) * quarter]).astype(BF16)
            for k in range(SEQ):

                @pl.when(s == k)
                def _(k=k):
                    for j in range(4):
                        old = fold(attn_moment[j, :, k * quarter : (k + 1) * quarter])
                        attn_send[j] = (matrix_decay * old + attn_bf[j].astype(F32)).astype(BF16)
            main.send_attn()
            yield
            main.attn_turn()
            yield from spaced(attn_op.run(attn_bf, attn_all, *parts[1]), 2)

        def vectors():
            def here(k, value):
                return jnp.where(s == k, value, 0.0)

            lines = [
                jnp.concatenate(
                    [here(k, bias_sums[:, j * quarter : (j + 1) * quarter]) for k in range(SEQ)], axis=1
                )
                for j in (0, 2)
            ]
            lines += [vec_grad[j : j + 1] for j in range(6)]
            hidden = vec_grad[6:7]
            pieces = [
                here(k, hidden[:, b * hid_own : (b + 1) * hid_own]) for b in range(n) for k in range(SEQ)
            ]
            each = n * SEQ // 4
            lines += [jnp.concatenate(pieces[j * each : (j + 1) * each], axis=1) for j in range(4)]
            whole = jnp.concatenate(lines, axis=0)
            for b in range(n):
                vec_local[b] = whole[:, b * rows : (b + 1) * rows]
            yield from spaced(vec_sum.run(vec_local, vec_piece, *parts[2]), 3)
            yield from spaced(vec_op.run(vec_piece, vec_parts, *parts[3]), 2)
            vec_total[...] = (vec_parts[0] + vec_parts[1]) + (vec_parts[2] + vec_parts[3])

        run_together(
            vectors(),
            attention(),
            inputs(),
            spaced(wide_op.run(wide_bf, wide_all, *parts[6]), 6),
            main_move,
        )

    vmem = pl.BlockSpec(memory_space=pltpu.VMEM)
    far = pl.BlockSpec(memory_space=pl.ANY)
    ins = (grad_attn, wide_in, bias_sums, vec_grad, attn_moment, wide_bf, x_part, first_grad)
    return pl.pallas_call(
        kernel,
        out_shape=outs,
        in_specs=[vmem, far, vmem, vmem, far, vmem, far, far],
        out_specs=[vmem] * len(outs),
        scratch_shapes=[c for group in groups for c in group],
        compiler_params=pltpu.CompilerParams(
            collective_id=8, has_side_effects=True, vmem_limit_bytes=62 * 2**20
        ),
        name="muon",
    )(*ins)


def finish(
    n, out_rows, pool_sum, input_grad, attn_all, wide_all, attn_orth, wide_orth, vec_total,
    attn_weight, up_weight, down_weight, vectors, attn_moment, up_moment, down_moment, vector_moment,
    factors, vector_step,
):
    rows = wide_all.shape[2]
    quarter = wide_all.shape[3] // SEQ
    shape = jax.ShapeDtypeStruct
    ins = (
        attn_all, attn_moment, wide_all, up_moment, down_moment, out_rows, input_grad, pool_sum, vec_total,
        vectors, vector_moment, attn_orth, attn_weight, wide_orth, up_weight, down_weight,
    )
    token, pool = shape(out_rows.shape, F32), shape((out_rows.shape[0], quarter), F32)
    attn, up, down, vec = [shape(a.shape, F32) for a in (attn_weight, up_weight, down_weight, vectors)]
    outs = [token, pool, token] + [attn, up, down, vec] * 3
    direct = {0: 5, 2: 6}
    held = [k for k in range(len(outs)) if k not in direct]

    def kernel(*refs):
        far_in, far_out = refs[: len(ins)], refs[len(ins) : len(ins) + len(outs)]
        refs = refs[len(ins) + len(outs) :]
        near_in = refs[: len(ins)]
        near_out = dict(zip(held, refs[len(ins) :]))
        near_out.update({k: near_in[j] for k, j in direct.items()})
        in_sem, out_sem = refs[-2:]
        arriving = [
            pltpu.make_async_copy(a, b, in_sem.at[k]) for k, (a, b) in enumerate(zip(far_in, near_in))
        ]
        leaving = [
            pltpu.make_async_copy(near_out[k], far_out[k], out_sem.at[k]) for k in range(len(outs))
        ]
        for c in arriving:
            c.start()
        (
            attn_all, attn_moment, wide_all, up_moment, down_moment, _, _, pool_sum, vec_total,
            vectors, vector_moment, attn_orth, attn_weight, wide_orth, up_weight, down_weight,
        ) = near_in
        (
            _, pooled, _, attn_grad, up_grad, down_grad, vec_grad, attn_next, up_next, down_next, vec_next,
            attn_new, up_new, down_new, vec_new,
        ) = [near_out[k] for k in range(len(outs))]

        def wait(*ks):
            for k in ks:
                arriving[k].wait()

        def leave(*ks):
            for k in ks:
                leaving[k].start()

        def attn_of(parts, j):
            return jnp.concatenate([unfold(parts[k, j]) for k in range(SEQ)], axis=1).astype(F32)

        wait(0, 1)
        for j in range(4):
            grad = attn_of(attn_all, j)
            attn_grad[j] = grad
            attn_next[j] = matrix_decay * attn_moment[j] + grad
        leave(3, 7)
        wait(2, 3)
        grad = join_up_parts([wide_all[k, 0] for k in range(SEQ)], n).astype(F32)
        up_grad[...] = grad
        up_next[...] = matrix_decay * up_moment[...] + grad
        leave(4, 8)
        wait(4)
        for k in range(SEQ):
            part = pl.ds(k * rows, rows)
            grad = wide_all[k, 1].astype(F32)
            down_grad[part] = grad
            down_next[part] = matrix_decay * down_moment[part] + grad
        leave(5, 9)
        wait(5)
        leave(0)
        wait(6)
        leave(2)
        wait(7, 8, 9, 10)
        s = lax.axis_index("seq")
        pooled[...] = sum(
            jnp.where(s == k, pool_sum[:, k * quarter : (k + 1) * quarter], 0.0) for k in range(SEQ)
        )
        vec_grad[...] = vec_total[...]
        moved = vector_decay * vector_moment[...] + vec_total[...]
        vec_next[...] = moved
        vec_new[...] = vectors[...] - vector_step * moved
        leave(1, 6, 10, 14)
        wait(11, 12)
        for j in range(4):
            attn_new[j] = attn_weight[j] - factors[0] * attn_of(attn_orth, j)
        leave(11)
        wait(13, 14)
        orth = join_up_parts([wide_orth[k, 0] for k in range(SEQ)], n).astype(F32)
        up_new[...] = up_weight[...] - factors[1] * orth
        leave(12)
        wait(15)
        for k in range(SEQ):
            part = pl.ds(k * rows, rows)
            down_new[part] = down_weight[part] - factors[2] * wide_orth[k, 1].astype(F32)
        leave(13)
        for c in leaving:
            c.wait()

    anywhere = pl.BlockSpec(memory_space=pl.ANY)
    return pl.pallas_call(
        kernel,
        out_shape=outs,
        in_specs=[anywhere] * len(ins),
        out_specs=[anywhere] * len(outs),
        scratch_shapes=[pltpu.VMEM(a.shape, a.dtype) for a in ins]
        + [pltpu.VMEM(outs[k].shape, F32) for k in held]
        + [pltpu.SemaphoreType.DMA((len(ins),)), pltpu.SemaphoreType.DMA((len(outs),))],
        compiler_params=pltpu.CompilerParams(vmem_limit_bytes=60 * 2**20),
        name="finish",
    )(*ins)


def step_factor(rows_all, cols_all):
    return matrix_rate * math.sqrt(max(1.0, rows_all / cols_all))


def make_body(n):
    def body(
        layer_input,
        lengths,
        attn_weight,
        up_weight,
        down_weight,
        vectors,
        attn_moment,
        up_moment,
        down_moment,
        vector_moment,
        out_grad,
        pool_grad,
    ):
        rows, span, width = layer_input.shape
        own_rows = width // n
        quarter = width // SEQ
        hidden = up_weight.shape[1]
        hid_q = hidden // SEQ
        hid_own = hidden // n // SEQ
        seq_index = lax.axis_index("seq")

        def attn_quarter(stacked):
            part = lax.dynamic_index_in_dim(
                stacked.reshape(4, own_rows, SEQ, quarter), seq_index, 2, False
            )
            return part

        def up_quarter(matrix):
            return lax.dynamic_index_in_dim(
                matrix.reshape(own_rows, n, SEQ, hid_own), seq_index, 2, False
            ).reshape(own_rows, hid_q)

        def down_quarter(matrix):
            return lax.dynamic_index_in_dim(
                matrix.reshape(SEQ, hid_own, width), seq_index, 0, False
            )

        aligned = own_rows % 16 == 0
        if aligned:
            own = [attn_weight, up_weight, down_weight]
            vec_own = vectors
        else:
            attn_low = attn_quarter(attn_weight).astype(BF16).transpose(1, 0, 2).reshape(own_rows, width)
            up_low = up_quarter(up_weight).astype(BF16)
            down_low = down_quarter(down_weight).astype(BF16)
            vec_low = lax.reduce_precision(vectors, 8, 7)
            placed = lax.dynamic_update_slice(
                jnp.zeros((vectors.shape[0], n, own_rows), F32),
                vec_low[:, None],
                (0, lax.axis_index("batch"), 0),
            ).reshape(-1, width)
            bias_up = lax.dynamic_index_in_dim(
                placed[8:].reshape(n, SEQ, hid_own), seq_index, 1, False
            ).reshape(1, hid_q)
            bias_qv = lax.dynamic_index_in_dim(
                placed[:2].reshape(2, SEQ, quarter), seq_index, 1, False
            )
            blank = jnp.zeros((quarter,), F32)
            bias_qkv = jnp.concatenate([bias_qv[0], blank, bias_qv[1], blank])[None]
            vec_own = jnp.concatenate([placed[2:8], bias_up, bias_qkv])
            own = exchange(
                n, 1, "gather_weights", *[GatherBatch(n, a) for a in (attn_low, up_low, down_low)]
            )
            own = [a.reshape(width, width) for a in own]
        out_rows, pool_sum, input_grad, vec_grad, bias_sums, x_part, *grads = layer(
            n, layer_input, *own, vec_own, pool_grad, lengths, out_grad, up_moment, down_moment
        )
        factors = [
            step_factor(width, width),
            step_factor(width, hidden),
            step_factor(hidden, width),
        ]
        vector_step = vector_rate / math.sqrt(rows * n)
        if aligned:
            grad_attn, wide_bf, wide_in = grads
            attn_all, wide_all, vec_total, input_grad, attn_orth, wide_orth = muon(
                n, grad_attn, wide_in, bias_sums, vec_grad, attn_moment, wide_bf, x_part, input_grad
            )
            return tuple(
                finish(
                    n, out_rows, pool_sum, input_grad, attn_all, wide_all, attn_orth, wide_orth, vec_total,
                    attn_weight, up_weight, down_weight, vectors,
                    attn_moment, up_moment, down_moment, vector_moment, factors, vector_step,
                )
            )
        pooled = lax.dynamic_slice_in_dim(pool_sum, seq_index * quarter, quarter, 1)
        attn_piece, up_piece, down_piece = exchange(
            n, 2, "sum_grads", *[BatchSum(n, a.reshape(n, own_rows, width)) for a in grads]
        )
        bias_sums = bias_sums.reshape(3, quarter)

        vec_head = jnp.zeros((2, SEQ, quarter), F32)
        vec_head = lax.dynamic_update_slice(
            vec_head, bias_sums[jnp.array([0, 2])][:, None], (0, seq_index, 0)
        ).reshape(2, width)
        vec_mid = vec_grad[:6]
        grad_bias_up = vec_grad[6]
        vec_tail = lax.dynamic_update_slice(
            jnp.zeros((n, SEQ, hid_own), F32),
            grad_bias_up.reshape(n, 1, hid_own),
            (0, seq_index, 0),
        ).reshape(-1, width)
        vec_local = jnp.concatenate([vec_head, vec_mid, vec_tail])
        vec_local = vec_local.reshape(-1, n, own_rows).transpose(1, 0, 2)
        (vec_piece,) = exchange(n, 7, "sum_vectors", ScatterBatch(n, vec_local, F32))
        attn_bf = attn_piece.astype(BF16).reshape(own_rows, 4, quarter).transpose(1, 0, 2)
        wide_bf = jnp.stack([up_piece, down_piece]).astype(BF16)
        attn_send = (matrix_decay * attn_quarter(attn_moment) + attn_bf.astype(F32)).astype(BF16)
        wide_moment = jnp.stack([up_quarter(up_moment), down_quarter(down_moment)])
        wide_send = (matrix_decay * wide_moment + wide_bf.astype(F32)).astype(BF16)
        short = -own_rows % 16
        attn_send = jnp.pad(attn_send, ((0, 0), (0, short), (0, 0)))
        wide_send = jnp.pad(wide_send, ((0, 0), (0, short), (0, 0)))
        attn_all, wide_all, vec_parts, attn_orth, wide_orth = exchange(
            n,
            8,
            "muon",
            GatherSeq(n, attn_bf),
            GatherSeq(n, wide_bf),
            GatherSeq(n, vec_piece),
            Muon(n, attn_send, wide_send),
        )
        attn_orth = attn_orth[:, :, :own_rows]
        wide_orth = wide_orth[:, :, :own_rows]

        def join_attn(parts):
            return parts.astype(F32).transpose(1, 2, 0, 3).reshape(4, own_rows, width)

        def join_up(parts):
            return (
                parts.astype(F32)
                .reshape(SEQ, own_rows, n, hid_own)
                .transpose(1, 2, 0, 3)
                .reshape(own_rows, hidden)
            )

        def join_down(parts):
            return parts.astype(F32).reshape(SEQ * hid_own, width)

        attn_grad = join_attn(attn_all)
        up_grad, down_grad = join_up(wide_all[:, 0]), join_down(wide_all[:, 1])
        vector_grad = (vec_parts[0] + vec_parts[1]) + (vec_parts[2] + vec_parts[3])
        attn_next = matrix_decay * attn_moment + attn_grad
        up_next = matrix_decay * up_moment + up_grad
        down_next = matrix_decay * down_moment + down_grad

        attn_new = attn_weight - factors[0] * join_attn(attn_orth)
        up_new = up_weight - factors[1] * join_up(wide_orth[:, 0])
        down_new = down_weight - factors[2] * join_down(wide_orth[:, 1])
        vector_next = vector_decay * vector_moment + vector_grad
        vectors_new = vectors - vector_step * vector_next
        return (
            out_rows,
            pooled,
            input_grad,
            attn_grad,
            up_grad,
            down_grad,
            vector_grad,
            attn_next,
            up_next,
            down_next,
            vector_next,
            attn_new,
            up_new,
            down_new,
            vectors_new,
        )

    return body


def solution(mesh):
    placed = (
        P("batch", "seq", None),
        P("batch"),
        P(None, "batch", None),
        P("batch", None),
        P("batch", None),
        P(None, "batch"),
        P(None, "batch", None),
        P("batch", None),
        P("batch", None),
        P(None, "batch"),
        P("batch", "seq", None),
        P("batch", "seq"),
    )
    return jax.shard_map(
        make_body(mesh.shape["batch"]),
        mesh=mesh,
        in_specs=placed,
        out_specs=(
            P("batch", "seq", None),
            P("batch", "seq"),
            P("batch", "seq", None),
            P(None, "batch", None),
            P("batch", None),
            P("batch", None),
            P(None, "batch"),
            P(None, "batch", None),
            P("batch", None),
            P("batch", None),
            P(None, "batch"),
            P(None, "batch", None),
            P("batch", None),
            P("batch", None),
            P(None, "batch"),
        ),
        check_vma=False,
    )
```
